32 devices in a mesh: dp: 4 (over y, x), seq: 8 (over z, core).
Axes of the slice: x: 2, y: 2, z: 4, core: 2. Of those that a mesh axis runs over, the one named last changes fastest.
Arguments:
- queries: bfloat16 [4, 1024, 512], P('dp', 'seq'), may hold values from -6 to 6
- key_rows: bfloat16 [4, 1024, 512], P('dp', 'seq'), may hold values from -6 to 6
- value_rows: bfloat16 [4, 1024, 512], P('dp', 'seq'), may hold values from -6 to 6
- out_grad: bfloat16 [4, 1024, 1024], P('dp', 'seq'), may hold values from -6 to 6
- out_weight: bfloat16 [512, 1024], P('seq'), may hold values from -0.25 to 0.25
- norm_gain: float32 [256], replicated, may hold values from 0.1 to 1.9
Outputs:
- query_grad: bfloat16 [4, 1024, 512], P('dp', 'seq')
- key_grad: bfloat16 [4, 1024, 512], P('dp', 'seq')
- value_grad: bfloat16 [4, 1024, 512], P('dp', 'seq')
- weight_grad: float32 [512, 1024], P('seq')
The draws below stay inside these ranges and needn't reach their ends.
All inputs are finite; a program needn't handle non-finite values.
Results may differ from the reference program's by a relative error of at most 0.025.
Values may be sent and summed in bfloat16 or wider, within the bound.
No kernel may reach another device: no remote copies, remote signals or barrier semaphores. Data moves between devices by JAX's collectives and lax.ppermute only.
A program may use at most 64 MiB of HBM per device.

```python
import math
import jax
import jax.numpy as jnp
from jax import lax

D = 1024
DH = 128
SOFT_HEADS = 2
LIN_HEADS = 2
HD = 512
WINDOW = 256
HALF = 128
TOKENS = 1024
PLASMIDS = 4


def drawn_pair(key):
    query_key = jax.random.fold_in(key, 101)
    key_key = jax.random.fold_in(key, 202)
    full_shape = (PLASMIDS, TOKENS, HD)
    query_draw = jax.random.truncated_normal(query_key, -4.0, 4.0, full_shape, jnp.float32)
    key_draw = jax.random.truncated_normal(key_key, -4.0, 4.0, full_shape, jnp.float32)
    return (query_draw, key_draw)


def linear_columns(key):
    lin_shape = (PLASMIDS, TOKENS, LIN_HEADS, DH)
    query_hot = jax.random.bernoulli(jax.random.fold_in(key, 404), 4.0 / DH, lin_shape)
    key_pick = jax.random.randint(jax.random.fold_in(key, 505), (PLASMIDS, TOKENS, LIN_HEADS, 1), 0, DH)
    key_hot = jnp.arange(DH, dtype=jnp.int32) == key_pick
    low_lo, low_hi, high_lo, high_hi = (-6.0, -2.0, 2.0, 6.0)
    boost_lo, boost_hi = (1.5, 3.5)
    value_base = jax.random.truncated_normal(jax.random.fold_in(key, 1010), -5.0, 5.0, lin_shape, jnp.float32)
    query_low = jax.random.uniform(jax.random.fold_in(key, 606), lin_shape, jnp.float32, low_lo, low_hi)
    query_high = jax.random.uniform(jax.random.fold_in(key, 707), lin_shape, jnp.float32, high_lo, high_hi)
    key_low = jax.random.uniform(jax.random.fold_in(key, 808), lin_shape, jnp.float32, low_lo, low_hi)
    key_high = jax.random.uniform(jax.random.fold_in(key, 909), lin_shape, jnp.float32, high_lo, high_hi)
    value_boost = jax.random.uniform(jax.random.fold_in(key, 1111), lin_shape, jnp.float32, boost_lo, boost_hi)
    query_lin = jnp.where(query_hot, query_high, query_low)
    key_lin = jnp.where(key_hot, key_high, key_low)
    value_lin = jnp.where(key_hot, value_boost, value_base)
    flat_shape = (PLASMIDS, TOKENS, LIN_HEADS * DH)
    return (query_lin.reshape(flat_shape), key_lin.reshape(flat_shape), value_lin.reshape(flat_shape))


def draw_queries(key, part):
    soft = SOFT_HEADS * DH
    soft_part = drawn_pair(key)[0][:, :, :soft]
    lin_part = linear_columns(key)[0]
    return jnp.concatenate([soft_part, lin_part], axis=2).astype(jnp.bfloat16)


def draw_key_rows(key, part):
    soft = SOFT_HEADS * DH
    soft_part = drawn_pair(key)[1][:, :, :soft]
    lin_part = linear_columns(key)[1]
    return jnp.concatenate([soft_part, lin_part], axis=2).astype(jnp.bfloat16)


def draw_value_rows(key, part):
    soft = SOFT_HEADS * DH
    soft_shape = (PLASMIDS, TOKENS, soft)
    soft_part = jax.random.truncated_normal(jax.random.fold_in(key, 1212), -6.0, 6.0, soft_shape, jnp.float32)
    lin_part = linear_columns(key)[2]
    return jnp.concatenate([soft_part, lin_part], axis=2).astype(jnp.bfloat16)


def steps_of(rng, dims, split, least, largest):
    def one(dim, blocks):
        draws = jax.random.uniform(jax.random.fold_in(jax.random.fold_in(rng, 6), dim), (blocks,), jnp.float32, least / len(split), largest / len(split))
        return jnp.repeat(jnp.exp(draws), dims[dim] // blocks).reshape((-1,) + (1,) * (len(dims) - dim - 1))

    level = one(*split[0])
    for cut in split[1:]:
        level = level * one(*cut)
    return level


def normal_values(rng, shape, spread, bound, shards=(), held_as=jnp.bfloat16):
    entries = spread * jax.random.normal(rng, shape, jnp.float32)
    if shards:
        entries = entries * steps_of(rng, shape, shards, -0.22, 0.18)
    return jnp.clip(entries, -bound, bound).astype(held_as)


def setup_inputs(seed: int = 0) -> dict:
    seeds = jax.random.split(jax.random.key(seed), 7)
    queries = draw_queries(jax.random.fold_in(seeds[6], 71), 0)
    key_rows = draw_key_rows(jax.random.fold_in(seeds[6], 71), 0)
    value_rows = draw_value_rows(jax.random.fold_in(seeds[6], 71), 0)
    out_grad = normal_values(seeds[3], (PLASMIDS, TOKENS, D), 1.0, 6.0, ((0, 4), (1, 8)))
    out_weight = normal_values(seeds[4], (HD, D), HD ** -0.5, 0.25, ((0, 8),))
    norm_gain = jnp.clip(1.0 + 0.18 * jax.random.normal(seeds[5], (LIN_HEADS * DH,), jnp.float32), 0.1, 1.9)
    return dict(queries=queries, key_rows=key_rows, value_rows=value_rows, out_grad=out_grad, out_weight=out_weight, norm_gain=norm_gain)


norm_eps = 1e-06

def unit_plus(values):
    return jnp.where(values > 0, values + 1.0, jnp.exp(jnp.minimum(values, 0.0)))

def unit_slope(values):
    return jnp.where(values > 0, 1.0, jnp.exp(jnp.minimum(values, 0.0)))

def one_plasmid(query_all, key_all, value_all, grad_out, out_weight, norm_gain):
    soft = SOFT_HEADS * DH
    factor = DH ** (-0.5)
    highest = lax.Precision.HIGHEST
    d_attn = jnp.dot(grad_out, out_weight.T, preferred_element_type=jnp.float32).astype(jnp.bfloat16)
    query_lin = query_all[:, soft:].astype(jnp.float32).reshape(TOKENS, LIN_HEADS, DH)
    key_lin = key_all[:, soft:].astype(jnp.float32).reshape(TOKENS, LIN_HEADS, DH)
    value_lin = value_all[:, soft:].astype(jnp.float32).reshape(TOKENS, LIN_HEADS, DH)
    phi_query = unit_plus(query_lin)
    phi_key = unit_plus(key_lin)
    lin_state = jnp.einsum('jha,jhb->hab', phi_key, value_lin, precision=highest)
    lin_u = jnp.einsum('iha,hab->ihb', phi_query, lin_state, precision=highest)
    lin_r = lax.rsqrt(lax.optimization_barrier(jnp.mean(lin_u * lin_u, axis=2, keepdims=True)) + norm_eps)
    gain_heads = norm_gain.reshape(LIN_HEADS, DH)
    attn_lin = (gain_heads * lin_u * lin_r).astype(jnp.bfloat16)
    lin_grad = gain_heads * d_attn[:, soft:].astype(jnp.float32).reshape(TOKENS, LIN_HEADS, DH)
    grad_u = lin_r * lin_grad - lin_u * lin_r ** 3 * lax.optimization_barrier(jnp.mean(lin_grad * lin_u, axis=2, keepdims=True))
    dstate = jnp.einsum('iha,ihb->hab', phi_query, grad_u, precision=highest)
    dq_lin = jnp.einsum('ihb,hab->iha', grad_u, lin_state, precision=highest) * unit_slope(query_lin)
    dk_lin = jnp.einsum('jhb,hab->jha', value_lin, dstate, precision=highest) * unit_slope(key_lin)
    dv_lin = jnp.einsum('jha,hab->jhb', phi_key, dstate, precision=highest)
    soft_query = query_all[:, :soft]
    soft_key = key_all[:, :soft]
    soft_value = value_all[:, :soft]
    soft_dattn = d_attn[:, :soft]
    span_rows = 3 * HALF
    row_pos = lax.broadcasted_iota(jnp.int32, (HALF, span_rows), 0)
    col_pos = lax.broadcasted_iota(jnp.int32, (HALF, span_rows), 1)
    inside = (col_pos >= row_pos) & (col_pos < row_pos + WINDOW)

    def block_step(totals, block_index):
        key_total, value_total = totals
        first_row = block_index * HALF
        key_index = (first_row - HALF + jnp.arange(span_rows, dtype=jnp.int32)) % TOKENS
        q_block = lax.dynamic_slice_in_dim(soft_query, first_row, HALF, 0).astype(jnp.float32).reshape(HALF, SOFT_HEADS, DH)
        da_block = lax.dynamic_slice_in_dim(soft_dattn, first_row, HALF, 0).astype(jnp.float32).reshape(HALF, SOFT_HEADS, DH)
        k_span = jnp.take(soft_key, key_index, axis=0).astype(jnp.float32).reshape(span_rows, SOFT_HEADS, DH)
        v_span = jnp.take(soft_value, key_index, axis=0).astype(jnp.float32).reshape(span_rows, SOFT_HEADS, DH)
        scores = jnp.einsum('ihd,jhd->hij', q_block, k_span) * factor
        scores = jnp.where(inside, scores, -1e+30)
        row_peak = lax.optimization_barrier(jnp.max(scores, axis=2, keepdims=True))
        exp_terms = jnp.where(inside, jnp.exp(scores - row_peak), 0.0)
        attn_probs = exp_terms / lax.optimization_barrier(jnp.sum(exp_terms, axis=2, keepdims=True))
        probs_low = attn_probs.astype(jnp.bfloat16)
        probs_wide = probs_low.astype(jnp.float32)
        attn_soft = jnp.einsum('hij,jhd->ihd', probs_wide, v_span).astype(jnp.bfloat16)
        dprob = jnp.einsum('ihd,jhd->hij', da_block, v_span)
        row_delta = lax.optimization_barrier(jnp.sum(da_block * attn_soft.astype(jnp.float32), axis=2))
        dscore = (attn_probs * (dprob - row_delta.T[:, :, None])).astype(jnp.bfloat16).astype(jnp.float32)
        dq_soft = jnp.einsum('hij,jhd->ihd', dscore, k_span) * factor
        dk_span = jnp.einsum('hij,ihd->jhd', dscore, q_block) * factor
        dv_span = jnp.einsum('hij,ihd->jhd', probs_wide, da_block)
        key_total = key_total.at[key_index].add(dk_span.reshape(span_rows, soft))
        value_total = value_total.at[key_index].add(dv_span.reshape(span_rows, soft))
        return ((key_total, value_total), (attn_soft.reshape(HALF, soft), dq_soft.reshape(HALF, soft)))
    zeros_init = jnp.zeros((TOKENS, soft), jnp.float32)
    block_ids = jnp.arange(TOKENS // HALF, dtype=jnp.int32)
    (dk_soft, dv_soft), (attn_soft, dq_soft) = lax.scan(block_step, (zeros_init, zeros_init), block_ids)
    attn = jnp.concatenate([attn_soft.reshape(TOKENS, soft), attn_lin.reshape(TOKENS, LIN_HEADS * DH)], axis=1)
    weight_term = jnp.dot(attn.T, grad_out, preferred_element_type=jnp.float32)
    query_grad = jnp.concatenate([dq_soft.reshape(TOKENS, soft), dq_lin.reshape(TOKENS, LIN_HEADS * DH)], axis=1).astype(jnp.bfloat16)
    key_grad = jnp.concatenate([dk_soft, dk_lin.reshape(TOKENS, LIN_HEADS * DH)], axis=1).astype(jnp.bfloat16)
    value_grad = jnp.concatenate([dv_soft, dv_lin.reshape(TOKENS, LIN_HEADS * DH)], axis=1).astype(jnp.bfloat16)
    return (query_grad, key_grad, value_grad, weight_term)

def reference(queries, key_rows, value_rows, out_grad, out_weight, norm_gain):
    query_list = []
    key_list = []
    value_list = []
    weight_sum = jnp.zeros((HD, D), jnp.float32)
    for plasmid in range(PLASMIDS):
        query_grad, key_grad, value_grad, weight_term = one_plasmid(queries[plasmid], key_rows[plasmid], value_rows[plasmid], out_grad[plasmid], out_weight, norm_gain)
        query_list.append(query_grad)
        key_list.append(key_grad)
        value_list.append(value_grad)
        weight_sum = weight_sum + weight_term
    weight_grad = weight_sum * (1.0 / math.sqrt(PLASMIDS * TOKENS))
    return (jnp.stack(query_list), jnp.stack(key_list), jnp.stack(value_list), weight_grad)
```

```python
import functools
import math

import jax
import jax.numpy as jnp
from jax import lax
from jax.experimental import pallas as pl
from jax.experimental.pallas import tpu as pltpu
from jax.sharding import PartitionSpec as P

DH = 128
SOFT_HEADS = 2
LIN_HEADS = 2
HEADS = SOFT_HEADS + LIN_HEADS
WINDOW = 256
HALF = 128
norm_eps = 1e-06
FACTOR = DH ** (-0.5)
BF = jnp.bfloat16
F32 = jnp.float32
NN = (((1,), (0,)), ((), ()))
NT = (((1,), (1,)), ((), ()))
TN = (((0,), (0,)), ((), ()))


def unit_plus(values):
    return jnp.where(values > 0, values + 1.0, jnp.exp(jnp.minimum(values, 0.0)))


def unit_slope(values):
    return jnp.where(values > 0, 1.0, jnp.exp(jnp.minimum(values, 0.0)))


def mm(a, b, dims=NN):
    return lax.dot_general(a, b, dims, preferred_element_type=F32)


def halves(x):
    high = x.astype(BF)
    return high, (x - high.astype(F32)).astype(BF)


def mm3(a, b, dims=NN):
    a_high, a_low = halves(a)
    b_high, b_low = halves(b)
    return mm(a_high, b_high, dims) + (mm(a_high, b_low, dims) + mm(a_low, b_high, dims))


def mm2(a, b, dims=NN):
    a_high, a_low = halves(a)
    return mm(a_high, b, dims) + mm(a_low, b, dims)


def at(start, size=DH):
    return pl.ds(pl.multiple_of(start, size), size)


def places():
    seq = lax.axis_index("seq")
    return lax.rem(seq, 2), lax.div(seq, 2), lax.axis_index("dp")


def call(kernel, name, outs, args, scratch=(), flops=0):
    vmem = pl.BlockSpec(memory_space=pltpu.VMEM)
    size = sum(math.prod(x.shape) * x.dtype.itemsize for x in list(args) + list(outs))
    return pl.pallas_call(
        kernel,
        name=name,
        out_shape=list(outs),
        in_specs=[vmem] * len(args),
        out_specs=[vmem] * len(outs),
        scratch_shapes=list(scratch),
        compiler_params=pltpu.CompilerParams(vmem_limit_bytes=24 * 2**20),
        cost_estimate=pl.CostEstimate(flops=flops, bytes_accessed=size, transcendentals=0),
    )(*args)


def like(shape, dtype):
    return jax.ShapeDtypeStruct(shape, dtype)


def pack_kernel(q, k, v, lin_other, mixed_other, kv_other, kv_mine):
    core, _, _ = places()
    mine, other = core * DH, (1 - core) * DH
    soft = SOFT_HEADS * DH
    lin_other[:, :DH] = k[:, at(soft + other)]
    lin_other[:, DH:] = v[:, at(soft + other)]
    mixed_other[:, :DH] = q[:, at(other)]
    mixed_other[:, DH : 2 * DH] = q[:, at(soft + other)]
    mixed_other[:, 2 * DH : 3 * DH] = k[:, at(other)]
    mixed_other[:, 3 * DH :] = v[:, at(other)]
    kv_other[:, :DH] = k[:, at(other)]
    kv_other[:, DH:] = v[:, at(other)]
    kv_mine[:, :DH] = k[:, at(mine)]
    kv_mine[:, DH:] = v[:, at(mine)]


def state_kernel(k, v, lin_recv, state, state_low):
    core, _, _ = places()
    mine = SOFT_HEADS * DH + core * DH
    own = mm2(unit_plus(k[:, at(mine)].astype(F32)), v[:, at(mine)], TN)
    far = mm2(unit_plus(lin_recv[:, :DH].astype(F32)), lin_recv[:, DH:], TN)
    total = own + far
    state[...] = total
    state_low[...] = total.astype(BF)


def soft_forward_kernel(
    q, k, v, og, mixed, og_recv, near, far,
    qs, ks, vs, ogs, probs, attn, *wg,
):
    core, _, dp = places()
    rows = q.shape[0]
    mine = core * DH
    own, pair = core * rows, (1 - core) * rows
    qs[at(own, rows), :] = q[:, at(mine)]
    qs[at(pair, rows), :] = mixed[:, :DH]
    ks[at(HALF + own), :] = k[:, at(mine)]
    vs[at(HALF + own), :] = v[:, at(mine)]
    ks[at(HALF + pair), :] = mixed[:, 2 * DH : 3 * DH]
    vs[at(HALF + pair), :] = mixed[:, 3 * DH :]
    near_at, far_at = core * (HALF + 2 * rows), (1 - core) * (HALF + 2 * rows)
    ks[at(near_at), :] = near[:, :DH]
    vs[at(near_at), :] = near[:, DH:]
    ks[at(far_at), :] = far[:, :DH]
    vs[at(far_at), :] = far[:, DH:]
    ogs[at(own, rows), :] = og[...]
    ogs[at(pair, rows), :] = og_recv[...]
    span = rows + 2 * HALF
    row_pos = lax.broadcasted_iota(jnp.int32, (rows, span), 0)
    col_pos = lax.broadcasted_iota(jnp.int32, (rows, span), 1)
    inside = (col_pos >= row_pos) & (col_pos < row_pos + WINDOW)
    for block in range(2):
        first = block * rows
        scores = mm(qs[first : first + rows, :], ks[first : first + span, :], NT) * FACTOR
        scores = jnp.where(inside, scores, -1e30)
        peak = jnp.max(scores, axis=1, keepdims=True)
        terms = jnp.where(inside, jnp.exp(scores - peak), 0.0)
        share = terms / jnp.sum(terms, axis=1, keepdims=True)
        probs[block] = share
        attn[first : first + rows, :] = mm(share.astype(BF), vs[first : first + span, :]).astype(BF)
    weight_parts(attn[...], ogs, dp, wg)


def weight_parts(attn, ogs, dp, outs):
    if len(outs) == 1:
        outs[0][...] = mm(attn, ogs[...], TN)
        return
    width = ogs.shape[1] // len(outs)
    for step, out in enumerate(outs):
        part = mm(attn, ogs[:, at((dp ^ step) * width, width)], TN)
        out[...] = part.astype(out.dtype)


def lin_forward_kernel(count, state, *refs):
    others = refs[:count]
    q, mixed, ogs, gain, u_out, total_out = refs[count : count + 6]
    wg = refs[count + 6 :]
    core, _, dp = places()
    total = state[...]
    for other in others:
        total = total + other[...].astype(F32)
    total_out[...] = total
    rows = q.shape[0]
    own, pair = core * rows, (1 - core) * rows
    mine = SOFT_HEADS * DH + core * DH
    u_out[at(own, rows), :] = mm3(unit_plus(q[:, at(mine)].astype(F32)), total)
    u_out[at(pair, rows), :] = mm3(unit_plus(mixed[:, DH : 2 * DH].astype(F32)), total)
    u = u_out[...]
    r = lax.rsqrt(jnp.mean(u * u, axis=1, keepdims=True) + norm_eps)
    attn = (gain[pl.ds(core, 1), :] * u * r).astype(BF)
    weight_parts(attn, ogs, dp, wg)


def dattn_kernel(count, *refs):
    ogs, out, weights = refs[count : count + 3]
    core, z, dp = places()
    if count == 1:
        weights[...] = refs[0][...]
    else:
        for step in range(count):
            parts, rows, width = refs[step].shape
            for index in range(parts):
                weights[at((z ^ index) * rows, rows), at((dp ^ step) * width, width)] = refs[step][index]
    out[...] = mm(ogs[...], weights[...], NT)


def lin_backward_kernel(
    u, total, dattn, q, mixed, gain, dq_own, dq_pair, dstate, dstate_low, grads
):
    core, _, _ = places()
    rows = q.shape[0]
    mine = SOFT_HEADS * DH + core * DH
    u_all = u[...]
    r = lax.rsqrt(jnp.mean(u_all * u_all, axis=1, keepdims=True) + norm_eps)
    lin_grad = gain[pl.ds(core, 1), :] * dattn[:, DH:]
    grad_u = r * lin_grad - u_all * (r * r * r) * jnp.mean(lin_grad * u_all, axis=1, keepdims=True)
    grads[...] = grad_u
    total_state = total[...]
    result = jnp.zeros(dstate.shape, F32)
    own, pair = core * rows, (1 - core) * rows
    for first, values, out in (
        (own, q[:, at(mine)], dq_own),
        (pair, mixed[:, DH : 2 * DH], dq_pair),
    ):
        wide = values.astype(F32)
        part = grads[at(first, rows), :]
        result = result + mm3(unit_plus(wide), part, TN)
        out[...] = (mm3(part, total_state, NT) * unit_slope(wide)).astype(BF)
    dstate[...] = result
    dstate_low[...] = result.astype(BF)


def soft_backward_kernel(
    qs, ks, vs, probs, attn, dattn, dq_own, dk_own, dv_own, to_pair, to_near, to_far,
    dq_all, dk_all, dv_all,
):
    core, _, _ = places()
    rows = qs.shape[0] // 2
    span = rows + 2 * HALF
    dk_all[...] = jnp.zeros_like(dk_all)
    dv_all[...] = jnp.zeros_like(dv_all)
    for block in range(2):
        first = block * rows
        here, window = slice(first, first + rows), slice(first, first + span)
        grad = dattn[here, :DH].astype(BF)
        share = probs[block]
        delta = jnp.sum(grad.astype(F32) * attn[here, :].astype(F32), axis=1, keepdims=True)
        dscore = (share * (mm(grad, vs[window, :], NT) - delta)).astype(BF)
        dq_all[here, :] = mm(dscore, ks[window, :]) * FACTOR
        dk_all[window, :] += mm(dscore, qs[here, :], TN) * FACTOR
        dv_all[window, :] += mm(share.astype(BF), grad, TN)
    own, pair = core * rows, (1 - core) * rows
    near_at, far_at = core * (HALF + 2 * rows), (1 - core) * (HALF + 2 * rows)
    dq_own[...] = dq_all[at(own, rows), :].astype(BF)
    dk_own[...] = dk_all[at(HALF + own), :]
    dv_own[...] = dv_all[at(HALF + own), :]
    to_pair[:, :DH] = dq_all[at(pair, rows), :].astype(BF)
    to_pair[:, DH : 2 * DH] = dk_all[at(HALF + pair), :].astype(BF)
    to_pair[:, 2 * DH :] = dv_all[at(HALF + pair), :].astype(BF)
    to_near[:, :DH] = dk_all[at(near_at), :].astype(BF)
    to_near[:, DH:] = dv_all[at(near_at), :].astype(BF)
    to_far[:, :DH] = dk_all[at(far_at), :].astype(BF)
    to_far[:, DH:] = dv_all[at(far_at), :].astype(BF)


def lin_final_kernel(count, dstate, *refs):
    others = refs[:count]
    k, v, lin_recv, own_out, pair_out = refs[count:]
    core, _, _ = places()
    total = dstate[...]
    for other in others:
        total = total + other[...].astype(F32)
    mine = SOFT_HEADS * DH + core * DH
    for keys, values, out in (
        (k[:, at(mine)], v[:, at(mine)], own_out),
        (lin_recv[:, :DH], lin_recv[:, DH:], pair_out),
    ):
        wide = keys.astype(F32)
        high, low = halves(total)
        dk = mm(values, high, NT) + mm(values, low, NT)
        out[:, :DH] = (dk * unit_slope(wide)).astype(BF)
        out[:, DH:] = mm3(unit_plus(wide), total).astype(BF)


def output_kernel(
    dq_soft, dk_soft, dv_soft, dq_lin, lin_own, soft_pair, dq_pair, lin_pair, near, far,
    dq, dk, dv,
):
    core, _, _ = places()
    soft = SOFT_HEADS * DH
    mine, other = core * DH, (1 - core) * DH
    dq[0, :, at(mine)] = dq_soft[...]
    dq[0, :, at(other)] = soft_pair[:, :DH]
    dq[0, :, at(soft + mine)] = dq_lin[...]
    dq[0, :, at(soft + other)] = dq_pair[...]
    for out, own, first in ((dk, dk_soft, 0), (dv, dv_soft, DH)):
        cols = slice(first, first + DH)
        out[0, :, at(mine)] = (own[...] + far[:, cols].astype(F32)).astype(BF)
        out[0, :, at(other)] = (
            soft_pair[:, DH + first : 2 * DH + first].astype(F32) + near[:, cols].astype(F32)
        ).astype(BF)
        out[0, :, at(soft + mine)] = lin_own[:, cols]
        out[0, :, at(soft + other)] = lin_pair[:, cols]


def weight_rows_kernel(count, *refs):
    outs = refs[2 * count : 3 * count]
    sums = refs[3 * count]
    _, z, _ = places()
    rows = outs[0].shape[0]
    for group in range(2):
        total = refs[group * count][...]
        for other in refs[group * count + 1 : (group + 1) * count]:
            total = total + other[...].astype(F32)
        for half in range(2):
            sums[2 * group + half] = total[half * rows : (half + 1) * rows]
    for step, out in enumerate(outs):
        out[...] = sums[z ^ step].astype(out.dtype)


def weight_sum_kernel(scale, *refs):
    total = refs[0][...].astype(F32)
    for other in refs[1:-1]:
        total = total + other[...].astype(F32)
    refs[-1][...] = total * scale


def weight_join_kernel(*refs):
    _, _, dp = places()
    out = refs[-1]
    width = refs[0].shape[1]
    for step, part in enumerate(refs[:-1]):
        out[:, at((dp ^ step) * width, width)] = part[...].astype(F32)


def body(n_dp, n_seq, queries, key_rows, value_rows, out_grad, out_weight, norm_gain):
    q, k, v, og = queries[0], key_rows[0], value_rows[0], out_grad[0]
    rows, model = og.shape
    chips = n_seq // 2
    every = range(n_seq)
    pair = [(s, s ^ 1) for s in every]
    to_near = [(s, (s + 1) % n_seq if s % 2 else (s - 1) % n_seq) for s in every]
    to_far = [(s, (s + 2) % n_seq if s % 2 else (s - 2) % n_seq) for s in every]
    from_far = [(target, source) for source, target in to_far]
    core = lax.axis_index("seq") % 2
    direct = chips == HEADS and n_dp == 4
    count = n_dp if direct else 1
    move = functools.partial(lax.ppermute, axis_name="seq")

    def over_chips(low, wide):
        if direct:
            return [
                move(low, perm=[(s, s ^ (2 * step)) for s in every]) for step in range(1, chips)
            ]
        slots = jnp.stack([jnp.where(core == head, wide, 0.0) for head in range(2)])
        total = lax.psum(slots, "seq")
        return [jnp.where(core == 0, total[0], total[1]) - wide]

    def over_dp(value):
        return [
            lax.ppermute(value if not isinstance(value, list) else value[step], "dp",
                         [(d, d ^ step) for d in range(n_dp)])
            for step in range(1, n_dp)
        ]

    og_recv = move(og, perm=pair)
    if direct:
        width = model // n_dp
        w_part = lax.dynamic_slice_in_dim(out_weight, lax.axis_index("dp") * width, width, axis=1)
        w_got = []
        for step in range(chips):
            perm = []
            for s in every:
                z, b = s // 2, s % 2
                perm.append((s, 2 * (((z // 2) * 2 + b) ^ step) + z % 2))
            w_got.append(move(w_part, perm=perm))
        w_mine = jnp.stack(w_got)
        weights = [w_mine] + over_dp(w_mine)
    else:
        w_all = lax.all_gather(out_weight, "seq", axis=0, tiled=True).reshape(2, 2, DH, model)
        weights = [jnp.where(core == 0, w_all[:, 0], w_all[:, 1]).reshape(2 * DH, model)]

    lin_other, mixed_other, kv_other, kv_mine = call(
        pack_kernel, "pack",
        [like((rows, 2 * DH), BF), like((rows, 4 * DH), BF), like((rows, 2 * DH), BF), like((rows, 2 * DH), BF)],
        [q, k, v],
    )
    lin_recv = move(lin_other, perm=pair)
    near = move(kv_other, perm=to_near)
    far = move(kv_mine, perm=to_far)
    mixed = move(mixed_other, perm=pair)

    state, state_low = call(
        state_kernel, "state", [like((DH, DH), F32), like((DH, DH), BF)], [k, v, lin_recv],
        flops=4 * 2 * rows * DH * DH,
    )
    state_others = over_chips(state_low, state)

    span = 2 * rows + 2 * HALF
    part = model // count
    wg_shapes = [like((DH, part), F32)] + [like((DH, part), BF)] * (count - 1)
    wg_flops = 2 * 2 * rows * DH * model
    qs, ks, vs, ogs, probs, attn, *wg_soft = call(
        soft_forward_kernel, "soft_forward",
        [
            like((2 * rows, DH), BF), like((span, DH), BF), like((span, DH), BF),
            like((2 * rows, model), BF), like((2, rows, rows + 2 * HALF), F32), like((2 * rows, DH), BF),
        ] + wg_shapes,
        [q, k, v, og, mixed, og_recv, near, far],
        flops=wg_flops,
    )
    gain = norm_gain.reshape(LIN_HEADS, DH)
    u, total, *wg_lin = call(
        functools.partial(lin_forward_kernel, len(state_others)), "lin_forward",
        [like((2 * rows, DH), F32), like((DH, DH), F32)] + wg_shapes,
        [state] + state_others + [q, mixed, ogs, gain],
        flops=wg_flops,
    )
    dattn = call(
        functools.partial(dattn_kernel, count), "d_attn", [like((2 * rows, 2 * DH), F32)],
        weights + [ogs], scratch=[pltpu.VMEM((2 * DH, model), BF)],
        flops=2 * wg_flops,
    )[0]
    if direct:
        wg_soft = wg_soft[:1] + over_dp(wg_soft)
        wg_lin = wg_lin[:1] + over_dp(wg_lin)

    dq_lin, dq_lin_pair, dstate, dstate_low = call(
        lin_backward_kernel, "lin_backward",
        [like((rows, DH), BF), like((rows, DH), BF), like((DH, DH), F32), like((DH, DH), BF)],
        [u, total, dattn, q, mixed, gain],
        scratch=[pltpu.VMEM((2 * rows, DH), F32)],
        flops=wg_flops,
    )
    dstate_others = over_chips(dstate_low, dstate)
    dq_soft, dk_soft, dv_soft, soft_pair, back_near, back_far = call(
        soft_backward_kernel, "soft_backward",
        [
            like((rows, DH), BF), like((rows, DH), F32), like((rows, DH), F32),
            like((rows, 3 * DH), BF), like((rows, 2 * DH), BF), like((rows, 2 * DH), BF),
        ],
        [qs, ks, vs, probs, attn, dattn],
        scratch=[pltpu.VMEM((2 * rows, DH), F32), pltpu.VMEM((span, DH), F32), pltpu.VMEM((span, DH), F32)],
        flops=wg_flops,
    )
    dq_lin_pair = move(dq_lin_pair, perm=pair)
    soft_pair = move(soft_pair, perm=pair)
    back_near = move(back_near, perm=to_near)
    back_far = move(back_far, perm=from_far)

    scale = 1.0 / math.sqrt(n_dp * n_seq * rows)
    if direct:
        pieces = call(
            functools.partial(weight_rows_kernel, count), "weight_rows",
            [like((DH // 2, part), BF)] * chips,
            list(wg_soft) + list(wg_lin),
            scratch=[pltpu.VMEM((chips, DH // 2, part), F32)],
        )
        got = []
        for step in range(chips):
            perm = []
            for s in every:
                m = (s // 2) ^ step
                perm.append((s, 2 * (2 * (m // 2) + s % 2) + m % 2))
            got.append(move(pieces[step], perm=perm))
        summed = call(
            functools.partial(weight_sum_kernel, scale), "weight_sum", [like((DH // 2, part), F32)], got
        )[0]
        weight_grad = call(
            weight_join_kernel, "weight_join", [like((DH // 2, model), F32)], [summed] + over_dp(summed)
        )[0]
    else:
        groups = jnp.stack([wg_soft[0], wg_lin[0]])
        slots = jnp.stack([jnp.where(core == head, groups, 0.0) for head in range(2)], axis=1)
        local = lax.psum_scatter(
            slots.reshape(HEADS * DH, model), "seq", scatter_dimension=0, tiled=True
        )
        weight_grad = lax.psum(local, "dp") * scale

    lin_own, lin_pair = call(
        functools.partial(lin_final_kernel, len(dstate_others)), "lin_final",
        [like((rows, 2 * DH), BF), like((rows, 2 * DH), BF)],
        [dstate] + dstate_others + [k, v, lin_recv],
        flops=wg_flops // 4,
    )
    lin_pair = move(lin_pair, perm=pair)
    shape = like((1, rows, HEADS * DH), BF)
    dq, dk, dv = call(
        output_kernel, "outputs", [shape] * 3,
        [dq_soft, dk_soft, dv_soft, dq_lin, lin_own, soft_pair, dq_lin_pair, lin_pair, back_near, back_far],
    )
    return dq, dk, dv, weight_grad


def solution(mesh):
    return jax.shard_map(
        functools.partial(body, mesh.shape["dp"], mesh.shape["seq"]),
        mesh=mesh,
        in_specs=(
            P("dp", "seq", None),
            P("dp", "seq", None),
            P("dp", "seq", None),
            P("dp", "seq", None),
            P("seq", None),
            P(),
        ),
        out_specs=(
            P("dp", "seq", None),
            P("dp", "seq", None),
            P("dp", "seq", None),
            P("seq", None),
        ),
        check_vma=False,
    )
```

```python
import functools
import math

import jax
import jax.numpy as jnp
from jax import lax
from jax.experimental import pallas as pl
from jax.experimental.pallas import tpu as pltpu
from jax.sharding import Mesh
from jax.sharding import PartitionSpec as P

DH = 128
SOFT_HEADS = 2
LIN_HEADS = 2
HEADS = SOFT_HEADS + LIN_HEADS
WINDOW = 256
HALF = 128
norm_eps = 1e-06
FACTOR = DH ** (-0.5)
BF = jnp.bfloat16
F32 = jnp.float32
NN = (((1,), (0,)), ((), ()))
NT = (((1,), (1,)), ((), ()))
TN = (((0,), (0,)), ((), ()))


def unit_plus(values):
    return jnp.where(values > 0, values + 1.0, jnp.exp(jnp.minimum(values, 0.0)))


def unit_slope(values):
    return jnp.where(values > 0, 1.0, jnp.exp(jnp.minimum(values, 0.0)))


def mm(a, b, dims=NN):
    return lax.dot_general(a, b, dims, preferred_element_type=F32)


def halves(x):
    high = x.astype(BF)
    return high, (x - high.astype(F32)).astype(BF)


def mm3(a, b, dims=NN):
    a_high, a_low = halves(a)
    b_high, b_low = halves(b)
    return mm(a_high, b_high, dims) + (mm(a_high, b_low, dims) + mm(a_low, b_high, dims))


def mm2(a, b, dims=NN):
    a_high, a_low = halves(a)
    return mm(a_high, b, dims) + mm(a_low, b, dims)


def at(start, size=DH):
    return pl.ds(pl.multiple_of(start, size), size)


def places():
    return lax.axis_index("core"), lax.axis_index("z"), lax.axis_index("dp")


def call(kernel, name, outs, args, scratch=(), flops=0, outside=0):
    vmem = pl.BlockSpec(memory_space=pltpu.VMEM)
    size = sum(math.prod(x.shape) * x.dtype.itemsize for x in list(args) + list(outs))
    return pl.pallas_call(
        kernel,
        name=name,
        out_shape=list(outs),
        in_specs=[pl.BlockSpec(memory_space=pl.ANY)] * outside + [vmem] * (len(args) - outside),
        out_specs=[vmem] * len(outs),
        scratch_shapes=list(scratch),
        compiler_params=pltpu.CompilerParams(vmem_limit_bytes=24 * 2**20),
        cost_estimate=pl.CostEstimate(flops=flops, bytes_accessed=size, transcendentals=0),
    )(*args)


def like(shape, dtype):
    return jax.ShapeDtypeStruct(shape, dtype)


QS, KS, VS, QL, KL, VL = (slice(i * DH, (i + 1) * DH) for i in range(6))


def pack_kernel(q, k, v, w, mine_out, other_out, near_out, far_out, w_out, sems):
    core, _, dp = places()
    mine, other = core * DH, (1 - core) * DH
    soft = SOFT_HEADS * DH
    copies = []

    def fetch(source, target):
        copy = pltpu.make_async_copy(source, target, sems.at[len(copies)])
        copy.start()
        copies.append(copy)

    for index, array in enumerate((q, k, v)):
        for group in range(2):
            cols = slice((3 * group + index) * DH, (3 * group + index + 1) * DH)
            fetch(array.at[:, at(soft * group + other)], other_out.at[:, cols])
            fetch(array.at[:, at(soft * group + mine)], mine_out.at[:, cols])
    for index, array in enumerate((k, v)):
        cols = slice(index * DH, (index + 1) * DH)
        fetch(array.at[:, at(other)], near_out.at[:, cols])
        fetch(array.at[:, at(mine)], far_out.at[:, cols])
    width = w_out.shape[1]
    fetch(w.at[:, at(dp * width, width)], w_out)
    for copy in copies:
        copy.wait()


def state_kernel(mine, pair, state, state_low):
    total = mm2(unit_plus(mine[:, KL].astype(F32)), mine[:, VL], TN) + mm2(
        unit_plus(pair[:, KL].astype(F32)), pair[:, VL], TN
    )
    state[...] = total
    for index in range(state_low.shape[0]):
        state_low[index] = total.astype(BF)


def soft_forward_kernel(mine, pair, og, og_recv, near, far, qs, ks, vs, ogs, probs, attn, wg):
    core, _, _ = places()
    rows = og.shape[0]
    own_at, pair_at = core * rows, (1 - core) * rows
    for source, first in ((mine, own_at), (pair, pair_at)):
        qs[at(first, rows), :] = source[:, QS]
        ks[at(HALF + first, rows), :] = source[:, KS]
        vs[at(HALF + first, rows), :] = source[:, VS]
    for source, first in ((near, core * (HALF + 2 * rows)), (far, (1 - core) * (HALF + 2 * rows))):
        ks[at(first), :] = source[:, :DH]
        vs[at(first), :] = source[:, DH:]
    ogs[at(own_at, rows), :] = og[...]
    ogs[at(pair_at, rows), :] = og_recv[...]
    span = rows + 2 * HALF
    row_pos = lax.broadcasted_iota(jnp.int32, (rows, span), 0)
    col_pos = lax.broadcasted_iota(jnp.int32, (rows, span), 1)
    inside = (col_pos >= row_pos) & (col_pos < row_pos + WINDOW)
    for block in range(2):
        here, window = slice(block * rows, (block + 1) * rows), slice(block * rows, block * rows + span)
        scores = mm(qs[here, :], ks[window, :], NT) * FACTOR
        scores = jnp.where(inside, scores, -1e30)
        peak = jnp.max(scores, axis=1, keepdims=True)
        terms = jnp.where(inside, jnp.exp(scores - peak), 0.0)
        share = terms / jnp.sum(terms, axis=1, keepdims=True)
        probs[block] = share
        attn[here, :] = mm(share.astype(BF), vs[window, :]).astype(BF)
    wg[...] = mm(attn[...], ogs[...], TN).astype(wg.dtype)


def lin_forward_kernel(state, others, mine, pair, ogs, gain, u_out, total_out, wg):
    core, z, _ = places()
    rows = mine.shape[0]
    total = state[...]
    if others is not None:
        for index in range(others.shape[0]):
            total = total + jnp.where(z == index, 0.0, others[index].astype(F32))
    total_out[...] = total
    u_out[at(core * rows, rows), :] = mm3(unit_plus(mine[:, QL].astype(F32)), total)
    u_out[at((1 - core) * rows, rows), :] = mm3(unit_plus(pair[:, QL].astype(F32)), total)
    u = u_out[...]
    r = lax.rsqrt(jnp.mean(u * u, axis=1, keepdims=True) + norm_eps)
    attn = (gain[pl.ds(core, 1), :] * u * r).astype(BF)
    wg[...] = mm(attn, ogs[...], TN).astype(wg.dtype)


def dattn_kernel(weights, ogs, out, *scratch):
    if scratch:
        dps, cores, groups, rows, width = weights.shape
        for dp in range(dps):
            for half in range(cores):
                for group in range(groups):
                    first = (group * cores + half) * rows
                    scratch[0][first : first + rows, dp * width : (dp + 1) * width] = weights[dp, half, group]
        weights = scratch[0]
    out[...] = mm(ogs[...], weights[...], NT)


def lin_backward_kernel(u, total, dattn, mine, pair, gain, dq_own, dq_pair, dstate, dstate_low, grads):
    core, _, _ = places()
    rows = mine.shape[0]
    u_all = u[...]
    r = lax.rsqrt(jnp.mean(u_all * u_all, axis=1, keepdims=True) + norm_eps)
    lin_grad = gain[pl.ds(core, 1), :] * dattn[:, DH:]
    grads[...] = r * lin_grad - u_all * (r * r * r) * jnp.mean(lin_grad * u_all, axis=1, keepdims=True)
    total_state = total[...]
    result = jnp.zeros(dstate.shape, F32)
    for first, source, out in ((core * rows, mine, dq_own), ((1 - core) * rows, pair, dq_pair)):
        wide = source[:, QL].astype(F32)
        part = grads[at(first, rows), :]
        result = result + mm3(unit_plus(wide), part, TN)
        out[...] = (mm3(part, total_state, NT) * unit_slope(wide)).astype(BF)
    dstate[...] = result
    dstate_low[...] = result.astype(BF)


def soft_backward_kernel(
    qs, ks, vs, probs, attn, dattn, dq_own, dk_own, dv_own, to_pair, to_near, to_far,
    dq_all, dk_all, dv_all,
):
    core, _, _ = places()
    rows = qs.shape[0] // 2
    span = rows + 2 * HALF
    dk_all[...] = jnp.zeros_like(dk_all)
    dv_all[...] = jnp.zeros_like(dv_all)
    for block in range(2):
        here, window = slice(block * rows, (block + 1) * rows), slice(block * rows, block * rows + span)
        grad = dattn[here, :DH].astype(BF)
        share = probs[block]
        delta = jnp.sum(grad.astype(F32) * attn[here, :].astype(F32), axis=1, keepdims=True)
        dscore = (share * (mm(grad, vs[window, :], NT) - delta)).astype(BF)
        dq_all[here, :] = mm(dscore, ks[window, :]) * FACTOR
        dk_all[window, :] += mm(dscore, qs[here, :], TN) * FACTOR
        dv_all[window, :] += mm(share.astype(BF), grad, TN)
    own, pair = core * rows, (1 - core) * rows
    near_at, far_at = core * (HALF + 2 * rows), (1 - core) * (HALF + 2 * rows)
    dq_own[...] = dq_all[at(own, rows), :].astype(BF)
    dk_own[...] = dk_all[at(HALF + own, rows), :]
    dv_own[...] = dv_all[at(HALF + own, rows), :]
    to_pair[:, :DH] = dq_all[at(pair, rows), :].astype(BF)
    to_pair[:, DH : 2 * DH] = dk_all[at(HALF + pair, rows), :].astype(BF)
    to_pair[:, 2 * DH :] = dv_all[at(HALF + pair, rows), :].astype(BF)
    to_near[:, :DH] = dk_all[at(near_at), :].astype(BF)
    to_near[:, DH:] = dv_all[at(near_at), :].astype(BF)
    to_far[:, :DH] = dk_all[at(far_at), :].astype(BF)
    to_far[:, DH:] = dv_all[at(far_at), :].astype(BF)


def lin_final_kernel(dstate, others, mine, pair, soft_pair, dq_pair, own_out, pair_out):
    _, z, _ = places()
    total = dstate[...]
    if others is not None:
        for index in range(others.shape[0]):
            total = total + jnp.where(z == index, 0.0, others[index].astype(F32))
    high, low = halves(total)
    pair_out[:, : 3 * DH] = soft_pair[...]
    pair_out[:, 3 * DH : 4 * DH] = dq_pair[...]
    for source, out, first in ((mine, own_out, 0), (pair, pair_out, 4 * DH)):
        wide, values = source[:, KL].astype(F32), source[:, VL]
        dk = mm(values, high, NT) + mm(values, low, NT)
        out[:, first : first + DH] = (dk * unit_slope(wide)).astype(BF)
        out[:, first + DH : first + 2 * DH] = mm3(unit_plus(wide), total).astype(BF)


def output_kernel(dq_soft, dk_soft, dv_soft, dq_lin, lin_own, pair, near, far, dq, dk, dv):
    core, _, _ = places()
    soft = SOFT_HEADS * DH
    mine, other = core * DH, (1 - core) * DH
    dq[0, :, at(mine)] = dq_soft[...]
    dq[0, :, at(other)] = pair[:, :DH]
    dq[0, :, at(soft + mine)] = dq_lin[...]
    dq[0, :, at(soft + other)] = pair[:, 3 * DH : 4 * DH]
    for out, own, first in ((dk, dk_soft, 0), (dv, dv_soft, DH)):
        cols = slice(first, first + DH)
        out[0, :, at(mine)] = (own[...] + far[:, cols].astype(F32)).astype(BF)
        out[0, :, at(other)] = (
            pair[:, DH + first : 2 * DH + first].astype(F32) + near[:, cols].astype(F32)
        ).astype(BF)
        out[0, :, at(soft + mine)] = lin_own[:, cols]
        out[0, :, at(soft + other)] = pair[:, 4 * DH + first : 5 * DH + first]


def weight_rows_kernel(parts, dstate, out):
    dps, cores, groups, rows, width = parts.shape
    for head in range(out.shape[0]):
        total = parts[0, head % 2, head // 2].astype(F32)
        for dp in range(1, dps):
            total = total + parts[dp, head % 2, head // 2].astype(F32)
        out[head, :rows, :] = total[:, : width // 2].astype(BF)
        out[head, rows : 2 * rows, :] = total[:, width // 2 :].astype(BF)
        out[head, 2 * rows :, :] = dstate[...]


def weight_sum_kernel(scale, parts, out):
    rows, width = out.shape[1:]
    total = parts[0, : 2 * rows, :].astype(F32)
    for index in range(1, parts.shape[0]):
        total = total + parts[index, : 2 * rows, :].astype(F32)
    total = total * scale
    for index in range(out.shape[0]):
        out[index, :, : width // 2] = total[:rows]
        out[index, :, width // 2 :] = total[rows:]


def weight_join_kernel(parts, out):
    dps, rows, width = parts.shape
    for dp in range(dps):
        out[:, dp * width : (dp + 1) * width] = parts[dp].astype(F32)


def body(n_dp, n_z, queries, key_rows, value_rows, out_grad, out_weight, norm_gain):
    q, k, v, og = queries[0], key_rows[0], value_rows[0], out_grad[0]
    rows, model = og.shape
    n_seq = 2 * n_z
    every = range(n_seq)
    axes = ("z", "core")
    pair_perm = [(0, 1), (1, 0)]
    to_near = [(s, (s + 1) % n_seq if s % 2 else (s - 1) % n_seq) for s in every]
    to_far = [(s, (s + 2) % n_seq if s % 2 else (s - 2) % n_seq) for s in every]
    from_far = [(target, source) for source, target in to_far]
    core = lax.axis_index("core")
    direct = n_z == HEADS
    width = model // n_dp
    half = DH // 2

    def swap(value, axis):
        return lax.all_to_all(value, axis, 0, 0, tiled=True)

    og_recv = lax.ppermute(og, "core", pair_perm)
    mine, other, near_out, far_out, w_part = call(
        pack_kernel, "pack",
        [
            like((rows, 6 * DH), BF), like((rows, 6 * DH), BF), like((rows, 2 * DH), BF),
            like((rows, 2 * DH), BF), like((out_weight.shape[0], width), BF),
        ],
        [q, k, v, out_weight], outside=4, scratch=[pltpu.SemaphoreType.DMA((17,))],
    )
    pair = lax.ppermute(other, "core", pair_perm)
    near = lax.ppermute(near_out, axes, to_near)
    far = lax.ppermute(far_out, axes, to_far)
    if direct:
        w_rows = swap(jnp.broadcast_to(w_part, (n_z, half, width)), "z")
        w_rows = jnp.swapaxes(w_rows.reshape(2, 2, half, width), 0, 1)
        w_rows = jnp.broadcast_to(w_rows, (n_dp, 2, 2, half, width)).reshape(2 * n_dp, 2, half, width)
        weights = swap(w_rows, ("dp", "core")).reshape(n_dp, 2, 2, half, width)
    else:
        weights = lax.all_gather(out_weight, axes, axis=0, tiled=True).reshape(2, 2, DH, model)
        weights = jnp.where(core == 0, weights[:, 0], weights[:, 1]).reshape(2 * DH, model)

    copies = n_z if direct else 1
    state, state_low = call(
        state_kernel, "state", [like((DH, DH), F32), like((copies, DH, DH), BF)], [mine, pair],
        flops=4 * 2 * rows * DH * DH,
    )
    others = [swap(state_low, "z")] if direct else []
    if not direct:
        state = lax.psum(state, "z")

    span = 2 * rows + 2 * HALF
    low = BF if direct else F32
    wg_flops = 2 * 2 * rows * DH * model
    qs, ks, vs, ogs, probs, attn, wg_soft = call(
        soft_forward_kernel, "soft_forward",
        [
            like((2 * rows, DH), BF), like((span, DH), BF), like((span, DH), BF),
            like((2 * rows, model), BF), like((2, rows, rows + 2 * HALF), F32), like((2 * rows, DH), BF),
            like((DH, model), low),
        ],
        [mine, pair, og, og_recv, near, far],
        flops=wg_flops,
    )
    gain = norm_gain.reshape(LIN_HEADS, DH)

    def optional(kernel):
        if direct:
            return kernel
        return lambda first, *refs: kernel(first, None, *refs)

    u, total, wg_lin = call(
        optional(lin_forward_kernel), "lin_forward",
        [like((2 * rows, DH), F32), like((DH, DH), F32), like((DH, model), low)],
        [state] + others + [mine, pair, ogs, gain],
        flops=wg_flops,
    )
    dattn = call(
        dattn_kernel, "d_attn", [like((2 * rows, 2 * DH), F32)], [weights, ogs],
        scratch=[pltpu.VMEM((2 * DH, model), BF)] if direct else [],
        flops=2 * wg_flops,
    )[0]
    dq_lin, dq_lin_pair, dstate, dstate_low = call(
        lin_backward_kernel, "lin_backward",
        [like((rows, DH), BF), like((rows, DH), BF), like((DH, DH), F32), like((DH, DH), BF)],
        [u, total, dattn, mine, pair, gain],
        scratch=[pltpu.VMEM((2 * rows, DH), F32)],
        flops=wg_flops,
    )
    dq_soft, dk_soft, dv_soft, soft_pair, back_near, back_far = call(
        soft_backward_kernel, "soft_backward",
        [
            like((rows, DH), BF), like((rows, DH), F32), like((rows, DH), F32),
            like((rows, 3 * DH), BF), like((rows, 2 * DH), BF), like((rows, 2 * DH), BF),
        ],
        [qs, ks, vs, probs, attn, dattn],
        scratch=[pltpu.VMEM((2 * rows, DH), F32), pltpu.VMEM((span, DH), F32), pltpu.VMEM((span, DH), F32)],
        flops=wg_flops,
    )
    back_near = lax.ppermute(back_near, axes, to_near)
    back_far = lax.ppermute(back_far, axes, from_far)

    scale = 1.0 / math.sqrt(n_dp * n_seq * rows)
    if direct:
        groups = jnp.stack([wg_soft, wg_lin]).reshape(2, 2, half, n_dp, width)
        groups = groups.transpose(3, 1, 0, 2, 4).reshape(2 * n_dp, 2, half, width)
        parts = swap(groups, ("dp", "core")).reshape(n_dp, 2, 2, half, width)
        sums = call(
            weight_rows_kernel, "weight_rows", [like((n_z, 2 * DH, DH), BF)], [parts, dstate_low]
        )[0]
        others = [swap(sums, "z")]
        summed = call(
            functools.partial(weight_sum_kernel, scale), "weight_sum",
            [like((n_dp, half, width), F32)], others,
        )[0]
        weight_grad = call(
            weight_join_kernel, "weight_join", [like((half, model), F32)], [swap(summed, "dp")]
        )[0]
        others = [others[0][:, DH:]]
    else:
        groups = jnp.stack([wg_soft, wg_lin])
        slots = jnp.stack([jnp.where(core == head, groups, 0.0) for head in range(2)], axis=1)
        local = lax.psum_scatter(
            slots.reshape(HEADS * DH, model), axes, scatter_dimension=0, tiled=True
        )
        weight_grad = lax.psum(local, "dp") * scale
        dstate = lax.psum(dstate, "z")

    lin_own, to_pair = call(
        optional(lin_final_kernel), "lin_final",
        [like((rows, 2 * DH), BF), like((rows, 6 * DH), BF)],
        [dstate] + others + [mine, pair, soft_pair, dq_lin_pair],
        flops=wg_flops // 4,
    )
    from_pair = lax.ppermute(to_pair, "core", pair_perm)
    shape = like((1, rows, HEADS * DH), BF)
    dq, dk, dv = call(
        output_kernel, "outputs", [shape] * 3,
        [dq_soft, dk_soft, dv_soft, dq_lin, lin_own, from_pair, back_near, back_far],
    )
    return dq, dk, dv, weight_grad


def solution(mesh):
    n_dp, n_seq = mesh.shape["dp"], mesh.shape["seq"]
    blocks = Mesh(mesh.devices.reshape(n_dp, n_seq // 2, 2), ("dp", "z", "core"))
    tokens, heads = P("dp", ("z", "core"), None), P(("z", "core"), None)
    return jax.shard_map(
        functools.partial(body, n_dp, n_seq // 2),
        mesh=blocks,
        in_specs=(tokens, tokens, tokens, tokens, heads, P()),
        out_specs=(tokens, tokens, tokens, heads),
        check_vma=False,
    )
```

```python
import functools
import math

import jax
import jax.numpy as jnp
from jax import lax
from jax.experimental import pallas as pl
from jax.experimental.pallas import tpu as pltpu
from jax.sharding import Mesh
from jax.sharding import PartitionSpec as P

DH = 128
SOFT_HEADS = 2
LIN_HEADS = 2
HEADS = SOFT_HEADS + LIN_HEADS
WINDOW = 256
HALF = 128
norm_eps = 1e-06
FACTOR = DH ** (-0.5)
BF = jnp.bfloat16
F32 = jnp.float32
NN = (((1,), (0,)), ((), ()))
NT = (((1,), (1,)), ((), ()))
TN = (((0,), (0,)), ((), ()))


def unit_plus(values):
    return jnp.where(values > 0, values + 1.0, jnp.exp(jnp.minimum(values, 0.0)))


def unit_slope(values):
    return jnp.where(values > 0, 1.0, jnp.exp(jnp.minimum(values, 0.0)))


def mm(a, b, dims=NN):
    return lax.dot_general(a, b, dims, preferred_element_type=F32)


def halves(x):
    high = x.astype(BF)
    return high, (x - high.astype(F32)).astype(BF)


def mm3(a, b, dims=NN):
    a_high, a_low = halves(a)
    b_high, b_low = halves(b)
    return mm(a_high, b_high, dims) + (mm(a_high, b_low, dims) + mm(a_low, b_high, dims))


def mm2(a, b, dims=NN):
    a_high, a_low = halves(a)
    return mm(a_high, b, dims) + mm(a_low, b, dims)


def at(start, size=DH):
    return pl.ds(pl.multiple_of(start, size), size)


def places():
    return lax.axis_index("core"), lax.axis_index("z"), lax.axis_index("dp")


def call(kernel, name, outs, args, scratch=(), flops=0, spaces=None):
    vmem = pl.BlockSpec(memory_space=pltpu.VMEM)
    size = sum(math.prod(x.shape) * x.dtype.itemsize for x in list(args) + list(outs))
    return pl.pallas_call(
        kernel,
        name=name,
        out_shape=list(outs),
        in_specs=spaces or [vmem] * len(args),
        out_specs=[vmem] * len(outs),
        scratch_shapes=list(scratch),
        compiler_params=pltpu.CompilerParams(vmem_limit_bytes=24 * 2**20),
        cost_estimate=pl.CostEstimate(flops=flops, bytes_accessed=size, transcendentals=0),
    )(*args)


def like(shape, dtype):
    return jax.ShapeDtypeStruct(shape, dtype)


QS, KS, VS, QL, KL, VL = (slice(i * DH, (i + 1) * DH) for i in range(6))
SOFT = SOFT_HEADS * DH


def links(direct):
    core, z, dp = places()
    step = 1 + core
    turn = lax.rem(z + core, 2) if direct else 1
    return dict(
        first=1 + 2 * core, second=3 - 2 * core, step=step, other=3 - step,
        block_a=1 - turn, block_b=turn,
        halo_a=(1 - turn if direct else 1), halo_b=(turn if direct else 0),
    )


def pack_kernel(q, k, v, og, w, gain, mine_out, other_out, og_out, w_out, gain_out, sems):
    core, _, dp = places()
    mine, other = core * DH, (1 - core) * DH
    copies = []

    def fetch(source, target):
        copy = pltpu.make_async_copy(source, target, sems.at[len(copies)])
        copy.start()
        copies.append(copy)

    for index, array in enumerate((q, k, v)):
        for group in range(2):
            cols = slice((3 * group + index) * DH, (3 * group + index + 1) * DH)
            fetch(array.at[:, at(SOFT * group + other)], other_out.at[:, cols])
            fetch(array.at[:, at(SOFT * group + mine)], mine_out.at[:, cols])
    fetch(og, og_out)
    width = w_out.shape[1]
    fetch(w.at[:, at(dp * width, width)], w_out)
    fetch(gain, gain_out)
    for copy in copies:
        copy.wait()


def state_kernel(direct, mine, pair, w, state, to_a, to_b, *to_c):
    core, _, _ = places()
    total = mm2(unit_plus(mine[:, KL].astype(F32)), mine[:, VL], TN) + mm2(
        unit_plus(pair[:, KL].astype(F32)), pair[:, VL], TN
    )
    state[...] = total
    way = links(direct)
    for out, block in ((to_a, way["block_a"]), (to_b, way["block_b"])):
        here = block == core
        out[:, :DH] = jnp.where(here, mine[:, KS], pair[:, KS])
        out[:, DH : 2 * DH] = jnp.where(here, mine[:, VS], pair[:, VS])
    if direct:
        rows = w.shape[0]
        for out, first in ((to_a, 2 * DH), (to_b, 2 * DH), (to_c[0], 0)):
            out[:, first : first + DH] = total.astype(BF)
            out[:rows, first + DH :] = w[:, :DH]
            out[rows:, first + DH :] = w[:, DH:]


def relay_kernel(w, a, b, c, keep, send, heads):
    core, z, _ = places()
    way = links(True)
    rows = w.shape[0]
    heads[z] = w[...]
    for source, first, step in ((a, 3 * DH, way["first"]), (b, 3 * DH, way["second"]), (c, DH, 2)):
        heads[z ^ step, :, :DH] = source[:rows, first:]
        heads[z ^ step, :, DH:] = source[rows:, first:]
    for group in range(2):
        keep[group] = heads[2 * group + core]
        send[group] = heads[2 * group + 1 - core]


def weight_parts(direct, attn, ogs, send, keep):
    if not direct:
        keep[...] = mm(attn, ogs[...], TN)
        return
    _, _, dp = places()
    way = links(True)
    width = send.shape[1] // 2
    for index, step in enumerate((0, way["other"])):
        cols = slice(index * width, (index + 1) * width)
        keep[:, cols] = mm(attn, ogs[:, at((dp ^ step) * width, width)], TN)
        send[:, cols] = mm(attn, ogs[:, at((dp ^ step ^ way["step"]) * width, width)], TN).astype(BF)


def soft_forward_kernel(
    direct, mine, pair, og, og_recv, a, b, qs, ks, vs, ogs, probs, attn, keep, *send
):
    core, _, _ = places()
    way = links(direct)
    rows = og.shape[0]
    own_at, pair_at = core * rows, (1 - core) * rows
    for source, first in ((mine, own_at), (pair, pair_at)):
        qs[at(first, rows), :] = source[:, QS]
        ks[at(HALF + first, rows), :] = source[:, KS]
        vs[at(HALF + first, rows), :] = source[:, VS]
    for source, side in ((a, way["halo_a"]), (b, way["halo_b"])):
        first = side * (HALF + 2 * rows)
        ks[at(first), :] = source[:, :DH]
        vs[at(first), :] = source[:, DH : 2 * DH]
    ogs[at(own_at, rows), :] = og[...]
    ogs[at(pair_at, rows), :] = og_recv[...]
    span = rows + 2 * HALF
    row_pos = lax.broadcasted_iota(jnp.int32, (rows, span), 0)
    col_pos = lax.broadcasted_iota(jnp.int32, (rows, span), 1)
    inside = (col_pos >= row_pos) & (col_pos < row_pos + WINDOW)
    for block in range(2):
        here, window = slice(block * rows, (block + 1) * rows), slice(block * rows, block * rows + span)
        scores = mm(qs[here, :], ks[window, :], NT) * FACTOR
        scores = jnp.where(inside, scores, -1e30)
        peak = jnp.max(scores, axis=1, keepdims=True)
        terms = jnp.where(inside, jnp.exp(scores - peak), 0.0)
        share = terms / jnp.sum(terms, axis=1, keepdims=True)
        probs[block] = share
        attn[here, :] = mm(share.astype(BF), vs[window, :]).astype(BF)
    weight_parts(direct, attn[...], ogs, send[0] if send else None, keep)


def lin_forward_kernel(direct, state, mine, pair, ogs, gain, *refs):
    core, _, _ = places()
    rows = mine.shape[0]
    total = state[...]
    if direct:
        a, b, c, soft_send, w_keep, w_recv, u_out, total_out, keep, out, send = refs
        total = total + a[:, 2 * DH : 3 * DH].astype(F32) + b[:, 2 * DH : 3 * DH].astype(F32)
        total = total + c[:, :DH].astype(F32)
    else:
        u_out, total_out, keep = refs
        send = None
    total_out[...] = total
    u_out[at(core * rows, rows), :] = mm3(unit_plus(mine[:, QL].astype(F32)), total)
    u_out[at((1 - core) * rows, rows), :] = mm3(unit_plus(pair[:, QL].astype(F32)), total)
    u = u_out[...]
    r = lax.rsqrt(jnp.mean(u * u, axis=1, keepdims=True) + norm_eps)
    attn = (gain[pl.ds(core, 1), :] * u * r).astype(BF)
    weight_parts(direct, attn, ogs, send, keep)
    if direct:
        wide = soft_send.shape[1]
        out[:DH, :wide] = soft_send[...]
        out[DH:, :wide] = send[...]
        half = w_keep.shape[1]
        for group in range(2):
            out[at(group * DH + core * half, half), wide:] = w_keep[group]
            out[at(group * DH + (1 - core) * half, half), wide:] = w_recv[group]


def fold_kernel(keep_soft, keep_lin, sent, got, keep, send):
    width = keep.shape[1]
    for rows, source in ((slice(0, DH), keep_soft), (slice(DH, 2 * DH), keep_lin)):
        keep[rows, :] = source[:, :width] + got[rows, :width].astype(F32)
        send[rows, :width] = (source[:, width:] + got[rows, width : 2 * width].astype(F32)).astype(BF)
    send[:, width : 2 * width] = sent[:, 2 * width :]
    send[:, 2 * width :] = got[:, 2 * width :]


def rows_kernel(keep, got, own, send, total):
    core, _, _ = places()
    half = DH // 2
    width = keep.shape[1]
    total[...] = keep[...] + got[:, :width].astype(F32)
    for group in range(2):
        out = slice(group * half, (group + 1) * half)
        own[out, :] = total[at(group * DH + core * half, half), :]
        send[out, :] = total[at(group * DH + (1 - core) * half, half), :]


def lin_backward(u, total, dattn, mine, pair, gain, dq_own, dq_pair, dstate, grads):
    core, _, _ = places()
    rows = mine.shape[0]
    u_all = u[...]
    r = lax.rsqrt(jnp.mean(u_all * u_all, axis=1, keepdims=True) + norm_eps)
    lin_grad = gain[pl.ds(core, 1), :] * dattn[:, DH:]
    grads[...] = r * lin_grad - u_all * (r * r * r) * jnp.mean(lin_grad * u_all, axis=1, keepdims=True)
    total_state = total[...]
    result = jnp.zeros(dstate.shape, F32)
    for first, source, out in ((core * rows, mine, dq_own), ((1 - core) * rows, pair, dq_pair)):
        wide = source[:, QL].astype(F32)
        part = grads[at(first, rows), :]
        result = result + mm3(unit_plus(wide), part, TN)
        out[...] = (mm3(part, total_state, NT) * unit_slope(wide)).astype(BF)
    dstate[...] = result


def soft_backward(qs, ks, vs, probs, attn, dattn, dq_all, dk_all, dv_all):
    rows = qs.shape[0] // 2
    span = rows + 2 * HALF
    dk_all[...] = jnp.zeros_like(dk_all)
    dv_all[...] = jnp.zeros_like(dv_all)
    for block in range(2):
        here, window = slice(block * rows, (block + 1) * rows), slice(block * rows, block * rows + span)
        grad = dattn[here, :DH].astype(BF)
        share = probs[block]
        delta = jnp.sum(grad.astype(F32) * attn[here, :].astype(F32), axis=1, keepdims=True)
        dscore = (share * (mm(grad, vs[window, :], NT) - delta)).astype(BF)
        dq_all[here, :] = mm(dscore, ks[window, :]) * FACTOR
        dk_all[window, :] += mm(dscore, qs[here, :], TN) * FACTOR
        dv_all[window, :] += mm(share.astype(BF), grad, TN)


def backward_kernel(direct, *refs):
    if direct:
        sent, got = refs[:2]
        refs = refs[2:]
    else:
        weights = refs[0]
        refs = refs[1:]
    (ogs, u, total, mine, pair, gain, qs, ks, vs, probs, attn,
     dq_lin, dq_lin_pair, dstate, dq_soft, dk_soft, dv_soft, dattn, grads, *scratch) = refs
    if direct:
        _, _, dp = places()
        way = links(True)
        weights = scratch[0]
        width = weights.shape[1] // 4
        for source, index, step in (
            (sent, 1, 0), (sent, 2, way["step"]), (got, 1, way["other"]), (got, 2, 3),
        ):
            weights[:, at((dp ^ step) * width, width)] = source[:, index * width : (index + 1) * width]
    dattn[...] = mm(ogs[...], weights[...], NT)
    lin_backward(u, total, dattn, mine, pair, gain, dq_lin, dq_lin_pair, dstate, grads)
    soft_backward(qs, ks, vs, probs, attn, dattn, dq_soft, dk_soft, dv_soft)


def halo_kernel(direct, dk_soft, dv_soft, *refs):
    core, z, _ = places()
    way = links(direct)
    span = dk_soft.shape[0]
    if direct:
        dstate, own, got, to_a, to_b, to_c, chunk, heads = refs
        half = own.shape[0] // 2
        for group in range(2):
            rows = slice(group * half, (group + 1) * half)
            heads[2 * group + core] = own[rows, :]
            heads[2 * group + 1 - core] = got[rows, :]
        chunk[...] = heads[z]
        for out, first, step in ((to_a, 2 * DH, way["first"]), (to_b, 2 * DH, way["second"]), (to_c, 0, 2)):
            out[:, first : first + DH] = dstate[...].astype(BF)
            out[:half, first + DH :] = heads[z ^ step, :, :DH].astype(BF)
            out[half:, first + DH :] = heads[z ^ step, :, DH:].astype(BF)
    else:
        to_a, to_b = refs
    for out, side in ((to_a, way["halo_a"]), (to_b, way["halo_b"])):
        first = side * (span - HALF)
        out[:, :DH] = dk_soft[at(first), :].astype(BF)
        out[:, DH : 2 * DH] = dv_soft[at(first), :].astype(BF)


def final_kernel(
    direct, scale, dstate, mine, pair, dq_soft, dk_soft, dv_soft, dq_lin, dq_lin_pair, a, b, *refs
):
    core, _, _ = places()
    way = links(direct)
    rows = mine.shape[0]
    total = dstate[...]
    if direct:
        c, chunk, own_out, pair_out, weight_out, dk_all, dv_all = refs
        total = total + a[:, 2 * DH : 3 * DH].astype(F32) + b[:, 2 * DH : 3 * DH].astype(F32)
        total = total + c[:, :DH].astype(F32)
        half = chunk.shape[0]
        for side in range(2):
            cols, part = slice(side * DH, (side + 1) * DH), slice(side * half, (side + 1) * half)
            weight_out[:, cols] = scale * (
                chunk[:, cols] + a[part, 3 * DH :].astype(F32) + b[part, 3 * DH :].astype(F32)
                + c[part, DH:].astype(F32)
            )
    else:
        own_out, pair_out, dk_all, dv_all = refs
    for source, out, cols in ((dk_soft, dk_all, slice(0, DH)), (dv_soft, dv_all, slice(DH, 2 * DH))):
        out[...] = source[HALF : HALF + 2 * rows, :]
        out[at(way["block_a"] * rows, rows), :] += a[:, cols].astype(F32)
        out[at(way["block_b"] * rows, rows), :] += b[:, cols].astype(F32)
    high, low = halves(total)
    for source, dq, out, place in ((mine, dq_lin, own_out, core), (pair, dq_lin_pair, pair_out, 1 - core)):
        here = at(place * rows, rows)
        out[:, QS] = dq_soft[here, :].astype(BF)
        out[:, KS] = dk_all[here, :].astype(BF)
        out[:, VS] = dv_all[here, :].astype(BF)
        wide, values = source[:, KL].astype(F32), source[:, VL]
        out[:, QL] = dq[...]
        out[:, KL] = ((mm(values, high, NT) + mm(values, low, NT)) * unit_slope(wide)).astype(BF)
        out[:, VL] = mm3(unit_plus(wide), total).astype(BF)


def output_kernel(own, pair, dq, dk, dv):
    core, _, _ = places()
    for source, first in ((own, core * DH), (pair, (1 - core) * DH)):
        for index, out in enumerate((dq, dk, dv)):
            out[0, :, at(first)] = source[:, index * DH : (index + 1) * DH]
            out[0, :, at(SOFT + first)] = source[:, (3 + index) * DH : (4 + index) * DH]


def pair_up_kernel(first, second, out):
    width = first.shape[1]
    out[:, :width] = first[...]
    out[:, width:] = second[...]


def weight_join_kernel(both, got, out):
    _, _, dp = places()
    way = links(True)
    width = both.shape[1] // 2
    for source, index, step in ((both, 0, 0), (both, 1, way["step"]), (got, 0, way["other"]), (got, 1, 3)):
        out[:, at((dp ^ step) * width, width)] = source[:, index * width : (index + 1) * width].astype(F32)


def body(n_dp, n_z, queries, key_rows, value_rows, out_grad, out_weight, norm_gain):
    q, k, v, og = queries[0], key_rows[0], value_rows[0], out_grad[0]
    rows, model = og.shape
    axes = ("z", "core")
    pair_perm = [(0, 1), (1, 0)]
    core = lax.axis_index("core")
    direct = n_z == HEADS and n_dp == 4
    width = model // n_dp
    half = DH // 2

    def over_core(value):
        return lax.ppermute(value, "core", pair_perm)

    def over_z(value, which, back=False):
        pairs = []
        for z in range(n_z):
            for c in range(2):
                if direct:
                    there = z ^ (1 + 2 * c, 3 - 2 * c, 2)[which]
                else:
                    there = (z + (1 if (which == 1) != back else -1)) % n_z
                pairs.append((2 * z + c, 2 * there + c))
        return lax.ppermute(value, axes, pairs)

    def over_dp(value, which):
        pairs = [
            (2 * d + c, 2 * (d ^ (1 + c, 2 - c)[which]) + c) for d in range(n_dp) for c in range(2)
        ]
        return lax.ppermute(value, ("dp", "core"), pairs)

    og_recv = over_core(og)
    gain = norm_gain.reshape(LIN_HEADS, DH)
    mine, other, og_here, w_part, gain = call(
        pack_kernel, "pack",
        [
            like((rows, 6 * DH), BF), like((rows, 6 * DH), BF), like((rows, model), BF),
            like((out_weight.shape[0], width), BF), like((LIN_HEADS, DH), F32),
        ],
        [q, k, v, og, out_weight, gain], scratch=[pltpu.SemaphoreType.DMA((15,))],
        spaces=[pl.BlockSpec(memory_space=pltpu.HBM)] * 6,
    )
    pair = over_core(other)
    wide = 4 * DH if direct else 2 * DH
    state, to_a, to_b, *to_c = call(
        functools.partial(state_kernel, direct), "state",
        [like((DH, DH), F32), like((rows, wide), BF), like((rows, wide), BF)]
        + [like((rows, 2 * DH), BF)] * direct,
        [mine, pair, w_part],
        flops=4 * 2 * rows * DH * DH,
    )
    a, b = over_z(to_a, 0), over_z(to_b, 1)
    c = [over_z(value, 2) for value in to_c]
    if direct:
        w_keep, w_send = call(
            relay_kernel, "relay", [like((2, half, width), BF)] * 2, [w_part, a, b] + c,
            scratch=[pltpu.VMEM((HEADS, half, width), BF)],
        )
        w_recv = over_core(w_send)
    else:
        state = lax.psum(state, "z")
        weights = lax.all_gather(out_weight, axes, axis=0, tiled=True).reshape(2, 2, DH, model)
        weights = jnp.where(core == 0, weights[:, 0], weights[:, 1]).reshape(2 * DH, model)

    span = 2 * rows + 2 * HALF
    keep_width = 2 * width if direct else model
    wg_flops = 2 * 2 * rows * DH * model
    qs, ks, vs, ogs, probs, attn, keep_soft, *soft_send = call(
        functools.partial(soft_forward_kernel, direct), "soft_forward",
        [
            like((2 * rows, DH), BF), like((span, DH), BF), like((span, DH), BF),
            like((2 * rows, model), BF), like((2, rows, rows + 2 * HALF), F32), like((2 * rows, DH), BF),
            like((DH, keep_width), F32),
        ] + [like((DH, 2 * width), BF)] * direct,
        [mine, pair, og_here, og_recv, a, b],
        flops=wg_flops,
    )
    u, total, keep_lin, *sent = call(
        functools.partial(lin_forward_kernel, direct), "lin_forward",
        [like((2 * rows, DH), F32), like((DH, DH), F32), like((DH, keep_width), F32)]
        + [like((2 * DH, 3 * width), BF)] * direct,
        [state, mine, pair, ogs, gain] + ([a, b] + c + soft_send + [w_keep, w_recv] if direct else []),
        scratch=[pltpu.VMEM((DH, 2 * width), BF)] * direct,
        flops=wg_flops,
    )
    if direct:
        got = over_dp(sent[0], 0)
        keep, sent = call(
            fold_kernel, "fold", [like((2 * DH, width), F32), like((2 * DH, 3 * width), BF)],
            [keep_soft, keep_lin, sent[0], got],
        )
        got = over_dp(sent, 1)
        row_own, row_send = call(
            rows_kernel, "rows", [like((2 * half, width), F32)] * 2, [keep, got],
            scratch=[pltpu.VMEM((2 * DH, width), F32)],
        )
        row_recv = over_core(row_send)
        weights = [sent, got]
    else:
        weights = [weights]
    dq_lin, dq_lin_pair, dstate, dq_soft, dk_soft, dv_soft = call(
        functools.partial(backward_kernel, direct), "backward",
        [
            like((rows, DH), BF), like((rows, DH), BF), like((DH, DH), F32),
            like((2 * rows, DH), F32), like((span, DH), F32), like((span, DH), F32),
        ],
        weights + [ogs, u, total, mine, pair, gain, qs, ks, vs, probs, attn],
        scratch=[pltpu.VMEM((2 * rows, 2 * DH), F32), pltpu.VMEM((2 * rows, DH), F32)]
        + [pltpu.VMEM((2 * DH, model), BF)] * direct,
        flops=5 * wg_flops,
    )
    scale = 1.0 / math.sqrt(n_dp * n_z * 2 * rows)
    to_a, to_b, *rest = call(
        functools.partial(halo_kernel, direct), "halo",
        [like((rows, wide), BF), like((rows, wide), BF)]
        + [like((rows, 2 * DH), BF), like((half, width), F32)] * direct,
        [dk_soft, dv_soft] + ([dstate, row_own, row_recv] if direct else []),
        scratch=[pltpu.VMEM((HEADS, half, width), F32)] * direct,
    )
    a, b = over_z(to_a, 0, True), over_z(to_b, 1, True)
    if direct:
        rest = [over_z(rest[0], 2), rest[1]]
    else:
        dstate = lax.psum(dstate, "z")
        groups = jnp.stack([keep_soft, keep_lin])
        slots = jnp.stack([jnp.where(core == head, groups, 0.0) for head in range(2)], axis=1)
        local = lax.psum_scatter(
            slots.reshape(HEADS * DH, model), axes, scatter_dimension=0, tiled=True
        )
        weight_grad = lax.psum(local, "dp") * scale
    own_out, to_pair, *weight_part = call(
        functools.partial(final_kernel, direct, scale), "final",
        [like((rows, 6 * DH), BF), like((rows, 6 * DH), BF)] + [like((half, width), F32)] * direct,
        [dstate, mine, pair, dq_soft, dk_soft, dv_soft, dq_lin, dq_lin_pair, a, b] + rest,
        scratch=[pltpu.VMEM((2 * rows, DH), F32)] * 2,
        flops=wg_flops // 4,
    )
    from_pair = over_core(to_pair)
    if direct:
        got = over_dp(weight_part[0], 0)
        both = call(
            pair_up_kernel, "pair_up", [like((half, 2 * width), F32)], [weight_part[0], got]
        )[0]
        weight_grad = call(
            weight_join_kernel, "weight_join", [like((half, model), F32)], [both, over_dp(both, 1)]
        )[0]
    shape = like((1, rows, HEADS * DH), BF)
    dq, dk, dv = call(output_kernel, "outputs", [shape] * 3, [own_out, from_pair])
    return dq, dk, dv, weight_grad


def solution(mesh):
    n_dp, n_seq = mesh.shape["dp"], mesh.shape["seq"]
    blocks = Mesh(mesh.devices.reshape(n_dp, n_seq // 2, 2), ("dp", "z", "core"))
    tokens, heads = P("dp", ("z", "core"), None), P(("z", "core"), None)
    return jax.shard_map(
        functools.partial(body, n_dp, n_seq // 2),
        mesh=blocks,
        in_specs=(tokens, tokens, tokens, tokens, heads, P()),
        out_specs=(tokens, tokens, tokens, heads),
        check_vma=False,
    )
```

```python
import functools
import math

import jax
import jax.numpy as jnp
from jax import lax
from jax.experimental import pallas as pl
from jax.experimental.pallas import tpu as pltpu
from jax.sharding import Mesh
from jax.sharding import PartitionSpec as P

DH = 128
SOFT_HEADS = 2
LIN_HEADS = 2
HEADS = SOFT_HEADS + LIN_HEADS
WINDOW = 256
HALF = 128
norm_eps = 1e-06
FACTOR = DH ** (-0.5)
BF = jnp.bfloat16
F32 = jnp.float32
NN = (((1,), (0,)), ((), ()))
NT = (((1,), (1,)), ((), ()))
TN = (((0,), (0,)), ((), ()))


def unit_plus(values):
    return jnp.where(values > 0, values + 1.0, jnp.exp(jnp.minimum(values, 0.0)))


def unit_slope(values):
    return jnp.where(values > 0, 1.0, jnp.exp(jnp.minimum(values, 0.0)))


def mm(a, b, dims=NN):
    return lax.dot_general(a, b, dims, preferred_element_type=F32)


def halves(x):
    high = x.astype(BF)
    return high, (x - high.astype(F32)).astype(BF)


def mm3(a, b, dims=NN):
    a_high, a_low = halves(a)
    b_high, b_low = halves(b)
    return mm(a_high, b_high, dims) + (mm(a_high, b_low, dims) + mm(a_low, b_high, dims))


def mm2(a, b, dims=NN):
    a_high, a_low = halves(a)
    return mm(a_high, b, dims) + mm(a_low, b, dims)


def at(start, size=DH):
    return pl.ds(pl.multiple_of(start, size), size)


def places():
    return lax.axis_index("core"), lax.axis_index("z"), lax.axis_index("dp")


def call(kernel, name, outs, args, scratch=(), flops=0, spaces=None):
    vmem = pl.BlockSpec(memory_space=pltpu.VMEM)
    size = sum(math.prod(x.shape) * x.dtype.itemsize for x in list(args) + list(outs))
    return pl.pallas_call(
        kernel,
        name=name,
        out_shape=list(outs),
        in_specs=spaces or [vmem] * len(args),
        out_specs=[vmem] * len(outs),
        scratch_shapes=list(scratch),
        compiler_params=pltpu.CompilerParams(vmem_limit_bytes=24 * 2**20),
        cost_estimate=pl.CostEstimate(flops=flops, bytes_accessed=size, transcendentals=0),
    )(*args)


def like(shape, dtype):
    return jax.ShapeDtypeStruct(shape, dtype)


QS, KS, VS, QL, KL, VL = (slice(i * DH, (i + 1) * DH) for i in range(6))
SOFT = SOFT_HEADS * DH


def links(direct):
    core, z, dp = places()
    step = 1 + core
    turn = lax.rem(z + core, 2) if direct else 1
    return dict(
        first=1 + 2 * core, second=3 - 2 * core, step=step, other=3 - step,
        block_a=1 - turn, block_b=turn,
        halo_a=(1 - turn if direct else 1), halo_b=(turn if direct else 0),
    )


def pack_kernel(q, k, v, og, w, gain, mine_out, other_out, og_out, gain_out, sems):
    core, _, dp = places()
    mine, other = core * DH, (1 - core) * DH
    copies = []

    def fetch(source, target):
        copy = pltpu.make_async_copy(source, target, sems.at[len(copies)])
        copy.start()
        copies.append(copy)

    width = w.shape[1] // lax.axis_size("dp")
    rows = w.shape[0]
    for index, array in enumerate((q, k, v)):
        for group in range(2):
            cols = slice((3 * group + index) * DH, (3 * group + index + 1) * DH)
            fetch(array.at[0, :, at(SOFT * group + other)], other_out.at[:, cols])
            fetch(array.at[0, :, at(SOFT * group + mine)], mine_out.at[:, cols])
    if other_out.shape[1] > 6 * DH:
        for side in range(2):
            fetch(
                w.at[:, at(dp * width + side * DH)],
                other_out.at[side * rows : (side + 1) * rows, 6 * DH :],
            )
    fetch(og.at[0], og_out)
    fetch(gain.at[at(mine)], gain_out.at[0])
    for copy in copies:
        copy.wait()


def state_kernel(direct, mine, pair, *refs):
    core, _, _ = places()
    total = mm2(unit_plus(mine[:, KL].astype(F32)), mine[:, VL], TN) + mm2(
        unit_plus(pair[:, KL].astype(F32)), pair[:, VL], TN
    )
    if direct:
        other, state, to_a, to_b, to_c, w_head = refs
    else:
        state, to_a, to_b = refs
    state[...] = total
    way = links(direct)
    for out, block in ((to_a, way["block_a"]), (to_b, way["block_b"])):
        here = block == core
        out[:, :DH] = jnp.where(here, mine[:, KS], pair[:, KS])
        out[:, DH : 2 * DH] = jnp.where(here, mine[:, VS], pair[:, VS])
        if direct:
            out[:, 2 * DH :] = total.astype(BF)
    if direct:
        to_c[...] = total.astype(BF)
        rows = w_head.shape[0] // 2
        for source, place in ((other, core), (pair, 1 - core)):
            for side in range(2):
                w_head[at(place * rows, rows), side * DH : (side + 1) * DH] = source[
                    side * rows : (side + 1) * rows, 6 * DH :
                ]


def w_two_kernel(own, got, out):
    _, z, _ = places()
    group = lax.div(z, 2)
    out[at(group * DH), :] = own[...]
    out[at((1 - group) * DH), :] = got[...]


def w_pick_kernel(own, got, out):
    core, z, _ = places()
    out[...] = jnp.where(lax.rem(z, 2) == core, own[...], got[...])


def join_kernel(first, second, out):
    width = first.shape[1]
    out[:, :width] = first[...]
    out[:, width:] = second[...]


def weight_parts(direct, attn, ogs, send, keep):
    high, low = halves(attn)
    if not direct:
        keep[...] = mm(high, ogs[...], TN) + mm(low, ogs[...], TN)
        return
    _, _, dp = places()
    way = links(True)
    width = send.shape[1] // 2
    for index, step in enumerate((0, way["other"])):
        cols = slice(index * width, (index + 1) * width)
        near, far = at((dp ^ step) * width, width), at((dp ^ step ^ way["step"]) * width, width)
        keep[:, cols] = mm(high, ogs[:, near], TN) + mm(low, ogs[:, near], TN)
        send[:, cols] = (mm(high, ogs[:, far], TN) + mm(low, ogs[:, far], TN)).astype(BF)


def soft_forward_kernel(
    direct, mine, pair, og, og_recv, a, b, qs, ks, vs, ogs, probs, attn, keep, *send
):
    core, _, _ = places()
    way = links(direct)
    rows = og.shape[0]
    own_at, pair_at = core * rows, (1 - core) * rows
    for source, first in ((mine, own_at), (pair, pair_at)):
        qs[at(first, rows), :] = source[:, QS]
        ks[at(HALF + first, rows), :] = source[:, KS]
        vs[at(HALF + first, rows), :] = source[:, VS]
    for source, side in ((a, way["halo_a"]), (b, way["halo_b"])):
        first = side * (HALF + 2 * rows)
        ks[at(first), :] = source[:, :DH]
        vs[at(first), :] = source[:, DH : 2 * DH]
    ogs[at(own_at, rows), :] = og[...]
    ogs[at(pair_at, rows), :] = og_recv[...]
    span = rows + 2 * HALF
    row_pos = lax.broadcasted_iota(jnp.int32, (rows, span), 0)
    col_pos = lax.broadcasted_iota(jnp.int32, (rows, span), 1)
    inside = (col_pos >= row_pos) & (col_pos < row_pos + WINDOW)
    for block in range(2):
        here, window = slice(block * rows, (block + 1) * rows), slice(block * rows, block * rows + span)
        scores = mm(qs[here, :], ks[window, :], NT) * FACTOR
        scores = jnp.where(inside, scores, -1e30)
        peak = jnp.max(scores, axis=1, keepdims=True)
        terms = jnp.where(inside, jnp.exp(scores - peak), 0.0)
        share = terms / jnp.sum(terms, axis=1, keepdims=True)
        probs[block] = share
        attn[here, :] = mm(share.astype(BF), vs[window, :])
    weight_parts(direct, attn[...], ogs, send[0] if send else None, keep)


def lin_forward_kernel(direct, state, mine, pair, ogs, gain, *refs):
    core, _, _ = places()
    rows = mine.shape[0]
    total = state[...]
    if direct:
        a, b, c, soft_send, u_out, total_out, keep, out = refs
        total = total + a[:, 2 * DH :].astype(F32) + b[:, 2 * DH :].astype(F32) + c[...].astype(F32)
    else:
        u_out, total_out, keep = refs
    total_out[...] = total
    u_out[at(core * rows, rows), :] = mm3(unit_plus(mine[:, QL].astype(F32)), total)
    u_out[at((1 - core) * rows, rows), :] = mm3(unit_plus(pair[:, QL].astype(F32)), total)
    u = u_out[...]
    r = lax.rsqrt(jnp.mean(u * u, axis=1, keepdims=True) + norm_eps)
    attn = gain[...] * u * r
    weight_parts(direct, attn, ogs, out.at[DH:, :] if direct else None, keep)
    if direct:
        out[:DH, :] = soft_send[...]


def fold_kernel(keep_soft, keep_lin, got, keep, send):
    width = keep.shape[1]
    for rows, source in ((slice(0, DH), keep_soft), (slice(DH, 2 * DH), keep_lin)):
        keep[rows, :] = source[:, :width] + got[rows, :width].astype(F32)
        send[rows, :] = (source[:, width:] + got[rows, width:].astype(F32)).astype(BF)


def rows_kernel(keep, got, own, send, total):
    core, _, _ = places()
    half = DH // 2
    total[...] = keep[...] + got[...].astype(F32)
    for group in range(2):
        out = slice(group * half, (group + 1) * half)
        own[out, :] = total[at(group * DH + core * half, half), :]
        send[out, :] = total[at(group * DH + (1 - core) * half, half), :]


def lin_backward(u, total, dattn, mine, pair, gain, dq_own, dq_pair, dstate, grads):
    core, _, _ = places()
    rows = mine.shape[0]
    u_all = u[...]
    r = lax.rsqrt(jnp.mean(u_all * u_all, axis=1, keepdims=True) + norm_eps)
    lin_grad = gain[...] * dattn[:, DH:]
    grads[...] = r * lin_grad - u_all * (r * r * r) * jnp.mean(lin_grad * u_all, axis=1, keepdims=True)
    total_state = total[...]
    result = jnp.zeros(dstate.shape, F32)
    for first, source, out in ((core * rows, mine, dq_own), ((1 - core) * rows, pair, dq_pair)):
        wide = source[:, QL].astype(F32)
        part = grads[at(first, rows), :]
        result = result + mm3(unit_plus(wide), part, TN)
        out[...] = (mm3(part, total_state, NT) * unit_slope(wide)).astype(BF)
    dstate[...] = result


def soft_backward(qs, ks, vs, probs, attn, dattn, dq_all, dk_all, dv_all):
    rows = qs.shape[0] // 2
    span = rows + 2 * HALF
    dk_all[...] = jnp.zeros_like(dk_all)
    dv_all[...] = jnp.zeros_like(dv_all)
    for block in range(2):
        here, window = slice(block * rows, (block + 1) * rows), slice(block * rows, block * rows + span)
        grad = dattn[here, :DH].astype(BF)
        share = probs[block]
        delta = jnp.sum(grad.astype(F32) * attn[here, :], axis=1, keepdims=True)
        dscore = (share * (mm(grad, vs[window, :], NT) - delta)).astype(BF)
        dq_all[here, :] = mm(dscore, ks[window, :]) * FACTOR
        dk_all[window, :] += mm(dscore, qs[here, :], TN) * FACTOR
        dv_all[window, :] += mm(share.astype(BF), grad, TN)


def backward_kernel(direct, *refs):
    if direct:
        sent, got = refs[:2]
        refs = refs[2:]
    else:
        weights = refs[0]
        refs = refs[1:]
    (ogs, u, total, mine, pair, gain, qs, ks, vs, probs, attn,
     dq_lin, dq_lin_pair, dstate, dq_soft, dk_soft, dv_soft, dattn, grads, *scratch) = refs
    if direct:
        _, _, dp = places()
        way = links(True)
        weights = scratch[0]
        width = weights.shape[1] // 4
        for source, index, step in (
            (sent, 0, 0), (sent, 1, way["step"]), (got, 0, way["other"]), (got, 1, 3),
        ):
            weights[:, at((dp ^ step) * width, width)] = source[:, index * width : (index + 1) * width]
    dattn[...] = mm(ogs[...], weights[...], NT)
    lin_backward(u, total, dattn, mine, pair, gain, dq_lin, dq_lin_pair, dstate, grads)
    soft_backward(qs, ks, vs, probs, attn, dattn, dq_soft, dk_soft, dv_soft)


def halo_kernel(direct, dk_soft, dv_soft, *refs):
    way = links(direct)
    span = dk_soft.shape[0]
    if direct:
        dstate, to_a, to_b, to_c = refs
        to_c[...] = dstate[...].astype(BF)
    else:
        to_a, to_b = refs
    for out, side in ((to_a, way["halo_a"]), (to_b, way["halo_b"])):
        first = side * (span - HALF)
        out[:, :DH] = dk_soft[at(first), :].astype(BF)
        out[:, DH : 2 * DH] = dv_soft[at(first), :].astype(BF)
        if direct:
            out[:, 2 * DH :] = dstate[...].astype(BF)


def chunk_kernel(own, got, to_a, to_b, to_c, chunk, heads):
    core, z, _ = places()
    way = links(True)
    half = chunk.shape[0]
    for group in range(2):
        rows = slice(group * half, (group + 1) * half)
        heads[2 * group + core] = own[rows, :]
        heads[2 * group + 1 - core] = got[rows, :]
    chunk[...] = heads[z]
    for out, step in ((to_a, way["first"]), (to_b, way["second"]), (to_c, 2)):
        out[...] = heads[z ^ step].astype(BF)


def weight_sum_kernel(scale, chunk, a, b, c, out):
    out[...] = scale * (chunk[...] + a[...].astype(F32) + b[...].astype(F32) + c[...].astype(F32))


def final_kernel(
    direct, dstate, mine, pair, dq_soft, dk_soft, dv_soft, dq_lin, dq_lin_pair, a, b, *refs
):
    core, _, _ = places()
    way = links(direct)
    rows = mine.shape[0]
    total = dstate[...]
    own_out, pair_out, dk_all, dv_all = refs[-4:]
    if direct:
        total = total + a[:, 2 * DH :].astype(F32) + b[:, 2 * DH :].astype(F32)
        total = total + refs[0][...].astype(F32)
    for source, out, cols in ((dk_soft, dk_all, slice(0, DH)), (dv_soft, dv_all, slice(DH, 2 * DH))):
        out[...] = source[HALF : HALF + 2 * rows, :]
        out[at(way["block_a"] * rows, rows), :] += a[:, cols].astype(F32)
        out[at(way["block_b"] * rows, rows), :] += b[:, cols].astype(F32)
    high, low = halves(total)
    for source, dq, out, place in ((mine, dq_lin, own_out, core), (pair, dq_lin_pair, pair_out, 1 - core)):
        here = at(place * rows, rows)
        out[:, QS] = dq_soft[here, :].astype(BF)
        out[:, KS] = dk_all[here, :].astype(BF)
        out[:, VS] = dv_all[here, :].astype(BF)
        wide, values = source[:, KL].astype(F32), source[:, VL]
        out[:, QL] = dq[...]
        out[:, KL] = ((mm(values, high, NT) + mm(values, low, NT)) * unit_slope(wide)).astype(BF)
        out[:, VL] = mm3(unit_plus(wide), total).astype(BF)


def output_kernel(own, pair, dq, dk, dv):
    core, _, _ = places()
    for source, first in ((own, core * DH), (pair, (1 - core) * DH)):
        for index, out in enumerate((dq, dk, dv)):
            out[0, :, at(first)] = source[:, index * DH : (index + 1) * DH]
            out[0, :, at(SOFT + first)] = source[:, (3 + index) * DH : (4 + index) * DH]


def weight_join_kernel(both, got, _, out):
    _, _, dp = places()
    way = links(True)
    width = both.shape[1] // 2
    for source, index, step in ((both, 0, 0), (both, 1, way["step"]), (got, 0, way["other"]), (got, 1, 3)):
        out[:, at((dp ^ step) * width, width)] = source[:, index * width : (index + 1) * width].astype(F32)


def body(n_dp, n_z, queries, key_rows, value_rows, out_grad, out_weight, norm_gain):
    rows, model = out_grad.shape[1:]
    axes = ("z", "core")
    pair_perm = [(0, 1), (1, 0)]
    core = lax.axis_index("core")
    direct = n_z == HEADS and n_dp == 4
    width = model // n_dp
    half = DH // 2

    def over_core(value):
        return lax.ppermute(value, "core", pair_perm)

    def over_z(value, which, back=False):
        pairs = []
        for z in range(n_z):
            for c in range(2):
                if direct:
                    there = z ^ (1 + 2 * c, 3 - 2 * c, 2)[which]
                else:
                    there = (z + (1 if (which == 1) != back else -1)) % n_z
                pairs.append((2 * z + c, 2 * there + c))
        return lax.ppermute(value, axes, pairs)

    def from_matching(value, step):
        pairs = [(2 * z + z % 2, 2 * (z ^ step) + z % 2) for z in range(n_z)]
        return lax.ppermute(value, axes, pairs)

    def over_dp(value, which):
        pairs = [
            (2 * d + c, 2 * (d ^ (1 + c, 2 - c)[which]) + c) for d in range(n_dp) for c in range(2)
        ]
        return lax.ppermute(value, ("dp", "core"), pairs)

    def hbm(value):
        return pltpu.with_memory_space_constraint(value, pltpu.HBM)

    sent_cols = 7 * DH if direct else 6 * DH
    mine, other, og, gain = call(
        pack_kernel, "pack",
        [
            like((rows, 6 * DH), BF), like((rows, sent_cols), BF), like((rows, model), BF),
            like((1, DH), F32),
        ],
        [hbm(x) for x in (queries, key_rows, value_rows, out_grad, out_weight, norm_gain)],
        scratch=[pltpu.SemaphoreType.DMA((16,))],
        spaces=[pl.BlockSpec(memory_space=pltpu.HBM)] * 6,
    )
    pair = over_core(other)
    og_recv = over_core(og)
    wide = 3 * DH if direct else 2 * DH
    state, to_a, to_b, *rest = call(
        functools.partial(state_kernel, direct), "state",
        [like((DH, DH), F32), like((rows, wide), BF), like((rows, wide), BF)]
        + [like((DH, DH), BF), like((DH, width), BF)] * direct,
        [mine, pair] + [other] * direct,
        flops=4 * 2 * rows * DH * DH,
    )
    if direct:
        to_c, w_head = rest
        w_got = from_matching(w_head, 2)
        a, b, c = over_z(to_a, 0), over_z(to_b, 1), [over_z(to_c, 2)]
        w_two = call(w_two_kernel, "w_two", [like((2 * DH, width), BF)], [w_head, w_got])[0]
        w_got = from_matching(w_two, 1)
        w_own = call(w_pick_kernel, "w_pick", [like((2 * DH, width), BF)], [w_two, w_got])[0]
        w_got = over_dp(w_own, 0)
        w_half = call(join_kernel, "w_half", [like((2 * DH, 2 * width), BF)], [w_own, w_got])[0]
        weights = [w_half, over_dp(w_half, 1)]
    else:
        a, b, c = over_z(to_a, 0), over_z(to_b, 1), []
        state = lax.psum(state, "z")
        weights = lax.all_gather(out_weight, axes, axis=0, tiled=True).reshape(2, 2, DH, model)
        weights = [jnp.where(core == 0, weights[:, 0], weights[:, 1]).reshape(2 * DH, model)]

    span = 2 * rows + 2 * HALF
    keep_width = 2 * width if direct else model
    wg_flops = 2 * 2 * rows * DH * model
    qs, ks, vs, ogs, probs, attn, keep_soft, *soft_send = call(
        functools.partial(soft_forward_kernel, direct), "soft_forward",
        [
            like((2 * rows, DH), BF), like((span, DH), BF), like((span, DH), BF),
            like((2 * rows, model), BF), like((2, rows, rows + 2 * HALF), F32), like((2 * rows, DH), F32),
            like((DH, keep_width), F32),
        ] + [like((DH, 2 * width), BF)] * direct,
        [mine, pair, og, og_recv, a, b],
        flops=wg_flops,
    )
    u, total, keep_lin, *sent = call(
        functools.partial(lin_forward_kernel, direct), "lin_forward",
        [like((2 * rows, DH), F32), like((DH, DH), F32), like((DH, keep_width), F32)]
        + [like((2 * DH, 2 * width), BF)] * direct,
        [state, mine, pair, ogs, gain] + ([a, b] + c + soft_send if direct else []),
        flops=wg_flops,
    )
    if direct:
        got = over_dp(sent[0], 0)
        keep, sent = call(
            fold_kernel, "fold", [like((2 * DH, width), F32), like((2 * DH, width), BF)],
            [keep_soft, keep_lin, got],
        )
        got = over_dp(sent, 1)
        row_own, row_send = call(
            rows_kernel, "rows", [like((2 * half, width), F32)] * 2, [keep, got],
            scratch=[pltpu.VMEM((2 * DH, width), F32)],
        )
        row_recv = over_core(row_send)
        *to_chips, chunk = call(
            chunk_kernel, "chunk", [like((half, width), BF)] * 3 + [like((half, width), F32)],
            [row_own, row_recv], scratch=[pltpu.VMEM((HEADS, half, width), F32)],
        )
        chunks = [over_z(value, which) for which, value in enumerate(to_chips)]
    dq_lin, dq_lin_pair, dstate, dq_soft, dk_soft, dv_soft = call(
        functools.partial(backward_kernel, direct), "backward",
        [
            like((rows, DH), BF), like((rows, DH), BF), like((DH, DH), F32),
            like((2 * rows, DH), F32), like((span, DH), F32), like((span, DH), F32),
        ],
        weights + [ogs, u, total, mine, pair, gain, qs, ks, vs, probs, attn],
        scratch=[pltpu.VMEM((2 * rows, 2 * DH), F32), pltpu.VMEM((2 * rows, DH), F32)]
        + [pltpu.VMEM((2 * DH, model), BF)] * direct,
        flops=5 * wg_flops,
    )
    scale = 1.0 / math.sqrt(n_dp * n_z * 2 * rows)
    to_a, to_b, *to_c = call(
        functools.partial(halo_kernel, direct), "halo",
        [like((rows, wide), BF), like((rows, wide), BF)] + [like((DH, DH), BF)] * direct,
        [dk_soft, dv_soft] + [dstate] * direct,
    )
    a, b = over_z(to_a, 0, True), over_z(to_b, 1, True)
    c = [over_z(value, 2) for value in to_c]
    if not direct:
        dstate = lax.psum(dstate, "z")
        groups = jnp.stack([keep_soft, keep_lin])
        slots = jnp.stack([jnp.where(core == head, groups, 0.0) for head in range(2)], axis=1)
        local = lax.psum_scatter(
            slots.reshape(HEADS * DH, model), axes, scatter_dimension=0, tiled=True
        )
        weight_grad = lax.psum(local, "dp") * scale
    own_out, to_pair = call(
        functools.partial(final_kernel, direct), "final",
        [like((rows, 6 * DH), BF), like((rows, 6 * DH), BF)],
        [dstate, mine, pair, dq_soft, dk_soft, dv_soft, dq_lin, dq_lin_pair, a, b] + c,
        scratch=[pltpu.VMEM((2 * rows, DH), F32)] * 2,
        flops=wg_flops // 4,
    )
    from_pair = over_core(to_pair)
    shape = like((1, rows, HEADS * DH), BF)
    dq, dk, dv = call(output_kernel, "outputs", [shape] * 3, [own_out, from_pair])
    if direct:
        summed = call(
            functools.partial(weight_sum_kernel, scale), "weight_sum", [like((half, width), F32)],
            [chunk] + chunks,
        )[0]
        got = over_dp(summed, 0)
        both = call(join_kernel, "both", [like((half, 2 * width), F32)], [summed, got])[0]
        got = over_dp(both, 1)
        vmem = pl.BlockSpec(memory_space=pltpu.VMEM)
        weight_grad = call(
            weight_join_kernel, "weight_join", [like((half, model), F32)], [both, got, hbm(dq)],
            spaces=[vmem, vmem, pl.BlockSpec(memory_space=pltpu.HBM)],
        )[0]
    return dq, dk, dv, weight_grad


def solution(mesh):
    n_dp, n_seq = mesh.shape["dp"], mesh.shape["seq"]
    blocks = Mesh(mesh.devices.reshape(n_dp, n_seq // 2, 2), ("dp", "z", "core"))
    tokens, heads = P("dp", ("z", "core"), None), P(("z", "core"), None)
    return jax.shard_map(
        functools.partial(body, n_dp, n_seq // 2),
        mesh=blocks,
        in_specs=(tokens, tokens, tokens, tokens, heads, P()),
        out_specs=(tokens, tokens, tokens, heads),
        check_vma=False,
    )
```

```python
import functools
import math

import jax
import jax.numpy as jnp
from jax import lax
from jax.experimental import pallas as pl
from jax.experimental.pallas import tpu as pltpu
from jax.sharding import Mesh
from jax.sharding import PartitionSpec as P

DH = 128
SOFT_HEADS = 2
LIN_HEADS = 2
HEADS = SOFT_HEADS + LIN_HEADS
WINDOW = 256
HALF = 128
norm_eps = 1e-06
FACTOR = DH ** (-0.5)
BF = jnp.bfloat16
F32 = jnp.float32
NN = (((1,), (0,)), ((), ()))
NT = (((1,), (1,)), ((), ()))
TN = (((0,), (0,)), ((), ()))


def unit_plus(values):
    return jnp.where(values > 0, values + 1.0, jnp.exp(jnp.minimum(values, 0.0)))


def unit_slope(values):
    return jnp.where(values > 0, 1.0, jnp.exp(jnp.minimum(values, 0.0)))


def mm(a, b, dims=NN):
    return lax.dot_general(a, b, dims, preferred_element_type=F32)


def halves(x):
    high = x.astype(BF)
    return high, (x - high.astype(F32)).astype(BF)


def mm3(a, b, dims=NN):
    a_high, a_low = halves(a)
    b_high, b_low = halves(b)
    return mm(a_high, b_high, dims) + (mm(a_high, b_low, dims) + mm(a_low, b_high, dims))


def mm2(a, b, dims=NN):
    a_high, a_low = halves(a)
    return mm(a_high, b, dims) + mm(a_low, b, dims)


def at(start, size=DH):
    return pl.ds(pl.multiple_of(start, size), size)


def places():
    return lax.axis_index("core"), lax.axis_index("z"), lax.axis_index("dp")


def call(kernel, name, outs, args, scratch=(), flops=0, spaces=None):
    vmem = pl.BlockSpec(memory_space=pltpu.VMEM)
    size = sum(math.prod(x.shape) * x.dtype.itemsize for x in list(args) + list(outs))
    return pl.pallas_call(
        kernel,
        name=name,
        out_shape=list(outs),
        in_specs=spaces or [vmem] * len(args),
        out_specs=[vmem] * len(outs),
        scratch_shapes=list(scratch),
        compiler_params=pltpu.CompilerParams(vmem_limit_bytes=24 * 2**20),
        cost_estimate=pl.CostEstimate(flops=flops, bytes_accessed=size, transcendentals=0),
    )(*args)


def like(shape, dtype):
    return jax.ShapeDtypeStruct(shape, dtype)


QS, KS, VS, QL, KL, VL = (slice(i * DH, (i + 1) * DH) for i in range(6))
SOFT = SOFT_HEADS * DH


def links(direct):
    core, z, dp = places()
    step = 1 + core
    turn = lax.rem(z + core, 2) if direct else 1
    return dict(
        first=1 + 2 * core, second=3 - 2 * core, step=step, other=3 - step,
        block_a=1 - turn, block_b=turn,
        halo_a=(1 - turn if direct else 1), halo_b=(turn if direct else 0),
    )


def pack_kernel(q, k, v, og, w, gain, mine_out, other_out, og_out, w_out, gain_out, sems):
    core, _, dp = places()
    mine, other = core * DH, (1 - core) * DH
    copies = []

    def fetch(source, target):
        copy = pltpu.make_async_copy(source, target, sems.at[len(copies)])
        copy.start()
        copies.append(copy)

    for index, array in enumerate((q, k, v)):
        for group in range(2):
            cols = slice((3 * group + index) * DH, (3 * group + index + 1) * DH)
            fetch(array.at[0, :, at(SOFT * group + other)], other_out.at[:, cols])
            fetch(array.at[0, :, at(SOFT * group + mine)], mine_out.at[:, cols])
    width = w_out.shape[1]
    fetch(w.at[:, at(dp * width, width)], w_out)
    fetch(og.at[0], og_out)
    fetch(gain.at[at(mine)], gain_out.at[0])
    for copy in copies:
        copy.wait()


def state_kernel(direct, mine, pair, *refs):
    core, _, _ = places()
    total = mm2(unit_plus(mine[:, KL].astype(F32)), mine[:, VL], TN) + mm2(
        unit_plus(pair[:, KL].astype(F32)), pair[:, VL], TN
    )
    if direct:
        w, state, to_a, to_b, to_c = refs
    else:
        state, to_a, to_b = refs
    state[...] = total
    way = links(direct)
    for out, block in ((to_a, way["block_a"]), (to_b, way["block_b"])):
        here = block == core
        out[:, :DH] = jnp.where(here, mine[:, KS], pair[:, KS])
        out[:, DH : 2 * DH] = jnp.where(here, mine[:, VS], pair[:, VS])
    if direct:
        rows = w.shape[0]
        for out, first in ((to_a, 2 * DH), (to_b, 2 * DH), (to_c, 0)):
            out[:, first : first + DH] = total.astype(BF)
            out[:rows, first + DH :] = w[:, :DH]
            out[rows:, first + DH :] = w[:, DH:]


def relay_kernel(w, a, b, c, keep, send, heads):
    core, z, _ = places()
    way = links(True)
    rows = w.shape[0]
    heads[z] = w[...]
    for source, first, step in ((a, 3 * DH, way["first"]), (b, 3 * DH, way["second"]), (c, DH, 2)):
        heads[z ^ step, :, :DH] = source[:rows, first:]
        heads[z ^ step, :, DH:] = source[rows:, first:]
    for group in range(2):
        keep[group] = heads[2 * group + core]
        send[group] = heads[2 * group + 1 - core]


def w_rows_kernel(keep, got, out):
    core, _, _ = places()
    half = keep.shape[1]
    for group in range(2):
        out[at(group * DH + core * half, half), :] = keep[group]
        out[at(group * DH + (1 - core) * half, half), :] = got[group]


def join_kernel(first, second, *refs):
    out = refs[-1]
    width = first.shape[1]
    out[:, :width] = first[...]
    out[:, width:] = second[...]


def weight_parts(direct, attn, ogs, send, keep):
    high, low = halves(attn)
    if not direct:
        keep[...] = mm(high, ogs[...], TN) + mm(low, ogs[...], TN)
        return
    _, _, dp = places()
    way = links(True)
    width = send.shape[1] // 2
    for index, step in enumerate((0, way["other"])):
        cols = slice(index * width, (index + 1) * width)
        near, far = at((dp ^ step) * width, width), at((dp ^ step ^ way["step"]) * width, width)
        keep[:, cols] = mm(high, ogs[:, near], TN) + mm(low, ogs[:, near], TN)
        send[:, cols] = (mm(high, ogs[:, far], TN) + mm(low, ogs[:, far], TN)).astype(BF)


def soft_forward_kernel(
    direct, mine, pair, og, og_recv, a, b, qs, ks, vs, ogs, probs, attn, keep, *send
):
    core, _, _ = places()
    way = links(direct)
    rows = og.shape[0]
    own_at, pair_at = core * rows, (1 - core) * rows
    for source, first in ((mine, own_at), (pair, pair_at)):
        qs[at(first, rows), :] = source[:, QS]
        ks[at(HALF + first, rows), :] = source[:, KS]
        vs[at(HALF + first, rows), :] = source[:, VS]
    for source, side in ((a, way["halo_a"]), (b, way["halo_b"])):
        first = side * (HALF + 2 * rows)
        ks[at(first), :] = source[:, :DH]
        vs[at(first), :] = source[:, DH : 2 * DH]
    ogs[at(own_at, rows), :] = og[...]
    ogs[at(pair_at, rows), :] = og_recv[...]
    span = rows + 2 * HALF
    row_pos = lax.broadcasted_iota(jnp.int32, (rows, span), 0)
    col_pos = lax.broadcasted_iota(jnp.int32, (rows, span), 1)
    inside = (col_pos >= row_pos) & (col_pos < row_pos + WINDOW)
    for block in range(2):
        here, window = slice(block * rows, (block + 1) * rows), slice(block * rows, block * rows + span)
        scores = mm(qs[here, :], ks[window, :], NT) * FACTOR
        scores = jnp.where(inside, scores, -1e30)
        peak = jnp.max(scores, axis=1, keepdims=True)
        terms = jnp.where(inside, jnp.exp(scores - peak), 0.0)
        share = terms / jnp.sum(terms, axis=1, keepdims=True)
        probs[block] = share
        attn[here, :] = mm(share.astype(BF), vs[window, :])
    weight_parts(direct, attn[...], ogs, send[0] if send else None, keep)


def lin_forward_kernel(direct, state, mine, pair, ogs, gain, *refs):
    core, _, _ = places()
    rows = mine.shape[0]
    total = state[...]
    if direct:
        a, b, c, soft_send, u_out, total_out, keep, out = refs
        total = total + a[:, 2 * DH : 3 * DH].astype(F32) + b[:, 2 * DH : 3 * DH].astype(F32)
        total = total + c[:, :DH].astype(F32)
    else:
        u_out, total_out, keep = refs
    total_out[...] = total
    u_out[at(core * rows, rows), :] = mm3(unit_plus(mine[:, QL].astype(F32)), total)
    u_out[at((1 - core) * rows, rows), :] = mm3(unit_plus(pair[:, QL].astype(F32)), total)
    u = u_out[...]
    r = lax.rsqrt(jnp.mean(u * u, axis=1, keepdims=True) + norm_eps)
    attn = gain[...] * u * r
    weight_parts(direct, attn, ogs, out.at[DH:, :] if direct else None, keep)
    if direct:
        out[:DH, :] = soft_send[...]


def fold_kernel(keep_soft, keep_lin, got, keep, send):
    width = keep.shape[1]
    for rows, source in ((slice(0, DH), keep_soft), (slice(DH, 2 * DH), keep_lin)):
        keep[rows, :] = source[:, :width] + got[rows, :width].astype(F32)
        send[rows, :] = (source[:, width:] + got[rows, width:].astype(F32)).astype(BF)


def rows_kernel(keep, got, own, send, total):
    core, _, _ = places()
    half = DH // 2
    total[...] = keep[...] + got[...].astype(F32)
    for group in range(2):
        out = slice(group * half, (group + 1) * half)
        own[out, :] = total[at(group * DH + core * half, half), :]
        send[out, :] = total[at(group * DH + (1 - core) * half, half), :]


def lin_backward(u, total, dattn, mine, pair, gain, dq_own, dq_pair, dstate, grads):
    core, _, _ = places()
    rows = mine.shape[0]
    u_all = u[...]
    r = lax.rsqrt(jnp.mean(u_all * u_all, axis=1, keepdims=True) + norm_eps)
    lin_grad = gain[...] * dattn[:, DH:]
    grads[...] = r * lin_grad - u_all * (r * r * r) * jnp.mean(lin_grad * u_all, axis=1, keepdims=True)
    total_state = total[...]
    result = jnp.zeros(dstate.shape, F32)
    for first, source, out in ((core * rows, mine, dq_own), ((1 - core) * rows, pair, dq_pair)):
        wide = source[:, QL].astype(F32)
        part = grads[at(first, rows), :]
        result = result + mm3(unit_plus(wide), part, TN)
        out[...] = (mm3(part, total_state, NT) * unit_slope(wide)).astype(BF)
    dstate[...] = result


def soft_backward(qs, ks, vs, probs, attn, dattn, dq_all, dk_all, dv_all):
    rows = qs.shape[0] // 2
    span = rows + 2 * HALF
    dk_all[...] = jnp.zeros_like(dk_all)
    dv_all[...] = jnp.zeros_like(dv_all)
    for block in range(2):
        here, window = slice(block * rows, (block + 1) * rows), slice(block * rows, block * rows + span)
        grad = dattn[here, :DH].astype(BF)
        share = probs[block]
        delta = jnp.sum(grad.astype(F32) * attn[here, :], axis=1, keepdims=True)
        dscore = (share * (mm(grad, vs[window, :], NT) - delta)).astype(BF)
        dq_all[here, :] = mm(dscore, ks[window, :]) * FACTOR
        dk_all[window, :] += mm(dscore, qs[here, :], TN) * FACTOR
        dv_all[window, :] += mm(share.astype(BF), grad, TN)


def backward_kernel(direct, *refs):
    if direct:
        sent, got = refs[:2]
        refs = refs[3:]
    else:
        weights = refs[0]
        refs = refs[1:]
    (ogs, u, total, mine, pair, gain, qs, ks, vs, probs, attn,
     dq_lin, dq_lin_pair, dstate, dq_soft, dk_soft, dv_soft, dattn, grads, *scratch) = refs
    if direct:
        _, _, dp = places()
        way = links(True)
        weights = scratch[0]
        width = weights.shape[1] // 4
        for source, index, step in (
            (sent, 0, 0), (sent, 1, way["step"]), (got, 0, way["other"]), (got, 1, 3),
        ):
            weights[:, at((dp ^ step) * width, width)] = source[:, index * width : (index + 1) * width]
    dattn[...] = mm(ogs[...], weights[...], NT)
    lin_backward(u, total, dattn, mine, pair, gain, dq_lin, dq_lin_pair, dstate, grads)
    soft_backward(qs, ks, vs, probs, attn, dattn, dq_soft, dk_soft, dv_soft)


def halo_kernel(direct, dk_soft, dv_soft, *refs):
    way = links(direct)
    span = dk_soft.shape[0]
    if direct:
        dstate, _, to_a, to_b, to_c = refs
        to_c[...] = dstate[...].astype(BF)
    else:
        to_a, to_b = refs
    for out, side in ((to_a, way["halo_a"]), (to_b, way["halo_b"])):
        first = side * (span - HALF)
        out[:, :DH] = dk_soft[at(first), :].astype(BF)
        out[:, DH : 2 * DH] = dv_soft[at(first), :].astype(BF)
        if direct:
            out[:, 2 * DH :] = dstate[...].astype(BF)


def chunk_kernel(own, got, to_a, to_b, to_c, chunk, heads):
    core, z, _ = places()
    way = links(True)
    half = chunk.shape[0]
    for group in range(2):
        rows = slice(group * half, (group + 1) * half)
        heads[2 * group + core] = own[rows, :]
        heads[2 * group + 1 - core] = got[rows, :]
    chunk[...] = heads[z]
    for out, step in ((to_a, way["first"]), (to_b, way["second"]), (to_c, 2)):
        out[...] = heads[z ^ step].astype(BF)


def weight_sum_kernel(scale, chunk, a, b, c, out):
    total = chunk[...] + a[...].astype(F32) + b[...].astype(F32) + c[...].astype(F32)
    out[...] = (scale * total).astype(out.dtype)


def final_kernel(
    direct, dstate, mine, pair, dq_soft, dk_soft, dv_soft, dq_lin, dq_lin_pair, a, b, *refs
):
    core, _, _ = places()
    way = links(direct)
    rows = mine.shape[0]
    total = dstate[...]
    own_out, pair_out, dk_all, dv_all = refs[-4:]
    if direct:
        total = total + a[:, 2 * DH :].astype(F32) + b[:, 2 * DH :].astype(F32)
        total = total + refs[0][...].astype(F32)
    for source, out, cols in ((dk_soft, dk_all, slice(0, DH)), (dv_soft, dv_all, slice(DH, 2 * DH))):
        out[...] = source[HALF : HALF + 2 * rows, :]
        out[at(way["block_a"] * rows, rows), :] += a[:, cols].astype(F32)
        out[at(way["block_b"] * rows, rows), :] += b[:, cols].astype(F32)
    high, low = halves(total)
    for source, dq, out, place in ((mine, dq_lin, own_out, core), (pair, dq_lin_pair, pair_out, 1 - core)):
        here = at(place * rows, rows)
        out[:, QS] = dq_soft[here, :].astype(BF)
        out[:, KS] = dk_all[here, :].astype(BF)
        out[:, VS] = dv_all[here, :].astype(BF)
        wide, values = source[:, KL].astype(F32), source[:, VL]
        out[:, QL] = dq[...]
        out[:, KL] = ((mm(values, high, NT) + mm(values, low, NT)) * unit_slope(wide)).astype(BF)
        out[:, VL] = mm3(unit_plus(wide), total).astype(BF)


def output_kernel(own, pair, dq, dk, dv):
    core, _, _ = places()
    for source, first in ((own, core * DH), (pair, (1 - core) * DH)):
        for index, out in enumerate((dq, dk, dv)):
            out[0, :, at(first)] = source[:, index * DH : (index + 1) * DH]
            out[0, :, at(SOFT + first)] = source[:, (3 + index) * DH : (4 + index) * DH]


def weight_join_kernel(both, got, out):
    _, _, dp = places()
    way = links(True)
    width = both.shape[1] // 2
    for source, index, step in ((both, 0, 0), (both, 1, way["step"]), (got, 0, way["other"]), (got, 1, 3)):
        out[:, at((dp ^ step) * width, width)] = source[:, index * width : (index + 1) * width].astype(F32)


def body(n_dp, n_z, queries, key_rows, value_rows, out_grad, out_weight, norm_gain):
    rows, model = out_grad.shape[1:]
    axes = ("z", "core")
    pair_perm = [(0, 1), (1, 0)]
    core = lax.axis_index("core")
    direct = n_z == HEADS and n_dp == 4
    width = model // n_dp
    half = DH // 2

    scale = 1.0 / math.sqrt(n_dp * n_z * 2 * rows)

    def over_core(value):
        return lax.ppermute(value, "core", pair_perm)

    def over_z(value, which, back=False):
        pairs = []
        for z in range(n_z):
            for c in range(2):
                if direct:
                    there = z ^ (1 + 2 * c, 3 - 2 * c, 2)[which]
                else:
                    there = (z + (1 if (which == 1) != back else -1)) % n_z
                pairs.append((2 * z + c, 2 * there + c))
        return lax.ppermute(value, axes, pairs)

    def over_dp(value, which):
        pairs = [
            (2 * d + c, 2 * (d ^ (1 + c, 2 - c)[which]) + c) for d in range(n_dp) for c in range(2)
        ]
        return lax.ppermute(value, ("dp", "core"), pairs)

    vmem = pl.BlockSpec(memory_space=pltpu.VMEM)

    def hbm(value):
        return pltpu.with_memory_space_constraint(value, pltpu.HBM)

    mine, other, og, w_part, gain = call(
        pack_kernel, "pack",
        [
            like((rows, 6 * DH), BF), like((rows, 6 * DH), BF), like((rows, model), BF),
            like((out_weight.shape[0], width), BF), like((1, DH), F32),
        ],
        [hbm(x) for x in (queries, key_rows, value_rows, out_grad, out_weight, norm_gain)],
        scratch=[pltpu.SemaphoreType.DMA((16,))],
        spaces=[pl.BlockSpec(memory_space=pltpu.HBM)] * 6,
    )
    pair = over_core(other)
    og_recv = over_core(og)
    wide = 4 * DH if direct else 2 * DH
    state, to_a, to_b, *rest = call(
        functools.partial(state_kernel, direct), "state",
        [like((DH, DH), F32), like((rows, wide), BF), like((rows, wide), BF)]
        + [like((rows, 2 * DH), BF)] * direct,
        [mine, pair] + [w_part] * direct,
        flops=4 * 2 * rows * DH * DH,
    )
    if direct:
        a, b, c = over_z(to_a, 0), over_z(to_b, 1), [over_z(rest[0], 2)]
        w_keep, w_send = call(
            relay_kernel, "relay", [like((2, half, width), BF)] * 2, [w_part, a, b] + c,
            scratch=[pltpu.VMEM((HEADS, half, width), BF)],
        )
        w_own = call(
            w_rows_kernel, "w_rows", [like((2 * DH, width), BF)], [w_keep, over_core(w_send)]
        )[0]
        w_got = over_dp(w_own, 0)
    else:
        a, b, c = over_z(to_a, 0), over_z(to_b, 1), []
        state = lax.psum(state, "z")
        weights = lax.all_gather(out_weight, axes, axis=0, tiled=True).reshape(2, 2, DH, model)
        weights = [jnp.where(core == 0, weights[:, 0], weights[:, 1]).reshape(2 * DH, model)]

    span = 2 * rows + 2 * HALF
    keep_width = 2 * width if direct else model
    wg_flops = 2 * 2 * rows * DH * model
    qs, ks, vs, ogs, probs, attn, keep_soft, *soft_send = call(
        functools.partial(soft_forward_kernel, direct), "soft_forward",
        [
            like((2 * rows, DH), BF), like((span, DH), BF), like((span, DH), BF),
            like((2 * rows, model), BF), like((2, rows, rows + 2 * HALF), F32), like((2 * rows, DH), F32),
            like((DH, keep_width), F32),
        ] + [like((DH, 2 * width), BF)] * direct,
        [mine, pair, og, og_recv, a, b],
        flops=wg_flops,
    )
    u, total, keep_lin, *sent = call(
        functools.partial(lin_forward_kernel, direct), "lin_forward",
        [like((2 * rows, DH), F32), like((DH, DH), F32), like((DH, keep_width), F32)]
        + [like((2 * DH, 2 * width), BF)] * direct,
        [state, mine, pair, ogs, gain] + ([a, b] + c + soft_send if direct else []),
        flops=wg_flops,
    )
    if direct:
        got = over_dp(sent[0], 0)
        keep, sent = call(
            fold_kernel, "fold", [like((2 * DH, width), F32), like((2 * DH, width), BF)],
            [keep_soft, keep_lin, got],
        )
        w_half = call(
            join_kernel, "w_half", [like((2 * DH, 2 * width), BF)], [w_own, w_got, sent]
        )[0]
        weights = [w_half, over_dp(w_half, 1)]
        got = over_dp(sent, 1)
        row_own, row_send = call(
            rows_kernel, "rows", [like((2 * half, width), F32)] * 2, [keep, got],
            scratch=[pltpu.VMEM((2 * DH, width), F32)],
        )
        row_recv = over_core(row_send)
        *to_chips, chunk = call(
            chunk_kernel, "chunk", [like((half, width), BF)] * 3 + [like((half, width), F32)],
            [row_own, row_recv], scratch=[pltpu.VMEM((HEADS, half, width), F32)],
        )
        chunks = [over_z(value, which) for which, value in enumerate(to_chips)]
        summed = call(
            functools.partial(weight_sum_kernel, scale), "weight_sum", [like((half, width), BF)],
            [chunk] + chunks,
        )[0]
        got = over_dp(summed, 0)
        both = call(join_kernel, "both", [like((half, 2 * width), BF)], [summed, got])[0]
        got = over_dp(both, 1)
        weight_grad = call(
            weight_join_kernel, "weight_join", [like((half, model), F32)], [both, got]
        )[0]
    if direct:
        weights.append(chunk)
    dq_lin, dq_lin_pair, dstate, dq_soft, dk_soft, dv_soft = call(
        functools.partial(backward_kernel, direct), "backward",
        [
            like((rows, DH), BF), like((rows, DH), BF), like((DH, DH), F32),
            like((2 * rows, DH), F32), like((span, DH), F32), like((span, DH), F32),
        ],
        weights + [ogs, u, total, mine, pair, gain, qs, ks, vs, probs, attn],
        scratch=[pltpu.VMEM((2 * rows, 2 * DH), F32), pltpu.VMEM((2 * rows, DH), F32)]
        + [pltpu.VMEM((2 * DH, model), BF)] * direct,
        flops=5 * wg_flops,
    )
    wide = 3 * DH if direct else 2 * DH
    to_a, to_b, *to_c = call(
        functools.partial(halo_kernel, direct), "halo",
        [like((rows, wide), BF), like((rows, wide), BF)] + [like((DH, DH), BF)] * direct,
        [dk_soft, dv_soft] + ([dstate, summed] if direct else []),
    )
    a, b = over_z(to_a, 0, True), over_z(to_b, 1, True)
    c = [over_z(value, 2) for value in to_c]
    if not direct:
        dstate = lax.psum(dstate, "z")
        groups = jnp.stack([keep_soft, keep_lin])
        slots = jnp.stack([jnp.where(core == head, groups, 0.0) for head in range(2)], axis=1)
        local = lax.psum_scatter(
            slots.reshape(HEADS * DH, model), axes, scatter_dimension=0, tiled=True
        )
        weight_grad = lax.psum(local, "dp") * scale
    own_out, to_pair = call(
        functools.partial(final_kernel, direct), "final",
        [like((rows, 6 * DH), BF), like((rows, 6 * DH), BF)],
        [dstate, mine, pair, dq_soft, dk_soft, dv_soft, dq_lin, dq_lin_pair, a, b] + c
        + ([hbm(weight_grad)] if direct else []),
        scratch=[pltpu.VMEM((2 * rows, DH), F32)] * 2,
        spaces=[vmem] * 11 + [pl.BlockSpec(memory_space=pltpu.HBM)] if direct else None,
        flops=wg_flops // 4,
    )
    from_pair = over_core(to_pair)
    shape = like((1, rows, HEADS * DH), BF)
    dq, dk, dv = call(output_kernel, "outputs", [shape] * 3, [own_out, from_pair])
    return dq, dk, dv, weight_grad


def solution(mesh):
    n_dp, n_seq = mesh.shape["dp"], mesh.shape["seq"]
    blocks = Mesh(mesh.devices.reshape(n_dp, n_seq // 2, 2), ("dp", "z", "core"))
    tokens, heads = P("dp", ("z", "core"), None), P(("z", "core"), None)
    return jax.shard_map(
        functools.partial(body, n_dp, n_seq // 2),
        mesh=blocks,
        in_specs=(tokens, tokens, tokens, tokens, heads, P()),
        out_specs=(tokens, tokens, tokens, heads),
        check_vma=False,
    )
```

```python
import functools
import math

import jax
import jax.numpy as jnp
from jax import lax
from jax.experimental import pallas as pl
from jax.experimental.pallas import tpu as pltpu
from jax.sharding import Mesh
from jax.sharding import PartitionSpec as P

DH = 128
SOFT_HEADS = 2
LIN_HEADS = 2
HEADS = SOFT_HEADS + LIN_HEADS
WINDOW = 256
HALF = 128
norm_eps = 1e-06
FACTOR = DH ** (-0.5)
BF = jnp.bfloat16
F32 = jnp.float32
NN = (((1,), (0,)), ((), ()))
NT = (((1,), (1,)), ((), ()))
TN = (((0,), (0,)), ((), ()))


def unit_plus(values):
    return jnp.where(values > 0, values + 1.0, jnp.exp(jnp.minimum(values, 0.0)))


def unit_slope(values):
    return jnp.where(values > 0, 1.0, jnp.exp(jnp.minimum(values, 0.0)))


def mm(a, b, dims=NN):
    return lax.dot_general(a, b, dims, preferred_element_type=F32)


def halves(x):
    high = x.astype(BF)
    return high, (x - high.astype(F32)).astype(BF)


def mm3(a, b, dims=NN):
    a_high, a_low = halves(a)
    b_high, b_low = halves(b)
    return mm(a_high, b_high, dims) + (mm(a_high, b_low, dims) + mm(a_low, b_high, dims))


def mm2(a, b, dims=NN):
    a_high, a_low = halves(a)
    return mm(a_high, b, dims) + mm(a_low, b, dims)


def at(start, size=DH):
    return pl.ds(pl.multiple_of(start, size), size)


def places():
    return lax.axis_index("core"), lax.axis_index("z"), lax.axis_index("dp")


def call(kernel, name, outs, args, scratch=(), flops=0, spaces=None):
    vmem = pl.BlockSpec(memory_space=pltpu.VMEM)
    size = sum(math.prod(x.shape) * x.dtype.itemsize for x in list(args) + list(outs))
    return pl.pallas_call(
        kernel,
        name=name,
        out_shape=list(outs),
        in_specs=spaces or [vmem] * len(args),
        out_specs=[vmem] * len(outs),
        scratch_shapes=list(scratch),
        compiler_params=pltpu.CompilerParams(vmem_limit_bytes=24 * 2**20),
        cost_estimate=pl.CostEstimate(flops=flops, bytes_accessed=size, transcendentals=0),
    )(*args)


def like(shape, dtype):
    return jax.ShapeDtypeStruct(shape, dtype)


QS, KS, VS, QL, KL, VL = (slice(i * DH, (i + 1) * DH) for i in range(6))
SOFT = SOFT_HEADS * DH


def links(direct):
    core, z, dp = places()
    step = 1 + core
    turn = lax.rem(z + core, 2) if direct else 1
    return dict(
        first=1 + 2 * core, second=3 - 2 * core, step=step, other=3 - step,
        block_a=1 - turn, block_b=turn,
        halo_a=(1 - turn if direct else 1), halo_b=(turn if direct else 0),
    )


def pack_kernel(q, k, v, og, w, gain, mine_out, og_out, w_out, gain_out, sems):
    core, _, dp = places()
    mine = core * DH
    copies = []

    def fetch(source, target):
        copy = pltpu.make_async_copy(source, target, sems.at[len(copies)])
        copy.start()
        copies.append(copy)

    for index, array in enumerate((q, k, v)):
        for group in range(2):
            cols = slice((3 * group + index) * DH, (3 * group + index + 1) * DH)
            fetch(array.at[0, :, at(SOFT * group + mine)], mine_out.at[:, cols])
    width = w_out.shape[1]
    fetch(w.at[:, at(dp * width, width)], w_out)
    fetch(og.at[0], og_out)
    fetch(gain.at[at(mine)], gain_out.at[0])
    for copy in copies:
        copy.wait()


def state_kernel(direct, mine, q_pair, k_pair, v_pair, state, pair, to_a, to_b, *to_c):
    core, _, _ = places()
    own = core * DH
    for index, source in enumerate((q_pair, k_pair, v_pair)):
        for group in range(2):
            first = (3 * group + index) * DH
            pair[:, first : first + DH] = source[0, :, at(SOFT * group + own)]
    total = mm2(unit_plus(mine[:, KL].astype(F32)), mine[:, VL], TN) + mm2(
        unit_plus(pair[:, KL].astype(F32)), pair[:, VL], TN
    )
    state[...] = total
    way = links(direct)
    for out, block in ((to_a, way["block_a"]), (to_b, way["block_b"])):
        here = block == core
        out[:, :DH] = jnp.where(here, mine[:, KS], pair[:, KS])
        out[:, DH : 2 * DH] = jnp.where(here, mine[:, VS], pair[:, VS])
        if direct:
            out[:, 2 * DH :] = total.astype(BF)
    if direct:
        to_c[0][...] = total.astype(BF)


def w_head_kernel(own, pair, out):
    core, _, dp = places()
    rows, width = own.shape
    out[at(core * rows, rows), :] = own[...]
    out[at((1 - core) * rows, rows), :] = pair[:, at(dp * width, width)]


def w_rows_kernel(own, a, b, c, _, out):
    core, z, _ = places()
    way = links(True)
    group = lax.div(z, 2)

    @pl.when(lax.rem(z, 2) == core)
    def _():
        out[at(group * DH), :] = own[...]
        out[at((1 - group) * DH), :] = c[...]

    @pl.when(lax.rem(z, 2) != core)
    def _():
        out[at(lax.div(z ^ way["first"], 2) * DH), :] = a[...]
        out[at(lax.div(z ^ way["second"], 2) * DH), :] = b[...]


def join_kernel(first, second, *refs):
    out = refs[-1]
    width = first.shape[1]
    out[:, :width] = first[...]
    out[:, width:] = second[...]


def weight_parts(direct, attn, ogs, send, keep):
    high, low = halves(attn)
    if not direct:
        keep[...] = mm(high, ogs[...], TN) + mm(low, ogs[...], TN)
        return
    _, _, dp = places()
    way = links(True)
    width = send.shape[1] // 2
    for index, step in enumerate((0, way["other"])):
        cols = slice(index * width, (index + 1) * width)
        near, far = at((dp ^ step) * width, width), at((dp ^ step ^ way["step"]) * width, width)
        keep[:, cols] = mm(high, ogs[:, near], TN) + mm(low, ogs[:, near], TN)
        send[:, cols] = (mm(high, ogs[:, far], TN) + mm(low, ogs[:, far], TN)).astype(BF)


def soft_forward_kernel(
    direct, mine, pair, og, og_recv, a, b, qs, ks, vs, ogs, probs, attn, keep, *send
):
    core, _, _ = places()
    way = links(direct)
    rows = og.shape[0]
    own_at, pair_at = core * rows, (1 - core) * rows
    for source, first in ((mine, own_at), (pair, pair_at)):
        qs[at(first, rows), :] = source[:, QS]
        ks[at(HALF + first, rows), :] = source[:, KS]
        vs[at(HALF + first, rows), :] = source[:, VS]
    for source, side in ((a, way["halo_a"]), (b, way["halo_b"])):
        first = side * (HALF + 2 * rows)
        ks[at(first), :] = source[:, :DH]
        vs[at(first), :] = source[:, DH : 2 * DH]
    ogs[at(own_at, rows), :] = og[...]
    ogs[at(pair_at, rows), :] = og_recv[...]
    span = rows + 2 * HALF
    row_pos = lax.broadcasted_iota(jnp.int32, (rows, span), 0)
    col_pos = lax.broadcasted_iota(jnp.int32, (rows, span), 1)
    inside = (col_pos >= row_pos) & (col_pos < row_pos + WINDOW)
    for block in range(2):
        here, window = slice(block * rows, (block + 1) * rows), slice(block * rows, block * rows + span)
        scores = mm(qs[here, :], ks[window, :], NT) * FACTOR
        scores = jnp.where(inside, scores, -1e30)
        peak = jnp.max(scores, axis=1, keepdims=True)
        terms = jnp.where(inside, jnp.exp(scores - peak), 0.0)
        share = terms / jnp.sum(terms, axis=1, keepdims=True)
        probs[block] = share
        attn[here, :] = mm(share.astype(BF), vs[window, :])
    weight_parts(direct, attn[...], ogs, send[0] if send else None, keep)


def lin_forward_kernel(direct, state, mine, pair, ogs, gain, *refs):
    core, _, _ = places()
    rows = mine.shape[0]
    total = state[...]
    if direct:
        a, b, c, soft_send, u_out, total_out, keep, out = refs
        total = total + a[:, 2 * DH :].astype(F32) + b[:, 2 * DH :].astype(F32) + c[...].astype(F32)
    else:
        u_out, total_out, keep = refs
    total_out[...] = total
    u_out[at(core * rows, rows), :] = mm3(unit_plus(mine[:, QL].astype(F32)), total)
    u_out[at((1 - core) * rows, rows), :] = mm3(unit_plus(pair[:, QL].astype(F32)), total)
    u = u_out[...]
    r = lax.rsqrt(jnp.mean(u * u, axis=1, keepdims=True) + norm_eps)
    attn = gain[...] * u * r
    weight_parts(direct, attn, ogs, out.at[DH:, :] if direct else None, keep)
    if direct:
        out[:DH, :] = soft_send[...]


def fold_kernel(keep_soft, keep_lin, got, _a, _b, _c, keep, send):
    width = keep.shape[1]
    for rows, source in ((slice(0, DH), keep_soft), (slice(DH, 2 * DH), keep_lin)):
        keep[rows, :] = source[:, :width] + got[rows, :width].astype(F32)
        send[rows, :] = (source[:, width:] + got[rows, width:].astype(F32)).astype(BF)


def rows_kernel(keep, got, own, send, total):
    core, _, _ = places()
    half = DH // 2
    total[...] = keep[...] + got[...].astype(F32)
    for group in range(2):
        out = slice(group * half, (group + 1) * half)
        own[out, :] = total[at(group * DH + core * half, half), :]
        send[out, :] = total[at(group * DH + (1 - core) * half, half), :]


def lin_backward(u, total, dattn, mine, pair, gain, dq_own, dq_pair, dstate, grads):
    core, _, _ = places()
    rows = mine.shape[0]
    u_all = u[...]
    r = lax.rsqrt(jnp.mean(u_all * u_all, axis=1, keepdims=True) + norm_eps)
    lin_grad = gain[...] * dattn[:, DH:]
    grads[...] = r * lin_grad - u_all * (r * r * r) * jnp.mean(lin_grad * u_all, axis=1, keepdims=True)
    total_state = total[...]
    result = jnp.zeros(dstate.shape, F32)
    for first, source, out in ((core * rows, mine, dq_own), ((1 - core) * rows, pair, dq_pair)):
        wide = source[:, QL].astype(F32)
        part = grads[at(first, rows), :]
        result = result + mm3(unit_plus(wide), part, TN)
        out[...] = (mm3(part, total_state, NT) * unit_slope(wide)).astype(BF)
    dstate[...] = result


def soft_backward(qs, ks, vs, probs, attn, dattn, dq_all, dk_all, dv_all):
    rows = qs.shape[0] // 2
    span = rows + 2 * HALF
    dk_all[...] = jnp.zeros_like(dk_all)
    dv_all[...] = jnp.zeros_like(dv_all)
    for block in range(2):
        here, window = slice(block * rows, (block + 1) * rows), slice(block * rows, block * rows + span)
        grad = dattn[here, :DH].astype(BF)
        share = probs[block]
        delta = jnp.sum(grad.astype(F32) * attn[here, :], axis=1, keepdims=True)
        dscore = (share * (mm(grad, vs[window, :], NT) - delta)).astype(BF)
        dq_all[here, :] = mm(dscore, ks[window, :]) * FACTOR
        dk_all[window, :] += mm(dscore, qs[here, :], TN) * FACTOR
        dv_all[window, :] += mm(share.astype(BF), grad, TN)


def backward_kernel(direct, *refs):
    if direct:
        sent, got = refs[:2]
        refs = refs[2:]
    else:
        weights = refs[0]
        refs = refs[1:]
    (ogs, u, total, mine, pair, gain, qs, ks, vs, probs, attn,
     dq_lin, dq_lin_pair, dstate, dq_soft, dk_soft, dv_soft, dattn, grads, *scratch) = refs
    if direct:
        _, _, dp = places()
        way = links(True)
        weights = scratch[0]
        width = weights.shape[1] // 4
        for source, index, step in (
            (sent, 0, 0), (sent, 1, way["step"]), (got, 0, way["other"]), (got, 1, 3),
        ):
            weights[:, at((dp ^ step) * width, width)] = source[:, index * width : (index + 1) * width]
    dattn[...] = mm(ogs[...], weights[...], NT)
    lin_backward(u, total, dattn, mine, pair, gain, dq_lin, dq_lin_pair, dstate, grads)
    soft_backward(qs, ks, vs, probs, attn, dattn, dq_soft, dk_soft, dv_soft)


def halo_kernel(direct, dk_soft, dv_soft, *refs):
    way = links(direct)
    span = dk_soft.shape[0]
    if direct:
        dstate, _, _, _, to_a, to_b, to_c = refs
        to_c[...] = dstate[...].astype(BF)
    else:
        to_a, to_b = refs
    for out, side in ((to_a, way["halo_a"]), (to_b, way["halo_b"])):
        first = side * (span - HALF)
        out[:, :DH] = dk_soft[at(first), :].astype(BF)
        out[:, DH : 2 * DH] = dv_soft[at(first), :].astype(BF)
        if direct:
            out[:, 2 * DH :] = dstate[...].astype(BF)


def chunk_kernel(own, got, to_a, to_b, to_c, chunk, heads):
    core, z, _ = places()
    way = links(True)
    half = chunk.shape[0]
    for group in range(2):
        rows = slice(group * half, (group + 1) * half)
        heads[2 * group + core] = own[rows, :]
        heads[2 * group + 1 - core] = got[rows, :]
    chunk[...] = heads[z]
    for out, step in ((to_a, way["first"]), (to_b, way["second"]), (to_c, 2)):
        out[...] = heads[z ^ step].astype(BF)


def weight_sum_kernel(scale, chunk, a, b, c, out):
    total = chunk[...] + a[...].astype(F32) + b[...].astype(F32) + c[...].astype(F32)
    out[...] = (scale * total).astype(out.dtype)


def final_kernel(
    direct, dstate, mine, pair, dq_soft, dk_soft, dv_soft, dq_lin, dq_lin_pair, a, b, *refs
):
    core, _, _ = places()
    way = links(direct)
    rows = mine.shape[0]
    total = dstate[...]
    own_out, pair_out, dk_all, dv_all = refs[-4:]
    if direct:
        total = total + a[:, 2 * DH :].astype(F32) + b[:, 2 * DH :].astype(F32)
        total = total + refs[0][...].astype(F32)
    for source, out, cols in ((dk_soft, dk_all, slice(0, DH)), (dv_soft, dv_all, slice(DH, 2 * DH))):
        out[...] = source[HALF : HALF + 2 * rows, :]
        out[at(way["block_a"] * rows, rows), :] += a[:, cols].astype(F32)
        out[at(way["block_b"] * rows, rows), :] += b[:, cols].astype(F32)
    high, low = halves(total)
    for source, dq, out, place in ((mine, dq_lin, own_out, core), (pair, dq_lin_pair, pair_out, 1 - core)):
        here = at(place * rows, rows)
        out[:, QS] = dq_soft[here, :].astype(BF)
        out[:, KS] = dk_all[here, :].astype(BF)
        out[:, VS] = dv_all[here, :].astype(BF)
        wide, values = source[:, KL].astype(F32), source[:, VL]
        out[:, QL] = dq[...]
        out[:, KL] = ((mm(values, high, NT) + mm(values, low, NT)) * unit_slope(wide)).astype(BF)
        out[:, VL] = mm3(unit_plus(wide), total).astype(BF)


def output_kernel(own, pair, dq, dk, dv):
    core, _, _ = places()
    for source, first in ((own, core * DH), (pair, (1 - core) * DH)):
        for index, out in enumerate((dq, dk, dv)):
            out[0, :, at(first)] = source[:, index * DH : (index + 1) * DH]
            out[0, :, at(SOFT + first)] = source[:, (3 + index) * DH : (4 + index) * DH]


def weight_join_kernel(both, got, out):
    _, _, dp = places()
    way = links(True)
    width = both.shape[1] // 2
    for source, index, step in ((both, 0, 0), (both, 1, way["step"]), (got, 0, way["other"]), (got, 1, 3)):
        out[:, at((dp ^ step) * width, width)] = source[:, index * width : (index + 1) * width].astype(F32)


def body(n_dp, n_z, queries, key_rows, value_rows, out_grad, out_weight, norm_gain):
    rows, model = out_grad.shape[1:]
    axes = ("z", "core")
    pair_perm = [(0, 1), (1, 0)]
    core = lax.axis_index("core")
    direct = n_z == HEADS and n_dp == 4
    width = model // n_dp
    half = DH // 2

    scale = 1.0 / math.sqrt(n_dp * n_z * 2 * rows)

    def over_core(value):
        return lax.ppermute(value, "core", pair_perm)

    def over_z(value, which, back=False):
        pairs = []
        for z in range(n_z):
            for c in range(2):
                if direct:
                    there = z ^ (1 + 2 * c, 3 - 2 * c, 2)[which]
                else:
                    there = (z + (1 if (which == 1) != back else -1)) % n_z
                pairs.append((2 * z + c, 2 * there + c))
        return lax.ppermute(value, axes, pairs)

    def from_matching(value, which):
        pairs = []
        for z in range(n_z):
            c = z % 2
            pairs.append((2 * z + c, 2 * (z ^ (1 + 2 * c, 3 - 2 * c, 2)[which]) + c))
        return lax.ppermute(value, axes, pairs)

    def over_dp(value, which):
        pairs = [
            (2 * d + c, 2 * (d ^ (1 + c, 2 - c)[which]) + c) for d in range(n_dp) for c in range(2)
        ]
        return lax.ppermute(value, ("dp", "core"), pairs)

    vmem = pl.BlockSpec(memory_space=pltpu.VMEM)

    def hbm(value):
        return pltpu.with_memory_space_constraint(value, pltpu.HBM)

    q_pair, k_pair, v_pair = over_core(queries), over_core(key_rows), over_core(value_rows)
    og_recv = over_core(out_grad[0])
    w_pair = over_core(out_weight)
    mine, og, w_part, gain = call(
        pack_kernel, "pack",
        [
            like((rows, 6 * DH), BF), like((rows, model), BF),
            like((out_weight.shape[0], width), BF), like((1, DH), F32),
        ],
        [hbm(x) for x in (queries, key_rows, value_rows, out_grad, out_weight, norm_gain)],
        scratch=[pltpu.SemaphoreType.DMA((9,))],
        spaces=[pl.BlockSpec(memory_space=pltpu.HBM)] * 6,
    )
    wide = 3 * DH if direct else 2 * DH
    state, pair, to_a, to_b, *rest = call(
        functools.partial(state_kernel, direct), "state",
        [like((DH, DH), F32), like((rows, 6 * DH), BF), like((rows, wide), BF), like((rows, wide), BF)]
        + [like((DH, DH), BF)] * direct,
        [mine, q_pair, k_pair, v_pair],
        flops=4 * 2 * rows * DH * DH,
    )
    if direct:
        a, b, c = over_z(to_a, 0), over_z(to_b, 1), [over_z(rest[0], 2)]
    else:
        a, b, c = over_z(to_a, 0), over_z(to_b, 1), []
        state = lax.psum(state, "z")
        weights = lax.all_gather(out_weight, axes, axis=0, tiled=True).reshape(2, 2, DH, model)
        weights = [jnp.where(core == 0, weights[:, 0], weights[:, 1]).reshape(2 * DH, model)]

    span = 2 * rows + 2 * HALF
    keep_width = 2 * width if direct else model
    wg_flops = 2 * 2 * rows * DH * model
    qs, ks, vs, ogs, probs, attn, keep_soft, *soft_send = call(
        functools.partial(soft_forward_kernel, direct), "soft_forward",
        [
            like((2 * rows, DH), BF), like((span, DH), BF), like((span, DH), BF),
            like((2 * rows, model), BF), like((2, rows, rows + 2 * HALF), F32), like((2 * rows, DH), F32),
            like((DH, keep_width), F32),
        ] + [like((DH, 2 * width), BF)] * direct,
        [mine, pair, og, og_recv, a, b],
        flops=wg_flops,
    )
    u, total, keep_lin, *sent = call(
        functools.partial(lin_forward_kernel, direct), "lin_forward",
        [like((2 * rows, DH), F32), like((DH, DH), F32), like((DH, keep_width), F32)]
        + [like((2 * DH, 2 * width), BF)] * direct,
        [state, mine, pair, ogs, gain] + ([a, b] + c + soft_send if direct else []),
        flops=wg_flops,
    )
    if direct:
        got = over_dp(sent[0], 0)
        w_head = call(w_head_kernel, "w_head", [like((DH, width), BF)], [w_part, w_pair])[0]
        w_far = [from_matching(w_head, which) for which in range(3)]
        keep, sent = call(
            fold_kernel, "fold", [like((2 * DH, width), F32), like((2 * DH, width), BF)],
            [keep_soft, keep_lin, got] + w_far,
        )
        w_own = call(
            w_rows_kernel, "w_rows", [like((2 * DH, width), BF)],
            [w_head] + w_far + [sent],
        )[0]
        w_got = over_dp(w_own, 0)
        got = over_dp(sent, 1)
        row_own, row_send = call(
            rows_kernel, "rows", [like((2 * half, width), F32)] * 2, [keep, got],
            scratch=[pltpu.VMEM((2 * DH, width), F32)],
        )
        row_recv = over_core(row_send)
        *to_chips, chunk = call(
            chunk_kernel, "chunk", [like((half, width), BF)] * 3 + [like((half, width), F32)],
            [row_own, row_recv], scratch=[pltpu.VMEM((HEADS, half, width), F32)],
        )
        w_half = call(
            join_kernel, "w_half", [like((2 * DH, 2 * width), BF)], [w_own, w_got, chunk]
        )[0]
        weights = [w_half, over_dp(w_half, 1)]
        chunks = [over_z(value, which) for which, value in enumerate(to_chips)]
        summed = call(
            functools.partial(weight_sum_kernel, scale), "weight_sum", [like((half, width), BF)],
            [chunk] + chunks,
        )[0]
        got = over_dp(summed, 0)
        both = call(join_kernel, "both", [like((half, 2 * width), BF)], [summed, got])[0]
        got = over_dp(both, 1)
        weight_grad = call(
            weight_join_kernel, "weight_join", [like((half, model), F32)], [both, got]
        )[0]
    dq_lin, dq_lin_pair, dstate, dq_soft, dk_soft, dv_soft = call(
        functools.partial(backward_kernel, direct), "backward",
        [
            like((rows, DH), BF), like((rows, DH), BF), like((DH, DH), F32),
            like((2 * rows, DH), F32), like((span, DH), F32), like((span, DH), F32),
        ],
        weights + [ogs, u, total, mine, pair, gain, qs, ks, vs, probs, attn],
        scratch=[pltpu.VMEM((2 * rows, 2 * DH), F32), pltpu.VMEM((2 * rows, DH), F32)]
        + [pltpu.VMEM((2 * DH, model), BF)] * direct,
        flops=5 * wg_flops,
    )
    to_a, to_b, *to_c = call(
        functools.partial(halo_kernel, direct), "halo",
        [like((rows, wide), BF), like((rows, wide), BF)] + [like((DH, DH), BF)] * direct,
        [dk_soft, dv_soft] + ([dstate] + chunks if direct else []),
    )
    a, b = over_z(to_a, 0, True), over_z(to_b, 1, True)
    c = [over_z(value, 2) for value in to_c]
    if not direct:
        dstate = lax.psum(dstate, "z")
        groups = jnp.stack([keep_soft, keep_lin])
        slots = jnp.stack([jnp.where(core == head, groups, 0.0) for head in range(2)], axis=1)
        local = lax.psum_scatter(
            slots.reshape(HEADS * DH, model), axes, scatter_dimension=0, tiled=True
        )
        weight_grad = lax.psum(local, "dp") * scale
    own_out, to_pair = call(
        functools.partial(final_kernel, direct), "final",
        [like((rows, 6 * DH), BF), like((rows, 6 * DH), BF)],
        [dstate, mine, pair, dq_soft, dk_soft, dv_soft, dq_lin, dq_lin_pair, a, b] + c
        + ([both] if direct else []),
        scratch=[pltpu.VMEM((2 * rows, DH), F32)] * 2,
        flops=wg_flops // 4,
    )
    from_pair = over_core(to_pair)
    shape = like((1, rows, HEADS * DH), BF)
    dq, dk, dv = call(output_kernel, "outputs", [shape] * 3, [own_out, from_pair])
    return dq, dk, dv, weight_grad


def solution(mesh):
    n_dp, n_seq = mesh.shape["dp"], mesh.shape["seq"]
    blocks = Mesh(mesh.devices.reshape(n_dp, n_seq // 2, 2), ("dp", "z", "core"))
    tokens, heads = P("dp", ("z", "core"), None), P(("z", "core"), None)
    return jax.shard_map(
        functools.partial(body, n_dp, n_seq // 2),
        mesh=blocks,
        in_specs=(tokens, tokens, tokens, tokens, heads, P()),
        out_specs=(tokens, tokens, tokens, heads),
        check_vma=False,
    )
```

```python
import functools
import math

import jax
import jax.numpy as jnp
from jax import lax
from jax.experimental import pallas as pl
from jax.experimental.pallas import tpu as pltpu
from jax.sharding import Mesh
from jax.sharding import PartitionSpec as P

DH = 128
SOFT_HEADS = 2
LIN_HEADS = 2
HEADS = SOFT_HEADS + LIN_HEADS
WINDOW = 256
HALF = 128
norm_eps = 1e-06
FACTOR = DH ** (-0.5)
BF = jnp.bfloat16
F32 = jnp.float32
NN = (((1,), (0,)), ((), ()))
NT = (((1,), (1,)), ((), ()))
TN = (((0,), (0,)), ((), ()))


def unit_plus(values):
    return jnp.where(values > 0, values + 1.0, jnp.exp(jnp.minimum(values, 0.0)))


def unit_slope(values):
    return jnp.where(values > 0, 1.0, jnp.exp(jnp.minimum(values, 0.0)))


def mm(a, b, dims=NN):
    return lax.dot_general(a, b, dims, preferred_element_type=F32)


def halves(x):
    high = x.astype(BF)
    return high, (x - high.astype(F32)).astype(BF)


def mm3(a, b, dims=NN):
    a_high, a_low = halves(a)
    b_high, b_low = halves(b)
    return mm(a_high, b_high, dims) + (mm(a_high, b_low, dims) + mm(a_low, b_high, dims))


def mm2(a, b, dims=NN):
    a_high, a_low = halves(a)
    return mm(a_high, b, dims) + mm(a_low, b, dims)


def at(start, size=DH):
    return pl.ds(pl.multiple_of(start, size), size)


def places():
    return lax.axis_index("core"), lax.axis_index("z"), lax.axis_index("dp")


def call(kernel, name, outs, args, scratch=(), flops=0, spaces=None):
    vmem = pl.BlockSpec(memory_space=pltpu.VMEM)
    size = sum(math.prod(x.shape) * x.dtype.itemsize for x in list(args) + list(outs))
    return pl.pallas_call(
        kernel,
        name=name,
        out_shape=list(outs),
        in_specs=spaces or [vmem] * len(args),
        out_specs=[vmem] * len(outs),
        scratch_shapes=list(scratch),
        compiler_params=pltpu.CompilerParams(vmem_limit_bytes=24 * 2**20),
        cost_estimate=pl.CostEstimate(flops=flops, bytes_accessed=size, transcendentals=0),
    )(*args)


def like(shape, dtype):
    return jax.ShapeDtypeStruct(shape, dtype)


QS, KS, VS, QL, KL, VL = (slice(i * DH, (i + 1) * DH) for i in range(6))
SOFT = SOFT_HEADS * DH


def links(direct):
    core, z, dp = places()
    step = 1 + core
    turn = lax.rem(z + core, 2) if direct else 1
    return dict(
        first=1 + 2 * core, second=3 - 2 * core, step=step, other=3 - step,
        block_a=1 - turn, block_b=turn,
        halo_a=(1 - turn if direct else 1), halo_b=(turn if direct else 0),
    )


def pack_kernel(q, k, v, og, w, gain, mine_out, og_out, w_out, gain_out, sems):
    core, _, dp = places()
    mine = core * DH
    copies = []

    def fetch(source, target):
        copy = pltpu.make_async_copy(source, target, sems.at[len(copies)])
        copy.start()
        copies.append(copy)

    for index, array in enumerate((q, k, v)):
        for group in range(2):
            cols = slice((3 * group + index) * DH, (3 * group + index + 1) * DH)
            fetch(array.at[0, :, at(SOFT * group + mine)], mine_out.at[:, cols])
    width = w_out.shape[1]
    fetch(w.at[:, at(dp * width, width)], w_out)
    fetch(og.at[0], og_out)
    fetch(gain.at[at(mine)], gain_out.at[0])
    for copy in copies:
        copy.wait()


def state_kernel(direct, mine, q_pair, k_pair, v_pair, state, pair, to_a, to_b, *to_c):
    core, _, _ = places()
    own = core * DH
    for index, source in enumerate((q_pair, k_pair, v_pair)):
        for group in range(2):
            first = (3 * group + index) * DH
            pair[:, first : first + DH] = source[0, :, at(SOFT * group + own)]
    total = mm2(unit_plus(mine[:, KL].astype(F32)), mine[:, VL], TN) + mm2(
        unit_plus(pair[:, KL].astype(F32)), pair[:, VL], TN
    )
    state[...] = total
    way = links(direct)
    for out, block in ((to_a, way["block_a"]), (to_b, way["block_b"])):
        here = block == core
        out[:, :DH] = jnp.where(here, mine[:, KS], pair[:, KS])
        out[:, DH : 2 * DH] = jnp.where(here, mine[:, VS], pair[:, VS])
        if direct:
            out[:, 2 * DH :] = total.astype(BF)
    if direct:
        to_c[0][...] = total.astype(BF)


def relay_kernel(w, a, b, c, keep, send, heads):
    core, z, _ = places()
    way = links(True)
    heads[z] = w[...]
    for source, step in ((a, way["first"]), (b, way["second"]), (c, 2)):
        heads[z ^ step] = source[...]
    for group in range(2):
        keep[group] = heads[2 * group + core]
        send[group] = heads[2 * group + 1 - core]


def w_rows_kernel(keep, got, out):
    core, _, _ = places()
    half = keep.shape[1]
    for group in range(2):
        out[at(group * DH + core * half, half), :] = keep[group]
        out[at(group * DH + (1 - core) * half, half), :] = got[group]


def join_kernel(first, second, *refs):
    out = refs[-1]
    width = first.shape[1]
    out[:, :width] = first[...]
    out[:, width:] = second[...]


def weight_parts(direct, attn, ogs, send, keep):
    high, low = halves(attn)
    if not direct:
        keep[...] = mm(high, ogs[...], TN) + mm(low, ogs[...], TN)
        return
    _, _, dp = places()
    way = links(True)
    width = send.shape[1] // 2
    for index, step in enumerate((0, way["other"])):
        cols = slice(index * width, (index + 1) * width)
        near, far = at((dp ^ step) * width, width), at((dp ^ step ^ way["step"]) * width, width)
        keep[:, cols] = mm(high, ogs[:, near], TN) + mm(low, ogs[:, near], TN)
        send[:, cols] = (mm(high, ogs[:, far], TN) + mm(low, ogs[:, far], TN)).astype(BF)


def soft_forward_kernel(
    direct, mine, pair, og, og_recv, a, b, qs, ks, vs, ogs, probs, attn, keep, *send
):
    core, _, _ = places()
    way = links(direct)
    rows = og.shape[0]
    own_at, pair_at = core * rows, (1 - core) * rows
    for source, first in ((mine, own_at), (pair, pair_at)):
        qs[at(first, rows), :] = source[:, QS]
        ks[at(HALF + first, rows), :] = source[:, KS]
        vs[at(HALF + first, rows), :] = source[:, VS]
    for source, side in ((a, way["halo_a"]), (b, way["halo_b"])):
        first = side * (HALF + 2 * rows)
        ks[at(first), :] = source[:, :DH]
        vs[at(first), :] = source[:, DH : 2 * DH]
    ogs[at(own_at, rows), :] = og[...]
    ogs[at(pair_at, rows), :] = og_recv[...]
    span = rows + 2 * HALF
    row_pos = lax.broadcasted_iota(jnp.int32, (rows, span), 0)
    col_pos = lax.broadcasted_iota(jnp.int32, (rows, span), 1)
    inside = (col_pos >= row_pos) & (col_pos < row_pos + WINDOW)
    for block in range(2):
        here, window = slice(block * rows, (block + 1) * rows), slice(block * rows, block * rows + span)
        scores = mm(qs[here, :], ks[window, :], NT) * FACTOR
        scores = jnp.where(inside, scores, -1e30)
        peak = jnp.max(scores, axis=1, keepdims=True)
        terms = jnp.where(inside, jnp.exp(scores - peak), 0.0)
        share = terms / jnp.sum(terms, axis=1, keepdims=True)
        probs[block] = share
        attn[here, :] = mm(share.astype(BF), vs[window, :])
    weight_parts(direct, attn[...], ogs, send[0] if send else None, keep)


def lin_forward_kernel(direct, state, mine, pair, ogs, gain, *refs):
    core, _, _ = places()
    rows = mine.shape[0]
    total = state[...]
    if direct:
        a, b, c, soft_send, _, u_out, total_out, keep, out = refs
        total = total + a[:, 2 * DH :].astype(F32) + b[:, 2 * DH :].astype(F32) + c[...].astype(F32)
    else:
        u_out, total_out, keep = refs
    total_out[...] = total
    u_out[at(core * rows, rows), :] = mm3(unit_plus(mine[:, QL].astype(F32)), total)
    u_out[at((1 - core) * rows, rows), :] = mm3(unit_plus(pair[:, QL].astype(F32)), total)
    u = u_out[...]
    r = lax.rsqrt(jnp.mean(u * u, axis=1, keepdims=True) + norm_eps)
    attn = gain[...] * u * r
    weight_parts(direct, attn, ogs, out.at[DH:, :] if direct else None, keep)
    if direct:
        out[:DH, :] = soft_send[...]


def fold_kernel(keep_soft, keep_lin, got, keep, send):
    width = keep.shape[1]
    for rows, source in ((slice(0, DH), keep_soft), (slice(DH, 2 * DH), keep_lin)):
        keep[rows, :] = source[:, :width] + got[rows, :width].astype(F32)
        send[rows, :] = (source[:, width:] + got[rows, width:].astype(F32)).astype(BF)


def rows_kernel(keep, got, own, send, total):
    core, _, _ = places()
    half = DH // 2
    total[...] = keep[...] + got[...].astype(F32)
    for group in range(2):
        out = slice(group * half, (group + 1) * half)
        own[out, :] = total[at(group * DH + core * half, half), :]
        send[out, :] = total[at(group * DH + (1 - core) * half, half), :]


def lin_backward(u, total, dattn, mine, pair, gain, dq_own, dq_pair, dstate, grads):
    core, _, _ = places()
    rows = mine.shape[0]
    u_all = u[...]
    r = lax.rsqrt(jnp.mean(u_all * u_all, axis=1, keepdims=True) + norm_eps)
    lin_grad = gain[...] * dattn[:, DH:]
    grads[...] = r * lin_grad - u_all * (r * r * r) * jnp.mean(lin_grad * u_all, axis=1, keepdims=True)
    total_state = total[...]
    result = jnp.zeros(dstate.shape, F32)
    for first, source, out in ((core * rows, mine, dq_own), ((1 - core) * rows, pair, dq_pair)):
        wide = source[:, QL].astype(F32)
        part = grads[at(first, rows), :]
        result = result + mm3(unit_plus(wide), part, TN)
        out[...] = (mm3(part, total_state, NT) * unit_slope(wide)).astype(BF)
    dstate[...] = result


def soft_backward(qs, ks, vs, probs, attn, dattn, dq_all, dk_all, dv_all):
    rows = qs.shape[0] // 2
    span = rows + 2 * HALF
    dk_all[...] = jnp.zeros_like(dk_all)
    dv_all[...] = jnp.zeros_like(dv_all)
    for block in range(2):
        here, window = slice(block * rows, (block + 1) * rows), slice(block * rows, block * rows + span)
        grad = dattn[here, :DH].astype(BF)
        share = probs[block]
        delta = jnp.sum(grad.astype(F32) * attn[here, :], axis=1, keepdims=True)
        dscore = (share * (mm(grad, vs[window, :], NT) - delta)).astype(BF)
        dq_all[here, :] = mm(dscore, ks[window, :]) * FACTOR
        dk_all[window, :] += mm(dscore, qs[here, :], TN) * FACTOR
        dv_all[window, :] += mm(share.astype(BF), grad, TN)


def backward_kernel(direct, *refs):
    if direct:
        sent, got = refs[:2]
        refs = refs[2:]
    else:
        weights = refs[0]
        refs = refs[1:]
    (ogs, u, total, mine, pair, gain, qs, ks, vs, probs, attn,
     dq_lin, dq_lin_pair, dstate, dq_soft, dk_soft, dv_soft, dattn, grads, *scratch) = refs
    if direct:
        _, _, dp = places()
        way = links(True)
        weights = scratch[0]
        width = weights.shape[1] // 4
        for source, index, step in (
            (sent, 0, 0), (sent, 1, way["step"]), (got, 0, way["other"]), (got, 1, 3),
        ):
            weights[:, at((dp ^ step) * width, width)] = source[:, index * width : (index + 1) * width]
    dattn[...] = mm(ogs[...], weights[...], NT)
    lin_backward(u, total, dattn, mine, pair, gain, dq_lin, dq_lin_pair, dstate, grads)
    soft_backward(qs, ks, vs, probs, attn, dattn, dq_soft, dk_soft, dv_soft)


def halo_kernel(direct, dk_soft, dv_soft, *refs):
    way = links(direct)
    span = dk_soft.shape[0]
    if direct:
        dstate, _, _, _, to_a, to_b, to_c = refs
        to_c[...] = dstate[...].astype(BF)
    else:
        to_a, to_b = refs
    for out, side in ((to_a, way["halo_a"]), (to_b, way["halo_b"])):
        first = side * (span - HALF)
        out[:, :DH] = dk_soft[at(first), :].astype(BF)
        out[:, DH : 2 * DH] = dv_soft[at(first), :].astype(BF)
        if direct:
            out[:, 2 * DH :] = dstate[...].astype(BF)


def chunk_kernel(own, got, to_a, to_b, to_c, chunk, heads):
    core, z, _ = places()
    way = links(True)
    half = chunk.shape[0]
    for group in range(2):
        rows = slice(group * half, (group + 1) * half)
        heads[2 * group + core] = own[rows, :]
        heads[2 * group + 1 - core] = got[rows, :]
    chunk[...] = heads[z]
    for out, step in ((to_a, way["first"]), (to_b, way["second"]), (to_c, 2)):
        out[...] = heads[z ^ step].astype(BF)


def weight_sum_kernel(scale, chunk, a, b, c, out):
    total = chunk[...] + a[...].astype(F32) + b[...].astype(F32) + c[...].astype(F32)
    out[...] = (scale * total).astype(out.dtype)


def final_kernel(
    direct, dstate, mine, pair, dq_soft, dk_soft, dv_soft, dq_lin, dq_lin_pair, a, b, *refs
):
    core, _, _ = places()
    way = links(direct)
    rows = mine.shape[0]
    total = dstate[...]
    own_out, pair_out, dk_all, dv_all = refs[-4:]
    if direct:
        total = total + a[:, 2 * DH :].astype(F32) + b[:, 2 * DH :].astype(F32)
        total = total + refs[0][...].astype(F32)
    for source, out, cols in ((dk_soft, dk_all, slice(0, DH)), (dv_soft, dv_all, slice(DH, 2 * DH))):
        out[...] = source[HALF : HALF + 2 * rows, :]
        out[at(way["block_a"] * rows, rows), :] += a[:, cols].astype(F32)
        out[at(way["block_b"] * rows, rows), :] += b[:, cols].astype(F32)
    high, low = halves(total)
    for source, dq, out, place in ((mine, dq_lin, own_out, core), (pair, dq_lin_pair, pair_out, 1 - core)):
        here = at(place * rows, rows)
        out[:, QS] = dq_soft[here, :].astype(BF)
        out[:, KS] = dk_all[here, :].astype(BF)
        out[:, VS] = dv_all[here, :].astype(BF)
        wide, values = source[:, KL].astype(F32), source[:, VL]
        out[:, QL] = dq[...]
        out[:, KL] = ((mm(values, high, NT) + mm(values, low, NT)) * unit_slope(wide)).astype(BF)
        out[:, VL] = mm3(unit_plus(wide), total).astype(BF)


def output_kernel(own, pair, dq, dk, dv):
    core, _, _ = places()
    for source, first in ((own, core * DH), (pair, (1 - core) * DH)):
        for index, out in enumerate((dq, dk, dv)):
            out[0, :, at(first)] = source[:, index * DH : (index + 1) * DH]
            out[0, :, at(SOFT + first)] = source[:, (3 + index) * DH : (4 + index) * DH]


def weight_join_kernel(both, got, out):
    _, _, dp = places()
    way = links(True)
    width = both.shape[1] // 2
    for source, index, step in ((both, 0, 0), (both, 1, way["step"]), (got, 0, way["other"]), (got, 1, 3)):
        out[:, at((dp ^ step) * width, width)] = source[:, index * width : (index + 1) * width].astype(F32)


def body(n_dp, n_z, queries, key_rows, value_rows, out_grad, out_weight, norm_gain):
    rows, model = out_grad.shape[1:]
    axes = ("z", "core")
    pair_perm = [(0, 1), (1, 0)]
    core = lax.axis_index("core")
    direct = n_z == HEADS and n_dp == 4
    width = model // n_dp
    half = DH // 2

    scale = 1.0 / math.sqrt(n_dp * n_z * 2 * rows)

    def over_core(value):
        return lax.ppermute(value, "core", pair_perm)

    def over_z(value, which, back=False):
        pairs = []
        for z in range(n_z):
            for c in range(2):
                if direct:
                    there = z ^ (1 + 2 * c, 3 - 2 * c, 2)[which]
                else:
                    there = (z + (1 if (which == 1) != back else -1)) % n_z
                pairs.append((2 * z + c, 2 * there + c))
        return lax.ppermute(value, axes, pairs)

    def over_dp(value, which):
        pairs = [
            (2 * d + c, 2 * (d ^ (1 + c, 2 - c)[which]) + c) for d in range(n_dp) for c in range(2)
        ]
        return lax.ppermute(value, ("dp", "core"), pairs)

    vmem = pl.BlockSpec(memory_space=pltpu.VMEM)

    def hbm(value):
        return pltpu.with_memory_space_constraint(value, pltpu.HBM)

    q_pair, k_pair, v_pair = over_core(queries), over_core(key_rows), over_core(value_rows)
    og_recv = over_core(out_grad[0])
    mine, og, w_part, gain = call(
        pack_kernel, "pack",
        [
            like((rows, 6 * DH), BF), like((rows, model), BF),
            like((out_weight.shape[0], width), BF), like((1, DH), F32),
        ],
        [hbm(x) for x in (queries, key_rows, value_rows, out_grad, out_weight, norm_gain)],
        scratch=[pltpu.SemaphoreType.DMA((9,))],
        spaces=[pl.BlockSpec(memory_space=pltpu.HBM)] * 6,
    )
    wide = 3 * DH if direct else 2 * DH
    state, pair, to_a, to_b, *rest = call(
        functools.partial(state_kernel, direct), "state",
        [like((DH, DH), F32), like((rows, 6 * DH), BF), like((rows, wide), BF), like((rows, wide), BF)]
        + [like((DH, DH), BF)] * direct,
        [mine, q_pair, k_pair, v_pair],
        flops=4 * 2 * rows * DH * DH,
    )
    if direct:
        a, b, c = over_z(to_a, 0), over_z(to_b, 1), [over_z(rest[0], 2)]
        w_keep, w_send = call(
            relay_kernel, "relay", [like((2, half, width), BF)] * 2,
            [w_part] + [over_z(w_part, which) for which in range(3)],
            scratch=[pltpu.VMEM((HEADS, half, width), BF)],
        )
        w_own = call(
            w_rows_kernel, "w_rows", [like((2 * DH, width), BF)], [w_keep, over_core(w_send)]
        )[0]
        w_got = over_dp(w_own, 0)
        w_half = call(
            join_kernel, "w_half", [like((2 * DH, 2 * width), BF)], [w_own, w_got]
        )[0]
        weights = [w_half, over_dp(w_half, 1)]
    else:
        a, b, c = over_z(to_a, 0), over_z(to_b, 1), []
        state = lax.psum(state, "z")
        weights = lax.all_gather(out_weight, axes, axis=0, tiled=True).reshape(2, 2, DH, model)
        weights = [jnp.where(core == 0, weights[:, 0], weights[:, 1]).reshape(2 * DH, model)]

    span = 2 * rows + 2 * HALF
    keep_width = 2 * width if direct else model
    wg_flops = 2 * 2 * rows * DH * model
    qs, ks, vs, ogs, probs, attn, keep_soft, *soft_send = call(
        functools.partial(soft_forward_kernel, direct), "soft_forward",
        [
            like((2 * rows, DH), BF), like((span, DH), BF), like((span, DH), BF),
            like((2 * rows, model), BF), like((2, rows, rows + 2 * HALF), F32), like((2 * rows, DH), F32),
            like((DH, keep_width), F32),
        ] + [like((DH, 2 * width), BF)] * direct,
        [mine, pair, og, og_recv, a, b],
        flops=wg_flops,
    )
    u, total, keep_lin, *sent = call(
        functools.partial(lin_forward_kernel, direct), "lin_forward",
        [like((2 * rows, DH), F32), like((DH, DH), F32), like((DH, keep_width), F32)]
        + [like((2 * DH, 2 * width), BF)] * direct,
        [state, mine, pair, ogs, gain] + ([a, b] + c + soft_send + [w_own] if direct else []),
        flops=wg_flops,
    )
    if direct:
        got = over_dp(sent[0], 0)
        keep, sent = call(
            fold_kernel, "fold", [like((2 * DH, width), F32), like((2 * DH, width), BF)],
            [keep_soft, keep_lin, got],
        )
        got = over_dp(sent, 1)
        row_own, row_send = call(
            rows_kernel, "rows", [like((2 * half, width), F32)] * 2, [keep, got],
            scratch=[pltpu.VMEM((2 * DH, width), F32)],
        )
        row_recv = over_core(row_send)
        *to_chips, chunk = call(
            chunk_kernel, "chunk", [like((half, width), BF)] * 3 + [like((half, width), F32)],
            [row_own, row_recv], scratch=[pltpu.VMEM((HEADS, half, width), F32)],
        )
        chunks = [over_z(value, which) for which, value in enumerate(to_chips)]
        summed = call(
            functools.partial(weight_sum_kernel, scale), "weight_sum", [like((half, width), BF)],
            [chunk] + chunks,
        )[0]
        got = over_dp(summed, 0)
        both = call(join_kernel, "both", [like((half, 2 * width), BF)], [summed, got])[0]
        got = over_dp(both, 1)
        weight_grad = call(
            weight_join_kernel, "weight_join", [like((half, model), F32)], [both, got]
        )[0]
    dq_lin, dq_lin_pair, dstate, dq_soft, dk_soft, dv_soft = call(
        functools.partial(backward_kernel, direct), "backward",
        [
            like((rows, DH), BF), like((rows, DH), BF), like((DH, DH), F32),
            like((2 * rows, DH), F32), like((span, DH), F32), like((span, DH), F32),
        ],
        weights + [ogs, u, total, mine, pair, gain, qs, ks, vs, probs, attn],
        scratch=[pltpu.VMEM((2 * rows, 2 * DH), F32), pltpu.VMEM((2 * rows, DH), F32)]
        + [pltpu.VMEM((2 * DH, model), BF)] * direct,
        flops=5 * wg_flops,
    )
    to_a, to_b, *to_c = call(
        functools.partial(halo_kernel, direct), "halo",
        [like((rows, wide), BF), like((rows, wide), BF)] + [like((DH, DH), BF)] * direct,
        [dk_soft, dv_soft] + ([dstate] + chunks if direct else []),
    )
    a, b = over_z(to_a, 0, True), over_z(to_b, 1, True)
    c = [over_z(value, 2) for value in to_c]
    if not direct:
        dstate = lax.psum(dstate, "z")
        groups = jnp.stack([keep_soft, keep_lin])
        slots = jnp.stack([jnp.where(core == head, groups, 0.0) for head in range(2)], axis=1)
        local = lax.psum_scatter(
            slots.reshape(HEADS * DH, model), axes, scatter_dimension=0, tiled=True
        )
        weight_grad = lax.psum(local, "dp") * scale
    own_out, to_pair = call(
        functools.partial(final_kernel, direct), "final",
        [like((rows, 6 * DH), BF), like((rows, 6 * DH), BF)],
        [dstate, mine, pair, dq_soft, dk_soft, dv_soft, dq_lin, dq_lin_pair, a, b] + c
        + ([both] if direct else []),
        scratch=[pltpu.VMEM((2 * rows, DH), F32)] * 2,
        flops=wg_flops // 4,
    )
    from_pair = over_core(to_pair)
    shape = like((1, rows, HEADS * DH), BF)
    dq, dk, dv = call(output_kernel, "outputs", [shape] * 3, [own_out, from_pair])
    return dq, dk, dv, weight_grad


def solution(mesh):
    n_dp, n_seq = mesh.shape["dp"], mesh.shape["seq"]
    blocks = Mesh(mesh.devices.reshape(n_dp, n_seq // 2, 2), ("dp", "z", "core"))
    tokens, heads = P("dp", ("z", "core"), None), P(("z", "core"), None)
    return jax.shard_map(
        functools.partial(body, n_dp, n_seq // 2),
        mesh=blocks,
        in_specs=(tokens, tokens, tokens, tokens, heads, P()),
        out_specs=(tokens, tokens, tokens, heads),
        check_vma=False,
    )
```

```python
import functools
import math

import jax
import jax.numpy as jnp
from jax import lax
from jax.experimental import pallas as pl
from jax.experimental.pallas import tpu as pltpu
from jax.sharding import Mesh
from jax.sharding import PartitionSpec as P

DH = 128
SOFT_HEADS = 2
LIN_HEADS = 2
HEADS = SOFT_HEADS + LIN_HEADS
WINDOW = 256
HALF = 128
norm_eps = 1e-06
FACTOR = DH ** (-0.5)
BF = jnp.bfloat16
F32 = jnp.float32
NN = (((1,), (0,)), ((), ()))
NT = (((1,), (1,)), ((), ()))
TN = (((0,), (0,)), ((), ()))


def unit_plus(values):
    return jnp.where(values > 0, values + 1.0, jnp.exp(jnp.minimum(values, 0.0)))


def unit_slope(values):
    return jnp.where(values > 0, 1.0, jnp.exp(jnp.minimum(values, 0.0)))


def mm(a, b, dims=NN):
    return lax.dot_general(a, b, dims, preferred_element_type=F32)


def halves(x):
    high = x.astype(BF)
    return high, (x - high.astype(F32)).astype(BF)


def mm3(a, b, dims=NN):
    a_high, a_low = halves(a)
    b_high, b_low = halves(b)
    return mm(a_high, b_high, dims) + (mm(a_high, b_low, dims) + mm(a_low, b_high, dims))


def mm2(a, b, dims=NN):
    a_high, a_low = halves(a)
    return mm(a_high, b, dims) + mm(a_low, b, dims)


def at(start, size=DH):
    return pl.ds(pl.multiple_of(start, size), size)


def places():
    return lax.axis_index("core"), lax.axis_index("z"), lax.axis_index("dp")


def call(kernel, name, outs, args, scratch=(), flops=0, spaces=None):
    vmem = pl.BlockSpec(memory_space=pltpu.VMEM)
    size = sum(math.prod(x.shape) * x.dtype.itemsize for x in list(args) + list(outs))
    return pl.pallas_call(
        kernel,
        name=name,
        out_shape=list(outs),
        in_specs=spaces or [vmem] * len(args),
        out_specs=[vmem] * len(outs),
        scratch_shapes=list(scratch),
        compiler_params=pltpu.CompilerParams(vmem_limit_bytes=24 * 2**20),
        cost_estimate=pl.CostEstimate(flops=flops, bytes_accessed=size, transcendentals=0),
    )(*args)


def like(shape, dtype):
    return jax.ShapeDtypeStruct(shape, dtype)


QS, KS, VS, QL, KL, VL = (slice(i * DH, (i + 1) * DH) for i in range(6))
SOFT = SOFT_HEADS * DH


def links(direct):
    core, z, dp = places()
    step = 1 + core
    turn = lax.rem(z + core, 2) if direct else 1
    return dict(
        first=1 + 2 * core, second=3 - 2 * core, step=step, other=3 - step,
        block_a=1 - turn, block_b=turn,
        halo_a=(1 - turn if direct else 1), halo_b=(turn if direct else 0),
    )


def pack_kernel(q, k, v, og, w, gain, mine_out, og_out, w_out, gain_out, sems):
    core, _, dp = places()
    mine = core * DH
    copies = []

    def fetch(source, target):
        copy = pltpu.make_async_copy(source, target, sems.at[len(copies)])
        copy.start()
        copies.append(copy)

    for index, array in enumerate((q, k, v)):
        for group in range(2):
            cols = slice((3 * group + index) * DH, (3 * group + index + 1) * DH)
            fetch(array.at[0, :, at(SOFT * group + mine)], mine_out.at[:, cols])
    width = w_out.shape[1]
    fetch(w.at[:, at(dp * width, width)], w_out)
    fetch(og.at[0], og_out)
    fetch(gain.at[at(mine)], gain_out.at[0])
    for copy in copies:
        copy.wait()


def state_kernel(direct, mine, q_pair, k_pair, v_pair, *refs):
    if direct:
        w, state, pair, to_a, to_b, to_c = refs
    else:
        state, pair, to_a, to_b = refs
    core, _, _ = places()
    own = core * DH
    for index, source in enumerate((q_pair, k_pair, v_pair)):
        for group in range(2):
            first = (3 * group + index) * DH
            pair[:, first : first + DH] = source[0, :, at(SOFT * group + own)]
    total = mm2(unit_plus(mine[:, KL].astype(F32)), mine[:, VL], TN) + mm2(
        unit_plus(pair[:, KL].astype(F32)), pair[:, VL], TN
    )
    state[...] = total
    way = links(direct)
    for out, block in ((to_a, way["block_a"]), (to_b, way["block_b"])):
        here = block == core
        out[:, :DH] = jnp.where(here, mine[:, KS], pair[:, KS])
        out[:, DH : 2 * DH] = jnp.where(here, mine[:, VS], pair[:, VS])
    if direct:
        rows = w.shape[0]
        for out, first in ((to_a, 2 * DH), (to_b, 2 * DH), (to_c, 0)):
            out[:, first : first + DH] = total.astype(BF)
            out[:rows, first + DH :] = w[:, :DH]
            out[rows:, first + DH :] = w[:, DH:]


def relay_kernel(w, a, b, c, keep, send, heads):
    core, z, _ = places()
    way = links(True)
    rows = w.shape[0]
    heads[z] = w[...]
    for source, first, step in ((a, 3 * DH, way["first"]), (b, 3 * DH, way["second"]), (c, DH, 2)):
        heads[z ^ step, :, :DH] = source[:rows, first:]
        heads[z ^ step, :, DH:] = source[rows:, first:]
    for group in range(2):
        keep[group] = heads[2 * group + core]
        send[group] = heads[2 * group + 1 - core]


def w_rows_kernel(keep, got, out):
    core, _, _ = places()
    half = keep.shape[1]
    for group in range(2):
        out[at(group * DH + core * half, half), :] = keep[group]
        out[at(group * DH + (1 - core) * half, half), :] = got[group]


def join_kernel(first, second, *refs):
    out = refs[-1]
    width = first.shape[1]
    out[:, :width] = first[...]
    out[:, width:] = second[...]


def weight_parts(direct, attn, ogs, send, keep):
    high, low = halves(attn)
    if not direct:
        keep[...] = mm(high, ogs[...], TN) + mm(low, ogs[...], TN)
        return
    _, _, dp = places()
    way = links(True)
    width = send.shape[1] // 2
    for index, step in enumerate((0, way["other"])):
        cols = slice(index * width, (index + 1) * width)
        near, far = at((dp ^ step) * width, width), at((dp ^ step ^ way["step"]) * width, width)
        keep[:, cols] = mm(high, ogs[:, near], TN) + mm(low, ogs[:, near], TN)
        send[:, cols] = (mm(high, ogs[:, far], TN) + mm(low, ogs[:, far], TN)).astype(BF)


def soft_forward_kernel(
    direct, mine, pair, og, og_recv, a, b, qs, ks, vs, ogs, probs, attn, keep, *send
):
    core, _, _ = places()
    way = links(direct)
    rows = og.shape[0]
    own_at, pair_at = core * rows, (1 - core) * rows
    for source, first in ((mine, own_at), (pair, pair_at)):
        qs[at(first, rows), :] = source[:, QS]
        ks[at(HALF + first, rows), :] = source[:, KS]
        vs[at(HALF + first, rows), :] = source[:, VS]
    for source, side in ((a, way["halo_a"]), (b, way["halo_b"])):
        first = side * (HALF + 2 * rows)
        ks[at(first), :] = source[:, :DH]
        vs[at(first), :] = source[:, DH : 2 * DH]
    ogs[at(own_at, rows), :] = og[...]
    ogs[at(pair_at, rows), :] = og_recv[...]
    span = rows + 2 * HALF
    row_pos = lax.broadcasted_iota(jnp.int32, (rows, span), 0)
    col_pos = lax.broadcasted_iota(jnp.int32, (rows, span), 1)
    inside = (col_pos >= row_pos) & (col_pos < row_pos + WINDOW)
    for block in range(2):
        here, window = slice(block * rows, (block + 1) * rows), slice(block * rows, block * rows + span)
        scores = mm(qs[here, :], ks[window, :], NT) * FACTOR
        scores = jnp.where(inside, scores, -1e30)
        peak = jnp.max(scores, axis=1, keepdims=True)
        terms = jnp.where(inside, jnp.exp(scores - peak), 0.0)
        share = terms / jnp.sum(terms, axis=1, keepdims=True)
        probs[block] = share
        attn[here, :] = mm(share.astype(BF), vs[window, :])
    weight_parts(direct, attn[...], ogs, send[0] if send else None, keep)


def lin_forward_kernel(direct, state, mine, pair, ogs, gain, *refs):
    core, _, _ = places()
    rows = mine.shape[0]
    total = state[...]
    if direct:
        a, b, c, soft_send, u_out, total_out, keep, out = refs
        total = total + a[:, 2 * DH : 3 * DH].astype(F32) + b[:, 2 * DH : 3 * DH].astype(F32)
        total = total + c[:, :DH].astype(F32)
    else:
        u_out, total_out, keep = refs
    total_out[...] = total
    u_out[at(core * rows, rows), :] = mm3(unit_plus(mine[:, QL].astype(F32)), total)
    u_out[at((1 - core) * rows, rows), :] = mm3(unit_plus(pair[:, QL].astype(F32)), total)
    u = u_out[...]
    r = lax.rsqrt(jnp.mean(u * u, axis=1, keepdims=True) + norm_eps)
    attn = gain[...] * u * r
    weight_parts(direct, attn, ogs, out.at[DH:, :] if direct else None, keep)
    if direct:
        out[:DH, :] = soft_send[...]


def fold_kernel(keep_soft, keep_lin, got, keep, send):
    width = keep.shape[1]
    for rows, source in ((slice(0, DH), keep_soft), (slice(DH, 2 * DH), keep_lin)):
        keep[rows, :] = source[:, :width] + got[rows, :width].astype(F32)
        send[rows, :] = (source[:, width:] + got[rows, width:].astype(F32)).astype(BF)


def piece_kernel(keep, got, *refs):
    _, z, _ = places()
    *outs, pieces = refs
    half = DH // 2
    total = keep[...] + got[...].astype(F32)
    for index in range(len(outs)):
        pieces[index] = total[index * half : (index + 1) * half, :]
    for step, out in enumerate(outs):
        out[...] = pieces[z ^ step].astype(BF)


def lin_backward(u, total, dattn, mine, pair, gain, dq_own, dq_pair, dstate, grads):
    core, _, _ = places()
    rows = mine.shape[0]
    u_all = u[...]
    r = lax.rsqrt(jnp.mean(u_all * u_all, axis=1, keepdims=True) + norm_eps)
    lin_grad = gain[...] * dattn[:, DH:]
    grads[...] = r * lin_grad - u_all * (r * r * r) * jnp.mean(lin_grad * u_all, axis=1, keepdims=True)
    total_state = total[...]
    result = jnp.zeros(dstate.shape, F32)
    for first, source, out in ((core * rows, mine, dq_own), ((1 - core) * rows, pair, dq_pair)):
        wide = source[:, QL].astype(F32)
        part = grads[at(first, rows), :]
        result = result + mm3(unit_plus(wide), part, TN)
        out[...] = (mm3(part, total_state, NT) * unit_slope(wide)).astype(BF)
    dstate[...] = result


def soft_backward(qs, ks, vs, probs, attn, dattn, dq_all, dk_all, dv_all):
    rows = qs.shape[0] // 2
    span = rows + 2 * HALF
    dk_all[...] = jnp.zeros_like(dk_all)
    dv_all[...] = jnp.zeros_like(dv_all)
    for block in range(2):
        here, window = slice(block * rows, (block + 1) * rows), slice(block * rows, block * rows + span)
        grad = dattn[here, :DH].astype(BF)
        share = probs[block]
        delta = jnp.sum(grad.astype(F32) * attn[here, :], axis=1, keepdims=True)
        dscore = (share * (mm(grad, vs[window, :], NT) - delta)).astype(BF)
        dq_all[here, :] = mm(dscore, ks[window, :]) * FACTOR
        dk_all[window, :] += mm(dscore, qs[here, :], TN) * FACTOR
        dv_all[window, :] += mm(share.astype(BF), grad, TN)


def backward_kernel(direct, *refs):
    if direct:
        sent, got = refs[:2]
        refs = refs[2:]
    else:
        weights = refs[0]
        refs = refs[1:]
    (ogs, u, total, mine, pair, gain, qs, ks, vs, probs, attn,
     dq_lin, dq_lin_pair, dstate, dq_soft, dk_soft, dv_soft, dattn, grads, *scratch) = refs
    if direct:
        _, _, dp = places()
        way = links(True)
        weights = scratch[0]
        width = weights.shape[1] // 4
        for source, index, step in (
            (sent, 0, 0), (sent, 1, way["step"]), (got, 0, way["other"]), (got, 1, 3),
        ):
            weights[:, at((dp ^ step) * width, width)] = source[:, index * width : (index + 1) * width]
    dattn[...] = mm(ogs[...], weights[...], NT)
    lin_backward(u, total, dattn, mine, pair, gain, dq_lin, dq_lin_pair, dstate, grads)
    soft_backward(qs, ks, vs, probs, attn, dattn, dq_soft, dk_soft, dv_soft)


def halo_kernel(direct, dk_soft, dv_soft, *refs):
    way = links(direct)
    span = dk_soft.shape[0]
    if direct:
        dstate, *_, to_a, to_b, to_c = refs
        to_c[...] = dstate[...].astype(BF)
    else:
        to_a, to_b = refs
    for out, side in ((to_a, way["halo_a"]), (to_b, way["halo_b"])):
        first = side * (span - HALF)
        out[:, :DH] = dk_soft[at(first), :].astype(BF)
        out[:, DH : 2 * DH] = dv_soft[at(first), :].astype(BF)
        if direct:
            out[:, 2 * DH :] = dstate[...].astype(BF)


def weight_sum_kernel(scale, a, b, c, d, out):
    total = (a[...].astype(F32) + b[...].astype(F32)) + (c[...].astype(F32) + d[...].astype(F32))
    out[...] = (scale * total).astype(out.dtype)


def final_kernel(
    direct, dstate, mine, pair, dq_soft, dk_soft, dv_soft, dq_lin, dq_lin_pair, a, b, *refs
):
    core, _, _ = places()
    way = links(direct)
    rows = mine.shape[0]
    total = dstate[...]
    own_out, pair_out, dk_all, dv_all = refs[-4:]
    if direct:
        total = total + a[:, 2 * DH :].astype(F32) + b[:, 2 * DH :].astype(F32)
        total = total + refs[0][...].astype(F32)
    for source, out, cols in ((dk_soft, dk_all, slice(0, DH)), (dv_soft, dv_all, slice(DH, 2 * DH))):
        out[...] = source[HALF : HALF + 2 * rows, :]
        out[at(way["block_a"] * rows, rows), :] += a[:, cols].astype(F32)
        out[at(way["block_b"] * rows, rows), :] += b[:, cols].astype(F32)
    high, low = halves(total)
    for source, dq, out, place in ((mine, dq_lin, own_out, core), (pair, dq_lin_pair, pair_out, 1 - core)):
        here = at(place * rows, rows)
        out[:, QS] = dq_soft[here, :].astype(BF)
        out[:, KS] = dk_all[here, :].astype(BF)
        out[:, VS] = dv_all[here, :].astype(BF)
        wide, values = source[:, KL].astype(F32), source[:, VL]
        out[:, QL] = dq[...]
        out[:, KL] = ((mm(values, high, NT) + mm(values, low, NT)) * unit_slope(wide)).astype(BF)
        out[:, VL] = mm3(unit_plus(wide), total).astype(BF)


def output_kernel(own, pair, dq, dk, dv):
    core, _, _ = places()
    for source, first in ((own, core * DH), (pair, (1 - core) * DH)):
        for index, out in enumerate((dq, dk, dv)):
            out[0, :, at(first)] = source[:, index * DH : (index + 1) * DH]
            out[0, :, at(SOFT + first)] = source[:, (3 + index) * DH : (4 + index) * DH]


def weight_join_kernel(both, got, out):
    _, _, dp = places()
    way = links(True)
    width = both.shape[1] // 2
    for source, index, step in ((both, 0, 0), (both, 1, way["step"]), (got, 0, way["other"]), (got, 1, 3)):
        out[:, at((dp ^ step) * width, width)] = source[:, index * width : (index + 1) * width].astype(F32)


def body(n_dp, n_z, queries, key_rows, value_rows, out_grad, out_weight, norm_gain):
    rows, model = out_grad.shape[1:]
    axes = ("z", "core")
    pair_perm = [(0, 1), (1, 0)]
    core = lax.axis_index("core")
    direct = n_z == HEADS and n_dp == 4
    width = model // n_dp
    half = DH // 2

    scale = 1.0 / math.sqrt(n_dp * n_z * 2 * rows)

    def over_core(value):
        return lax.ppermute(value, "core", pair_perm)

    def over_z(value, which, back=False):
        pairs = []
        for z in range(n_z):
            for c in range(2):
                if direct:
                    there = z ^ (1 + 2 * c, 3 - 2 * c, 2)[which]
                else:
                    there = (z + (1 if (which == 1) != back else -1)) % n_z
                pairs.append((2 * z + c, 2 * there + c))
        return lax.ppermute(value, axes, pairs)

    def to_owner(value, step):
        pairs = []
        for z in range(n_z):
            for c in range(2):
                piece = z ^ step
                pairs.append((2 * z + c, 2 * (2 * (piece // 2) + c) + piece % 2))
        return lax.ppermute(value, axes, pairs)

    def over_dp(value, which):
        pairs = [
            (2 * d + c, 2 * (d ^ (1 + c, 2 - c)[which]) + c) for d in range(n_dp) for c in range(2)
        ]
        return lax.ppermute(value, ("dp", "core"), pairs)

    vmem = pl.BlockSpec(memory_space=pltpu.VMEM)

    def hbm(value):
        return pltpu.with_memory_space_constraint(value, pltpu.HBM)

    q_pair, k_pair, v_pair = over_core(queries), over_core(key_rows), over_core(value_rows)
    og_recv = over_core(out_grad[0])
    mine, og, w_part, gain = call(
        pack_kernel, "pack",
        [
            like((rows, 6 * DH), BF), like((rows, model), BF),
            like((out_weight.shape[0], width), BF), like((1, DH), F32),
        ],
        [hbm(x) for x in (queries, key_rows, value_rows, out_grad, out_weight, norm_gain)],
        scratch=[pltpu.SemaphoreType.DMA((9,))],
        spaces=[pl.BlockSpec(memory_space=pltpu.HBM)] * 6,
    )
    wide = 4 * DH if direct else 2 * DH
    state, pair, to_a, to_b, *rest = call(
        functools.partial(state_kernel, direct), "state",
        [like((DH, DH), F32), like((rows, 6 * DH), BF), like((rows, wide), BF), like((rows, wide), BF)]
        + [like((rows, 2 * DH), BF)] * direct,
        [mine, q_pair, k_pair, v_pair] + [w_part] * direct,
        flops=4 * 2 * rows * DH * DH,
    )
    if direct:
        a, b, c = over_z(to_a, 0), over_z(to_b, 1), [over_z(rest[0], 2)]
        w_keep, w_send = call(
            relay_kernel, "relay", [like((2, half, width), BF)] * 2, [w_part, a, b] + c,
            scratch=[pltpu.VMEM((HEADS, half, width), BF)],
        )
        w_own = call(
            w_rows_kernel, "w_rows", [like((2 * DH, width), BF)], [w_keep, over_core(w_send)]
        )[0]
        w_got = over_dp(w_own, 0)
    else:
        a, b, c = over_z(to_a, 0), over_z(to_b, 1), []
        state = lax.psum(state, "z")
        weights = lax.all_gather(out_weight, axes, axis=0, tiled=True).reshape(2, 2, DH, model)
        weights = [jnp.where(core == 0, weights[:, 0], weights[:, 1]).reshape(2 * DH, model)]

    span = 2 * rows + 2 * HALF
    keep_width = 2 * width if direct else model
    wg_flops = 2 * 2 * rows * DH * model
    qs, ks, vs, ogs, probs, attn, keep_soft, *soft_send = call(
        functools.partial(soft_forward_kernel, direct), "soft_forward",
        [
            like((2 * rows, DH), BF), like((span, DH), BF), like((span, DH), BF),
            like((2 * rows, model), BF), like((2, rows, rows + 2 * HALF), F32), like((2 * rows, DH), F32),
            like((DH, keep_width), F32),
        ] + [like((DH, 2 * width), BF)] * direct,
        [mine, pair, og, og_recv, a, b],
        flops=wg_flops,
    )
    u, total, keep_lin, *sent = call(
        functools.partial(lin_forward_kernel, direct), "lin_forward",
        [like((2 * rows, DH), F32), like((DH, DH), F32), like((DH, keep_width), F32)]
        + [like((2 * DH, 2 * width), BF)] * direct,
        [state, mine, pair, ogs, gain] + ([a, b] + c + soft_send if direct else []),
        flops=wg_flops,
    )
    if direct:
        got = over_dp(sent[0], 0)
        keep, sent = call(
            fold_kernel, "fold", [like((2 * DH, width), F32), like((2 * DH, width), BF)],
            [keep_soft, keep_lin, got],
        )
        got = over_dp(sent, 1)
        pieces = call(
            piece_kernel, "pieces", [like((half, width), BF)] * HEADS, [keep, got],
            scratch=[pltpu.VMEM((HEADS, half, width), F32)],
        )
        w_half = call(
            join_kernel, "w_half", [like((2 * DH, 2 * width), BF)], [w_own, w_got, pieces[0]]
        )[0]
        weights = [w_half, over_dp(w_half, 1)]
        chunks = [to_owner(value, step) for step, value in enumerate(pieces)]
        summed = call(
            functools.partial(weight_sum_kernel, scale), "weight_sum", [like((half, width), BF)],
            chunks,
        )[0]
        got = over_dp(summed, 0)
        both = call(join_kernel, "both", [like((half, 2 * width), BF)], [summed, got])[0]
        got = over_dp(both, 1)
        weight_grad = call(
            weight_join_kernel, "weight_join", [like((half, model), F32)], [both, got]
        )[0]
    dq_lin, dq_lin_pair, dstate, dq_soft, dk_soft, dv_soft = call(
        functools.partial(backward_kernel, direct), "backward",
        [
            like((rows, DH), BF), like((rows, DH), BF), like((DH, DH), F32),
            like((2 * rows, DH), F32), like((span, DH), F32), like((span, DH), F32),
        ],
        weights + [ogs, u, total, mine, pair, gain, qs, ks, vs, probs, attn],
        scratch=[pltpu.VMEM((2 * rows, 2 * DH), F32), pltpu.VMEM((2 * rows, DH), F32)]
        + [pltpu.VMEM((2 * DH, model), BF)] * direct,
        flops=5 * wg_flops,
    )
    wide = 3 * DH if direct else 2 * DH
    to_a, to_b, *to_c = call(
        functools.partial(halo_kernel, direct), "halo",
        [like((rows, wide), BF), like((rows, wide), BF)] + [like((DH, DH), BF)] * direct,
        [dk_soft, dv_soft] + ([dstate] + chunks if direct else []),
    )
    a, b = over_z(to_a, 0, True), over_z(to_b, 1, True)
    c = [over_z(value, 2) for value in to_c]
    if not direct:
        dstate = lax.psum(dstate, "z")
        groups = jnp.stack([keep_soft, keep_lin])
        slots = jnp.stack([jnp.where(core == head, groups, 0.0) for head in range(2)], axis=1)
        local = lax.psum_scatter(
            slots.reshape(HEADS * DH, model), axes, scatter_dimension=0, tiled=True
        )
        weight_grad = lax.psum(local, "dp") * scale
    own_out, to_pair = call(
        functools.partial(final_kernel, direct), "final",
        [like((rows, 6 * DH), BF), like((rows, 6 * DH), BF)],
        [dstate, mine, pair, dq_soft, dk_soft, dv_soft, dq_lin, dq_lin_pair, a, b] + c
        + ([both] if direct else []),
        scratch=[pltpu.VMEM((2 * rows, DH), F32)] * 2,
        flops=wg_flops // 4,
    )
    from_pair = over_core(to_pair)
    shape = like((1, rows, HEADS * DH), BF)
    dq, dk, dv = call(output_kernel, "outputs", [shape] * 3, [own_out, from_pair])
    return dq, dk, dv, weight_grad


def solution(mesh):
    n_dp, n_seq = mesh.shape["dp"], mesh.shape["seq"]
    blocks = Mesh(mesh.devices.reshape(n_dp, n_seq // 2, 2), ("dp", "z", "core"))
    tokens, heads = P("dp", ("z", "core"), None), P(("z", "core"), None)
    return jax.shard_map(
        functools.partial(body, n_dp, n_seq // 2),
        mesh=blocks,
        in_specs=(tokens, tokens, tokens, tokens, heads, P()),
        out_specs=(tokens, tokens, tokens, heads),
        check_vma=False,
    )
```

```python
import functools
import math

import jax
import jax.numpy as jnp
from jax import lax
from jax.experimental import pallas as pl
from jax.experimental.pallas import tpu as pltpu
from jax.sharding import Mesh
from jax.sharding import PartitionSpec as P

DH = 128
SOFT_HEADS = 2
LIN_HEADS = 2
HEADS = SOFT_HEADS + LIN_HEADS
WINDOW = 256
HALF = 128
norm_eps = 1e-06
FACTOR = DH ** (-0.5)
BF = jnp.bfloat16
F32 = jnp.float32
NN = (((1,), (0,)), ((), ()))
NT = (((1,), (1,)), ((), ()))
TN = (((0,), (0,)), ((), ()))


def unit_plus(values):
    return jnp.where(values > 0, values + 1.0, jnp.exp(jnp.minimum(values, 0.0)))


def unit_slope(values):
    return jnp.where(values > 0, 1.0, jnp.exp(jnp.minimum(values, 0.0)))


def mm(a, b, dims=NN):
    return lax.dot_general(a, b, dims, preferred_element_type=F32)


def halves(x):
    high = x.astype(BF)
    return high, (x - high.astype(F32)).astype(BF)


def mm3(a, b, dims=NN):
    a_high, a_low = halves(a)
    b_high, b_low = halves(b)
    return mm(a_high, b_high, dims) + (mm(a_high, b_low, dims) + mm(a_low, b_high, dims))


def mm2(a, b, dims=NN):
    a_high, a_low = halves(a)
    return mm(a_high, b, dims) + mm(a_low, b, dims)


def at(start, size=DH):
    return pl.ds(pl.multiple_of(start, size), size)


def places():
    return lax.axis_index("core"), lax.axis_index("z"), lax.axis_index("dp")


def call(kernel, name, outs, args, scratch=(), flops=0, spaces=None):
    vmem = pl.BlockSpec(memory_space=pltpu.VMEM)
    size = sum(math.prod(x.shape) * x.dtype.itemsize for x in list(args) + list(outs))
    return pl.pallas_call(
        kernel,
        name=name,
        out_shape=list(outs),
        in_specs=spaces or [vmem] * len(args),
        out_specs=[vmem] * len(outs),
        scratch_shapes=list(scratch),
        compiler_params=pltpu.CompilerParams(vmem_limit_bytes=24 * 2**20),
        cost_estimate=pl.CostEstimate(flops=flops, bytes_accessed=size, transcendentals=0),
    )(*args)


def like(shape, dtype):
    return jax.ShapeDtypeStruct(shape, dtype)


QS, KS, VS, QL, KL, VL = (slice(i * DH, (i + 1) * DH) for i in range(6))
SOFT = SOFT_HEADS * DH


def links(direct):
    core, z, dp = places()
    step = 1 + core
    turn = lax.rem(z + core, 2) if direct else 1
    return dict(
        first=1 + 2 * core, second=3 - 2 * core, step=step, other=3 - step,
        block_a=1 - turn, block_b=turn,
        halo_a=(1 - turn if direct else 1), halo_b=(turn if direct else 0),
    )


def pack_kernel(q, k, v, og, w, gain, mine_out, og_out, w_out, gain_out, sems):
    core, _, dp = places()
    mine = core * DH
    copies = []

    def fetch(source, target):
        copy = pltpu.make_async_copy(source, target, sems.at[len(copies)])
        copy.start()
        copies.append(copy)

    for index, array in enumerate((q, k, v)):
        for group in range(2):
            cols = slice((3 * group + index) * DH, (3 * group + index + 1) * DH)
            fetch(array.at[0, :, at(SOFT * group + mine)], mine_out.at[:, cols])
    width = w_out.shape[1]
    fetch(w.at[:, at(dp * width, width)], w_out)
    fetch(og.at[0], og_out)
    fetch(gain.at[at(mine)], gain_out.at[0])
    for copy in copies:
        copy.wait()


def state_kernel(direct, mine, q_pair, k_pair, v_pair, *refs):
    if direct:
        w, state, pair, to_a, to_b, to_c = refs
    else:
        state, pair, to_a, to_b = refs
    core, _, _ = places()
    own = core * DH
    for index, source in enumerate((q_pair, k_pair, v_pair)):
        for group in range(2):
            first = (3 * group + index) * DH
            pair[:, first : first + DH] = source[0, :, at(SOFT * group + own)]
    total = mm2(unit_plus(mine[:, KL].astype(F32)), mine[:, VL], TN) + mm2(
        unit_plus(pair[:, KL].astype(F32)), pair[:, VL], TN
    )
    state[...] = total
    way = links(direct)
    for out, block in ((to_a, way["block_a"]), (to_b, way["block_b"])):
        here = block == core
        out[:, :DH] = jnp.where(here, mine[:, KS], pair[:, KS])
        out[:, DH : 2 * DH] = jnp.where(here, mine[:, VS], pair[:, VS])
    if direct:
        rows = w.shape[0]
        for out, first in ((to_a, 2 * DH), (to_b, 2 * DH), (to_c, 0)):
            out[:, first : first + DH] = total.astype(BF)
            out[:rows, first + DH :] = w[:, :DH]
            out[rows:, first + DH :] = w[:, DH:]


def relay_kernel(w, a, b, c, keep, send, heads):
    core, z, _ = places()
    way = links(True)
    rows = w.shape[0]
    heads[z] = w[...]
    for source, first, step in ((a, 3 * DH, way["first"]), (b, 3 * DH, way["second"]), (c, DH, 2)):
        heads[z ^ step, :, :DH] = source[:rows, first:]
        heads[z ^ step, :, DH:] = source[rows:, first:]
    for group in range(2):
        keep[group] = heads[2 * group + core]
        send[group] = heads[2 * group + 1 - core]


def w_rows_kernel(keep, got, out):
    core, _, _ = places()
    half = keep.shape[1]
    for group in range(2):
        out[at(group * DH + core * half, half), :] = keep[group]
        out[at(group * DH + (1 - core) * half, half), :] = got[group]


def join_kernel(first, second, *refs):
    out = refs[-1]
    width = first.shape[1]
    out[:, :width] = first[...]
    out[:, width:] = second[...]


def weight_parts(direct, attn, ogs, send, keep):
    high, low = halves(attn)
    if not direct:
        keep[...] = mm(high, ogs[...], TN) + mm(low, ogs[...], TN)
        return
    _, _, dp = places()
    way = links(True)
    width = send.shape[1] // 2
    for index, step in enumerate((0, way["other"])):
        cols = slice(index * width, (index + 1) * width)
        near, far = at((dp ^ step) * width, width), at((dp ^ step ^ way["step"]) * width, width)
        keep[:, cols] = mm(high, ogs[:, near], TN) + mm(low, ogs[:, near], TN)
        send[:, cols] = (mm(high, ogs[:, far], TN) + mm(low, ogs[:, far], TN)).astype(BF)


def soft_forward_kernel(
    direct, mine, pair, og, og_recv, a, b, qs, ks, vs, ogs, probs, attn, keep, *send
):
    core, _, _ = places()
    way = links(direct)
    rows = og.shape[0]
    own_at, pair_at = core * rows, (1 - core) * rows
    for source, first in ((mine, own_at), (pair, pair_at)):
        qs[at(first, rows), :] = source[:, QS]
        ks[at(HALF + first, rows), :] = source[:, KS]
        vs[at(HALF + first, rows), :] = source[:, VS]
    for source, side in ((a, way["halo_a"]), (b, way["halo_b"])):
        first = side * (HALF + 2 * rows)
        ks[at(first), :] = source[:, :DH]
        vs[at(first), :] = source[:, DH : 2 * DH]
    ogs[at(own_at, rows), :] = og[...]
    ogs[at(pair_at, rows), :] = og_recv[...]
    span = rows + 2 * HALF
    row_pos = lax.broadcasted_iota(jnp.int32, (rows, span), 0)
    col_pos = lax.broadcasted_iota(jnp.int32, (rows, span), 1)
    inside = (col_pos >= row_pos) & (col_pos < row_pos + WINDOW)
    for block in range(2):
        here, window = slice(block * rows, (block + 1) * rows), slice(block * rows, block * rows + span)
        scores = mm(qs[here, :], ks[window, :], NT) * FACTOR
        scores = jnp.where(inside, scores, -1e30)
        peak = jnp.max(scores, axis=1, keepdims=True)
        terms = jnp.where(inside, jnp.exp(scores - peak), 0.0)
        share = terms / jnp.sum(terms, axis=1, keepdims=True)
        probs[block] = share
        attn[here, :] = mm(share.astype(BF), vs[window, :])
    weight_parts(direct, attn[...], ogs, send[0] if send else None, keep)


def lin_forward_kernel(direct, state, mine, pair, ogs, gain, *refs):
    core, _, _ = places()
    rows = mine.shape[0]
    total = state[...]
    if direct:
        a, b, c, soft_send, u_out, total_out, keep, out = refs
        total = total + a[:, 2 * DH : 3 * DH].astype(F32) + b[:, 2 * DH : 3 * DH].astype(F32)
        total = total + c[:, :DH].astype(F32)
    else:
        u_out, total_out, keep = refs
    total_out[...] = total
    u_out[at(core * rows, rows), :] = mm3(unit_plus(mine[:, QL].astype(F32)), total)
    u_out[at((1 - core) * rows, rows), :] = mm3(unit_plus(pair[:, QL].astype(F32)), total)
    u = u_out[...]
    r = lax.rsqrt(jnp.mean(u * u, axis=1, keepdims=True) + norm_eps)
    attn = gain[...] * u * r
    weight_parts(direct, attn, ogs, out.at[DH:, :] if direct else None, keep)
    if direct:
        out[:DH, :] = soft_send[...]


def fold_kernel(keep_soft, keep_lin, got, keep, send):
    width = keep.shape[1]
    for rows, source in ((slice(0, DH), keep_soft), (slice(DH, 2 * DH), keep_lin)):
        keep[rows, :] = source[:, :width] + got[rows, :width].astype(F32)
        send[rows, :] = (source[:, width:] + got[rows, width:].astype(F32)).astype(BF)


def rows_kernel(keep, got, own, send, total):
    core, _, _ = places()
    half = DH // 2
    total[...] = keep[...] + got[...].astype(F32)
    for group in range(2):
        out = slice(group * half, (group + 1) * half)
        own[out, :] = total[at(group * DH + core * half, half), :]
        send[out, :] = total[at(group * DH + (1 - core) * half, half), :]


def lin_backward(u, total, dattn, mine, pair, gain, dq_own, dq_pair, dstate, grads):
    core, _, _ = places()
    rows = mine.shape[0]
    u_all = u[...]
    r = lax.rsqrt(jnp.mean(u_all * u_all, axis=1, keepdims=True) + norm_eps)
    lin_grad = gain[...] * dattn[:, DH:]
    grads[...] = r * lin_grad - u_all * (r * r * r) * jnp.mean(lin_grad * u_all, axis=1, keepdims=True)
    total_state = total[...]
    result = jnp.zeros(dstate.shape, F32)
    for first, source, out in ((core * rows, mine, dq_own), ((1 - core) * rows, pair, dq_pair)):
        wide = source[:, QL].astype(F32)
        part = grads[at(first, rows), :]
        result = result + mm3(unit_plus(wide), part, TN)
        out[...] = (mm3(part, total_state, NT) * unit_slope(wide)).astype(BF)
    dstate[...] = result


def soft_backward(qs, ks, vs, probs, attn, dattn, dq_all, dk_all, dv_all):
    rows = qs.shape[0] // 2
    span = rows + 2 * HALF
    dk_all[...] = jnp.zeros_like(dk_all)
    dv_all[...] = jnp.zeros_like(dv_all)
    for block in range(2):
        here, window = slice(block * rows, (block + 1) * rows), slice(block * rows, block * rows + span)
        grad = dattn[here, :DH].astype(BF)
        share = probs[block]
        delta = jnp.sum(grad.astype(F32) * attn[here, :], axis=1, keepdims=True)
        dscore = (share * (mm(grad, vs[window, :], NT) - delta)).astype(BF)
        dq_all[here, :] = mm(dscore, ks[window, :]) * FACTOR
        dk_all[window, :] += mm(dscore, qs[here, :], TN) * FACTOR
        dv_all[window, :] += mm(share.astype(BF), grad, TN)


def backward_kernel(direct, *refs):
    if direct:
        sent, got = refs[:2]
        refs = refs[3:]
    else:
        weights = refs[0]
        refs = refs[1:]
    (ogs, u, total, mine, pair, gain, qs, ks, vs, probs, attn,
     dq_lin, dq_lin_pair, dstate, dq_soft, dk_soft, dv_soft, dattn, grads, *scratch) = refs
    if direct:
        _, _, dp = places()
        way = links(True)
        weights = scratch[0]
        width = weights.shape[1] // 4
        for source, index, step in (
            (sent, 0, 0), (sent, 1, way["step"]), (got, 0, way["other"]), (got, 1, 3),
        ):
            weights[:, at((dp ^ step) * width, width)] = source[:, index * width : (index + 1) * width]
    dattn[...] = mm(ogs[...], weights[...], NT)
    lin_backward(u, total, dattn, mine, pair, gain, dq_lin, dq_lin_pair, dstate, grads)
    soft_backward(qs, ks, vs, probs, attn, dattn, dq_soft, dk_soft, dv_soft)


def halo_kernel(direct, dk_soft, dv_soft, *refs):
    way = links(direct)
    span = dk_soft.shape[0]
    if direct:
        dstate, *_, to_a, to_b, to_c = refs
        to_c[...] = dstate[...].astype(BF)
    else:
        to_a, to_b = refs
    for out, side in ((to_a, way["halo_a"]), (to_b, way["halo_b"])):
        first = side * (span - HALF)
        out[:, :DH] = dk_soft[at(first), :].astype(BF)
        out[:, DH : 2 * DH] = dv_soft[at(first), :].astype(BF)
        if direct:
            out[:, 2 * DH :] = dstate[...].astype(BF)


def chunk_kernel(own, got, to_a, to_b, to_c, chunk, heads):
    core, z, _ = places()
    way = links(True)
    half = chunk.shape[0]
    for group in range(2):
        rows = slice(group * half, (group + 1) * half)
        heads[2 * group + core] = own[rows, :]
        heads[2 * group + 1 - core] = got[rows, :]
    chunk[...] = heads[z]
    for out, step in ((to_a, way["first"]), (to_b, way["second"]), (to_c, 2)):
        out[...] = heads[z ^ step].astype(BF)


def weight_sum_kernel(scale, chunk, a, b, c, out):
    total = chunk[...] + a[...].astype(F32) + b[...].astype(F32) + c[...].astype(F32)
    out[...] = (scale * total).astype(out.dtype)


def final_kernel(
    direct, dstate, mine, pair, dq_soft, dk_soft, dv_soft, dq_lin, dq_lin_pair, a, b, *refs
):
    core, _, _ = places()
    way = links(direct)
    rows = mine.shape[0]
    total = dstate[...]
    own_out, pair_out, dk_all, dv_all = refs[-4:]
    if direct:
        total = total + a[:, 2 * DH :].astype(F32) + b[:, 2 * DH :].astype(F32)
        total = total + refs[0][...].astype(F32)
    for source, out, cols in ((dk_soft, dk_all, slice(0, DH)), (dv_soft, dv_all, slice(DH, 2 * DH))):
        out[...] = source[HALF : HALF + 2 * rows, :]
        out[at(way["block_a"] * rows, rows), :] += a[:, cols].astype(F32)
        out[at(way["block_b"] * rows, rows), :] += b[:, cols].astype(F32)
    high, low = halves(total)
    for source, dq, out, place in ((mine, dq_lin, own_out, core), (pair, dq_lin_pair, pair_out, 1 - core)):
        here = at(place * rows, rows)
        out[:, QS] = dq_soft[here, :].astype(BF)
        out[:, KS] = dk_all[here, :].astype(BF)
        out[:, VS] = dv_all[here, :].astype(BF)
        wide, values = source[:, KL].astype(F32), source[:, VL]
        out[:, QL] = dq[...]
        out[:, KL] = ((mm(values, high, NT) + mm(values, low, NT)) * unit_slope(wide)).astype(BF)
        out[:, VL] = mm3(unit_plus(wide), total).astype(BF)


def output_kernel(own, pair, dq, dk, dv):
    core, _, _ = places()
    for source, first in ((own, core * DH), (pair, (1 - core) * DH)):
        for index, out in enumerate((dq, dk, dv)):
            out[0, :, at(first)] = source[:, index * DH : (index + 1) * DH]
            out[0, :, at(SOFT + first)] = source[:, (3 + index) * DH : (4 + index) * DH]


def weight_join_kernel(both, got, out):
    _, _, dp = places()
    way = links(True)
    width = both.shape[1] // 2
    for source, index, step in ((both, 0, 0), (both, 1, way["step"]), (got, 0, way["other"]), (got, 1, 3)):
        out[:, at((dp ^ step) * width, width)] = source[:, index * width : (index + 1) * width].astype(F32)


def body(n_dp, n_z, queries, key_rows, value_rows, out_grad, out_weight, norm_gain):
    rows, model = out_grad.shape[1:]
    axes = ("z", "core")
    pair_perm = [(0, 1), (1, 0)]
    core = lax.axis_index("core")
    direct = n_z == HEADS and n_dp == 4
    width = model // n_dp
    half = DH // 2

    scale = 1.0 / math.sqrt(n_dp * n_z * 2 * rows)

    def over_core(value):
        return lax.ppermute(value, "core", pair_perm)

    def over_z(value, which, back=False):
        pairs = []
        for z in range(n_z):
            for c in range(2):
                if direct:
                    there = z ^ (1 + 2 * c, 3 - 2 * c, 2)[which]
                else:
                    there = (z + (1 if (which == 1) != back else -1)) % n_z
                pairs.append((2 * z + c, 2 * there + c))
        return lax.ppermute(value, axes, pairs)

    def over_dp(value, which):
        pairs = [
            (2 * d + c, 2 * (d ^ (1 + c, 2 - c)[which]) + c) for d in range(n_dp) for c in range(2)
        ]
        return lax.ppermute(value, ("dp", "core"), pairs)

    vmem = pl.BlockSpec(memory_space=pltpu.VMEM)

    def hbm(value):
        return pltpu.with_memory_space_constraint(value, pltpu.HBM)

    q_pair, k_pair, v_pair = over_core(queries), over_core(key_rows), over_core(value_rows)
    og_recv = over_core(out_grad[0])
    mine, og, w_part, gain = call(
        pack_kernel, "pack",
        [
            like((rows, 6 * DH), BF), like((rows, model), BF),
            like((out_weight.shape[0], width), BF), like((1, DH), F32),
        ],
        [hbm(x) for x in (queries, key_rows, value_rows, out_grad, out_weight, norm_gain)],
        scratch=[pltpu.SemaphoreType.DMA((9,))],
        spaces=[pl.BlockSpec(memory_space=pltpu.HBM)] * 6,
    )
    wide = 4 * DH if direct else 2 * DH
    state, pair, to_a, to_b, *rest = call(
        functools.partial(state_kernel, direct), "state",
        [like((DH, DH), F32), like((rows, 6 * DH), BF), like((rows, wide), BF), like((rows, wide), BF)]
        + [like((rows, 2 * DH), BF)] * direct,
        [mine, q_pair, k_pair, v_pair] + [w_part] * direct,
        flops=4 * 2 * rows * DH * DH,
    )
    if direct:
        a, b, c = over_z(to_a, 0), over_z(to_b, 1), [over_z(rest[0], 2)]
        w_keep, w_send = call(
            relay_kernel, "relay", [like((2, half, width), BF)] * 2, [w_part, a, b] + c,
            scratch=[pltpu.VMEM((HEADS, half, width), BF)],
        )
        w_own = call(
            w_rows_kernel, "w_rows", [like((2 * DH, width), BF)], [w_keep, over_core(w_send)]
        )[0]
        w_got = over_dp(w_own, 0)
    else:
        a, b, c = over_z(to_a, 0), over_z(to_b, 1), []
        state = lax.psum(state, "z")
        weights = lax.all_gather(out_weight, axes, axis=0, tiled=True).reshape(2, 2, DH, model)
        weights = [jnp.where(core == 0, weights[:, 0], weights[:, 1]).reshape(2 * DH, model)]

    span = 2 * rows + 2 * HALF
    keep_width = 2 * width if direct else model
    wg_flops = 2 * 2 * rows * DH * model
    qs, ks, vs, ogs, probs, attn, keep_soft, *soft_send = call(
        functools.partial(soft_forward_kernel, direct), "soft_forward",
        [
            like((2 * rows, DH), BF), like((span, DH), BF), like((span, DH), BF),
            like((2 * rows, model), BF), like((2, rows, rows + 2 * HALF), F32), like((2 * rows, DH), F32),
            like((DH, keep_width), F32),
        ] + [like((DH, 2 * width), BF)] * direct,
        [mine, pair, og, og_recv, a, b],
        flops=wg_flops,
    )
    u, total, keep_lin, *sent = call(
        functools.partial(lin_forward_kernel, direct), "lin_forward",
        [like((2 * rows, DH), F32), like((DH, DH), F32), like((DH, keep_width), F32)]
        + [like((2 * DH, 2 * width), BF)] * direct,
        [state, mine, pair, ogs, gain] + ([a, b] + c + soft_send if direct else []),
        flops=wg_flops,
    )
    if direct:
        got = over_dp(sent[0], 0)
        keep, sent = call(
            fold_kernel, "fold", [like((2 * DH, width), F32), like((2 * DH, width), BF)],
            [keep_soft, keep_lin, got],
        )
        w_half = call(
            join_kernel, "w_half", [like((2 * DH, 2 * width), BF)], [w_own, w_got, sent]
        )[0]
        weights = [w_half, over_dp(w_half, 1)]
        got = over_dp(sent, 1)
        row_own, row_send = call(
            rows_kernel, "rows", [like((2 * half, width), F32)] * 2, [keep, got],
            scratch=[pltpu.VMEM((2 * DH, width), F32)],
        )
        row_recv = over_core(row_send)
        *to_chips, chunk = call(
            chunk_kernel, "chunk", [like((half, width), BF)] * 3 + [like((half, width), F32)],
            [row_own, row_recv], scratch=[pltpu.VMEM((HEADS, half, width), F32)],
        )
        chunks = [over_z(value, which) for which, value in enumerate(to_chips)]
        summed = call(
            functools.partial(weight_sum_kernel, scale), "weight_sum", [like((half, width), BF)],
            [chunk] + chunks,
        )[0]
        got = over_dp(summed, 0)
        both = call(join_kernel, "both", [like((half, 2 * width), BF)], [summed, got])[0]
        gathered = over_dp(both, 1)
        weight_grad = call(
            weight_join_kernel, "weight_join", [like((half, model), F32)], [both, gathered]
        )[0]
    if direct:
        weights.append(chunk)
    dq_lin, dq_lin_pair, dstate, dq_soft, dk_soft, dv_soft = call(
        functools.partial(backward_kernel, direct), "backward",
        [
            like((rows, DH), BF), like((rows, DH), BF), like((DH, DH), F32),
            like((2 * rows, DH), F32), like((span, DH), F32), like((span, DH), F32),
        ],
        weights + [ogs, u, total, mine, pair, gain, qs, ks, vs, probs, attn],
        scratch=[pltpu.VMEM((2 * rows, 2 * DH), F32), pltpu.VMEM((2 * rows, DH), F32)]
        + [pltpu.VMEM((2 * DH, model), BF)] * direct,
        flops=5 * wg_flops,
    )
    wide = 3 * DH if direct else 2 * DH
    to_a, to_b, *to_c = call(
        functools.partial(halo_kernel, direct), "halo",
        [like((rows, wide), BF), like((rows, wide), BF)] + [like((DH, DH), BF)] * direct,
        [dk_soft, dv_soft] + ([dstate] + chunks if direct else []),
    )
    a, b = over_z(to_a, 0, True), over_z(to_b, 1, True)
    c = [over_z(value, 2) for value in to_c]
    if not direct:
        dstate = lax.psum(dstate, "z")
        groups = jnp.stack([keep_soft, keep_lin])
        slots = jnp.stack([jnp.where(core == head, groups, 0.0) for head in range(2)], axis=1)
        local = lax.psum_scatter(
            slots.reshape(HEADS * DH, model), axes, scatter_dimension=0, tiled=True
        )
        weight_grad = lax.psum(local, "dp") * scale
    own_out, to_pair = call(
        functools.partial(final_kernel, direct), "final",
        [like((rows, 6 * DH), BF), like((rows, 6 * DH), BF)],
        [dstate, mine, pair, dq_soft, dk_soft, dv_soft, dq_lin, dq_lin_pair, a, b] + c
        + ([gathered] if direct else []),
        scratch=[pltpu.VMEM((2 * rows, DH), F32)] * 2,
        flops=wg_flops // 4,
    )
    from_pair = over_core(to_pair)
    shape = like((1, rows, HEADS * DH), BF)
    dq, dk, dv = call(output_kernel, "outputs", [shape] * 3, [own_out, from_pair])
    return dq, dk, dv, weight_grad


def solution(mesh):
    n_dp, n_seq = mesh.shape["dp"], mesh.shape["seq"]
    blocks = Mesh(mesh.devices.reshape(n_dp, n_seq // 2, 2), ("dp", "z", "core"))
    tokens, heads = P("dp", ("z", "core"), None), P(("z", "core"), None)
    return jax.shard_map(
        functools.partial(body, n_dp, n_seq // 2),
        mesh=blocks,
        in_specs=(tokens, tokens, tokens, tokens, heads, P()),
        out_specs=(tokens, tokens, tokens, heads),
        check_vma=False,
    )
```

```python
import functools
import math

import jax
import jax.numpy as jnp
from jax import lax
from jax.experimental import pallas as pl
from jax.experimental.pallas import tpu as pltpu
from jax.sharding import Mesh
from jax.sharding import PartitionSpec as P

DH = 128
SOFT_HEADS = 2
LIN_HEADS = 2
HEADS = SOFT_HEADS + LIN_HEADS
WINDOW = 256
HALF = 128
norm_eps = 1e-06
FACTOR = DH ** (-0.5)
BF = jnp.bfloat16
F32 = jnp.float32
NN = (((1,), (0,)), ((), ()))
NT = (((1,), (1,)), ((), ()))
TN = (((0,), (0,)), ((), ()))


def unit_plus(values):
    return jnp.where(values > 0, values + 1.0, jnp.exp(jnp.minimum(values, 0.0)))


def unit_slope(values):
    return jnp.where(values > 0, 1.0, jnp.exp(jnp.minimum(values, 0.0)))


def mm(a, b, dims=NN):
    return lax.dot_general(a, b, dims, preferred_element_type=F32)


def halves(x):
    high = x.astype(BF)
    return high, (x - high.astype(F32)).astype(BF)


def mm3(a, b, dims=NN):
    a_high, a_low = halves(a)
    b_high, b_low = halves(b)
    return mm(a_high, b_high, dims) + (mm(a_high, b_low, dims) + mm(a_low, b_high, dims))


def mm2(a, b, dims=NN):
    a_high, a_low = halves(a)
    return mm(a_high, b, dims) + mm(a_low, b, dims)


def at(start, size=DH):
    return pl.ds(pl.multiple_of(start, size), size)


def places():
    return lax.axis_index("core"), lax.axis_index("z"), lax.axis_index("dp")


def call(kernel, name, outs, args, scratch=(), flops=0, spaces=None):
    vmem = pl.BlockSpec(memory_space=pltpu.VMEM)
    size = sum(math.prod(x.shape) * x.dtype.itemsize for x in list(args) + list(outs))
    return pl.pallas_call(
        kernel,
        name=name,
        out_shape=list(outs),
        in_specs=spaces or [vmem] * len(args),
        out_specs=[vmem] * len(outs),
        scratch_shapes=list(scratch),
        compiler_params=pltpu.CompilerParams(vmem_limit_bytes=24 * 2**20),
        cost_estimate=pl.CostEstimate(flops=flops, bytes_accessed=size, transcendentals=0),
    )(*args)


def like(shape, dtype):
    return jax.ShapeDtypeStruct(shape, dtype)


QS, KS, VS, QL, KL, VL = (slice(i * DH, (i + 1) * DH) for i in range(6))
SOFT = SOFT_HEADS * DH


def links(direct):
    core, z, dp = places()
    step = 1 + core
    turn = lax.rem(z + core, 2) if direct else 1
    return dict(
        first=1 + 2 * core, second=3 - 2 * core, step=step, other=3 - step,
        block_a=1 - turn, block_b=turn,
        halo_a=(1 - turn if direct else 1), halo_b=(turn if direct else 0),
    )


def pack_kernel(q, k, v, og, w, gain, mine_out, og_out, w_out, gain_out, sems):
    core, _, dp = places()
    mine = core * DH
    copies = []

    def fetch(source, target):
        copy = pltpu.make_async_copy(source, target, sems.at[len(copies)])
        copy.start()
        copies.append(copy)

    for index, array in enumerate((q, k, v)):
        for group in range(2):
            cols = slice((3 * group + index) * DH, (3 * group + index + 1) * DH)
            fetch(array.at[0, :, at(SOFT * group + mine)], mine_out.at[:, cols])
    width = w_out.shape[1]
    fetch(w.at[:, at(dp * width, width)], w_out)
    fetch(og.at[0], og_out)
    fetch(gain.at[at(mine)], gain_out.at[0])
    for copy in copies:
        copy.wait()


def state_kernel(direct, mine, q_pair, k_pair, v_pair, *refs):
    if direct:
        w, state, pair, to_a, to_b, to_c = refs
    else:
        state, pair, to_a, to_b = refs
    core, _, _ = places()
    own = core * DH
    for index, source in enumerate((q_pair, k_pair, v_pair)):
        for group in range(2):
            first = (3 * group + index) * DH
            pair[:, first : first + DH] = source[0, :, at(SOFT * group + own)]
    total = mm2(unit_plus(mine[:, KL].astype(F32)), mine[:, VL], TN) + mm2(
        unit_plus(pair[:, KL].astype(F32)), pair[:, VL], TN
    )
    state[...] = total
    way = links(direct)
    for out, block in ((to_a, way["block_a"]), (to_b, way["block_b"])):
        here = block == core
        out[:, :DH] = jnp.where(here, mine[:, KS], pair[:, KS])
        out[:, DH : 2 * DH] = jnp.where(here, mine[:, VS], pair[:, VS])
    if direct:
        rows = w.shape[0]
        for out, first in ((to_a, 2 * DH), (to_b, 2 * DH), (to_c, 0)):
            out[:, first : first + DH] = total.astype(BF)
            out[:rows, first + DH :] = w[:, :DH]
            out[rows:, first + DH :] = w[:, DH:]


def join_kernel(first, second, *refs):
    out = refs[-1]
    width = first.shape[1]
    out[:, :width] = first[...]
    out[:, width:] = second[...]


def weight_parts(direct, attn, ogs, send, keep):
    high, low = halves(attn)
    if not direct:
        keep[...] = mm(high, ogs[...], TN) + mm(low, ogs[...], TN)
        return
    _, _, dp = places()
    way = links(True)
    width = send.shape[1] // 2
    for index, step in enumerate((0, way["other"])):
        cols = slice(index * width, (index + 1) * width)
        near, far = at((dp ^ step) * width, width), at((dp ^ step ^ way["step"]) * width, width)
        keep[:, cols] = mm(high, ogs[:, near], TN) + mm(low, ogs[:, near], TN)
        send[:, cols] = (mm(high, ogs[:, far], TN) + mm(low, ogs[:, far], TN)).astype(BF)


def soft_forward_kernel(
    direct, mine, pair, og, og_recv, a, b, qs, ks, vs, ogs, probs, attn, keep, *send
):
    core, _, _ = places()
    way = links(direct)
    rows = og.shape[0]
    own_at, pair_at = core * rows, (1 - core) * rows
    for source, first in ((mine, own_at), (pair, pair_at)):
        qs[at(first, rows), :] = source[:, QS]
        ks[at(HALF + first, rows), :] = source[:, KS]
        vs[at(HALF + first, rows), :] = source[:, VS]
    for source, side in ((a, way["halo_a"]), (b, way["halo_b"])):
        first = side * (HALF + 2 * rows)
        ks[at(first), :] = source[:, :DH]
        vs[at(first), :] = source[:, DH : 2 * DH]
    ogs[at(own_at, rows), :] = og[...]
    ogs[at(pair_at, rows), :] = og_recv[...]
    span = rows + 2 * HALF
    row_pos = lax.broadcasted_iota(jnp.int32, (rows, span), 0)
    col_pos = lax.broadcasted_iota(jnp.int32, (rows, span), 1)
    inside = (col_pos >= row_pos) & (col_pos < row_pos + WINDOW)
    for block in range(2):
        here, window = slice(block * rows, (block + 1) * rows), slice(block * rows, block * rows + span)
        scores = mm(qs[here, :], ks[window, :], NT) * FACTOR
        scores = jnp.where(inside, scores, -1e30)
        peak = jnp.max(scores, axis=1, keepdims=True)
        terms = jnp.where(inside, jnp.exp(scores - peak), 0.0)
        share = terms / jnp.sum(terms, axis=1, keepdims=True)
        probs[block] = share
        attn[here, :] = mm(share.astype(BF), vs[window, :])
    weight_parts(direct, attn[...], ogs, send[0] if send else None, keep)


def lin_forward_kernel(direct, state, mine, pair, ogs, gain, *refs):
    core, _, _ = places()
    rows = mine.shape[0]
    total = state[...]
    if direct:
        a, b, c, soft_send, w, u_out, total_out, keep, out = refs
        total = total + a[:, 2 * DH : 3 * DH].astype(F32) + b[:, 2 * DH : 3 * DH].astype(F32)
        total = total + c[:, :DH].astype(F32)
    else:
        u_out, total_out, keep = refs
    total_out[...] = total
    u_out[at(core * rows, rows), :] = mm3(unit_plus(mine[:, QL].astype(F32)), total)
    u_out[at((1 - core) * rows, rows), :] = mm3(unit_plus(pair[:, QL].astype(F32)), total)
    u = u_out[...]
    r = lax.rsqrt(jnp.mean(u * u, axis=1, keepdims=True) + norm_eps)
    attn = gain[...] * u * r
    weight_parts(direct, attn, ogs, out.at[DH:, : soft_send.shape[1]] if direct else None, keep)
    if direct:
        _, z, _ = places()
        way = links(True)
        rows, width = w.shape
        first = soft_send.shape[1]
        out[:DH, :first] = soft_send[...]
        out[at(z * rows, rows), first:] = w[...]
        for source, cols, step in ((a, 3 * DH, way["first"]), (b, 3 * DH, way["second"]), (c, DH, 2)):
            here = at((z ^ step) * rows, rows)
            out[here, first : first + DH] = source[:rows, cols:]
            out[here, first + DH :] = source[rows:, cols:]


def fold_kernel(keep_soft, keep_lin, sent, got, keep, send):
    width = keep.shape[1]
    for rows, source in ((slice(0, DH), keep_soft), (slice(DH, 2 * DH), keep_lin)):
        keep[rows, :] = source[:, :width] + got[rows, :width].astype(F32)
        send[rows, :width] = (source[:, width:] + got[rows, width : 2 * width].astype(F32)).astype(BF)
    send[:, width : 2 * width] = sent[:, 2 * width :]
    send[:, 2 * width :] = got[:, 2 * width :]


def rows_kernel(keep, sent, got, own, w_own, send, total, weights):
    core, _, dp = places()
    way = links(True)
    half = DH // 2
    width = keep.shape[1]
    total[...] = keep[...] + got[:, :width].astype(F32)
    for source, index, step in (
        (sent, 1, 0), (sent, 2, way["step"]), (got, 1, way["other"]), (got, 2, 3),
    ):
        weights[:, at((dp ^ step) * width, width)] = source[:, index * width : (index + 1) * width]
    for group in range(2):
        out = slice(group * half, (group + 1) * half)
        own[out, :] = total[at(group * DH + core * half, half), :]
        high, low = halves(total[at(group * DH + (1 - core) * half, half), :])
        send[out, :width] = high
        send[out, width : 2 * width] = low
        w_own[out, :] = weights[at((2 * group + core) * half, half), :]
        send[out, 2 * width :] = weights[at((2 * group + 1 - core) * half, half), :]


def lin_backward(u, total, dattn, mine, pair, gain, dq_own, dq_pair, dstate, grads):
    core, _, _ = places()
    rows = mine.shape[0]
    u_all = u[...]
    r = lax.rsqrt(jnp.mean(u_all * u_all, axis=1, keepdims=True) + norm_eps)
    lin_grad = gain[...] * dattn[:, DH:]
    grads[...] = r * lin_grad - u_all * (r * r * r) * jnp.mean(lin_grad * u_all, axis=1, keepdims=True)
    total_state = total[...]
    result = jnp.zeros(dstate.shape, F32)
    for first, source, out in ((core * rows, mine, dq_own), ((1 - core) * rows, pair, dq_pair)):
        wide = source[:, QL].astype(F32)
        part = grads[at(first, rows), :]
        result = result + mm3(unit_plus(wide), part, TN)
        out[...] = (mm3(part, total_state, NT) * unit_slope(wide)).astype(BF)
    dstate[...] = result


def soft_backward(qs, ks, vs, probs, attn, dattn, dq_all, dk_all, dv_all):
    rows = qs.shape[0] // 2
    span = rows + 2 * HALF
    dk_all[...] = jnp.zeros_like(dk_all)
    dv_all[...] = jnp.zeros_like(dv_all)
    for block in range(2):
        here, window = slice(block * rows, (block + 1) * rows), slice(block * rows, block * rows + span)
        grad = dattn[here, :DH].astype(BF)
        share = probs[block]
        delta = jnp.sum(grad.astype(F32) * attn[here, :], axis=1, keepdims=True)
        dscore = (share * (mm(grad, vs[window, :], NT) - delta)).astype(BF)
        dq_all[here, :] = mm(dscore, ks[window, :]) * FACTOR
        dk_all[window, :] += mm(dscore, qs[here, :], TN) * FACTOR
        dv_all[window, :] += mm(share.astype(BF), grad, TN)


def backward_kernel(direct, *refs):
    if direct:
        w_own, got = refs[:2]
        refs = refs[2:]
    else:
        weights = refs[0]
        refs = refs[1:]
    (ogs, u, total, mine, pair, gain, qs, ks, vs, probs, attn,
     dq_lin, dq_lin_pair, dstate, dq_soft, dk_soft, dv_soft, dattn, grads, *scratch) = refs
    if direct:
        core, _, _ = places()
        weights = scratch[0]
        rows, model = w_own.shape[0] // 2, weights.shape[1]
        for group in range(2):
            here = slice(group * rows, (group + 1) * rows)
            weights[at(group * DH + core * rows, rows), :] = w_own[here, :]
            weights[at(group * DH + (1 - core) * rows, rows), :] = got[here, got.shape[1] - model :]
    dattn[...] = mm(ogs[...], weights[...], NT)
    lin_backward(u, total, dattn, mine, pair, gain, dq_lin, dq_lin_pair, dstate, grads)
    soft_backward(qs, ks, vs, probs, attn, dattn, dq_soft, dk_soft, dv_soft)


def halo_kernel(direct, dk_soft, dv_soft, *refs):
    way = links(direct)
    span = dk_soft.shape[0]
    if direct:
        dstate, piece, _, _, to_a, to_b, to_c = refs
        half = piece.shape[0]
        to_c[:, :DH] = dstate[...].astype(BF)
        to_c[:half, DH:] = piece[:, :DH]
        to_c[half:, DH:] = piece[:, DH:]
    else:
        to_a, to_b = refs
    for out, side in ((to_a, way["halo_a"]), (to_b, way["halo_b"])):
        first = side * (span - HALF)
        out[:, :DH] = dk_soft[at(first), :].astype(BF)
        out[:, DH : 2 * DH] = dv_soft[at(first), :].astype(BF)
        if direct:
            out[:, 2 * DH :] = dstate[...].astype(BF)


def chunk_kernel(own, got, to_a, to_b, to_c, chunk, heads):
    core, z, _ = places()
    way = links(True)
    half, width = chunk.shape
    for group in range(2):
        rows = slice(group * half, (group + 1) * half)
        heads[2 * group + core] = own[rows, :]
        heads[2 * group + 1 - core] = got[rows, :width].astype(F32) + got[rows, width : 2 * width].astype(F32)
    chunk[...] = heads[z]
    for out, step in ((to_a, way["first"]), (to_b, way["second"]), (to_c, 2)):
        out[...] = heads[z ^ step].astype(BF)


def weight_sum_kernel(scale, chunk, a, b, c, out):
    half = chunk.shape[0]
    for side in range(2):
        cols, rows = slice(side * DH, (side + 1) * DH), slice(side * half, (side + 1) * half)
        total = chunk[:, cols] + a[:, cols].astype(F32) + b[:, cols].astype(F32)
        out[:, cols] = (scale * (total + c[rows, DH:].astype(F32))).astype(out.dtype)


def final_kernel(
    direct, dstate, mine, pair, dq_soft, dk_soft, dv_soft, dq_lin, dq_lin_pair, a, b, *refs
):
    core, _, _ = places()
    way = links(direct)
    rows = mine.shape[0]
    total = dstate[...]
    own_out, pair_out, dk_all, dv_all = refs[-4:]
    if direct:
        total = total + a[:, 2 * DH :].astype(F32) + b[:, 2 * DH :].astype(F32)
        total = total + refs[0][:, :DH].astype(F32)
    for source, out, cols in ((dk_soft, dk_all, slice(0, DH)), (dv_soft, dv_all, slice(DH, 2 * DH))):
        out[...] = source[HALF : HALF + 2 * rows, :]
        out[at(way["block_a"] * rows, rows), :] += a[:, cols].astype(F32)
        out[at(way["block_b"] * rows, rows), :] += b[:, cols].astype(F32)
    high, low = halves(total)
    for source, dq, out, place in ((mine, dq_lin, own_out, core), (pair, dq_lin_pair, pair_out, 1 - core)):
        here = at(place * rows, rows)
        out[:, QS] = dq_soft[here, :].astype(BF)
        out[:, KS] = dk_all[here, :].astype(BF)
        out[:, VS] = dv_all[here, :].astype(BF)
        wide, values = source[:, KL].astype(F32), source[:, VL]
        out[:, QL] = dq[...]
        out[:, KL] = ((mm(values, high, NT) + mm(values, low, NT)) * unit_slope(wide)).astype(BF)
        out[:, VL] = mm3(unit_plus(wide), total).astype(BF)


def output_kernel(own, pair, dq, dk, dv):
    core, _, _ = places()
    for source, first in ((own, core * DH), (pair, (1 - core) * DH)):
        for index, out in enumerate((dq, dk, dv)):
            out[0, :, at(first)] = source[:, index * DH : (index + 1) * DH]
            out[0, :, at(SOFT + first)] = source[:, (3 + index) * DH : (4 + index) * DH]


def weight_join_kernel(both, got, _, out):
    _, _, dp = places()
    way = links(True)
    width = both.shape[1] // 2
    for source, index, step in ((both, 0, 0), (both, 1, way["step"]), (got, 0, way["other"]), (got, 1, 3)):
        out[:, at((dp ^ step) * width, width)] = source[:, index * width : (index + 1) * width].astype(F32)


def body(n_dp, n_z, queries, key_rows, value_rows, out_grad, out_weight, norm_gain):
    rows, model = out_grad.shape[1:]
    axes = ("z", "core")
    pair_perm = [(0, 1), (1, 0)]
    core = lax.axis_index("core")
    direct = n_z == HEADS and n_dp == 4
    width = model // n_dp
    half = DH // 2

    scale = 1.0 / math.sqrt(n_dp * n_z * 2 * rows)

    def over_core(value):
        return lax.ppermute(value, "core", pair_perm)

    def over_z(value, which, back=False):
        pairs = []
        for z in range(n_z):
            for c in range(2):
                if direct:
                    there = z ^ (1 + 2 * c, 3 - 2 * c, 2)[which]
                else:
                    there = (z + (1 if (which == 1) != back else -1)) % n_z
                pairs.append((2 * z + c, 2 * there + c))
        return lax.ppermute(value, axes, pairs)

    def over_dp(value, which):
        pairs = [
            (2 * d + c, 2 * (d ^ (1 + c, 2 - c)[which]) + c) for d in range(n_dp) for c in range(2)
        ]
        return lax.ppermute(value, ("dp", "core"), pairs)

    vmem = pl.BlockSpec(memory_space=pltpu.VMEM)

    def hbm(value):
        return pltpu.with_memory_space_constraint(value, pltpu.HBM)

    q_pair, k_pair, v_pair = over_core(queries), over_core(key_rows), over_core(value_rows)
    og_recv = over_core(out_grad[0])
    mine, og, w_part, gain = call(
        pack_kernel, "pack",
        [
            like((rows, 6 * DH), BF), like((rows, model), BF),
            like((out_weight.shape[0], width), BF), like((1, DH), F32),
        ],
        [hbm(x) for x in (queries, key_rows, value_rows, out_grad, out_weight, norm_gain)],
        scratch=[pltpu.SemaphoreType.DMA((9,))],
        spaces=[pl.BlockSpec(memory_space=pltpu.HBM)] * 6,
    )
    wide = 4 * DH if direct else 2 * DH
    state, pair, to_a, to_b, *rest = call(
        functools.partial(state_kernel, direct), "state",
        [like((DH, DH), F32), like((rows, 6 * DH), BF), like((rows, wide), BF), like((rows, wide), BF)]
        + [like((rows, 2 * DH), BF)] * direct,
        [mine, q_pair, k_pair, v_pair] + [w_part] * direct,
        flops=4 * 2 * rows * DH * DH,
    )
    if direct:
        a, b, c = over_z(to_a, 0), over_z(to_b, 1), [over_z(rest[0], 2)]
    else:
        a, b, c = over_z(to_a, 0), over_z(to_b, 1), []
        state = lax.psum(state, "z")
        weights = lax.all_gather(out_weight, axes, axis=0, tiled=True).reshape(2, 2, DH, model)
        weights = [jnp.where(core == 0, weights[:, 0], weights[:, 1]).reshape(2 * DH, model)]

    span = 2 * rows + 2 * HALF
    keep_width = 2 * width if direct else model
    wg_flops = 2 * 2 * rows * DH * model
    qs, ks, vs, ogs, probs, attn, keep_soft, *soft_send = call(
        functools.partial(soft_forward_kernel, direct), "soft_forward",
        [
            like((2 * rows, DH), BF), like((span, DH), BF), like((span, DH), BF),
            like((2 * rows, model), BF), like((2, rows, rows + 2 * HALF), F32), like((2 * rows, DH), F32),
            like((DH, keep_width), F32),
        ] + [like((DH, 2 * width), BF)] * direct,
        [mine, pair, og, og_recv, a, b],
        flops=wg_flops,
    )
    u, total, keep_lin, *sent = call(
        functools.partial(lin_forward_kernel, direct), "lin_forward",
        [like((2 * rows, DH), F32), like((DH, DH), F32), like((DH, keep_width), F32)]
        + [like((2 * DH, 3 * width), BF)] * direct,
        [state, mine, pair, ogs, gain] + ([a, b] + c + soft_send + [w_part] if direct else []),
        flops=wg_flops,
    )
    if direct:
        got = over_dp(sent[0], 0)
        keep, sent = call(
            fold_kernel, "fold", [like((2 * DH, width), F32), like((2 * DH, 3 * width), BF)],
            [keep_soft, keep_lin, sent[0], got],
        )
        got = over_dp(sent, 1)
        row_own, w_own, swap = call(
            rows_kernel, "rows",
            [like((DH, width), F32), like((DH, model), BF), like((DH, 2 * width + model), BF)],
            [keep, sent, got],
            scratch=[pltpu.VMEM((2 * DH, width), F32), pltpu.VMEM((2 * DH, model), BF)],
        )
        swap = over_core(swap)
        weights = [w_own, swap]
        piece_a, piece_b, piece_c, chunk = call(
            chunk_kernel, "chunk", [like((half, width), BF)] * 3 + [like((half, width), F32)],
            [row_own, swap], scratch=[pltpu.VMEM((HEADS, half, width), F32)],
        )
        chunks = [over_z(piece_a, 0), over_z(piece_b, 1)]
    dq_lin, dq_lin_pair, dstate, dq_soft, dk_soft, dv_soft = call(
        functools.partial(backward_kernel, direct), "backward",
        [
            like((rows, DH), BF), like((rows, DH), BF), like((DH, DH), F32),
            like((2 * rows, DH), F32), like((span, DH), F32), like((span, DH), F32),
        ],
        weights + [ogs, u, total, mine, pair, gain, qs, ks, vs, probs, attn],
        scratch=[pltpu.VMEM((2 * rows, 2 * DH), F32), pltpu.VMEM((2 * rows, DH), F32)]
        + [pltpu.VMEM((2 * DH, model), BF)] * direct,
        flops=5 * wg_flops,
    )
    wide = 3 * DH if direct else 2 * DH
    to_a, to_b, *to_c = call(
        functools.partial(halo_kernel, direct), "halo",
        [like((rows, wide), BF), like((rows, wide), BF)] + [like((rows, 2 * DH), BF)] * direct,
        [dk_soft, dv_soft] + ([dstate, piece_c] + chunks if direct else []),
    )
    a, b = over_z(to_a, 0, True), over_z(to_b, 1, True)
    c = [over_z(value, 2) for value in to_c]
    if direct:
        summed = call(
            functools.partial(weight_sum_kernel, scale), "weight_sum", [like((half, width), BF)],
            [chunk] + chunks + c,
        )[0]
        got = over_dp(summed, 0)
        both = call(join_kernel, "both", [like((half, 2 * width), BF)], [summed, got])[0]
        gathered = over_dp(both, 1)
    if not direct:
        dstate = lax.psum(dstate, "z")
        groups = jnp.stack([keep_soft, keep_lin])
        slots = jnp.stack([jnp.where(core == head, groups, 0.0) for head in range(2)], axis=1)
        local = lax.psum_scatter(
            slots.reshape(HEADS * DH, model), axes, scatter_dimension=0, tiled=True
        )
        weight_grad = lax.psum(local, "dp") * scale
    own_out, to_pair = call(
        functools.partial(final_kernel, direct), "final",
        [like((rows, 6 * DH), BF), like((rows, 6 * DH), BF)],
        [dstate, mine, pair, dq_soft, dk_soft, dv_soft, dq_lin, dq_lin_pair, a, b] + c
        + ([both] if direct else []),
        scratch=[pltpu.VMEM((2 * rows, DH), F32)] * 2,
        flops=wg_flops // 4,
    )
    from_pair = over_core(to_pair)
    shape = like((1, rows, HEADS * DH), BF)
    dq, dk, dv = call(output_kernel, "outputs", [shape] * 3, [own_out, from_pair])
    if direct:
        weight_grad = call(
            weight_join_kernel, "weight_join", [like((half, model), F32)], [both, gathered, hbm(dq)],
            spaces=[vmem, vmem, pl.BlockSpec(memory_space=pltpu.HBM)],
        )[0]
    return dq, dk, dv, weight_grad


def solution(mesh):
    n_dp, n_seq = mesh.shape["dp"], mesh.shape["seq"]
    blocks = Mesh(mesh.devices.reshape(n_dp, n_seq // 2, 2), ("dp", "z", "core"))
    tokens, heads = P("dp", ("z", "core"), None), P(("z", "core"), None)
    return jax.shard_map(
        functools.partial(body, n_dp, n_seq // 2),
        mesh=blocks,
        in_specs=(tokens, tokens, tokens, tokens, heads, P()),
        out_specs=(tokens, tokens, tokens, heads),
        check_vma=False,
    )
```

```python
import functools
import math

import jax
import jax.numpy as jnp
from jax import lax
from jax.experimental import pallas as pl
from jax.experimental.pallas import tpu as pltpu
from jax.sharding import Mesh
from jax.sharding import PartitionSpec as P

DH = 128
SOFT_HEADS = 2
LIN_HEADS = 2
HEADS = SOFT_HEADS + LIN_HEADS
WINDOW = 256
HALF = 128
norm_eps = 1e-06
FACTOR = DH ** (-0.5)
BF = jnp.bfloat16
F32 = jnp.float32
NN = (((1,), (0,)), ((), ()))
NT = (((1,), (1,)), ((), ()))
TN = (((0,), (0,)), ((), ()))


def unit_plus(values):
    return jnp.where(values > 0, values + 1.0, jnp.exp(jnp.minimum(values, 0.0)))


def unit_slope(values):
    return jnp.where(values > 0, 1.0, jnp.exp(jnp.minimum(values, 0.0)))


def mm(a, b, dims=NN):
    return lax.dot_general(a, b, dims, preferred_element_type=F32)


def halves(x):
    high = x.astype(BF)
    return high, (x - high.astype(F32)).astype(BF)


def mm3(a, b, dims=NN):
    a_high, a_low = halves(a)
    b_high, b_low = halves(b)
    return mm(a_high, b_high, dims) + (mm(a_high, b_low, dims) + mm(a_low, b_high, dims))


def mm2(a, b, dims=NN):
    a_high, a_low = halves(a)
    return mm(a_high, b, dims) + mm(a_low, b, dims)


def at(start, size=DH):
    return pl.ds(pl.multiple_of(start, size), size)


def places():
    return lax.axis_index("core"), lax.axis_index("z"), lax.axis_index("dp")


def call(kernel, name, outs, args, scratch=(), flops=0, spaces=None):
    vmem = pl.BlockSpec(memory_space=pltpu.VMEM)
    size = sum(math.prod(x.shape) * x.dtype.itemsize for x in list(args) + list(outs))
    return pl.pallas_call(
        kernel,
        name=name,
        out_shape=list(outs),
        in_specs=spaces or [vmem] * len(args),
        out_specs=[vmem] * len(outs),
        scratch_shapes=list(scratch),
        compiler_params=pltpu.CompilerParams(vmem_limit_bytes=24 * 2**20),
        cost_estimate=pl.CostEstimate(flops=flops, bytes_accessed=size, transcendentals=0),
    )(*args)


def like(shape, dtype):
    return jax.ShapeDtypeStruct(shape, dtype)


QS, KS, VS, QL, KL, VL = (slice(i * DH, (i + 1) * DH) for i in range(6))
SOFT = SOFT_HEADS * DH


def links(direct):
    core, z, dp = places()
    step = 1 + core
    turn = lax.rem(z + core, 2) if direct else 1
    return dict(
        first=1 + 2 * core, second=3 - 2 * core, step=step, other=3 - step,
        block_a=1 - turn, block_b=turn,
        halo_a=(1 - turn if direct else 1), halo_b=(turn if direct else 0),
    )


def pack_kernel(q, k, v, og, w, gain, mine_out, og_out, w_out, gain_out, sems):
    core, _, dp = places()
    mine = core * DH
    copies = []

    def fetch(source, target):
        copy = pltpu.make_async_copy(source, target, sems.at[len(copies)])
        copy.start()
        copies.append(copy)

    for index, array in enumerate((q, k, v)):
        for group in range(2):
            cols = slice((3 * group + index) * DH, (3 * group + index + 1) * DH)
            fetch(array.at[0, :, at(SOFT * group + mine)], mine_out.at[:, cols])
    width = w_out.shape[1]
    fetch(w.at[:, at(dp * width, width)], w_out)
    fetch(og.at[0], og_out)
    fetch(gain.at[at(mine)], gain_out.at[0])
    for copy in copies:
        copy.wait()


def state_kernel(direct, mine, q_pair, k_pair, v_pair, *refs):
    if direct:
        w, state, pair, to_a, to_b, to_c = refs
    else:
        state, pair, to_a, to_b = refs
    core, _, _ = places()
    own = core * DH
    for index, source in enumerate((q_pair, k_pair, v_pair)):
        for group in range(2):
            first = (3 * group + index) * DH
            pair[:, first : first + DH] = source[0, :, at(SOFT * group + own)]
    total = mm2(unit_plus(mine[:, KL].astype(F32)), mine[:, VL], TN) + mm2(
        unit_plus(pair[:, KL].astype(F32)), pair[:, VL], TN
    )
    state[...] = total
    way = links(direct)
    for out, block in ((to_a, way["block_a"]), (to_b, way["block_b"])):
        here = block == core
        out[:, :DH] = jnp.where(here, mine[:, KS], pair[:, KS])
        out[:, DH : 2 * DH] = jnp.where(here, mine[:, VS], pair[:, VS])
    if direct:
        rows = w.shape[0]
        for out, first in ((to_a, 2 * DH), (to_b, 2 * DH), (to_c, 0)):
            out[:, first : first + DH] = total.astype(BF)
            out[:rows, first + DH :] = w[:, :DH]
            out[rows:, first + DH :] = w[:, DH:]


def relay_kernel(w, a, b, c, keep, send, heads):
    core, z, _ = places()
    way = links(True)
    rows = w.shape[0]
    heads[z] = w[...]
    for source, first, step in ((a, 3 * DH, way["first"]), (b, 3 * DH, way["second"]), (c, DH, 2)):
        heads[z ^ step, :, :DH] = source[:rows, first:]
        heads[z ^ step, :, DH:] = source[rows:, first:]
    for group in range(2):
        keep[group] = heads[2 * group + core]
        send[group] = heads[2 * group + 1 - core]


def w_rows_kernel(keep, got, out):
    core, _, _ = places()
    half = keep.shape[1]
    for group in range(2):
        out[at(group * DH + core * half, half), :] = keep[group]
        out[at(group * DH + (1 - core) * half, half), :] = got[group]


def join_kernel(first, second, *refs):
    out = refs[-1]
    width = first.shape[1]
    out[:, :width] = first[...]
    out[:, width:] = second[...]


def weight_parts(direct, attn, ogs, send, keep):
    high, low = halves(attn)
    if not direct:
        keep[...] = mm(high, ogs[...], TN) + mm(low, ogs[...], TN)
        return
    _, _, dp = places()
    way = links(True)
    width = send.shape[1] // 2
    for index, step in enumerate((0, way["other"])):
        cols = slice(index * width, (index + 1) * width)
        near, far = at((dp ^ step) * width, width), at((dp ^ step ^ way["step"]) * width, width)
        keep[:, cols] = mm(high, ogs[:, near], TN) + mm(low, ogs[:, near], TN)
        send[:, cols] = (mm(high, ogs[:, far], TN) + mm(low, ogs[:, far], TN)).astype(BF)


def soft_forward_kernel(
    direct, mine, pair, og, og_recv, a, b, qs, ks, vs, ogs, probs, attn, keep, *send
):
    core, _, _ = places()
    way = links(direct)
    rows = og.shape[0]
    own_at, pair_at = core * rows, (1 - core) * rows
    for source, first in ((mine, own_at), (pair, pair_at)):
        qs[at(first, rows), :] = source[:, QS]
        ks[at(HALF + first, rows), :] = source[:, KS]
        vs[at(HALF + first, rows), :] = source[:, VS]
    for source, side in ((a, way["halo_a"]), (b, way["halo_b"])):
        first = side * (HALF + 2 * rows)
        ks[at(first), :] = source[:, :DH]
        vs[at(first), :] = source[:, DH : 2 * DH]
    ogs[at(own_at, rows), :] = og[...]
    ogs[at(pair_at, rows), :] = og_recv[...]
    span = rows + 2 * HALF
    row_pos = lax.broadcasted_iota(jnp.int32, (rows, span), 0)
    col_pos = lax.broadcasted_iota(jnp.int32, (rows, span), 1)
    inside = (col_pos >= row_pos) & (col_pos < row_pos + WINDOW)
    for block in range(2):
        here, window = slice(block * rows, (block + 1) * rows), slice(block * rows, block * rows + span)
        scores = mm(qs[here, :], ks[window, :], NT) * FACTOR
        scores = jnp.where(inside, scores, -1e30)
        peak = jnp.max(scores, axis=1, keepdims=True)
        terms = jnp.where(inside, jnp.exp(scores - peak), 0.0)
        share = terms / jnp.sum(terms, axis=1, keepdims=True)
        probs[block] = share
        attn[here, :] = mm(share.astype(BF), vs[window, :])
    weight_parts(direct, attn[...], ogs, send[0] if send else None, keep)


def lin_forward_kernel(direct, state, mine, pair, ogs, gain, *refs):
    core, _, _ = places()
    rows = mine.shape[0]
    total = state[...]
    if direct:
        a, b, c, soft_send, u_out, total_out, keep, out = refs
        total = total + a[:, 2 * DH : 3 * DH].astype(F32) + b[:, 2 * DH : 3 * DH].astype(F32)
        total = total + c[:, :DH].astype(F32)
    else:
        u_out, total_out, keep = refs
    total_out[...] = total
    u_out[at(core * rows, rows), :] = mm3(unit_plus(mine[:, QL].astype(F32)), total)
    u_out[at((1 - core) * rows, rows), :] = mm3(unit_plus(pair[:, QL].astype(F32)), total)
    u = u_out[...]
    r = lax.rsqrt(jnp.mean(u * u, axis=1, keepdims=True) + norm_eps)
    attn = gain[...] * u * r
    weight_parts(direct, attn, ogs, out.at[DH:, :] if direct else None, keep)
    if direct:
        out[:DH, :] = soft_send[...]


def fold_kernel(keep_soft, keep_lin, got, keep, send):
    width = keep.shape[1]
    for rows, source in ((slice(0, DH), keep_soft), (slice(DH, 2 * DH), keep_lin)):
        keep[rows, :] = source[:, :width] + got[rows, :width].astype(F32)
        send[rows, :] = (source[:, width:] + got[rows, width:].astype(F32)).astype(BF)


def rows_kernel(keep, got, own, send, total):
    core, _, _ = places()
    half = DH // 2
    total[...] = keep[...] + got[...].astype(F32)
    for group in range(2):
        out = slice(group * half, (group + 1) * half)
        own[out, :] = total[at(group * DH + core * half, half), :]
        send[out, :] = total[at(group * DH + (1 - core) * half, half), :]


def lin_backward(u, total, dattn, mine, pair, gain, dq_own, dq_pair, dstate, grads):
    core, _, _ = places()
    rows = mine.shape[0]
    u_all = u[...]
    r = lax.rsqrt(jnp.mean(u_all * u_all, axis=1, keepdims=True) + norm_eps)
    lin_grad = gain[...] * dattn[:, DH:]
    grads[...] = r * lin_grad - u_all * (r * r * r) * jnp.mean(lin_grad * u_all, axis=1, keepdims=True)
    total_state = total[...]
    result = jnp.zeros(dstate.shape, F32)
    for first, source, out in ((core * rows, mine, dq_own), ((1 - core) * rows, pair, dq_pair)):
        wide = source[:, QL].astype(F32)
        part = grads[at(first, rows), :]
        result = result + mm3(unit_plus(wide), part, TN)
        out[...] = (mm3(part, total_state, NT) * unit_slope(wide)).astype(BF)
    dstate[...] = result


def soft_backward(qs, ks, vs, probs, attn, dattn, dq_all, dk_all, dv_all):
    rows = qs.shape[0] // 2
    span = rows + 2 * HALF
    dk_all[...] = jnp.zeros_like(dk_all)
    dv_all[...] = jnp.zeros_like(dv_all)
    for block in range(2):
        here, window = slice(block * rows, (block + 1) * rows), slice(block * rows, block * rows + span)
        grad = dattn[here, :DH].astype(BF)
        share = probs[block]
        delta = jnp.sum(grad.astype(F32) * attn[here, :], axis=1, keepdims=True)
        dscore = (share * (mm(grad, vs[window, :], NT) - delta)).astype(BF)
        dq_all[here, :] = mm(dscore, ks[window, :]) * FACTOR
        dk_all[window, :] += mm(dscore, qs[here, :], TN) * FACTOR
        dv_all[window, :] += mm(share.astype(BF), grad, TN)


def backward_kernel(direct, *refs):
    if direct:
        sent, got = refs[:2]
        refs = refs[3:]
    else:
        weights = refs[0]
        refs = refs[1:]
    (ogs, u, total, mine, pair, gain, qs, ks, vs, probs, attn,
     dq_lin, dq_lin_pair, dstate, dq_soft, dk_soft, dv_soft, dattn, grads, *scratch) = refs
    if direct:
        _, _, dp = places()
        way = links(True)
        weights = scratch[0]
        width = weights.shape[1] // 4
        for source, index, step in (
            (sent, 0, 0), (sent, 1, way["step"]), (got, 0, way["other"]), (got, 1, 3),
        ):
            weights[:, at((dp ^ step) * width, width)] = source[:, index * width : (index + 1) * width]
    dattn[...] = mm(ogs[...], weights[...], NT)
    lin_backward(u, total, dattn, mine, pair, gain, dq_lin, dq_lin_pair, dstate, grads)
    soft_backward(qs, ks, vs, probs, attn, dattn, dq_soft, dk_soft, dv_soft)


def halo_part(out, first, dk_soft, dv_soft, side):
    start = side * (dk_soft.shape[0] - HALF)
    out[:, first : first + DH] = dk_soft[at(start), :].astype(BF)
    out[:, first + DH : first + 2 * DH] = dv_soft[at(start), :].astype(BF)


def halo_kernel(dk_soft, dv_soft, to_a, to_b):
    way = links(False)
    halo_part(to_a, 0, dk_soft, dv_soft, way["halo_a"])
    halo_part(to_b, 0, dk_soft, dv_soft, way["halo_b"])


def chunk_kernel(own, got, send, keep, heads):
    core, z, _ = places()
    way = links(True)
    half = own.shape[0] // 2
    for group in range(2):
        rows = slice(group * half, (group + 1) * half)
        heads[2 * group + core] = own[rows, :]
        heads[2 * group + 1 - core] = got[rows, :]
    for index, step in enumerate((way["first"], 2)):
        send[index * half : (index + 1) * half, :] = heads[z ^ step].astype(BF)
    for index, step in enumerate((0, way["second"])):
        keep[index * half : (index + 1) * half, :] = heads[z ^ step]


def second_kernel(keep, got, dstate, dk_soft, dv_soft, chunk, send):
    way = links(True)
    half = chunk.shape[0]
    chunk[...] = keep[:half, :] + got[:half, :].astype(F32)
    for side in range(2):
        cols, rows = slice(side * DH, (side + 1) * DH), slice(side * half, (side + 1) * half)
        piece = keep[half:, cols] + got[half:, cols].astype(F32)
        send[rows, 3 * DH :] = piece.astype(BF)
    halo_part(send, 0, dk_soft, dv_soft, way["halo_b"])
    send[:, 2 * DH : 3 * DH] = dstate[...].astype(BF)


def third_kernel(scale, chunk, got, dstate, dk_soft, dv_soft, summed, total, send):
    way = links(True)
    half = chunk.shape[0]
    for side in range(2):
        cols, rows = slice(side * DH, (side + 1) * DH), slice(side * half, (side + 1) * half)
        summed[:, cols] = (scale * (chunk[:, cols] + got[rows, 3 * DH :].astype(F32))).astype(summed.dtype)
    total[...] = dstate[...] + got[:, 2 * DH : 3 * DH].astype(F32)
    halo_part(send, 0, dk_soft, dv_soft, way["halo_a"])
    send[:, 2 * DH :] = total[...].astype(BF)


def final_kernel(
    direct, dstate, mine, pair, dq_soft, dk_soft, dv_soft, dq_lin, dq_lin_pair, a, b, *refs
):
    core, _, _ = places()
    way = links(direct)
    rows = mine.shape[0]
    total = dstate[...]
    own_out, pair_out, dk_all, dv_all = refs[-4:]
    if direct:
        total = total + a[:, 2 * DH :].astype(F32)
    for source, out, cols in ((dk_soft, dk_all, slice(0, DH)), (dv_soft, dv_all, slice(DH, 2 * DH))):
        out[...] = source[HALF : HALF + 2 * rows, :]
        out[at(way["block_a"] * rows, rows), :] += a[:, cols].astype(F32)
        out[at(way["block_b"] * rows, rows), :] += b[:, cols].astype(F32)
    high, low = halves(total)
    for source, dq, out, place in ((mine, dq_lin, own_out, core), (pair, dq_lin_pair, pair_out, 1 - core)):
        here = at(place * rows, rows)
        out[:, QS] = dq_soft[here, :].astype(BF)
        out[:, KS] = dk_all[here, :].astype(BF)
        out[:, VS] = dv_all[here, :].astype(BF)
        wide, values = source[:, KL].astype(F32), source[:, VL]
        out[:, QL] = dq[...]
        out[:, KL] = ((mm(values, high, NT) + mm(values, low, NT)) * unit_slope(wide)).astype(BF)
        out[:, VL] = mm3(unit_plus(wide), total).astype(BF)


def output_kernel(own, pair, dq, dk, dv):
    core, _, _ = places()
    for source, first in ((own, core * DH), (pair, (1 - core) * DH)):
        for index, out in enumerate((dq, dk, dv)):
            out[0, :, at(first)] = source[:, index * DH : (index + 1) * DH]
            out[0, :, at(SOFT + first)] = source[:, (3 + index) * DH : (4 + index) * DH]


def weight_join_kernel(both, got, _, out):
    _, _, dp = places()
    way = links(True)
    width = both.shape[1] // 2
    for source, index, step in ((both, 0, 0), (both, 1, way["step"]), (got, 0, way["other"]), (got, 1, 3)):
        out[:, at((dp ^ step) * width, width)] = source[:, index * width : (index + 1) * width].astype(F32)


def body(n_dp, n_z, queries, key_rows, value_rows, out_grad, out_weight, norm_gain):
    rows, model = out_grad.shape[1:]
    axes = ("z", "core")
    pair_perm = [(0, 1), (1, 0)]
    core = lax.axis_index("core")
    direct = n_z == HEADS and n_dp == 4
    width = model // n_dp
    half = DH // 2

    scale = 1.0 / math.sqrt(n_dp * n_z * 2 * rows)

    def over_core(value):
        return lax.ppermute(value, "core", pair_perm)

    def over_z(value, which, back=False):
        pairs = []
        for z in range(n_z):
            for c in range(2):
                if direct:
                    there = z ^ (1 + 2 * c, 3 - 2 * c, 2)[which]
                else:
                    there = (z + (1 if (which == 1) != back else -1)) % n_z
                pairs.append((2 * z + c, 2 * there + c))
        return lax.ppermute(value, axes, pairs)

    def over_dp(value, which):
        pairs = [
            (2 * d + c, 2 * (d ^ (1 + c, 2 - c)[which]) + c) for d in range(n_dp) for c in range(2)
        ]
        return lax.ppermute(value, ("dp", "core"), pairs)

    vmem = pl.BlockSpec(memory_space=pltpu.VMEM)

    def hbm(value):
        return pltpu.with_memory_space_constraint(value, pltpu.HBM)

    q_pair, k_pair, v_pair = over_core(queries), over_core(key_rows), over_core(value_rows)
    og_recv = over_core(out_grad[0])
    mine, og, w_part, gain = call(
        pack_kernel, "pack",
        [
            like((rows, 6 * DH), BF), like((rows, model), BF),
            like((out_weight.shape[0], width), BF), like((1, DH), F32),
        ],
        [hbm(x) for x in (queries, key_rows, value_rows, out_grad, out_weight, norm_gain)],
        scratch=[pltpu.SemaphoreType.DMA((9,))],
        spaces=[pl.BlockSpec(memory_space=pltpu.HBM)] * 6,
    )
    wide = 4 * DH if direct else 2 * DH
    state, pair, to_a, to_b, *rest = call(
        functools.partial(state_kernel, direct), "state",
        [like((DH, DH), F32), like((rows, 6 * DH), BF), like((rows, wide), BF), like((rows, wide), BF)]
        + [like((rows, 2 * DH), BF)] * direct,
        [mine, q_pair, k_pair, v_pair] + [w_part] * direct,
        flops=4 * 2 * rows * DH * DH,
    )
    if direct:
        a, b, c = over_z(to_a, 0), over_z(to_b, 1), [over_z(rest[0], 2)]
        w_keep, w_send = call(
            relay_kernel, "relay", [like((2, half, width), BF)] * 2, [w_part, a, b] + c,
            scratch=[pltpu.VMEM((HEADS, half, width), BF)],
        )
        w_own = call(
            w_rows_kernel, "w_rows", [like((2 * DH, width), BF)], [w_keep, over_core(w_send)]
        )[0]
        w_got = over_dp(w_own, 0)
    else:
        a, b, c = over_z(to_a, 0), over_z(to_b, 1), []
        state = lax.psum(state, "z")
        weights = lax.all_gather(out_weight, axes, axis=0, tiled=True).reshape(2, 2, DH, model)
        weights = [jnp.where(core == 0, weights[:, 0], weights[:, 1]).reshape(2 * DH, model)]

    span = 2 * rows + 2 * HALF
    keep_width = 2 * width if direct else model
    wg_flops = 2 * 2 * rows * DH * model
    qs, ks, vs, ogs, probs, attn, keep_soft, *soft_send = call(
        functools.partial(soft_forward_kernel, direct), "soft_forward",
        [
            like((2 * rows, DH), BF), like((span, DH), BF), like((span, DH), BF),
            like((2 * rows, model), BF), like((2, rows, rows + 2 * HALF), F32), like((2 * rows, DH), F32),
            like((DH, keep_width), F32),
        ] + [like((DH, 2 * width), BF)] * direct,
        [mine, pair, og, og_recv, a, b],
        flops=wg_flops,
    )
    u, total, keep_lin, *sent = call(
        functools.partial(lin_forward_kernel, direct), "lin_forward",
        [like((2 * rows, DH), F32), like((DH, DH), F32), like((DH, keep_width), F32)]
        + [like((2 * DH, 2 * width), BF)] * direct,
        [state, mine, pair, ogs, gain] + ([a, b] + c + soft_send if direct else []),
        flops=wg_flops,
    )
    if direct:
        got = over_dp(sent[0], 0)
        keep, sent = call(
            fold_kernel, "fold", [like((2 * DH, width), F32), like((2 * DH, width), BF)],
            [keep_soft, keep_lin, got],
        )
        w_half = call(
            join_kernel, "w_half", [like((2 * DH, 2 * width), BF)], [w_own, w_got, sent]
        )[0]
        weights = [w_half, over_dp(w_half, 1)]
        got = over_dp(sent, 1)
        row_own, row_send = call(
            rows_kernel, "rows", [like((2 * half, width), F32)] * 2, [keep, got],
            scratch=[pltpu.VMEM((2 * DH, width), F32)],
        )
        row_recv = over_core(row_send)
        piece_send, piece_keep = call(
            chunk_kernel, "chunk", [like((DH, width), BF), like((DH, width), F32)],
            [row_own, row_recv], scratch=[pltpu.VMEM((HEADS, half, width), F32)],
        )
        piece_got = over_z(piece_send, 0)
        weights.append(piece_keep)
    dq_lin, dq_lin_pair, dstate, dq_soft, dk_soft, dv_soft = call(
        functools.partial(backward_kernel, direct), "backward",
        [
            like((rows, DH), BF), like((rows, DH), BF), like((DH, DH), F32),
            like((2 * rows, DH), F32), like((span, DH), F32), like((span, DH), F32),
        ],
        weights + [ogs, u, total, mine, pair, gain, qs, ks, vs, probs, attn],
        scratch=[pltpu.VMEM((2 * rows, 2 * DH), F32), pltpu.VMEM((2 * rows, DH), F32)]
        + [pltpu.VMEM((2 * DH, model), BF)] * direct,
        flops=5 * wg_flops,
    )
    wide = 3 * DH if direct else 2 * DH
    if direct:
        chunk, to_b = call(
            second_kernel, "second", [like((half, width), F32), like((rows, 4 * DH), BF)],
            [piece_keep, piece_got, dstate, dk_soft, dv_soft],
        )
        b = over_z(to_b, 1)
        summed, dstate, to_a = call(
            functools.partial(third_kernel, scale), "third",
            [like((half, width), BF), like((DH, DH), F32), like((rows, 3 * DH), BF)],
            [chunk, b, dstate, dk_soft, dv_soft],
        )
        a = over_z(to_a, 0)
        got = over_dp(summed, 0)
        both = call(join_kernel, "both", [like((half, 2 * width), BF)], [summed, got])[0]
        gathered = over_dp(both, 1)
    else:
        to_a, to_b = call(halo_kernel, "halo", [like((rows, 2 * DH), BF)] * 2, [dk_soft, dv_soft])
        a, b = over_z(to_a, 0, True), over_z(to_b, 1, True)
    if not direct:
        dstate = lax.psum(dstate, "z")
        groups = jnp.stack([keep_soft, keep_lin])
        slots = jnp.stack([jnp.where(core == head, groups, 0.0) for head in range(2)], axis=1)
        local = lax.psum_scatter(
            slots.reshape(HEADS * DH, model), axes, scatter_dimension=0, tiled=True
        )
        weight_grad = lax.psum(local, "dp") * scale
    own_out, to_pair = call(
        functools.partial(final_kernel, direct), "final",
        [like((rows, 6 * DH), BF), like((rows, 6 * DH), BF)],
        [dstate, mine, pair, dq_soft, dk_soft, dv_soft, dq_lin, dq_lin_pair, a, b]
        + ([both] if direct else []),
        scratch=[pltpu.VMEM((2 * rows, DH), F32)] * 2,
        flops=wg_flops // 4,
    )
    from_pair = over_core(to_pair)
    shape = like((1, rows, HEADS * DH), BF)
    dq, dk, dv = call(output_kernel, "outputs", [shape] * 3, [own_out, from_pair])
    if direct:
        weight_grad = call(
            weight_join_kernel, "weight_join", [like((half, model), F32)], [both, gathered, hbm(dq)],
            spaces=[vmem, vmem, pl.BlockSpec(memory_space=pltpu.HBM)],
        )[0]
    return dq, dk, dv, weight_grad


def solution(mesh):
    n_dp, n_seq = mesh.shape["dp"], mesh.shape["seq"]
    blocks = Mesh(mesh.devices.reshape(n_dp, n_seq // 2, 2), ("dp", "z", "core"))
    tokens, heads = P("dp", ("z", "core"), None), P(("z", "core"), None)
    return jax.shard_map(
        functools.partial(body, n_dp, n_seq // 2),
        mesh=blocks,
        in_specs=(tokens, tokens, tokens, tokens, heads, P()),
        out_specs=(tokens, tokens, tokens, heads),
        check_vma=False,
    )
```

```python
import functools
import math

import jax
import jax.numpy as jnp
from jax import lax
from jax.experimental import pallas as pl
from jax.experimental.pallas import tpu as pltpu
from jax.sharding import Mesh
from jax.sharding import PartitionSpec as P

DH = 128
SOFT_HEADS = 2
LIN_HEADS = 2
HEADS = SOFT_HEADS + LIN_HEADS
WINDOW = 256
HALF = 128
norm_eps = 1e-06
FACTOR = DH ** (-0.5)
BF = jnp.bfloat16
F32 = jnp.float32
NN = (((1,), (0,)), ((), ()))
NT = (((1,), (1,)), ((), ()))
TN = (((0,), (0,)), ((), ()))


def unit_plus(values):
    return jnp.where(values > 0, values + 1.0, jnp.exp(jnp.minimum(values, 0.0)))


def unit_slope(values):
    return jnp.where(values > 0, 1.0, jnp.exp(jnp.minimum(values, 0.0)))


def mm(a, b, dims=NN):
    return lax.dot_general(a, b, dims, preferred_element_type=F32)


def halves(x):
    high = x.astype(BF)
    return high, (x - high.astype(F32)).astype(BF)


def mm3(a, b, dims=NN):
    a_high, a_low = halves(a)
    b_high, b_low = halves(b)
    return mm(a_high, b_high, dims) + (mm(a_high, b_low, dims) + mm(a_low, b_high, dims))


def mm2(a, b, dims=NN):
    a_high, a_low = halves(a)
    return mm(a_high, b, dims) + mm(a_low, b, dims)


def at(start, size=DH):
    return pl.ds(pl.multiple_of(start, size), size)


def places():
    return lax.axis_index("core"), lax.axis_index("z"), lax.axis_index("dp")


def call(kernel, name, outs, args, scratch=(), flops=0, spaces=None):
    vmem = pl.BlockSpec(memory_space=pltpu.VMEM)
    size = sum(math.prod(x.shape) * x.dtype.itemsize for x in list(args) + list(outs))
    return pl.pallas_call(
        kernel,
        name=name,
        out_shape=list(outs),
        in_specs=spaces or [vmem] * len(args),
        out_specs=[vmem] * len(outs),
        scratch_shapes=list(scratch),
        compiler_params=pltpu.CompilerParams(vmem_limit_bytes=24 * 2**20),
        cost_estimate=pl.CostEstimate(flops=flops, bytes_accessed=size, transcendentals=0),
    )(*args)


def like(shape, dtype):
    return jax.ShapeDtypeStruct(shape, dtype)


QS, KS, VS, QL, KL, VL = (slice(i * DH, (i + 1) * DH) for i in range(6))
SOFT = SOFT_HEADS * DH


def links(direct):
    core, z, dp = places()
    step = 1 + core
    turn = lax.rem(z + core, 2) if direct else 1
    return dict(
        first=1 + 2 * core, second=3 - 2 * core, step=step, other=3 - step,
        block_a=1 - turn, block_b=turn,
        halo_a=(1 - turn if direct else 1), halo_b=(turn if direct else 0),
    )


def pack_kernel(q, k, v, og, w, gain, mine_out, og_out, w_out, gain_out, sems):
    core, _, dp = places()
    mine = core * DH
    copies = []

    def fetch(source, target):
        copy = pltpu.make_async_copy(source, target, sems.at[len(copies)])
        copy.start()
        copies.append(copy)

    for index, array in enumerate((q, k, v)):
        for group in range(2):
            cols = slice((3 * group + index) * DH, (3 * group + index + 1) * DH)
            fetch(array.at[0, :, at(SOFT * group + mine)], mine_out.at[:, cols])
    width = w_out.shape[1]
    fetch(w.at[:, at(dp * width, width)], w_out)
    fetch(og.at[0], og_out)
    fetch(gain.at[at(mine)], gain_out.at[0])
    for copy in copies:
        copy.wait()


def state_kernel(direct, mine, q_pair, k_pair, v_pair, *refs):
    if direct:
        w, state, pair, to_a, to_b, to_c = refs
    else:
        state, pair, to_a, to_b = refs
    core, _, _ = places()
    own = core * DH
    for index, source in enumerate((q_pair, k_pair, v_pair)):
        for group in range(2):
            first = (3 * group + index) * DH
            pair[:, first : first + DH] = source[0, :, at(SOFT * group + own)]
    total = mm2(unit_plus(mine[:, KL].astype(F32)), mine[:, VL], TN) + mm2(
        unit_plus(pair[:, KL].astype(F32)), pair[:, VL], TN
    )
    state[...] = total
    way = links(direct)
    for out, block in ((to_a, way["block_a"]), (to_b, way["block_b"])):
        here = block == core
        out[:, :DH] = jnp.where(here, mine[:, KS], pair[:, KS])
        out[:, DH : 2 * DH] = jnp.where(here, mine[:, VS], pair[:, VS])
    if direct:
        rows = w.shape[0]
        for out, first in ((to_a, 2 * DH), (to_b, 2 * DH), (to_c, 0)):
            out[:, first : first + DH] = total.astype(BF)
            out[:rows, first + DH :] = w[:, :DH]
            out[rows:, first + DH :] = w[:, DH:]


def relay_kernel(w, a, b, c, keep, send, heads):
    core, z, _ = places()
    way = links(True)
    rows = w.shape[0]
    heads[z] = w[...]
    for source, first, step in ((a, 3 * DH, way["first"]), (b, 3 * DH, way["second"]), (c, DH, 2)):
        heads[z ^ step, :, :DH] = source[:rows, first:]
        heads[z ^ step, :, DH:] = source[rows:, first:]
    for group in range(2):
        keep[group] = heads[2 * group + core]
        send[group] = heads[2 * group + 1 - core]


def w_rows_kernel(keep, got, out):
    core, _, _ = places()
    half = keep.shape[1]
    for group in range(2):
        out[at(group * DH + core * half, half), :] = keep[group]
        out[at(group * DH + (1 - core) * half, half), :] = got[group]


def join_kernel(first, second, *refs):
    out = refs[-1]
    width = first.shape[1]
    out[:, :width] = first[...]
    out[:, width:] = second[...]


def weight_parts(direct, attn, ogs, send, keep):
    high, low = halves(attn)
    if not direct:
        keep[...] = mm(high, ogs[...], TN) + mm(low, ogs[...], TN)
        return
    _, _, dp = places()
    way = links(True)
    width = send.shape[1] // 2
    for index, step in enumerate((0, way["other"])):
        cols = slice(index * width, (index + 1) * width)
        near, far = at((dp ^ step) * width, width), at((dp ^ step ^ way["step"]) * width, width)
        keep[:, cols] = mm(high, ogs[:, near], TN) + mm(low, ogs[:, near], TN)
        send[:, cols] = (mm(high, ogs[:, far], TN) + mm(low, ogs[:, far], TN)).astype(BF)


def soft_forward_kernel(
    direct, mine, pair, og, og_recv, a, b, qs, ks, vs, ogs, probs, attn, keep, *send
):
    core, _, _ = places()
    way = links(direct)
    rows = og.shape[0]
    own_at, pair_at = core * rows, (1 - core) * rows
    for source, first in ((mine, own_at), (pair, pair_at)):
        qs[at(first, rows), :] = source[:, QS]
        ks[at(HALF + first, rows), :] = source[:, KS]
        vs[at(HALF + first, rows), :] = source[:, VS]
    for source, side in ((a, way["halo_a"]), (b, way["halo_b"])):
        first = side * (HALF + 2 * rows)
        ks[at(first), :] = source[:, :DH]
        vs[at(first), :] = source[:, DH : 2 * DH]
    ogs[at(own_at, rows), :] = og[...]
    ogs[at(pair_at, rows), :] = og_recv[...]
    span = rows + 2 * HALF
    row_pos = lax.broadcasted_iota(jnp.int32, (rows, span), 0)
    col_pos = lax.broadcasted_iota(jnp.int32, (rows, span), 1)
    inside = (col_pos >= row_pos) & (col_pos < row_pos + WINDOW)
    for block in range(2):
        here, window = slice(block * rows, (block + 1) * rows), slice(block * rows, block * rows + span)
        scores = mm(qs[here, :], ks[window, :], NT) * FACTOR
        scores = jnp.where(inside, scores, -1e30)
        peak = jnp.max(scores, axis=1, keepdims=True)
        terms = jnp.where(inside, jnp.exp(scores - peak), 0.0)
        share = terms / jnp.sum(terms, axis=1, keepdims=True)
        probs[block] = share
        attn[here, :] = mm(share.astype(BF), vs[window, :])
    weight_parts(direct, attn[...], ogs, send[0] if send else None, keep)


def lin_forward_kernel(direct, state, mine, pair, ogs, gain, *refs):
    core, _, _ = places()
    rows = mine.shape[0]
    total = state[...]
    if direct:
        a, b, c, soft_send, u_out, total_out, keep, out = refs
        total = total + a[:, 2 * DH : 3 * DH].astype(F32) + b[:, 2 * DH : 3 * DH].astype(F32)
        total = total + c[:, :DH].astype(F32)
    else:
        u_out, total_out, keep = refs
    total_out[...] = total
    u_out[at(core * rows, rows), :] = mm3(unit_plus(mine[:, QL].astype(F32)), total)
    u_out[at((1 - core) * rows, rows), :] = mm3(unit_plus(pair[:, QL].astype(F32)), total)
    u = u_out[...]
    r = lax.rsqrt(jnp.mean(u * u, axis=1, keepdims=True) + norm_eps)
    attn = gain[...] * u * r
    weight_parts(direct, attn, ogs, out.at[DH:, :] if direct else None, keep)
    if direct:
        out[:DH, :] = soft_send[...]


def fold_kernel(keep_soft, keep_lin, got, keep, send):
    width = keep.shape[1]
    for rows, source in ((slice(0, DH), keep_soft), (slice(DH, 2 * DH), keep_lin)):
        keep[rows, :] = source[:, :width] + got[rows, :width].astype(F32)
        send[rows, :] = (source[:, width:] + got[rows, width:].astype(F32)).astype(BF)


def rows_kernel(keep, got, own, send, total):
    core, _, _ = places()
    half = DH // 2
    total[...] = keep[...] + got[...].astype(F32)
    for group in range(2):
        out = slice(group * half, (group + 1) * half)
        own[out, :] = total[at(group * DH + core * half, half), :]
        send[out, :] = total[at(group * DH + (1 - core) * half, half), :]


def lin_backward(u, total, dattn, mine, pair, gain, dq_own, dq_pair, dstate, grads):
    core, _, _ = places()
    rows = mine.shape[0]
    u_all = u[...]
    r = lax.rsqrt(jnp.mean(u_all * u_all, axis=1, keepdims=True) + norm_eps)
    lin_grad = gain[...] * dattn[:, DH:]
    grads[...] = r * lin_grad - u_all * (r * r * r) * jnp.mean(lin_grad * u_all, axis=1, keepdims=True)
    total_state = total[...]
    result = jnp.zeros(dstate.shape, F32)
    for first, source, out in ((core * rows, mine, dq_own), ((1 - core) * rows, pair, dq_pair)):
        wide = source[:, QL].astype(F32)
        part = grads[at(first, rows), :]
        result = result + mm3(unit_plus(wide), part, TN)
        out[...] = (mm3(part, total_state, NT) * unit_slope(wide)).astype(BF)
    dstate[...] = result


def soft_backward(qs, ks, vs, probs, attn, dattn, dq_all, dk_all, dv_all):
    rows = qs.shape[0] // 2
    span = rows + 2 * HALF
    dk_all[...] = jnp.zeros_like(dk_all)
    dv_all[...] = jnp.zeros_like(dv_all)
    for block in range(2):
        here, window = slice(block * rows, (block + 1) * rows), slice(block * rows, block * rows + span)
        grad = dattn[here, :DH].astype(BF)
        share = probs[block]
        delta = jnp.sum(grad.astype(F32) * attn[here, :], axis=1, keepdims=True)
        dscore = (share * (mm(grad, vs[window, :], NT) - delta)).astype(BF)
        dq_all[here, :] = mm(dscore, ks[window, :]) * FACTOR
        dk_all[window, :] += mm(dscore, qs[here, :], TN) * FACTOR
        dv_all[window, :] += mm(share.astype(BF), grad, TN)


def backward_kernel(direct, *refs):
    if direct:
        sent, got = refs[:2]
        refs = refs[3:]
    else:
        weights = refs[0]
        refs = refs[1:]
    (ogs, u, total, mine, pair, gain, qs, ks, vs, probs, attn,
     dq_lin, dq_lin_pair, dstate, dq_soft, dk_soft, dv_soft, dattn, grads, *scratch) = refs
    if direct:
        _, _, dp = places()
        way = links(True)
        weights = scratch[0]
        width = weights.shape[1] // 4
        for source, index, step in (
            (sent, 0, 0), (sent, 1, way["step"]), (got, 0, way["other"]), (got, 1, 3),
        ):
            weights[:, at((dp ^ step) * width, width)] = source[:, index * width : (index + 1) * width]
    dattn[...] = mm(ogs[...], weights[...], NT)
    lin_backward(u, total, dattn, mine, pair, gain, dq_lin, dq_lin_pair, dstate, grads)
    soft_backward(qs, ks, vs, probs, attn, dattn, dq_soft, dk_soft, dv_soft)


def halo_part(out, first, dk_soft, dv_soft, side):
    start = side * (dk_soft.shape[0] - HALF)
    out[:, first : first + DH] = dk_soft[at(start), :].astype(BF)
    out[:, first + DH : first + 2 * DH] = dv_soft[at(start), :].astype(BF)


def halo_kernel(dk_soft, dv_soft, to_a, to_b):
    way = links(False)
    halo_part(to_a, 0, dk_soft, dv_soft, way["halo_a"])
    halo_part(to_b, 0, dk_soft, dv_soft, way["halo_b"])


def chunk_kernel(own, got, send, keep, heads):
    core, z, _ = places()
    way = links(True)
    half = own.shape[0] // 2
    for group in range(2):
        rows = slice(group * half, (group + 1) * half)
        heads[2 * group + core] = own[rows, :]
        heads[2 * group + 1 - core] = got[rows, :]
    for index, step in enumerate((way["first"], 2)):
        send[index * half : (index + 1) * half, :] = heads[z ^ step].astype(BF)
    for index, step in enumerate((0, way["second"])):
        keep[index * half : (index + 1) * half, :] = heads[z ^ step]


def second_kernel(keep, got, dstate, dk_soft, dv_soft, chunk, to_a, to_b, to_c):
    way = links(True)
    half = chunk.shape[0]
    chunk[...] = keep[:half, :] + got[:half, :].astype(F32)
    for side in range(2):
        cols, rows = slice(side * DH, (side + 1) * DH), slice(side * half, (side + 1) * half)
        piece = keep[half:, cols] + got[half:, cols].astype(F32)
        to_b[rows, 3 * DH :] = piece.astype(BF)
    halo_part(to_a, 0, dk_soft, dv_soft, way["halo_a"])
    halo_part(to_b, 0, dk_soft, dv_soft, way["halo_b"])
    low = dstate[...].astype(BF)
    to_a[:, 2 * DH :] = low
    to_b[:, 2 * DH : 3 * DH] = low
    to_c[...] = low


def weight_sum_kernel(scale, chunk, got, summed):
    half = chunk.shape[0]
    for side in range(2):
        cols, rows = slice(side * DH, (side + 1) * DH), slice(side * half, (side + 1) * half)
        summed[:, cols] = (scale * (chunk[:, cols] + got[rows, 3 * DH :].astype(F32))).astype(summed.dtype)


def final_kernel(
    direct, dstate, mine, pair, dq_soft, dk_soft, dv_soft, dq_lin, dq_lin_pair, a, b, *refs
):
    core, _, _ = places()
    way = links(direct)
    rows = mine.shape[0]
    total = dstate[...]
    own_out, pair_out, dk_all, dv_all = refs[-4:]
    if direct:
        total = total + a[:, 2 * DH :].astype(F32) + b[:, 2 * DH : 3 * DH].astype(F32)
        total = total + refs[0][...].astype(F32)
    for source, out, cols in ((dk_soft, dk_all, slice(0, DH)), (dv_soft, dv_all, slice(DH, 2 * DH))):
        out[...] = source[HALF : HALF + 2 * rows, :]
        out[at(way["block_a"] * rows, rows), :] += a[:, cols].astype(F32)
        out[at(way["block_b"] * rows, rows), :] += b[:, cols].astype(F32)
    high, low = halves(total)
    for source, dq, out, place in ((mine, dq_lin, own_out, core), (pair, dq_lin_pair, pair_out, 1 - core)):
        here = at(place * rows, rows)
        out[:, QS] = dq_soft[here, :].astype(BF)
        out[:, KS] = dk_all[here, :].astype(BF)
        out[:, VS] = dv_all[here, :].astype(BF)
        wide, values = source[:, KL].astype(F32), source[:, VL]
        out[:, QL] = dq[...]
        out[:, KL] = ((mm(values, high, NT) + mm(values, low, NT)) * unit_slope(wide)).astype(BF)
        out[:, VL] = mm3(unit_plus(wide), total).astype(BF)


def output_kernel(own, pair, dq, dk, dv):
    core, _, _ = places()
    for source, first in ((own, core * DH), (pair, (1 - core) * DH)):
        for index, out in enumerate((dq, dk, dv)):
            out[0, :, at(first)] = source[:, index * DH : (index + 1) * DH]
            out[0, :, at(SOFT + first)] = source[:, (3 + index) * DH : (4 + index) * DH]


def weight_join_kernel(both, got, _, out):
    _, _, dp = places()
    way = links(True)
    width = both.shape[1] // 2
    for source, index, step in ((both, 0, 0), (both, 1, way["step"]), (got, 0, way["other"]), (got, 1, 3)):
        out[:, at((dp ^ step) * width, width)] = source[:, index * width : (index + 1) * width].astype(F32)


def body(n_dp, n_z, queries, key_rows, value_rows, out_grad, out_weight, norm_gain):
    rows, model = out_grad.shape[1:]
    axes = ("z", "core")
    pair_perm = [(0, 1), (1, 0)]
    core = lax.axis_index("core")
    direct = n_z == HEADS and n_dp == 4
    width = model // n_dp
    half = DH // 2

    scale = 1.0 / math.sqrt(n_dp * n_z * 2 * rows)

    def over_core(value):
        return lax.ppermute(value, "core", pair_perm)

    def over_z(value, which, back=False):
        pairs = []
        for z in range(n_z):
            for c in range(2):
                if direct:
                    there = z ^ (1 + 2 * c, 3 - 2 * c, 2)[which]
                else:
                    there = (z + (1 if (which == 1) != back else -1)) % n_z
                pairs.append((2 * z + c, 2 * there + c))
        return lax.ppermute(value, axes, pairs)

    def over_dp(value, which):
        pairs = [
            (2 * d + c, 2 * (d ^ (1 + c, 2 - c)[which]) + c) for d in range(n_dp) for c in range(2)
        ]
        return lax.ppermute(value, ("dp", "core"), pairs)

    vmem = pl.BlockSpec(memory_space=pltpu.VMEM)

    def hbm(value):
        return pltpu.with_memory_space_constraint(value, pltpu.HBM)

    q_pair, k_pair, v_pair = over_core(queries), over_core(key_rows), over_core(value_rows)
    og_recv = over_core(out_grad[0])
    mine, og, w_part, gain = call(
        pack_kernel, "pack",
        [
            like((rows, 6 * DH), BF), like((rows, model), BF),
            like((out_weight.shape[0], width), BF), like((1, DH), F32),
        ],
        [hbm(x) for x in (queries, key_rows, value_rows, out_grad, out_weight, norm_gain)],
        scratch=[pltpu.SemaphoreType.DMA((9,))],
        spaces=[pl.BlockSpec(memory_space=pltpu.HBM)] * 6,
    )
    wide = 4 * DH if direct else 2 * DH
    state, pair, to_a, to_b, *rest = call(
        functools.partial(state_kernel, direct), "state",
        [like((DH, DH), F32), like((rows, 6 * DH), BF), like((rows, wide), BF), like((rows, wide), BF)]
        + [like((rows, 2 * DH), BF)] * direct,
        [mine, q_pair, k_pair, v_pair] + [w_part] * direct,
        flops=4 * 2 * rows * DH * DH,
    )
    if direct:
        a, b, c = over_z(to_a, 0), over_z(to_b, 1), [over_z(rest[0], 2)]
        w_keep, w_send = call(
            relay_kernel, "relay", [like((2, half, width), BF)] * 2, [w_part, a, b] + c,
            scratch=[pltpu.VMEM((HEADS, half, width), BF)],
        )
        w_own = call(
            w_rows_kernel, "w_rows", [like((2 * DH, width), BF)], [w_keep, over_core(w_send)]
        )[0]
        w_got = over_dp(w_own, 0)
    else:
        a, b, c = over_z(to_a, 0), over_z(to_b, 1), []
        state = lax.psum(state, "z")
        weights = lax.all_gather(out_weight, axes, axis=0, tiled=True).reshape(2, 2, DH, model)
        weights = [jnp.where(core == 0, weights[:, 0], weights[:, 1]).reshape(2 * DH, model)]

    span = 2 * rows + 2 * HALF
    keep_width = 2 * width if direct else model
    wg_flops = 2 * 2 * rows * DH * model
    qs, ks, vs, ogs, probs, attn, keep_soft, *soft_send = call(
        functools.partial(soft_forward_kernel, direct), "soft_forward",
        [
            like((2 * rows, DH), BF), like((span, DH), BF), like((span, DH), BF),
            like((2 * rows, model), BF), like((2, rows, rows + 2 * HALF), F32), like((2 * rows, DH), F32),
            like((DH, keep_width), F32),
        ] + [like((DH, 2 * width), BF)] * direct,
        [mine, pair, og, og_recv, a, b],
        flops=wg_flops,
    )
    u, total, keep_lin, *sent = call(
        functools.partial(lin_forward_kernel, direct), "lin_forward",
        [like((2 * rows, DH), F32), like((DH, DH), F32), like((DH, keep_width), F32)]
        + [like((2 * DH, 2 * width), BF)] * direct,
        [state, mine, pair, ogs, gain] + ([a, b] + c + soft_send if direct else []),
        flops=wg_flops,
    )
    if direct:
        got = over_dp(sent[0], 0)
        keep, sent = call(
            fold_kernel, "fold", [like((2 * DH, width), F32), like((2 * DH, width), BF)],
            [keep_soft, keep_lin, got],
        )
        w_half = call(
            join_kernel, "w_half", [like((2 * DH, 2 * width), BF)], [w_own, w_got, sent]
        )[0]
        weights = [w_half, over_dp(w_half, 1)]
        got = over_dp(sent, 1)
        row_own, row_send = call(
            rows_kernel, "rows", [like((2 * half, width), F32)] * 2, [keep, got],
            scratch=[pltpu.VMEM((2 * DH, width), F32)],
        )
        row_recv = over_core(row_send)
        piece_send, piece_keep = call(
            chunk_kernel, "chunk", [like((DH, width), BF), like((DH, width), F32)],
            [row_own, row_recv], scratch=[pltpu.VMEM((HEADS, half, width), F32)],
        )
        piece_got = over_z(piece_send, 0)
        weights.append(piece_keep)
    dq_lin, dq_lin_pair, dstate, dq_soft, dk_soft, dv_soft = call(
        functools.partial(backward_kernel, direct), "backward",
        [
            like((rows, DH), BF), like((rows, DH), BF), like((DH, DH), F32),
            like((2 * rows, DH), F32), like((span, DH), F32), like((span, DH), F32),
        ],
        weights + [ogs, u, total, mine, pair, gain, qs, ks, vs, probs, attn],
        scratch=[pltpu.VMEM((2 * rows, 2 * DH), F32), pltpu.VMEM((2 * rows, DH), F32)]
        + [pltpu.VMEM((2 * DH, model), BF)] * direct,
        flops=5 * wg_flops,
    )
    wide = 3 * DH if direct else 2 * DH
    if direct:
        chunk, to_a, to_b, to_c = call(
            second_kernel, "second",
            [
                like((half, width), F32), like((rows, 3 * DH), BF), like((rows, 4 * DH), BF),
                like((DH, DH), BF),
            ],
            [piece_keep, piece_got, dstate, dk_soft, dv_soft],
        )
        b, a, c = over_z(to_b, 1), over_z(to_a, 0), [over_z(to_c, 2)]
        summed = call(
            functools.partial(weight_sum_kernel, scale), "weight_sum", [like((half, width), BF)],
            [chunk, b],
        )[0]
        got = over_dp(summed, 0)
        both = call(join_kernel, "both", [like((half, 2 * width), BF)], [summed, got])[0]
        gathered = over_dp(both, 1)
    else:
        to_a, to_b = call(halo_kernel, "halo", [like((rows, 2 * DH), BF)] * 2, [dk_soft, dv_soft])
        a, b = over_z(to_a, 0, True), over_z(to_b, 1, True)
    if not direct:
        dstate = lax.psum(dstate, "z")
        groups = jnp.stack([keep_soft, keep_lin])
        slots = jnp.stack([jnp.where(core == head, groups, 0.0) for head in range(2)], axis=1)
        local = lax.psum_scatter(
            slots.reshape(HEADS * DH, model), axes, scatter_dimension=0, tiled=True
        )
        weight_grad = lax.psum(local, "dp") * scale
    own_out, to_pair = call(
        functools.partial(final_kernel, direct), "final",
        [like((rows, 6 * DH), BF), like((rows, 6 * DH), BF)],
        [dstate, mine, pair, dq_soft, dk_soft, dv_soft, dq_lin, dq_lin_pair, a, b]
        + (c if direct else []),
        scratch=[pltpu.VMEM((2 * rows, DH), F32)] * 2,
        flops=wg_flops // 4,
    )
    from_pair = over_core(to_pair)
    shape = like((1, rows, HEADS * DH), BF)
    dq, dk, dv = call(output_kernel, "outputs", [shape] * 3, [own_out, from_pair])
    if direct:
        weight_grad = call(
            weight_join_kernel, "weight_join", [like((half, model), F32)], [both, gathered, hbm(dq)],
            spaces=[vmem, vmem, pl.BlockSpec(memory_space=pltpu.HBM)],
        )[0]
    return dq, dk, dv, weight_grad


def solution(mesh):
    n_dp, n_seq = mesh.shape["dp"], mesh.shape["seq"]
    blocks = Mesh(mesh.devices.reshape(n_dp, n_seq // 2, 2), ("dp", "z", "core"))
    tokens, heads = P("dp", ("z", "core"), None), P(("z", "core"), None)
    return jax.shard_map(
        functools.partial(body, n_dp, n_seq // 2),
        mesh=blocks,
        in_specs=(tokens, tokens, tokens, tokens, heads, P()),
        out_specs=(tokens, tokens, tokens, heads),
        check_vma=False,
    )
```

```python
import functools
import math

import jax
import jax.numpy as jnp
from jax import lax
from jax.experimental import pallas as pl
from jax.experimental.pallas import tpu as pltpu
from jax.sharding import Mesh
from jax.sharding import PartitionSpec as P

DH = 128
SOFT_HEADS = 2
LIN_HEADS = 2
HEADS = SOFT_HEADS + LIN_HEADS
WINDOW = 256
HALF = 128
norm_eps = 1e-06
FACTOR = DH ** (-0.5)
BF = jnp.bfloat16
F32 = jnp.float32
NN = (((1,), (0,)), ((), ()))
NT = (((1,), (1,)), ((), ()))
TN = (((0,), (0,)), ((), ()))


def unit_plus(values):
    return jnp.where(values > 0, values + 1.0, jnp.exp(jnp.minimum(values, 0.0)))


def unit_slope(values):
    return jnp.where(values > 0, 1.0, jnp.exp(jnp.minimum(values, 0.0)))


def mm(a, b, dims=NN):
    return lax.dot_general(a, b, dims, preferred_element_type=F32)


def halves(x):
    high = x.astype(BF)
    return high, (x - high.astype(F32)).astype(BF)


def mm3(a, b, dims=NN):
    a_high, a_low = halves(a)
    b_high, b_low = halves(b)
    return mm(a_high, b_high, dims) + (mm(a_high, b_low, dims) + mm(a_low, b_high, dims))


def mm2(a, b, dims=NN):
    a_high, a_low = halves(a)
    return mm(a_high, b, dims) + mm(a_low, b, dims)


def at(start, size=DH):
    return pl.ds(pl.multiple_of(start, size), size)


def places():
    return lax.axis_index("core"), lax.axis_index("z"), lax.axis_index("dp")


def call(kernel, name, outs, args, scratch=(), flops=0, spaces=None):
    vmem = pl.BlockSpec(memory_space=pltpu.VMEM)
    size = sum(math.prod(x.shape) * x.dtype.itemsize for x in list(args) + list(outs))
    return pl.pallas_call(
        kernel,
        name=name,
        out_shape=list(outs),
        in_specs=spaces or [vmem] * len(args),
        out_specs=[vmem] * len(outs),
        scratch_shapes=list(scratch),
        compiler_params=pltpu.CompilerParams(vmem_limit_bytes=24 * 2**20),
        cost_estimate=pl.CostEstimate(flops=flops, bytes_accessed=size, transcendentals=0),
    )(*args)


def like(shape, dtype):
    return jax.ShapeDtypeStruct(shape, dtype)


QS, KS, VS, QL, KL, VL = (slice(i * DH, (i + 1) * DH) for i in range(6))
SOFT = SOFT_HEADS * DH


def links(direct):
    core, z, dp = places()
    step = 1 + core
    turn = lax.rem(z + core, 2) if direct else 1
    return dict(
        first=1 + 2 * core, second=3 - 2 * core, step=step, other=3 - step,
        block_a=1 - turn, block_b=turn,
        halo_a=(1 - turn if direct else 1), halo_b=(turn if direct else 0),
    )


def pack_kernel(q, k, v, og, w, gain, mine_out, og_out, w_out, gain_out, sems):
    core, _, dp = places()
    mine = core * DH
    copies = []

    def fetch(source, target):
        copy = pltpu.make_async_copy(source, target, sems.at[len(copies)])
        copy.start()
        copies.append(copy)

    for index, array in enumerate((q, k, v)):
        for group in range(2):
            cols = slice((3 * group + index) * DH, (3 * group + index + 1) * DH)
            fetch(array.at[0, :, at(SOFT * group + mine)], mine_out.at[:, cols])
    width = w_out.shape[1]
    fetch(w.at[:, at(dp * width, width)], w_out)
    fetch(og.at[0], og_out)
    fetch(gain.at[at(mine)], gain_out.at[0])
    for copy in copies:
        copy.wait()


def state_kernel(direct, mine, q_pair, k_pair, v_pair, *refs):
    if direct:
        w, state, pair, to_a, to_b, to_c = refs
    else:
        state, pair, to_a, to_b = refs
    core, _, _ = places()
    own = core * DH
    for index, source in enumerate((q_pair, k_pair, v_pair)):
        for group in range(2):
            first = (3 * group + index) * DH
            pair[:, first : first + DH] = source[0, :, at(SOFT * group + own)]
    total = mm2(unit_plus(mine[:, KL].astype(F32)), mine[:, VL], TN) + mm2(
        unit_plus(pair[:, KL].astype(F32)), pair[:, VL], TN
    )
    state[...] = total
    way = links(direct)
    for out, block in ((to_a, way["block_a"]), (to_b, way["block_b"])):
        here = block == core
        out[:, :DH] = jnp.where(here, mine[:, KS], pair[:, KS])
        out[:, DH : 2 * DH] = jnp.where(here, mine[:, VS], pair[:, VS])
    if direct:
        rows = w.shape[0]
        for out, first in ((to_a, 2 * DH), (to_b, 2 * DH), (to_c, 0)):
            out[:, first : first + DH] = total.astype(BF)
            out[:rows, first + DH :] = w[:, :DH]
            out[rows:, first + DH :] = w[:, DH:]


def relay_kernel(w, a, b, c, keep, send, heads):
    core, z, _ = places()
    way = links(True)
    rows = w.shape[0]
    heads[z] = w[...]
    for source, first, step in ((a, 3 * DH, way["first"]), (b, 3 * DH, way["second"]), (c, DH, 2)):
        heads[z ^ step, :, :DH] = source[:rows, first:]
        heads[z ^ step, :, DH:] = source[rows:, first:]
    for group in range(2):
        keep[group] = heads[2 * group + core]
        send[group] = heads[2 * group + 1 - core]


def w_rows_kernel(keep, got, out):
    core, _, _ = places()
    half = keep.shape[1]
    for group in range(2):
        out[at(group * DH + core * half, half), :] = keep[group]
        out[at(group * DH + (1 - core) * half, half), :] = got[group]


def join_kernel(first, second, *refs):
    out = refs[-1]
    width = first.shape[1]
    out[:, :width] = first[...]
    out[:, width:] = second[...]


def weight_parts(direct, attn, ogs, send, keep):
    high, low = halves(attn)
    if not direct:
        keep[...] = mm(high, ogs[...], TN) + mm(low, ogs[...], TN)
        return
    _, _, dp = places()
    way = links(True)
    width = send.shape[1] // 2
    for index, step in enumerate((0, way["other"])):
        cols = slice(index * width, (index + 1) * width)
        near, far = at((dp ^ step) * width, width), at((dp ^ step ^ way["step"]) * width, width)
        keep[:, cols] = mm(high, ogs[:, near], TN) + mm(low, ogs[:, near], TN)
        send[:, cols] = (mm(high, ogs[:, far], TN) + mm(low, ogs[:, far], TN)).astype(BF)


def soft_forward_kernel(
    direct, mine, pair, og, og_recv, a, b, qs, ks, vs, ogs, probs, attn, keep, *send
):
    core, _, _ = places()
    way = links(direct)
    rows = og.shape[0]
    own_at, pair_at = core * rows, (1 - core) * rows
    for source, first in ((mine, own_at), (pair, pair_at)):
        qs[at(first, rows), :] = source[:, QS]
        ks[at(HALF + first, rows), :] = source[:, KS]
        vs[at(HALF + first, rows), :] = source[:, VS]
    for source, side in ((a, way["halo_a"]), (b, way["halo_b"])):
        first = side * (HALF + 2 * rows)
        ks[at(first), :] = source[:, :DH]
        vs[at(first), :] = source[:, DH : 2 * DH]
    ogs[at(own_at, rows), :] = og[...]
    ogs[at(pair_at, rows), :] = og_recv[...]
    span = rows + 2 * HALF
    row_pos = lax.broadcasted_iota(jnp.int32, (rows, span), 0)
    col_pos = lax.broadcasted_iota(jnp.int32, (rows, span), 1)
    inside = (col_pos >= row_pos) & (col_pos < row_pos + WINDOW)
    for block in range(2):
        here, window = slice(block * rows, (block + 1) * rows), slice(block * rows, block * rows + span)
        scores = mm(qs[here, :], ks[window, :], NT) * FACTOR
        scores = jnp.where(inside, scores, -1e30)
        peak = jnp.max(scores, axis=1, keepdims=True)
        terms = jnp.where(inside, jnp.exp(scores - peak), 0.0)
        share = terms / jnp.sum(terms, axis=1, keepdims=True)
        probs[block] = share
        attn[here, :] = mm(share.astype(BF), vs[window, :])
    weight_parts(direct, attn[...], ogs, send[0] if send else None, keep)


def lin_forward_kernel(direct, state, mine, pair, ogs, gain, *refs):
    core, _, _ = places()
    rows = mine.shape[0]
    total = state[...]
    if direct:
        a, b, c, soft_send, u_out, total_out, keep, out = refs
        total = total + a[:, 2 * DH : 3 * DH].astype(F32) + b[:, 2 * DH : 3 * DH].astype(F32)
        total = total + c[:, :DH].astype(F32)
    else:
        u_out, total_out, keep = refs
    total_out[...] = total
    u_out[at(core * rows, rows), :] = mm3(unit_plus(mine[:, QL].astype(F32)), total)
    u_out[at((1 - core) * rows, rows), :] = mm3(unit_plus(pair[:, QL].astype(F32)), total)
    u = u_out[...]
    r = lax.rsqrt(jnp.mean(u * u, axis=1, keepdims=True) + norm_eps)
    attn = gain[...] * u * r
    weight_parts(direct, attn, ogs, out.at[DH:, :] if direct else None, keep)
    if direct:
        out[:DH, :] = soft_send[...]


def fold_kernel(keep_soft, keep_lin, got, keep, send):
    width = keep.shape[1]
    for rows, source in ((slice(0, DH), keep_soft), (slice(DH, 2 * DH), keep_lin)):
        keep[rows, :] = source[:, :width] + got[rows, :width].astype(F32)
        send[rows, :] = (source[:, width:] + got[rows, width:].astype(F32)).astype(BF)


def rows_kernel(keep, got, own, send, total):
    core, _, _ = places()
    half = DH // 2
    total[...] = keep[...] + got[...].astype(F32)
    for group in range(2):
        out = slice(group * half, (group + 1) * half)
        own[out, :] = total[at(group * DH + core * half, half), :]
        send[out, :] = total[at(group * DH + (1 - core) * half, half), :]


def lin_backward(u, total, dattn, mine, pair, gain, dq_own, dq_pair, dstate, grads):
    core, _, _ = places()
    rows = mine.shape[0]
    u_all = u[...]
    r = lax.rsqrt(jnp.mean(u_all * u_all, axis=1, keepdims=True) + norm_eps)
    lin_grad = gain[...] * dattn[:, DH:]
    grads[...] = r * lin_grad - u_all * (r * r * r) * jnp.mean(lin_grad * u_all, axis=1, keepdims=True)
    total_state = total[...]
    result = jnp.zeros(dstate.shape, F32)
    for first, source, out in ((core * rows, mine, dq_own), ((1 - core) * rows, pair, dq_pair)):
        wide = source[:, QL].astype(F32)
        part = grads[at(first, rows), :]
        result = result + mm3(unit_plus(wide), part, TN)
        out[...] = (mm3(part, total_state, NT) * unit_slope(wide)).astype(BF)
    dstate[...] = result


def soft_backward(qs, ks, vs, probs, attn, dattn, dq_all, dk_all, dv_all):
    rows = qs.shape[0] // 2
    span = rows + 2 * HALF
    dk_all[...] = jnp.zeros_like(dk_all)
    dv_all[...] = jnp.zeros_like(dv_all)
    for block in range(2):
        here, window = slice(block * rows, (block + 1) * rows), slice(block * rows, block * rows + span)
        grad = dattn[here, :DH].astype(BF)
        share = probs[block]
        delta = jnp.sum(grad.astype(F32) * attn[here, :], axis=1, keepdims=True)
        dscore = (share * (mm(grad, vs[window, :], NT) - delta)).astype(BF)
        dq_all[here, :] = mm(dscore, ks[window, :]) * FACTOR
        dk_all[window, :] += mm(dscore, qs[here, :], TN) * FACTOR
        dv_all[window, :] += mm(share.astype(BF), grad, TN)


def backward_kernel(direct, *refs):
    if direct:
        sent, got = refs[:2]
        refs = refs[3:]
    else:
        weights = refs[0]
        refs = refs[1:]
    (ogs, u, total, mine, pair, gain, qs, ks, vs, probs, attn,
     dq_lin, dq_lin_pair, dstate, dq_soft, dk_soft, dv_soft, dattn, grads, *scratch) = refs
    if direct:
        _, _, dp = places()
        way = links(True)
        weights = scratch[0]
        width = weights.shape[1] // 4
        for source, index, step in (
            (sent, 0, 0), (sent, 1, way["step"]), (got, 0, way["other"]), (got, 1, 3),
        ):
            weights[:, at((dp ^ step) * width, width)] = source[:, index * width : (index + 1) * width]
    dattn[...] = mm(ogs[...], weights[...], NT)
    lin_backward(u, total, dattn, mine, pair, gain, dq_lin, dq_lin_pair, dstate, grads)
    soft_backward(qs, ks, vs, probs, attn, dattn, dq_soft, dk_soft, dv_soft)


def halo_part(out, first, dk_soft, dv_soft, side):
    start = side * (dk_soft.shape[0] - HALF)
    out[:, first : first + DH] = dk_soft[at(start), :].astype(BF)
    out[:, first + DH : first + 2 * DH] = dv_soft[at(start), :].astype(BF)


def halo_kernel(dk_soft, dv_soft, to_a, to_b):
    way = links(False)
    halo_part(to_a, 0, dk_soft, dv_soft, way["halo_a"])
    halo_part(to_b, 0, dk_soft, dv_soft, way["halo_b"])


def chunk_kernel(own, got, send, keep, heads):
    core, z, _ = places()
    way = links(True)
    half = own.shape[0] // 2
    for group in range(2):
        rows = slice(group * half, (group + 1) * half)
        heads[2 * group + core] = own[rows, :]
        heads[2 * group + 1 - core] = got[rows, :]
    for index, step in enumerate((way["first"], way["second"])):
        send[index * half : (index + 1) * half, :] = heads[z ^ step].astype(BF)
    for index, step in enumerate((0, 2)):
        keep[index * half : (index + 1) * half, :] = heads[z ^ step]


def second_kernel(keep, got, dstate, dk_soft, dv_soft, chunk, to_a, to_b, to_c):
    way = links(True)
    half = chunk.shape[0]
    chunk[...] = keep[:half, :] + got[:half, :].astype(F32)
    for side in range(2):
        cols, rows = slice(side * DH, (side + 1) * DH), slice(side * half, (side + 1) * half)
        piece = keep[half:, cols] + got[half:, cols].astype(F32)
        to_c[rows, DH:] = piece.astype(BF)
    halo_part(to_a, 0, dk_soft, dv_soft, way["halo_a"])
    halo_part(to_b, 0, dk_soft, dv_soft, way["halo_b"])
    low = dstate[...].astype(BF)
    to_a[:, 2 * DH :] = low
    to_b[:, 2 * DH :] = low
    to_c[:, :DH] = low


def weight_sum_kernel(scale, chunk, got, summed):
    half = chunk.shape[0]
    for side in range(2):
        cols, rows = slice(side * DH, (side + 1) * DH), slice(side * half, (side + 1) * half)
        summed[:, cols] = (scale * (chunk[:, cols] + got[rows, DH:].astype(F32))).astype(summed.dtype)


def final_kernel(
    direct, dstate, mine, pair, dq_soft, dk_soft, dv_soft, dq_lin, dq_lin_pair, a, b, *refs
):
    core, _, _ = places()
    way = links(direct)
    rows = mine.shape[0]
    total = dstate[...]
    own_out, pair_out, dk_all, dv_all = refs[-4:]
    if direct:
        total = total + a[:, 2 * DH :].astype(F32) + b[:, 2 * DH :].astype(F32)
        total = total + refs[0][:, :DH].astype(F32)
    for source, out, cols in ((dk_soft, dk_all, slice(0, DH)), (dv_soft, dv_all, slice(DH, 2 * DH))):
        out[...] = source[HALF : HALF + 2 * rows, :]
        out[at(way["block_a"] * rows, rows), :] += a[:, cols].astype(F32)
        out[at(way["block_b"] * rows, rows), :] += b[:, cols].astype(F32)
    high, low = halves(total)
    for source, dq, out, place in ((mine, dq_lin, own_out, core), (pair, dq_lin_pair, pair_out, 1 - core)):
        here = at(place * rows, rows)
        out[:, QS] = dq_soft[here, :].astype(BF)
        out[:, KS] = dk_all[here, :].astype(BF)
        out[:, VS] = dv_all[here, :].astype(BF)
        wide, values = source[:, KL].astype(F32), source[:, VL]
        out[:, QL] = dq[...]
        out[:, KL] = ((mm(values, high, NT) + mm(values, low, NT)) * unit_slope(wide)).astype(BF)
        out[:, VL] = mm3(unit_plus(wide), total).astype(BF)


def output_kernel(own, pair, dq, dk, dv):
    core, _, _ = places()
    for source, first in ((own, core * DH), (pair, (1 - core) * DH)):
        for index, out in enumerate((dq, dk, dv)):
            out[0, :, at(first)] = source[:, index * DH : (index + 1) * DH]
            out[0, :, at(SOFT + first)] = source[:, (3 + index) * DH : (4 + index) * DH]


def weight_join_kernel(both, got, _, out):
    _, _, dp = places()
    way = links(True)
    width = both.shape[1] // 2
    for source, index, step in ((both, 0, 0), (both, 1, way["step"]), (got, 0, way["other"]), (got, 1, 3)):
        out[:, at((dp ^ step) * width, width)] = source[:, index * width : (index + 1) * width].astype(F32)


def body(n_dp, n_z, queries, key_rows, value_rows, out_grad, out_weight, norm_gain):
    rows, model = out_grad.shape[1:]
    axes = ("z", "core")
    pair_perm = [(0, 1), (1, 0)]
    core = lax.axis_index("core")
    direct = n_z == HEADS and n_dp == 4
    width = model // n_dp
    half = DH // 2

    scale = 1.0 / math.sqrt(n_dp * n_z * 2 * rows)

    def over_core(value):
        return lax.ppermute(value, "core", pair_perm)

    def over_z(value, which, back=False):
        pairs = []
        for z in range(n_z):
            for c in range(2):
                if direct:
                    there = z ^ (1 + 2 * c, 3 - 2 * c, 2)[which]
                else:
                    there = (z + (1 if (which == 1) != back else -1)) % n_z
                pairs.append((2 * z + c, 2 * there + c))
        return lax.ppermute(value, axes, pairs)

    def over_dp(value, which):
        pairs = [
            (2 * d + c, 2 * (d ^ (1 + c, 2 - c)[which]) + c) for d in range(n_dp) for c in range(2)
        ]
        return lax.ppermute(value, ("dp", "core"), pairs)

    vmem = pl.BlockSpec(memory_space=pltpu.VMEM)

    def hbm(value):
        return pltpu.with_memory_space_constraint(value, pltpu.HBM)

    q_pair, k_pair, v_pair = over_core(queries), over_core(key_rows), over_core(value_rows)
    og_recv = over_core(out_grad[0])
    mine, og, w_part, gain = call(
        pack_kernel, "pack",
        [
            like((rows, 6 * DH), BF), like((rows, model), BF),
            like((out_weight.shape[0], width), BF), like((1, DH), F32),
        ],
        [hbm(x) for x in (queries, key_rows, value_rows, out_grad, out_weight, norm_gain)],
        scratch=[pltpu.SemaphoreType.DMA((9,))],
        spaces=[pl.BlockSpec(memory_space=pltpu.HBM)] * 6,
    )
    wide = 4 * DH if direct else 2 * DH
    state, pair, to_a, to_b, *rest = call(
        functools.partial(state_kernel, direct), "state",
        [like((DH, DH), F32), like((rows, 6 * DH), BF), like((rows, wide), BF), like((rows, wide), BF)]
        + [like((rows, 2 * DH), BF)] * direct,
        [mine, q_pair, k_pair, v_pair] + [w_part] * direct,
        flops=4 * 2 * rows * DH * DH,
    )
    if direct:
        a, b, c = over_z(to_a, 0), over_z(to_b, 1), [over_z(rest[0], 2)]
        w_keep, w_send = call(
            relay_kernel, "relay", [like((2, half, width), BF)] * 2, [w_part, a, b] + c,
            scratch=[pltpu.VMEM((HEADS, half, width), BF)],
        )
        w_own = call(
            w_rows_kernel, "w_rows", [like((2 * DH, width), BF)], [w_keep, over_core(w_send)]
        )[0]
        w_got = over_dp(w_own, 0)
    else:
        a, b, c = over_z(to_a, 0), over_z(to_b, 1), []
        state = lax.psum(state, "z")
        weights = lax.all_gather(out_weight, axes, axis=0, tiled=True).reshape(2, 2, DH, model)
        weights = [jnp.where(core == 0, weights[:, 0], weights[:, 1]).reshape(2 * DH, model)]

    span = 2 * rows + 2 * HALF
    keep_width = 2 * width if direct else model
    wg_flops = 2 * 2 * rows * DH * model
    qs, ks, vs, ogs, probs, attn, keep_soft, *soft_send = call(
        functools.partial(soft_forward_kernel, direct), "soft_forward",
        [
            like((2 * rows, DH), BF), like((span, DH), BF), like((span, DH), BF),
            like((2 * rows, model), BF), like((2, rows, rows + 2 * HALF), F32), like((2 * rows, DH), F32),
            like((DH, keep_width), F32),
        ] + [like((DH, 2 * width), BF)] * direct,
        [mine, pair, og, og_recv, a, b],
        flops=wg_flops,
    )
    u, total, keep_lin, *sent = call(
        functools.partial(lin_forward_kernel, direct), "lin_forward",
        [like((2 * rows, DH), F32), like((DH, DH), F32), like((DH, keep_width), F32)]
        + [like((2 * DH, 2 * width), BF)] * direct,
        [state, mine, pair, ogs, gain] + ([a, b] + c + soft_send if direct else []),
        flops=wg_flops,
    )
    if direct:
        got = over_dp(sent[0], 0)
        keep, sent = call(
            fold_kernel, "fold", [like((2 * DH, width), F32), like((2 * DH, width), BF)],
            [keep_soft, keep_lin, got],
        )
        w_half = call(
            join_kernel, "w_half", [like((2 * DH, 2 * width), BF)], [w_own, w_got, sent]
        )[0]
        weights = [w_half, over_dp(w_half, 1)]
        got = over_dp(sent, 1)
        row_own, row_send = call(
            rows_kernel, "rows", [like((2 * half, width), F32)] * 2, [keep, got],
            scratch=[pltpu.VMEM((2 * DH, width), F32)],
        )
        row_recv = over_core(row_send)
        piece_send, piece_keep = call(
            chunk_kernel, "chunk", [like((DH, width), BF), like((DH, width), F32)],
            [row_own, row_recv], scratch=[pltpu.VMEM((HEADS, half, width), F32)],
        )
        piece_got = over_z(piece_send, 0)
        weights.append(piece_keep)
    dq_lin, dq_lin_pair, dstate, dq_soft, dk_soft, dv_soft = call(
        functools.partial(backward_kernel, direct), "backward",
        [
            like((rows, DH), BF), like((rows, DH), BF), like((DH, DH), F32),
            like((2 * rows, DH), F32), like((span, DH), F32), like((span, DH), F32),
        ],
        weights + [ogs, u, total, mine, pair, gain, qs, ks, vs, probs, attn],
        scratch=[pltpu.VMEM((2 * rows, 2 * DH), F32), pltpu.VMEM((2 * rows, DH), F32)]
        + [pltpu.VMEM((2 * DH, model), BF)] * direct,
        flops=5 * wg_flops,
    )
    wide = 3 * DH if direct else 2 * DH
    if direct:
        chunk, to_a, to_b, to_c = call(
            second_kernel, "second",
            [
                like((half, width), F32), like((rows, 3 * DH), BF), like((rows, 3 * DH), BF),
                like((rows, 2 * DH), BF),
            ],
            [piece_keep, piece_got, dstate, dk_soft, dv_soft],
        )
        a, b, c = over_z(to_a, 0), over_z(to_b, 1), [over_z(to_c, 2)]
        summed = call(
            functools.partial(weight_sum_kernel, scale), "weight_sum", [like((half, width), BF)],
            [chunk] + c,
        )[0]
        got = over_dp(summed, 0)
        both = call(join_kernel, "both", [like((half, 2 * width), BF)], [summed, got])[0]
        gathered = over_dp(both, 1)
    else:
        to_a, to_b = call(halo_kernel, "halo", [like((rows, 2 * DH), BF)] * 2, [dk_soft, dv_soft])
        a, b = over_z(to_a, 0, True), over_z(to_b, 1, True)
    if not direct:
        dstate = lax.psum(dstate, "z")
        groups = jnp.stack([keep_soft, keep_lin])
        slots = jnp.stack([jnp.where(core == head, groups, 0.0) for head in range(2)], axis=1)
        local = lax.psum_scatter(
            slots.reshape(HEADS * DH, model), axes, scatter_dimension=0, tiled=True
        )
        weight_grad = lax.psum(local, "dp") * scale
    own_out, to_pair = call(
        functools.partial(final_kernel, direct), "final",
        [like((rows, 6 * DH), BF), like((rows, 6 * DH), BF)],
        [dstate, mine, pair, dq_soft, dk_soft, dv_soft, dq_lin, dq_lin_pair, a, b]
        + (c + [both] if direct else []),
        scratch=[pltpu.VMEM((2 * rows, DH), F32)] * 2,
        flops=wg_flops // 4,
    )
    from_pair = over_core(to_pair)
    shape = like((1, rows, HEADS * DH), BF)
    dq, dk, dv = call(output_kernel, "outputs", [shape] * 3, [own_out, from_pair])
    if direct:
        weight_grad = call(
            weight_join_kernel, "weight_join", [like((half, model), F32)], [both, gathered, hbm(dq)],
            spaces=[vmem, vmem, pl.BlockSpec(memory_space=pltpu.HBM)],
        )[0]
    return dq, dk, dv, weight_grad


def solution(mesh):
    n_dp, n_seq = mesh.shape["dp"], mesh.shape["seq"]
    blocks = Mesh(mesh.devices.reshape(n_dp, n_seq // 2, 2), ("dp", "z", "core"))
    tokens, heads = P("dp", ("z", "core"), None), P(("z", "core"), None)
    return jax.shard_map(
        functools.partial(body, n_dp, n_seq // 2),
        mesh=blocks,
        in_specs=(tokens, tokens, tokens, tokens, heads, P()),
        out_specs=(tokens, tokens, tokens, heads),
        check_vma=False,
    )
```

```python
import functools
import math

import jax
import jax.numpy as jnp
from jax import lax
from jax.experimental import pallas as pl
from jax.experimental.pallas import tpu as pltpu
from jax.sharding import Mesh
from jax.sharding import PartitionSpec as P

DH = 128
SOFT_HEADS = 2
LIN_HEADS = 2
HEADS = SOFT_HEADS + LIN_HEADS
WINDOW = 256
HALF = 128
norm_eps = 1e-06
FACTOR = DH ** (-0.5)
BF = jnp.bfloat16
F32 = jnp.float32
NN = (((1,), (0,)), ((), ()))
NT = (((1,), (1,)), ((), ()))
TN = (((0,), (0,)), ((), ()))


def unit_plus(values):
    return jnp.where(values > 0, values + 1.0, jnp.exp(jnp.minimum(values, 0.0)))


def unit_slope(values):
    return jnp.where(values > 0, 1.0, jnp.exp(jnp.minimum(values, 0.0)))


def mm(a, b, dims=NN):
    return lax.dot_general(a, b, dims, preferred_element_type=F32)


def halves(x):
    high = x.astype(BF)
    return high, (x - high.astype(F32)).astype(BF)


def mm3(a, b, dims=NN):
    a_high, a_low = halves(a)
    b_high, b_low = halves(b)
    return mm(a_high, b_high, dims) + (mm(a_high, b_low, dims) + mm(a_low, b_high, dims))


def mm2(a, b, dims=NN):
    a_high, a_low = halves(a)
    return mm(a_high, b, dims) + mm(a_low, b, dims)


def at(start, size=DH):
    return pl.ds(pl.multiple_of(start, size), size)


def places():
    return lax.axis_index("core"), lax.axis_index("z"), lax.axis_index("dp")


def call(kernel, name, outs, args, scratch=(), flops=0, spaces=None):
    vmem = pl.BlockSpec(memory_space=pltpu.VMEM)
    size = sum(math.prod(x.shape) * x.dtype.itemsize for x in list(args) + list(outs))
    return pl.pallas_call(
        kernel,
        name=name,
        out_shape=list(outs),
        in_specs=spaces or [vmem] * len(args),
        out_specs=[vmem] * len(outs),
        scratch_shapes=list(scratch),
        compiler_params=pltpu.CompilerParams(vmem_limit_bytes=24 * 2**20),
        cost_estimate=pl.CostEstimate(flops=flops, bytes_accessed=size, transcendentals=0),
    )(*args)


def like(shape, dtype):
    return jax.ShapeDtypeStruct(shape, dtype)


QS, KS, VS, QL, KL, VL = (slice(i * DH, (i + 1) * DH) for i in range(6))
SOFT = SOFT_HEADS * DH


def links(direct):
    core, z, dp = places()
    step = 1 + core
    turn = lax.rem(z + 1, 2) if direct else 1
    return dict(
        first=3, second=1, step=step, other=3 - step,
        block_a=1 - turn, block_b=turn,
        halo_a=(1 - turn if direct else 1), halo_b=(turn if direct else 0),
    )


def pack_kernel(q, k, v, og, w, gain, mine_out, og_out, w_out, gain_out, sems):
    core, _, dp = places()
    mine = core * DH
    copies = []

    def fetch(source, target):
        copy = pltpu.make_async_copy(source, target, sems.at[len(copies)])
        copy.start()
        copies.append(copy)

    for index, array in enumerate((q, k, v)):
        for group in range(2):
            cols = slice((3 * group + index) * DH, (3 * group + index + 1) * DH)
            fetch(array.at[0, :, at(SOFT * group + mine)], mine_out.at[:, cols])
    width = w_out.shape[1]
    fetch(w.at[:, at(dp * width, width)], w_out)
    fetch(og.at[0], og_out)
    fetch(gain.at[at(mine)], gain_out.at[0])
    for copy in copies:
        copy.wait()


def state_kernel(direct, mine, q_pair, k_pair, v_pair, *refs):
    if direct:
        w, state, pair, to_a, to_b, to_c = refs
    else:
        state, pair, to_a, to_b = refs
    core, _, _ = places()
    own = core * DH
    for index, source in enumerate((q_pair, k_pair, v_pair)):
        for group in range(2):
            first = (3 * group + index) * DH
            pair[:, first : first + DH] = source[0, :, at(SOFT * group + own)]
    total = mm2(unit_plus(mine[:, KL].astype(F32)), mine[:, VL], TN) + mm2(
        unit_plus(pair[:, KL].astype(F32)), pair[:, VL], TN
    )
    state[...] = total
    way = links(direct)
    for out, block in ((to_a, way["block_a"]), (to_b, way["block_b"])):
        here = block == core
        out[:, :DH] = jnp.where(here, mine[:, KS], pair[:, KS])
        out[:, DH : 2 * DH] = jnp.where(here, mine[:, VS], pair[:, VS])
    if direct:
        rows = w.shape[0]
        for out, first in ((to_a, 2 * DH), (to_b, 2 * DH), (to_c, 0)):
            out[:, first : first + DH] = total.astype(BF)
            out[:rows, first + DH :] = w[:, :DH]
            out[rows:, first + DH :] = w[:, DH:]


def relay_kernel(w, a, b, c, keep, send, heads):
    core, z, _ = places()
    way = links(True)
    rows = w.shape[0]
    heads[z] = w[...]
    for source, first, step in ((a, 3 * DH, way["first"]), (b, 3 * DH, way["second"]), (c, DH, 2)):
        heads[z ^ step, :, :DH] = source[:rows, first:]
        heads[z ^ step, :, DH:] = source[rows:, first:]
    for group in range(2):
        keep[group] = heads[2 * group + core]
        send[group] = heads[2 * group + 1 - core]


def w_rows_kernel(keep, got, out):
    core, _, _ = places()
    half = keep.shape[1]
    for group in range(2):
        out[at(group * DH + core * half, half), :] = keep[group]
        out[at(group * DH + (1 - core) * half, half), :] = got[group]


def join_kernel(first, second, *refs):
    out = refs[-1]
    width = first.shape[1]
    out[:, :width] = first[...]
    out[:, width:] = second[...]


def weight_parts(direct, attn, ogs, send, keep):
    high, low = halves(attn)
    if not direct:
        keep[...] = mm(high, ogs[...], TN) + mm(low, ogs[...], TN)
        return
    _, _, dp = places()
    way = links(True)
    width = send.shape[1] // 2
    for index, step in enumerate((0, way["other"])):
        cols = slice(index * width, (index + 1) * width)
        near, far = at((dp ^ step) * width, width), at((dp ^ step ^ way["step"]) * width, width)
        keep[:, cols] = mm(high, ogs[:, near], TN) + mm(low, ogs[:, near], TN)
        send[:, cols] = (mm(high, ogs[:, far], TN) + mm(low, ogs[:, far], TN)).astype(BF)


def soft_forward_kernel(
    direct, mine, pair, og, og_recv, a, b, qs, ks, vs, ogs, probs, attn, keep, *send
):
    core, _, _ = places()
    way = links(direct)
    rows = og.shape[0]
    own_at, pair_at = core * rows, (1 - core) * rows
    for source, first in ((mine, own_at), (pair, pair_at)):
        qs[at(first, rows), :] = source[:, QS]
        ks[at(HALF + first, rows), :] = source[:, KS]
        vs[at(HALF + first, rows), :] = source[:, VS]
    for source, side in ((a, way["halo_a"]), (b, way["halo_b"])):
        first = side * (HALF + 2 * rows)
        ks[at(first), :] = source[:, :DH]
        vs[at(first), :] = source[:, DH : 2 * DH]
    ogs[at(own_at, rows), :] = og[...]
    ogs[at(pair_at, rows), :] = og_recv[...]
    span = rows + 2 * HALF
    row_pos = lax.broadcasted_iota(jnp.int32, (rows, span), 0)
    col_pos = lax.broadcasted_iota(jnp.int32, (rows, span), 1)
    inside = (col_pos >= row_pos) & (col_pos < row_pos + WINDOW)
    for block in range(2):
        here, window = slice(block * rows, (block + 1) * rows), slice(block * rows, block * rows + span)
        scores = mm(qs[here, :], ks[window, :], NT) * FACTOR
        scores = jnp.where(inside, scores, -1e30)
        peak = jnp.max(scores, axis=1, keepdims=True)
        terms = jnp.where(inside, jnp.exp(scores - peak), 0.0)
        share = terms / jnp.sum(terms, axis=1, keepdims=True)
        probs[block] = share
        attn[here, :] = mm(share.astype(BF), vs[window, :])
    weight_parts(direct, attn[...], ogs, send[0] if send else None, keep)


def lin_forward_kernel(direct, state, mine, pair, ogs, gain, *refs):
    core, _, _ = places()
    rows = mine.shape[0]
    total = state[...]
    if direct:
        a, b, c, soft_send, u_out, total_out, keep, out = refs
        total = total + a[:, 2 * DH : 3 * DH].astype(F32) + b[:, 2 * DH : 3 * DH].astype(F32)
        total = total + c[:, :DH].astype(F32)
    else:
        u_out, total_out, keep = refs
    total_out[...] = total
    u_out[at(core * rows, rows), :] = mm3(unit_plus(mine[:, QL].astype(F32)), total)
    u_out[at((1 - core) * rows, rows), :] = mm3(unit_plus(pair[:, QL].astype(F32)), total)
    u = u_out[...]
    r = lax.rsqrt(jnp.mean(u * u, axis=1, keepdims=True) + norm_eps)
    attn = gain[...] * u * r
    weight_parts(direct, attn, ogs, out.at[DH:, :] if direct else None, keep)
    if direct:
        out[:DH, :] = soft_send[...]


def fold_kernel(keep_soft, keep_lin, got, keep, send):
    width = keep.shape[1]
    for rows, source in ((slice(0, DH), keep_soft), (slice(DH, 2 * DH), keep_lin)):
        keep[rows, :] = source[:, :width] + got[rows, :width].astype(F32)
        send[rows, :] = (source[:, width:] + got[rows, width:].astype(F32)).astype(BF)


def rows_kernel(keep, got, own, send, total):
    core, _, _ = places()
    half = DH // 2
    total[...] = keep[...] + got[...].astype(F32)
    for group in range(2):
        out = slice(group * half, (group + 1) * half)
        own[out, :] = total[at(group * DH + core * half, half), :]
        send[out, :] = total[at(group * DH + (1 - core) * half, half), :]


def lin_backward(u, total, dattn, mine, pair, gain, dq_own, dq_pair, dstate, grads):
    core, _, _ = places()
    rows = mine.shape[0]
    u_all = u[...]
    r = lax.rsqrt(jnp.mean(u_all * u_all, axis=1, keepdims=True) + norm_eps)
    lin_grad = gain[...] * dattn[:, DH:]
    grads[...] = r * lin_grad - u_all * (r * r * r) * jnp.mean(lin_grad * u_all, axis=1, keepdims=True)
    total_state = total[...]
    result = jnp.zeros(dstate.shape, F32)
    for first, source, out in ((core * rows, mine, dq_own), ((1 - core) * rows, pair, dq_pair)):
        wide = source[:, QL].astype(F32)
        part = grads[at(first, rows), :]
        result = result + mm3(unit_plus(wide), part, TN)
        out[...] = (mm3(part, total_state, NT) * unit_slope(wide)).astype(BF)
    dstate[...] = result


def soft_backward(qs, ks, vs, probs, attn, dattn, dq_all, dk_all, dv_all):
    rows = qs.shape[0] // 2
    span = rows + 2 * HALF
    dk_all[...] = jnp.zeros_like(dk_all)
    dv_all[...] = jnp.zeros_like(dv_all)
    for block in range(2):
        here, window = slice(block * rows, (block + 1) * rows), slice(block * rows, block * rows + span)
        grad = dattn[here, :DH].astype(BF)
        share = probs[block]
        delta = jnp.sum(grad.astype(F32) * attn[here, :], axis=1, keepdims=True)
        dscore = (share * (mm(grad, vs[window, :], NT) - delta)).astype(BF)
        dq_all[here, :] = mm(dscore, ks[window, :]) * FACTOR
        dk_all[window, :] += mm(dscore, qs[here, :], TN) * FACTOR
        dv_all[window, :] += mm(share.astype(BF), grad, TN)


def backward_kernel(direct, *refs):
    if direct:
        sent, got = refs[:2]
        refs = refs[3:]
    else:
        weights = refs[0]
        refs = refs[1:]
    (ogs, u, total, mine, pair, gain, qs, ks, vs, probs, attn,
     dq_lin, dq_lin_pair, dstate, dq_soft, dk_soft, dv_soft, dattn, grads, *scratch) = refs
    if direct:
        _, _, dp = places()
        way = links(True)
        weights = scratch[0]
        width = weights.shape[1] // 4
        for source, index, step in (
            (sent, 0, 0), (sent, 1, way["step"]), (got, 0, way["other"]), (got, 1, 3),
        ):
            weights[:, at((dp ^ step) * width, width)] = source[:, index * width : (index + 1) * width]
    dattn[...] = mm(ogs[...], weights[...], NT)
    lin_backward(u, total, dattn, mine, pair, gain, dq_lin, dq_lin_pair, dstate, grads)
    soft_backward(qs, ks, vs, probs, attn, dattn, dq_soft, dk_soft, dv_soft)


def halo_part(out, first, dk_soft, dv_soft, side):
    start = side * (dk_soft.shape[0] - HALF)
    out[:, first : first + DH] = dk_soft[at(start), :].astype(BF)
    out[:, first + DH : first + 2 * DH] = dv_soft[at(start), :].astype(BF)


def halo_kernel(dk_soft, dv_soft, to_a, to_b):
    way = links(False)
    halo_part(to_a, 0, dk_soft, dv_soft, way["halo_a"])
    halo_part(to_b, 0, dk_soft, dv_soft, way["halo_b"])


def chunk_kernel(own, got, send, keep, heads):
    core, z, _ = places()
    way = links(True)
    half = own.shape[0] // 2
    for group in range(2):
        rows = slice(group * half, (group + 1) * half)
        heads[2 * group + core] = own[rows, :]
        heads[2 * group + 1 - core] = got[rows, :]
    for index, step in enumerate((2, way["first"])):
        send[index * half : (index + 1) * half, :] = heads[z ^ step].astype(BF)
    for index, step in enumerate((0, way["second"])):
        keep[index * half : (index + 1) * half, :] = heads[z ^ step]


def second_kernel(keep, got, dstate, dk_soft, dv_soft, chunk, to_a, to_b, to_c):
    way = links(True)
    half = chunk.shape[0]
    chunk[...] = keep[:half, :] + got[:half, :].astype(F32)
    for side in range(2):
        cols, rows = slice(side * DH, (side + 1) * DH), slice(side * half, (side + 1) * half)
        piece = keep[half:, cols] + got[half:, cols].astype(F32)
        to_b[rows, 3 * DH :] = piece.astype(BF)
    halo_part(to_a, 0, dk_soft, dv_soft, way["halo_a"])
    halo_part(to_b, 0, dk_soft, dv_soft, way["halo_b"])
    low = dstate[...].astype(BF)
    to_a[:, 2 * DH :] = low
    to_b[:, 2 * DH : 3 * DH] = low
    to_c[...] = low


def weight_sum_kernel(scale, chunk, got, summed):
    half = chunk.shape[0]
    for side in range(2):
        cols, rows = slice(side * DH, (side + 1) * DH), slice(side * half, (side + 1) * half)
        summed[:, cols] = (scale * (chunk[:, cols] + got[rows, 3 * DH :].astype(F32))).astype(summed.dtype)


def final_kernel(
    direct, dstate, mine, pair, dq_soft, dk_soft, dv_soft, dq_lin, dq_lin_pair, a, b, *refs
):
    core, _, _ = places()
    way = links(direct)
    rows = mine.shape[0]
    total = dstate[...]
    own_out, pair_out, dk_all, dv_all = refs[-4:]
    if direct:
        total = total + a[:, 2 * DH :].astype(F32) + b[:, 2 * DH : 3 * DH].astype(F32)
        total = total + refs[0][...].astype(F32)
    for source, out, cols in ((dk_soft, dk_all, slice(0, DH)), (dv_soft, dv_all, slice(DH, 2 * DH))):
        out[...] = source[HALF : HALF + 2 * rows, :]
        out[at(way["block_a"] * rows, rows), :] += a[:, cols].astype(F32)
        out[at(way["block_b"] * rows, rows), :] += b[:, cols].astype(F32)
    high, low = halves(total)
    for source, dq, out, place in ((mine, dq_lin, own_out, core), (pair, dq_lin_pair, pair_out, 1 - core)):
        here = at(place * rows, rows)
        out[:, QS] = dq_soft[here, :].astype(BF)
        out[:, KS] = dk_all[here, :].astype(BF)
        out[:, VS] = dv_all[here, :].astype(BF)
        wide, values = source[:, KL].astype(F32), source[:, VL]
        out[:, QL] = dq[...]
        out[:, KL] = ((mm(values, high, NT) + mm(values, low, NT)) * unit_slope(wide)).astype(BF)
        out[:, VL] = mm3(unit_plus(wide), total).astype(BF)


def output_kernel(own, pair, dq, dk, dv):
    core, _, _ = places()
    for source, first in ((own, core * DH), (pair, (1 - core) * DH)):
        for index, out in enumerate((dq, dk, dv)):
            out[0, :, at(first)] = source[:, index * DH : (index + 1) * DH]
            out[0, :, at(SOFT + first)] = source[:, (3 + index) * DH : (4 + index) * DH]


def weight_join_kernel(both, got, _, out):
    _, _, dp = places()
    way = links(True)
    width = both.shape[1] // 2
    for source, index, step in ((both, 0, 0), (both, 1, way["step"]), (got, 0, way["other"]), (got, 1, 3)):
        out[:, at((dp ^ step) * width, width)] = source[:, index * width : (index + 1) * width].astype(F32)


def body(n_dp, n_z, queries, key_rows, value_rows, out_grad, out_weight, norm_gain):
    rows, model = out_grad.shape[1:]
    axes = ("z", "core")
    pair_perm = [(0, 1), (1, 0)]
    core = lax.axis_index("core")
    direct = n_z == HEADS and n_dp == 4
    width = model // n_dp
    half = DH // 2

    scale = 1.0 / math.sqrt(n_dp * n_z * 2 * rows)

    def over_core(value):
        return lax.ppermute(value, "core", pair_perm)

    def over_z(value, which, back=False):
        pairs = []
        for z in range(n_z):
            for c in range(2):
                if direct:
                    there = z ^ (3, 1, 2)[which]
                else:
                    there = (z + (1 if (which == 1) != back else -1)) % n_z
                pairs.append((2 * z + c, 2 * there + c))
        return lax.ppermute(value, axes, pairs)

    def over_dp(value, which):
        pairs = [
            (2 * d + c, 2 * (d ^ (1 + c, 2 - c)[which]) + c) for d in range(n_dp) for c in range(2)
        ]
        return lax.ppermute(value, ("dp", "core"), pairs)

    vmem = pl.BlockSpec(memory_space=pltpu.VMEM)

    def hbm(value):
        return pltpu.with_memory_space_constraint(value, pltpu.HBM)

    q_pair, k_pair, v_pair = over_core(queries), over_core(key_rows), over_core(value_rows)
    og_recv = over_core(out_grad[0])
    mine, og, w_part, gain = call(
        pack_kernel, "pack",
        [
            like((rows, 6 * DH), BF), like((rows, model), BF),
            like((out_weight.shape[0], width), BF), like((1, DH), F32),
        ],
        [hbm(x) for x in (queries, key_rows, value_rows, out_grad, out_weight, norm_gain)],
        scratch=[pltpu.SemaphoreType.DMA((9,))],
        spaces=[pl.BlockSpec(memory_space=pltpu.HBM)] * 6,
    )
    wide = 4 * DH if direct else 2 * DH
    state, pair, to_a, to_b, *rest = call(
        functools.partial(state_kernel, direct), "state",
        [like((DH, DH), F32), like((rows, 6 * DH), BF), like((rows, wide), BF), like((rows, wide), BF)]
        + [like((rows, 2 * DH), BF)] * direct,
        [mine, q_pair, k_pair, v_pair] + [w_part] * direct,
        flops=4 * 2 * rows * DH * DH,
    )
    if direct:
        a, b, c = over_z(to_a, 0), over_z(to_b, 1), [over_z(rest[0], 2)]
        w_keep, w_send = call(
            relay_kernel, "relay", [like((2, half, width), BF)] * 2, [w_part, a, b] + c,
            scratch=[pltpu.VMEM((HEADS, half, width), BF)],
        )
        w_own = call(
            w_rows_kernel, "w_rows", [like((2 * DH, width), BF)], [w_keep, over_core(w_send)]
        )[0]
        w_got = over_dp(w_own, 0)
    else:
        a, b, c = over_z(to_a, 0), over_z(to_b, 1), []
        state = lax.psum(state, "z")
        weights = lax.all_gather(out_weight, axes, axis=0, tiled=True).reshape(2, 2, DH, model)
        weights = [jnp.where(core == 0, weights[:, 0], weights[:, 1]).reshape(2 * DH, model)]

    span = 2 * rows + 2 * HALF
    keep_width = 2 * width if direct else model
    wg_flops = 2 * 2 * rows * DH * model
    qs, ks, vs, ogs, probs, attn, keep_soft, *soft_send = call(
        functools.partial(soft_forward_kernel, direct), "soft_forward",
        [
            like((2 * rows, DH), BF), like((span, DH), BF), like((span, DH), BF),
            like((2 * rows, model), BF), like((2, rows, rows + 2 * HALF), F32), like((2 * rows, DH), F32),
            like((DH, keep_width), F32),
        ] + [like((DH, 2 * width), BF)] * direct,
        [mine, pair, og, og_recv, a, b],
        flops=wg_flops,
    )
    u, total, keep_lin, *sent = call(
        functools.partial(lin_forward_kernel, direct), "lin_forward",
        [like((2 * rows, DH), F32), like((DH, DH), F32), like((DH, keep_width), F32)]
        + [like((2 * DH, 2 * width), BF)] * direct,
        [state, mine, pair, ogs, gain] + ([a, b] + c + soft_send if direct else []),
        flops=wg_flops,
    )
    if direct:
        got = over_dp(sent[0], 0)
        keep, sent = call(
            fold_kernel, "fold", [like((2 * DH, width), F32), like((2 * DH, width), BF)],
            [keep_soft, keep_lin, got],
        )
        w_half = call(
            join_kernel, "w_half", [like((2 * DH, 2 * width), BF)], [w_own, w_got, sent]
        )[0]
        weights = [w_half, over_dp(w_half, 1)]
        got = over_dp(sent, 1)
        row_own, row_send = call(
            rows_kernel, "rows", [like((2 * half, width), F32)] * 2, [keep, got],
            scratch=[pltpu.VMEM((2 * DH, width), F32)],
        )
        row_recv = over_core(row_send)
        piece_send, piece_keep = call(
            chunk_kernel, "chunk", [like((DH, width), BF), like((DH, width), F32)],
            [row_own, row_recv], scratch=[pltpu.VMEM((HEADS, half, width), F32)],
        )
        piece_got = over_z(piece_send, 2)
        weights.append(piece_keep)
    dq_lin, dq_lin_pair, dstate, dq_soft, dk_soft, dv_soft = call(
        functools.partial(backward_kernel, direct), "backward",
        [
            like((rows, DH), BF), like((rows, DH), BF), like((DH, DH), F32),
            like((2 * rows, DH), F32), like((span, DH), F32), like((span, DH), F32),
        ],
        weights + [ogs, u, total, mine, pair, gain, qs, ks, vs, probs, attn],
        scratch=[pltpu.VMEM((2 * rows, 2 * DH), F32), pltpu.VMEM((2 * rows, DH), F32)]
        + [pltpu.VMEM((2 * DH, model), BF)] * direct,
        flops=5 * wg_flops,
    )
    wide = 3 * DH if direct else 2 * DH
    if direct:
        chunk, to_a, to_b, to_c = call(
            second_kernel, "second",
            [
                like((half, width), F32), like((rows, 3 * DH), BF), like((rows, 4 * DH), BF),
                like((DH, DH), BF),
            ],
            [piece_keep, piece_got, dstate, dk_soft, dv_soft],
        )
        a, b, c = over_z(to_a, 0), over_z(to_b, 1), [over_z(to_c, 2)]
        summed = call(
            functools.partial(weight_sum_kernel, scale), "weight_sum", [like((half, width), BF)],
            [chunk, b],
        )[0]
        got = over_dp(summed, 0)
        both = call(join_kernel, "both", [like((half, 2 * width), BF)], [summed, got])[0]
        gathered = over_dp(both, 1)
    else:
        to_a, to_b = call(halo_kernel, "halo", [like((rows, 2 * DH), BF)] * 2, [dk_soft, dv_soft])
        a, b = over_z(to_a, 0, True), over_z(to_b, 1, True)
    if not direct:
        dstate = lax.psum(dstate, "z")
        groups = jnp.stack([keep_soft, keep_lin])
        slots = jnp.stack([jnp.where(core == head, groups, 0.0) for head in range(2)], axis=1)
        local = lax.psum_scatter(
            slots.reshape(HEADS * DH, model), axes, scatter_dimension=0, tiled=True
        )
        weight_grad = lax.psum(local, "dp") * scale
    own_out, to_pair = call(
        functools.partial(final_kernel, direct), "final",
        [like((rows, 6 * DH), BF), like((rows, 6 * DH), BF)],
        [dstate, mine, pair, dq_soft, dk_soft, dv_soft, dq_lin, dq_lin_pair, a, b]
        + (c + [both] if direct else []),
        scratch=[pltpu.VMEM((2 * rows, DH), F32)] * 2,
        flops=wg_flops // 4,
    )
    from_pair = over_core(to_pair)
    shape = like((1, rows, HEADS * DH), BF)
    dq, dk, dv = call(output_kernel, "outputs", [shape] * 3, [own_out, from_pair])
    if direct:
        weight_grad = call(
            weight_join_kernel, "weight_join", [like((half, model), F32)], [both, gathered, hbm(dq)],
            spaces=[vmem, vmem, pl.BlockSpec(memory_space=pltpu.HBM)],
        )[0]
    return dq, dk, dv, weight_grad


def solution(mesh):
    n_dp, n_seq = mesh.shape["dp"], mesh.shape["seq"]
    blocks = Mesh(mesh.devices.reshape(n_dp, n_seq // 2, 2), ("dp", "z", "core"))
    tokens, heads = P("dp", ("z", "core"), None), P(("z", "core"), None)
    return jax.shard_map(
        functools.partial(body, n_dp, n_seq // 2),
        mesh=blocks,
        in_specs=(tokens, tokens, tokens, tokens, heads, P()),
        out_specs=(tokens, tokens, tokens, heads),
        check_vma=False,
    )
```

```python
import functools
import math

import jax
import jax.numpy as jnp
from jax import lax
from jax.experimental import pallas as pl
from jax.experimental.pallas import tpu as pltpu
from jax.sharding import Mesh
from jax.sharding import PartitionSpec as P

DH = 128
SOFT_HEADS = 2
LIN_HEADS = 2
HEADS = SOFT_HEADS + LIN_HEADS
WINDOW = 256
HALF = 128
norm_eps = 1e-06
FACTOR = DH ** (-0.5)
BF = jnp.bfloat16
F32 = jnp.float32
NN = (((1,), (0,)), ((), ()))
NT = (((1,), (1,)), ((), ()))
TN = (((0,), (0,)), ((), ()))


def unit_plus(values):
    return jnp.where(values > 0, values + 1.0, jnp.exp(jnp.minimum(values, 0.0)))


def unit_slope(values):
    return jnp.where(values > 0, 1.0, jnp.exp(jnp.minimum(values, 0.0)))


def mm(a, b, dims=NN):
    return lax.dot_general(a, b, dims, preferred_element_type=F32)


def halves(x):
    high = x.astype(BF)
    return high, (x - high.astype(F32)).astype(BF)


def mm3(a, b, dims=NN):
    a_high, a_low = halves(a)
    b_high, b_low = halves(b)
    return mm(a_high, b_high, dims) + (mm(a_high, b_low, dims) + mm(a_low, b_high, dims))


def mm2(a, b, dims=NN):
    a_high, a_low = halves(a)
    return mm(a_high, b, dims) + mm(a_low, b, dims)


def at(start, size=DH):
    return pl.ds(pl.multiple_of(start, size), size)


def places():
    return lax.axis_index("core"), lax.axis_index("z"), lax.axis_index("dp")


def call(kernel, name, outs, args, scratch=(), flops=0, spaces=None):
    vmem = pl.BlockSpec(memory_space=pltpu.VMEM)
    size = sum(math.prod(x.shape) * x.dtype.itemsize for x in list(args) + list(outs))
    return pl.pallas_call(
        kernel,
        name=name,
        out_shape=list(outs),
        in_specs=spaces or [vmem] * len(args),
        out_specs=[vmem] * len(outs),
        scratch_shapes=list(scratch),
        compiler_params=pltpu.CompilerParams(vmem_limit_bytes=24 * 2**20),
        cost_estimate=pl.CostEstimate(flops=flops, bytes_accessed=size, transcendentals=0),
    )(*args)


def like(shape, dtype):
    return jax.ShapeDtypeStruct(shape, dtype)


QS, KS, VS, QL, KL, VL = (slice(i * DH, (i + 1) * DH) for i in range(6))
SOFT = SOFT_HEADS * DH


def links(direct):
    core, z, dp = places()
    step = 1 + core
    turn = lax.rem(z + core, 2) if direct else 1
    return dict(
        first=1 + 2 * core, second=3 - 2 * core, step=step, other=3 - step,
        block_a=1 - turn, block_b=turn,
        halo_a=(1 - turn if direct else 1), halo_b=(turn if direct else 0),
    )


def pack_kernel(q, k, v, og, w, gain, mine_out, og_out, w_out, gain_out, sems):
    core, _, dp = places()
    mine = core * DH
    copies = []

    def fetch(source, target):
        copy = pltpu.make_async_copy(source, target, sems.at[len(copies)])
        copy.start()
        copies.append(copy)

    for index, array in enumerate((q, k, v)):
        for group in range(2):
            cols = slice((3 * group + index) * DH, (3 * group + index + 1) * DH)
            fetch(array.at[0, :, at(SOFT * group + mine)], mine_out.at[:, cols])
    width = w_out.shape[1]
    fetch(w.at[:, at(dp * width, width)], w_out)
    fetch(og.at[0], og_out)
    fetch(gain.at[at(mine)], gain_out.at[0])
    for copy in copies:
        copy.wait()


def state_kernel(direct, mine, q_pair, k_pair, v_pair, *refs):
    if direct:
        w, state, pair, to_a, to_b, to_c = refs
    else:
        state, pair, to_a, to_b = refs
    core, _, _ = places()
    own = core * DH
    for index, source in enumerate((q_pair, k_pair, v_pair)):
        for group in range(2):
            first = (3 * group + index) * DH
            pair[:, first : first + DH] = source[0, :, at(SOFT * group + own)]
    total = mm2(unit_plus(mine[:, KL].astype(F32)), mine[:, VL], TN) + mm2(
        unit_plus(pair[:, KL].astype(F32)), pair[:, VL], TN
    )
    state[...] = total
    way = links(direct)
    for out, block in ((to_a, way["block_a"]), (to_b, way["block_b"])):
        here = block == core
        out[:, :DH] = jnp.where(here, mine[:, KS], pair[:, KS])
        out[:, DH : 2 * DH] = jnp.where(here, mine[:, VS], pair[:, VS])
    if direct:
        rows = w.shape[0]
        low = total.astype(BF)
        to_a[:, 2 * DH :] = low
        to_b[:, 2 * DH :] = low
        to_c[:, :DH] = low
        to_c[:rows, DH:] = w[:, :DH]
        to_c[rows:, DH:] = w[:, DH:]


def w_two_kernel(w, c, out):
    _, z, _ = places()
    group = lax.div(z, 2)
    rows = w.shape[0]
    out[group] = w[...]
    out[1 - group, :, :DH] = c[:rows, DH:]
    out[1 - group, :, DH:] = c[rows:, DH:]


def w_rows_kernel(own, cycle, diagonal, out):
    core, z, _ = places()
    half = own.shape[1]
    matching = lax.rem(z, 2) == core
    for group in range(2):
        near, far = at(group * DH + core * half, half), at(group * DH + (1 - core) * half, half)
        out[near, :] = jnp.where(matching, own[group], cycle[group])
        out[far, :] = jnp.where(matching, cycle[group], diagonal[group])


def join_kernel(first, second, *refs):
    out = refs[-1]
    width = first.shape[1]
    out[:, :width] = first[...]
    out[:, width:] = second[...]


def weight_parts(direct, attn, ogs, send, keep):
    high, low = halves(attn)
    if not direct:
        keep[...] = mm(high, ogs[...], TN) + mm(low, ogs[...], TN)
        return
    _, _, dp = places()
    way = links(True)
    width = send.shape[1] // 2
    for index, step in enumerate((0, way["other"])):
        cols = slice(index * width, (index + 1) * width)
        near, far = at((dp ^ step) * width, width), at((dp ^ step ^ way["step"]) * width, width)
        keep[:, cols] = mm(high, ogs[:, near], TN) + mm(low, ogs[:, near], TN)
        send[:, cols] = (mm(high, ogs[:, far], TN) + mm(low, ogs[:, far], TN)).astype(BF)


def soft_forward_kernel(
    direct, mine, pair, og, og_recv, a, b, qs, ks, vs, ogs, probs, attn, keep, *send
):
    core, _, _ = places()
    way = links(direct)
    rows = og.shape[0]
    own_at, pair_at = core * rows, (1 - core) * rows
    for source, first in ((mine, own_at), (pair, pair_at)):
        qs[at(first, rows), :] = source[:, QS]
        ks[at(HALF + first, rows), :] = source[:, KS]
        vs[at(HALF + first, rows), :] = source[:, VS]
    for source, side in ((a, way["halo_a"]), (b, way["halo_b"])):
        first = side * (HALF + 2 * rows)
        ks[at(first), :] = source[:, :DH]
        vs[at(first), :] = source[:, DH : 2 * DH]
    ogs[at(own_at, rows), :] = og[...]
    ogs[at(pair_at, rows), :] = og_recv[...]
    span = rows + 2 * HALF
    row_pos = lax.broadcasted_iota(jnp.int32, (rows, span), 0)
    col_pos = lax.broadcasted_iota(jnp.int32, (rows, span), 1)
    inside = (col_pos >= row_pos) & (col_pos < row_pos + WINDOW)
    for block in range(2):
        here, window = slice(block * rows, (block + 1) * rows), slice(block * rows, block * rows + span)
        scores = mm(qs[here, :], ks[window, :], NT) * FACTOR
        scores = jnp.where(inside, scores, -1e30)
        peak = jnp.max(scores, axis=1, keepdims=True)
        terms = jnp.where(inside, jnp.exp(scores - peak), 0.0)
        share = terms / jnp.sum(terms, axis=1, keepdims=True)
        probs[block] = share
        attn[here, :] = mm(share.astype(BF), vs[window, :])
    weight_parts(direct, attn[...], ogs, send[0] if send else None, keep)


def lin_forward_kernel(direct, state, mine, pair, ogs, gain, *refs):
    core, _, _ = places()
    rows = mine.shape[0]
    total = state[...]
    if direct:
        a, b, c, soft_send, u_out, total_out, keep, out = refs
        total = total + a[:, 2 * DH :].astype(F32) + b[:, 2 * DH :].astype(F32)
        total = total + c[:, :DH].astype(F32)
    else:
        u_out, total_out, keep = refs
    total_out[...] = total
    u_out[at(core * rows, rows), :] = mm3(unit_plus(mine[:, QL].astype(F32)), total)
    u_out[at((1 - core) * rows, rows), :] = mm3(unit_plus(pair[:, QL].astype(F32)), total)
    u = u_out[...]
    r = lax.rsqrt(jnp.mean(u * u, axis=1, keepdims=True) + norm_eps)
    attn = gain[...] * u * r
    weight_parts(direct, attn, ogs, out.at[DH:, :] if direct else None, keep)
    if direct:
        out[:DH, :] = soft_send[...]


def fold_kernel(keep_soft, keep_lin, got, keep, send):
    width = keep.shape[1]
    for rows, source in ((slice(0, DH), keep_soft), (slice(DH, 2 * DH), keep_lin)):
        keep[rows, :] = source[:, :width] + got[rows, :width].astype(F32)
        send[rows, :] = (source[:, width:] + got[rows, width:].astype(F32)).astype(BF)


def rows_kernel(keep, got, own, send, total):
    core, _, _ = places()
    half = DH // 2
    total[...] = keep[...] + got[...].astype(F32)
    for group in range(2):
        out = slice(group * half, (group + 1) * half)
        own[out, :] = total[at(group * DH + core * half, half), :]
        send[out, :] = total[at(group * DH + (1 - core) * half, half), :]


def lin_backward(u, total, dattn, mine, pair, gain, dq_own, dq_pair, dstate, grads):
    core, _, _ = places()
    rows = mine.shape[0]
    u_all = u[...]
    r = lax.rsqrt(jnp.mean(u_all * u_all, axis=1, keepdims=True) + norm_eps)
    lin_grad = gain[...] * dattn[:, DH:]
    grads[...] = r * lin_grad - u_all * (r * r * r) * jnp.mean(lin_grad * u_all, axis=1, keepdims=True)
    total_state = total[...]
    result = jnp.zeros(dstate.shape, F32)
    for first, source, out in ((core * rows, mine, dq_own), ((1 - core) * rows, pair, dq_pair)):
        wide = source[:, QL].astype(F32)
        part = grads[at(first, rows), :]
        result = result + mm3(unit_plus(wide), part, TN)
        out[...] = (mm3(part, total_state, NT) * unit_slope(wide)).astype(BF)
    dstate[...] = result


def soft_backward(qs, ks, vs, probs, attn, dattn, dq_all, dk_all, dv_all):
    rows = qs.shape[0] // 2
    span = rows + 2 * HALF
    dk_all[...] = jnp.zeros_like(dk_all)
    dv_all[...] = jnp.zeros_like(dv_all)
    for block in range(2):
        here, window = slice(block * rows, (block + 1) * rows), slice(block * rows, block * rows + span)
        grad = dattn[here, :DH].astype(BF)
        share = probs[block]
        delta = jnp.sum(grad.astype(F32) * attn[here, :], axis=1, keepdims=True)
        dscore = (share * (mm(grad, vs[window, :], NT) - delta)).astype(BF)
        dq_all[here, :] = mm(dscore, ks[window, :]) * FACTOR
        dk_all[window, :] += mm(dscore, qs[here, :], TN) * FACTOR
        dv_all[window, :] += mm(share.astype(BF), grad, TN)


def backward_kernel(direct, *refs):
    if direct:
        sent, got = refs[:2]
        refs = refs[3:]
    else:
        weights = refs[0]
        refs = refs[1:]
    (ogs, u, total, mine, pair, gain, qs, ks, vs, probs, attn,
     dq_lin, dq_lin_pair, dstate, dq_soft, dk_soft, dv_soft, dattn, grads, *scratch) = refs
    if direct:
        _, _, dp = places()
        way = links(True)
        weights = scratch[0]
        width = weights.shape[1] // 4
        for source, index, step in (
            (sent, 0, 0), (sent, 1, way["step"]), (got, 0, way["other"]), (got, 1, 3),
        ):
            weights[:, at((dp ^ step) * width, width)] = source[:, index * width : (index + 1) * width]
    dattn[...] = mm(ogs[...], weights[...], NT)
    lin_backward(u, total, dattn, mine, pair, gain, dq_lin, dq_lin_pair, dstate, grads)
    soft_backward(qs, ks, vs, probs, attn, dattn, dq_soft, dk_soft, dv_soft)


def halo_part(out, first, dk_soft, dv_soft, side):
    start = side * (dk_soft.shape[0] - HALF)
    out[:, first : first + DH] = dk_soft[at(start), :].astype(BF)
    out[:, first + DH : first + 2 * DH] = dv_soft[at(start), :].astype(BF)


def halo_kernel(dk_soft, dv_soft, to_a, to_b):
    way = links(False)
    halo_part(to_a, 0, dk_soft, dv_soft, way["halo_a"])
    halo_part(to_b, 0, dk_soft, dv_soft, way["halo_b"])


def chunk_kernel(own, got, send, keep, heads):
    core, z, _ = places()
    way = links(True)
    half = own.shape[0] // 2
    for group in range(2):
        rows = slice(group * half, (group + 1) * half)
        heads[2 * group + core] = own[rows, :]
        heads[2 * group + 1 - core] = got[rows, :]
    for index, step in enumerate((way["first"], way["second"])):
        send[index * half : (index + 1) * half, :] = heads[z ^ step].astype(BF)
    for index, step in enumerate((0, 2)):
        keep[index * half : (index + 1) * half, :] = heads[z ^ step]


def second_kernel(keep, got, dstate, dk_soft, dv_soft, chunk, to_a, to_b, to_c):
    way = links(True)
    half = chunk.shape[0]
    chunk[...] = keep[:half, :] + got[:half, :].astype(F32)
    for side in range(2):
        cols, rows = slice(side * DH, (side + 1) * DH), slice(side * half, (side + 1) * half)
        piece = keep[half:, cols] + got[half:, cols].astype(F32)
        to_c[rows, DH:] = piece.astype(BF)
    halo_part(to_a, 0, dk_soft, dv_soft, way["halo_a"])
    halo_part(to_b, 0, dk_soft, dv_soft, way["halo_b"])
    low = dstate[...].astype(BF)
    to_a[:, 2 * DH :] = low
    to_b[:, 2 * DH :] = low
    to_c[:, :DH] = low


def weight_sum_kernel(scale, chunk, got, summed):
    half = chunk.shape[0]
    for side in range(2):
        cols, rows = slice(side * DH, (side + 1) * DH), slice(side * half, (side + 1) * half)
        summed[:, cols] = (scale * (chunk[:, cols] + got[rows, DH:].astype(F32))).astype(summed.dtype)


def final_kernel(
    direct, dstate, mine, pair, dq_soft, dk_soft, dv_soft, dq_lin, dq_lin_pair, a, b, *refs
):
    core, _, _ = places()
    way = links(direct)
    rows = mine.shape[0]
    total = dstate[...]
    own_out, pair_out, dk_all, dv_all = refs[-4:]
    if direct:
        total = total + a[:, 2 * DH :].astype(F32) + b[:, 2 * DH :].astype(F32)
        total = total + refs[0][:, :DH].astype(F32)
    for source, out, cols in ((dk_soft, dk_all, slice(0, DH)), (dv_soft, dv_all, slice(DH, 2 * DH))):
        out[...] = source[HALF : HALF + 2 * rows, :]
        out[at(way["block_a"] * rows, rows), :] += a[:, cols].astype(F32)
        out[at(way["block_b"] * rows, rows), :] += b[:, cols].astype(F32)
    high, low = halves(total)
    for source, dq, out, place in ((mine, dq_lin, own_out, core), (pair, dq_lin_pair, pair_out, 1 - core)):
        here = at(place * rows, rows)
        out[:, QS] = dq_soft[here, :].astype(BF)
        out[:, KS] = dk_all[here, :].astype(BF)
        out[:, VS] = dv_all[here, :].astype(BF)
        wide, values = source[:, KL].astype(F32), source[:, VL]
        out[:, QL] = dq[...]
        out[:, KL] = ((mm(values, high, NT) + mm(values, low, NT)) * unit_slope(wide)).astype(BF)
        out[:, VL] = mm3(unit_plus(wide), total).astype(BF)


def output_kernel(own, pair, dq, dk, dv):
    core, _, _ = places()
    for source, first in ((own, core * DH), (pair, (1 - core) * DH)):
        for index, out in enumerate((dq, dk, dv)):
            out[0, :, at(first)] = source[:, index * DH : (index + 1) * DH]
            out[0, :, at(SOFT + first)] = source[:, (3 + index) * DH : (4 + index) * DH]


def weight_join_kernel(both, got, _, out):
    _, _, dp = places()
    way = links(True)
    width = both.shape[1] // 2
    for source, index, step in ((both, 0, 0), (both, 1, way["step"]), (got, 0, way["other"]), (got, 1, 3)):
        out[:, at((dp ^ step) * width, width)] = source[:, index * width : (index + 1) * width].astype(F32)


def body(n_dp, n_z, queries, key_rows, value_rows, out_grad, out_weight, norm_gain):
    rows, model = out_grad.shape[1:]
    axes = ("z", "core")
    pair_perm = [(0, 1), (1, 0)]
    core = lax.axis_index("core")
    direct = n_z == HEADS and n_dp == 4
    width = model // n_dp
    half = DH // 2

    scale = 1.0 / math.sqrt(n_dp * n_z * 2 * rows)

    def over_core(value):
        return lax.ppermute(value, "core", pair_perm)

    def over_z(value, which, back=False):
        pairs = []
        for z in range(n_z):
            for c in range(2):
                if direct:
                    there = z ^ (1 + 2 * c, 3 - 2 * c, 2)[which]
                else:
                    there = (z + (1 if (which == 1) != back else -1)) % n_z
                pairs.append((2 * z + c, 2 * there + c))
        return lax.ppermute(value, axes, pairs)

    def to_neighbour(value, cycle):
        pairs = []
        for z in range(n_z):
            core_of = z % 2
            if cycle:
                pairs.append((2 * z + core_of, 2 * (z ^ 1) + core_of))
                pairs.append((2 * z + 1 - core_of, 2 * z + core_of))
            else:
                pairs.append((2 * z + 1 - core_of, 2 * (z ^ 1) + core_of))
        return lax.ppermute(value, axes, pairs)

    def over_dp(value, which):
        pairs = [
            (2 * d + c, 2 * (d ^ (1 + c, 2 - c)[which]) + c) for d in range(n_dp) for c in range(2)
        ]
        return lax.ppermute(value, ("dp", "core"), pairs)

    vmem = pl.BlockSpec(memory_space=pltpu.VMEM)

    def hbm(value):
        return pltpu.with_memory_space_constraint(value, pltpu.HBM)

    q_pair, k_pair, v_pair = over_core(queries), over_core(key_rows), over_core(value_rows)
    og_recv = over_core(out_grad[0])
    mine, og, w_part, gain = call(
        pack_kernel, "pack",
        [
            like((rows, 6 * DH), BF), like((rows, model), BF),
            like((out_weight.shape[0], width), BF), like((1, DH), F32),
        ],
        [hbm(x) for x in (queries, key_rows, value_rows, out_grad, out_weight, norm_gain)],
        scratch=[pltpu.SemaphoreType.DMA((9,))],
        spaces=[pl.BlockSpec(memory_space=pltpu.HBM)] * 6,
    )
    wide = 3 * DH if direct else 2 * DH
    state, pair, to_a, to_b, *rest = call(
        functools.partial(state_kernel, direct), "state",
        [like((DH, DH), F32), like((rows, 6 * DH), BF), like((rows, wide), BF), like((rows, wide), BF)]
        + [like((rows, 2 * DH), BF)] * direct,
        [mine, q_pair, k_pair, v_pair] + [w_part] * direct,
        flops=4 * 2 * rows * DH * DH,
    )
    if direct:
        a, b, c = over_z(to_a, 0), over_z(to_b, 1), [over_z(rest[0], 2)]
        w_two = call(w_two_kernel, "w_two", [like((2, half, width), BF)], [w_part] + c)[0]
        w_own = call(
            w_rows_kernel, "w_rows", [like((2 * DH, width), BF)],
            [w_two, to_neighbour(w_two, True), to_neighbour(w_two, False)],
        )[0]
        w_got = over_dp(w_own, 0)
    else:
        a, b, c = over_z(to_a, 0), over_z(to_b, 1), []
        state = lax.psum(state, "z")
        weights = lax.all_gather(out_weight, axes, axis=0, tiled=True).reshape(2, 2, DH, model)
        weights = [jnp.where(core == 0, weights[:, 0], weights[:, 1]).reshape(2 * DH, model)]

    span = 2 * rows + 2 * HALF
    keep_width = 2 * width if direct else model
    wg_flops = 2 * 2 * rows * DH * model
    qs, ks, vs, ogs, probs, attn, keep_soft, *soft_send = call(
        functools.partial(soft_forward_kernel, direct), "soft_forward",
        [
            like((2 * rows, DH), BF), like((span, DH), BF), like((span, DH), BF),
            like((2 * rows, model), BF), like((2, rows, rows + 2 * HALF), F32), like((2 * rows, DH), F32),
            like((DH, keep_width), F32),
        ] + [like((DH, 2 * width), BF)] * direct,
        [mine, pair, og, og_recv, a, b],
        flops=wg_flops,
    )
    u, total, keep_lin, *sent = call(
        functools.partial(lin_forward_kernel, direct), "lin_forward",
        [like((2 * rows, DH), F32), like((DH, DH), F32), like((DH, keep_width), F32)]
        + [like((2 * DH, 2 * width), BF)] * direct,
        [state, mine, pair, ogs, gain] + ([a, b] + c + soft_send if direct else []),
        flops=wg_flops,
    )
    if direct:
        got = over_dp(sent[0], 0)
        keep, sent = call(
            fold_kernel, "fold", [like((2 * DH, width), F32), like((2 * DH, width), BF)],
            [keep_soft, keep_lin, got],
        )
        w_half = call(
            join_kernel, "w_half", [like((2 * DH, 2 * width), BF)], [w_own, w_got, sent]
        )[0]
        weights = [w_half, over_dp(w_half, 1)]
        got = over_dp(sent, 1)
        row_own, row_send = call(
            rows_kernel, "rows", [like((2 * half, width), F32)] * 2, [keep, got],
            scratch=[pltpu.VMEM((2 * DH, width), F32)],
        )
        row_recv = over_core(row_send)
        piece_send, piece_keep = call(
            chunk_kernel, "chunk", [like((DH, width), BF), like((DH, width), F32)],
            [row_own, row_recv], scratch=[pltpu.VMEM((HEADS, half, width), F32)],
        )
        piece_got = over_z(piece_send, 0)
        weights.append(piece_keep)
    dq_lin, dq_lin_pair, dstate, dq_soft, dk_soft, dv_soft = call(
        functools.partial(backward_kernel, direct), "backward",
        [
            like((rows, DH), BF), like((rows, DH), BF), like((DH, DH), F32),
            like((2 * rows, DH), F32), like((span, DH), F32), like((span, DH), F32),
        ],
        weights + [ogs, u, total, mine, pair, gain, qs, ks, vs, probs, attn],
        scratch=[pltpu.VMEM((2 * rows, 2 * DH), F32), pltpu.VMEM((2 * rows, DH), F32)]
        + [pltpu.VMEM((2 * DH, model), BF)] * direct,
        flops=5 * wg_flops,
    )
    wide = 3 * DH if direct else 2 * DH
    if direct:
        chunk, to_a, to_b, to_c = call(
            second_kernel, "second",
            [
                like((half, width), F32), like((rows, 3 * DH), BF), like((rows, 3 * DH), BF),
                like((rows, 2 * DH), BF),
            ],
            [piece_keep, piece_got, dstate, dk_soft, dv_soft],
        )
        a, b, c = over_z(to_a, 0), over_z(to_b, 1), [over_z(to_c, 2)]
        summed = call(
            functools.partial(weight_sum_kernel, scale), "weight_sum", [like((half, width), BF)],
            [chunk] + c,
        )[0]
        got = over_dp(summed, 0)
        both = call(join_kernel, "both", [like((half, 2 * width), BF)], [summed, got])[0]
        gathered = over_dp(both, 1)
    else:
        to_a, to_b = call(halo_kernel, "halo", [like((rows, 2 * DH), BF)] * 2, [dk_soft, dv_soft])
        a, b = over_z(to_a, 0, True), over_z(to_b, 1, True)
    if not direct:
        dstate = lax.psum(dstate, "z")
        groups = jnp.stack([keep_soft, keep_lin])
        slots = jnp.stack([jnp.where(core == head, groups, 0.0) for head in range(2)], axis=1)
        local = lax.psum_scatter(
            slots.reshape(HEADS * DH, model), axes, scatter_dimension=0, tiled=True
        )
        weight_grad = lax.psum(local, "dp") * scale
    own_out, to_pair = call(
        functools.partial(final_kernel, direct), "final",
        [like((rows, 6 * DH), BF), like((rows, 6 * DH), BF)],
        [dstate, mine, pair, dq_soft, dk_soft, dv_soft, dq_lin, dq_lin_pair, a, b]
        + (c + [both] if direct else []),
        scratch=[pltpu.VMEM((2 * rows, DH), F32)] * 2,
        flops=wg_flops // 4,
    )
    from_pair = over_core(to_pair)
    shape = like((1, rows, HEADS * DH), BF)
    dq, dk, dv = call(output_kernel, "outputs", [shape] * 3, [own_out, from_pair])
    if direct:
        weight_grad = call(
            weight_join_kernel, "weight_join", [like((half, model), F32)], [both, gathered, hbm(dq)],
            spaces=[vmem, vmem, pl.BlockSpec(memory_space=pltpu.HBM)],
        )[0]
    return dq, dk, dv, weight_grad


def solution(mesh):
    n_dp, n_seq = mesh.shape["dp"], mesh.shape["seq"]
    blocks = Mesh(mesh.devices.reshape(n_dp, n_seq // 2, 2), ("dp", "z", "core"))
    tokens, heads = P("dp", ("z", "core"), None), P(("z", "core"), None)
    return jax.shard_map(
        functools.partial(body, n_dp, n_seq // 2),
        mesh=blocks,
        in_specs=(tokens, tokens, tokens, tokens, heads, P()),
        out_specs=(tokens, tokens, tokens, heads),
        check_vma=False,
    )
```

```python
import functools
import math

import jax
import jax.numpy as jnp
from jax import lax
from jax.experimental import pallas as pl
from jax.experimental.pallas import tpu as pltpu
from jax.sharding import Mesh
from jax.sharding import PartitionSpec as P

DH = 128
SOFT_HEADS = 2
LIN_HEADS = 2
HEADS = SOFT_HEADS + LIN_HEADS
WINDOW = 256
HALF = 128
norm_eps = 1e-06
FACTOR = DH ** (-0.5)
BF = jnp.bfloat16
F32 = jnp.float32
NN = (((1,), (0,)), ((), ()))
NT = (((1,), (1,)), ((), ()))
TN = (((0,), (0,)), ((), ()))


def unit_plus(values):
    return jnp.where(values > 0, values + 1.0, jnp.exp(jnp.minimum(values, 0.0)))


def unit_slope(values):
    return jnp.where(values > 0, 1.0, jnp.exp(jnp.minimum(values, 0.0)))


def mm(a, b, dims=NN):
    return lax.dot_general(a, b, dims, preferred_element_type=F32)


def halves(x):
    high = x.astype(BF)
    return high, (x - high.astype(F32)).astype(BF)


def mm3(a, b, dims=NN):
    a_high, a_low = halves(a)
    b_high, b_low = halves(b)
    return mm(a_high, b_high, dims) + (mm(a_high, b_low, dims) + mm(a_low, b_high, dims))


def mm2(a, b, dims=NN):
    a_high, a_low = halves(a)
    return mm(a_high, b, dims) + mm(a_low, b, dims)


def at(start, size=DH):
    return pl.ds(pl.multiple_of(start, size), size)


def places():
    return lax.axis_index("core"), lax.axis_index("z"), lax.axis_index("dp")


def call(kernel, name, outs, args, scratch=(), flops=0, spaces=None):
    vmem = pl.BlockSpec(memory_space=pltpu.VMEM)
    size = sum(math.prod(x.shape) * x.dtype.itemsize for x in list(args) + list(outs))
    return pl.pallas_call(
        kernel,
        name=name,
        out_shape=list(outs),
        in_specs=spaces or [vmem] * len(args),
        out_specs=[vmem] * len(outs),
        scratch_shapes=list(scratch),
        compiler_params=pltpu.CompilerParams(vmem_limit_bytes=24 * 2**20),
        cost_estimate=pl.CostEstimate(flops=flops, bytes_accessed=size, transcendentals=0),
    )(*args)


def like(shape, dtype):
    return jax.ShapeDtypeStruct(shape, dtype)


QS, KS, VS, QL, KL, VL = (slice(i * DH, (i + 1) * DH) for i in range(6))
SOFT = SOFT_HEADS * DH


def links(direct):
    core, z, dp = places()
    step = 1 + core
    turn = lax.rem(z + core, 2) if direct else 1
    return dict(
        first=1 + 2 * core, second=3 - 2 * core, step=step, other=3 - step,
        block_a=1 - turn, block_b=turn,
        halo_a=(1 - turn if direct else 1), halo_b=(turn if direct else 0),
    )


def pack_kernel(q, k, v, og, w, gain, mine_out, og_out, w_out, gain_out, sems):
    core, _, dp = places()
    mine = core * DH
    copies = []

    def fetch(source, target):
        copy = pltpu.make_async_copy(source, target, sems.at[len(copies)])
        copy.start()
        copies.append(copy)

    for index, array in enumerate((q, k, v)):
        for group in range(2):
            cols = slice((3 * group + index) * DH, (3 * group + index + 1) * DH)
            fetch(array.at[0, :, at(SOFT * group + mine)], mine_out.at[:, cols])
    width = w_out.shape[1]
    fetch(w.at[:, at(dp * width, width)], w_out)
    fetch(og.at[0], og_out)
    fetch(gain.at[at(mine)], gain_out.at[0])
    for copy in copies:
        copy.wait()


def state_kernel(direct, mine, q_pair, k_pair, v_pair, *refs):
    if direct:
        w, state, pair, to_a, to_b, to_c = refs
    else:
        state, pair, to_a, to_b = refs
    core, _, _ = places()
    own = core * DH
    for index, source in enumerate((q_pair, k_pair, v_pair)):
        for group in range(2):
            first = (3 * group + index) * DH
            pair[:, first : first + DH] = source[0, :, at(SOFT * group + own)]
    total = mm2(unit_plus(mine[:, KL].astype(F32)), mine[:, VL], TN) + mm2(
        unit_plus(pair[:, KL].astype(F32)), pair[:, VL], TN
    )
    state[...] = total
    way = links(direct)
    for out, block in ((to_a, way["block_a"]), (to_b, way["block_b"])):
        here = block == core
        out[:, :DH] = jnp.where(here, mine[:, KS], pair[:, KS])
        out[:, DH : 2 * DH] = jnp.where(here, mine[:, VS], pair[:, VS])
    if direct:
        rows = w.shape[0]
        for out, first in ((to_a, 2 * DH), (to_b, 2 * DH), (to_c, 0)):
            out[:, first : first + DH] = total.astype(BF)
            out[:rows, first + DH :] = w[:, :DH]
            out[rows:, first + DH :] = w[:, DH:]


def relay_kernel(w, a, b, c, keep, send, heads):
    core, z, _ = places()
    way = links(True)
    rows = w.shape[0]
    heads[z] = w[...]
    for source, first, step in ((a, 3 * DH, way["first"]), (b, 3 * DH, way["second"]), (c, DH, 2)):
        heads[z ^ step, :, :DH] = source[:rows, first:]
        heads[z ^ step, :, DH:] = source[rows:, first:]
    for group in range(2):
        keep[group] = heads[2 * group + core]
        send[group] = heads[2 * group + 1 - core]


def w_rows_kernel(keep, got, out):
    core, _, _ = places()
    half = keep.shape[1]
    for group in range(2):
        out[at(group * DH + core * half, half), :] = keep[group]
        out[at(group * DH + (1 - core) * half, half), :] = got[group]


def join_kernel(first, second, *refs):
    out = refs[-1]
    width = first.shape[1]
    out[:, :width] = first[...]
    out[:, width:] = second[...]


def weight_parts(direct, attn, ogs, send, keep):
    high, low = halves(attn)
    if not direct:
        keep[...] = mm(high, ogs[...], TN) + mm(low, ogs[...], TN)
        return
    _, _, dp = places()
    way = links(True)
    width = send.shape[1] // 2
    for index, step in enumerate((0, way["other"])):
        cols = slice(index * width, (index + 1) * width)
        near, far = at((dp ^ step) * width, width), at((dp ^ step ^ way["step"]) * width, width)
        keep[:, cols] = mm(high, ogs[:, near], TN) + mm(low, ogs[:, near], TN)
        send[:, cols] = (mm(high, ogs[:, far], TN) + mm(low, ogs[:, far], TN)).astype(BF)


def soft_forward_kernel(
    direct, mine, pair, og, og_recv, a, b, qs, ks, vs, ogs, probs, attn, keep, *send
):
    core, _, _ = places()
    way = links(direct)
    rows = og.shape[0]
    own_at, pair_at = core * rows, (1 - core) * rows
    for source, first in ((mine, own_at), (pair, pair_at)):
        qs[at(first, rows), :] = source[:, QS]
        ks[at(HALF + first, rows), :] = source[:, KS]
        vs[at(HALF + first, rows), :] = source[:, VS]
    for source, side in ((a, way["halo_a"]), (b, way["halo_b"])):
        first = side * (HALF + 2 * rows)
        ks[at(first), :] = source[:, :DH]
        vs[at(first), :] = source[:, DH : 2 * DH]
    ogs[at(own_at, rows), :] = og[...]
    ogs[at(pair_at, rows), :] = og_recv[...]
    span = rows + 2 * HALF
    row_pos = lax.broadcasted_iota(jnp.int32, (rows, span), 0)
    col_pos = lax.broadcasted_iota(jnp.int32, (rows, span), 1)
    inside = (col_pos >= row_pos) & (col_pos < row_pos + WINDOW)
    for block in range(2):
        here, window = slice(block * rows, (block + 1) * rows), slice(block * rows, block * rows + span)
        scores = mm(qs[here, :], ks[window, :], NT) * FACTOR
        scores = jnp.where(inside, scores, -1e30)
        peak = jnp.max(scores, axis=1, keepdims=True)
        terms = jnp.where(inside, jnp.exp(scores - peak), 0.0)
        share = terms / jnp.sum(terms, axis=1, keepdims=True)
        probs[block] = share
        attn[here, :] = mm(share.astype(BF), vs[window, :])
    weight_parts(direct, attn[...], ogs, send[0] if send else None, keep)


def lin_forward_kernel(direct, state, mine, pair, ogs, gain, *refs):
    core, _, _ = places()
    rows = mine.shape[0]
    total = state[...]
    if direct:
        a, b, c, soft_send, u_out, total_out, keep, out = refs
        total = total + a[:, 2 * DH : 3 * DH].astype(F32) + b[:, 2 * DH : 3 * DH].astype(F32)
        total = total + c[:, :DH].astype(F32)
    else:
        u_out, total_out, keep = refs
    total_out[...] = total
    u_out[at(core * rows, rows), :] = mm3(unit_plus(mine[:, QL].astype(F32)), total)
    u_out[at((1 - core) * rows, rows), :] = mm3(unit_plus(pair[:, QL].astype(F32)), total)
    u = u_out[...]
    r = lax.rsqrt(jnp.mean(u * u, axis=1, keepdims=True) + norm_eps)
    attn = gain[...] * u * r
    weight_parts(direct, attn, ogs, out.at[DH:, :] if direct else None, keep)
    if direct:
        out[:DH, :] = soft_send[...]


def fold_kernel(keep_soft, keep_lin, got, keep, send):
    width = keep.shape[1]
    for rows, source in ((slice(0, DH), keep_soft), (slice(DH, 2 * DH), keep_lin)):
        keep[rows, :] = source[:, :width] + got[rows, :width].astype(F32)
        send[rows, :] = (source[:, width:] + got[rows, width:].astype(F32)).astype(BF)


def rows_kernel(keep, got, own, send, total):
    core, _, _ = places()
    half = DH // 2
    total[...] = keep[...] + got[...].astype(F32)
    for group in range(2):
        out = slice(group * half, (group + 1) * half)
        own[out, :] = total[at(group * DH + core * half, half), :]
        send[out, :] = total[at(group * DH + (1 - core) * half, half), :]


def lin_backward(u, total, dattn, mine, pair, gain, dq_own, dq_pair, dstate, grads):
    core, _, _ = places()
    rows = mine.shape[0]
    u_all = u[...]
    r = lax.rsqrt(jnp.mean(u_all * u_all, axis=1, keepdims=True) + norm_eps)
    lin_grad = gain[...] * dattn[:, DH:]
    grads[...] = r * lin_grad - u_all * (r * r * r) * jnp.mean(lin_grad * u_all, axis=1, keepdims=True)
    total_state = total[...]
    result = jnp.zeros(dstate.shape, F32)
    for first, source, out in ((core * rows, mine, dq_own), ((1 - core) * rows, pair, dq_pair)):
        wide = source[:, QL].astype(F32)
        part = grads[at(first, rows), :]
        result = result + mm3(unit_plus(wide), part, TN)
        out[...] = (mm3(part, total_state, NT) * unit_slope(wide)).astype(BF)
    dstate[...] = result


def soft_backward(qs, ks, vs, probs, attn, dattn, dq_all, dk_all, dv_all):
    rows = qs.shape[0] // 2
    span = rows + 2 * HALF
    dk_all[...] = jnp.zeros_like(dk_all)
    dv_all[...] = jnp.zeros_like(dv_all)
    for block in range(2):
        here, window = slice(block * rows, (block + 1) * rows), slice(block * rows, block * rows + span)
        grad = dattn[here, :DH].astype(BF)
        share = probs[block]
        delta = jnp.sum(grad.astype(F32) * attn[here, :], axis=1, keepdims=True)
        dscore = (share * (mm(grad, vs[window, :], NT) - delta)).astype(BF)
        dq_all[here, :] = mm(dscore, ks[window, :]) * FACTOR
        dk_all[window, :] += mm(dscore, qs[here, :], TN) * FACTOR
        dv_all[window, :] += mm(share.astype(BF), grad, TN)


def backward_kernel(direct, *refs):
    if direct:
        sent, got = refs[:2]
        refs = refs[3:]
    else:
        weights = refs[0]
        refs = refs[1:]
    (ogs, u, total, mine, pair, gain, qs, ks, vs, probs, attn,
     dq_lin, dq_lin_pair, dstate, dq_soft, dk_soft, dv_soft, dattn, grads, *scratch) = refs
    if direct:
        _, _, dp = places()
        way = links(True)
        weights = scratch[0]
        width = weights.shape[1] // 4
        for source, index, step in (
            (sent, 0, 0), (sent, 1, way["step"]), (got, 0, way["other"]), (got, 1, 3),
        ):
            weights[:, at((dp ^ step) * width, width)] = source[:, index * width : (index + 1) * width]
    dattn[...] = mm(ogs[...], weights[...], NT)
    lin_backward(u, total, dattn, mine, pair, gain, dq_lin, dq_lin_pair, dstate, grads)
    soft_backward(qs, ks, vs, probs, attn, dattn, dq_soft, dk_soft, dv_soft)


def halo_part(out, first, dk_soft, dv_soft, side):
    start = side * (dk_soft.shape[0] - HALF)
    out[:, first : first + DH] = dk_soft[at(start), :].astype(BF)
    out[:, first + DH : first + 2 * DH] = dv_soft[at(start), :].astype(BF)


def halo_kernel(direct, dk_soft, dv_soft, *refs):
    way = links(direct)
    to_a, to_b = refs[-2:]
    for out, side in ((to_a, way["halo_a"]), (to_b, way["halo_b"])):
        halo_part(out, 0, dk_soft, dv_soft, side)
        if direct:
            out[:, 2 * DH :] = refs[0][...].astype(BF)


def chunk_kernel(own, got, send, keep, heads):
    core, z, _ = places()
    way = links(True)
    half = own.shape[0] // 2
    for group in range(2):
        rows = slice(group * half, (group + 1) * half)
        heads[2 * group + core] = own[rows, :]
        heads[2 * group + 1 - core] = got[rows, :]
    for index, step in enumerate((way["first"], way["second"])):
        send[index * half : (index + 1) * half, :] = heads[z ^ step].astype(BF)
    for index, step in enumerate((0, 2)):
        keep[index * half : (index + 1) * half, :] = heads[z ^ step]


def second_kernel(keep, got, dstate, chunk, to_c):
    half = chunk.shape[0]
    chunk[...] = keep[:half, :] + got[:half, :].astype(F32)
    for side in range(2):
        cols, rows = slice(side * DH, (side + 1) * DH), slice(side * half, (side + 1) * half)
        to_c[rows, DH:] = (keep[half:, cols] + got[half:, cols].astype(F32)).astype(BF)
    to_c[:, :DH] = dstate[...].astype(BF)


def weight_sum_kernel(scale, chunk, got, summed):
    half = chunk.shape[0]
    for side in range(2):
        cols, rows = slice(side * DH, (side + 1) * DH), slice(side * half, (side + 1) * half)
        summed[:, cols] = (scale * (chunk[:, cols] + got[rows, DH:].astype(F32))).astype(summed.dtype)


def final_kernel(
    direct, dstate, mine, pair, dq_soft, dk_soft, dv_soft, dq_lin, dq_lin_pair, a, b, *refs
):
    core, _, _ = places()
    way = links(direct)
    rows = mine.shape[0]
    total = dstate[...]
    own_out, pair_out, dk_all, dv_all = refs[-4:]
    if direct:
        total = total + a[:, 2 * DH :].astype(F32) + b[:, 2 * DH :].astype(F32)
        total = total + refs[0][:, :DH].astype(F32)
    for source, out, cols in ((dk_soft, dk_all, slice(0, DH)), (dv_soft, dv_all, slice(DH, 2 * DH))):
        out[...] = source[HALF : HALF + 2 * rows, :]
        out[at(way["block_a"] * rows, rows), :] += a[:, cols].astype(F32)
        out[at(way["block_b"] * rows, rows), :] += b[:, cols].astype(F32)
    high, low = halves(total)
    for source, dq, out, place in ((mine, dq_lin, own_out, core), (pair, dq_lin_pair, pair_out, 1 - core)):
        here = at(place * rows, rows)
        out[:, QS] = dq_soft[here, :].astype(BF)
        out[:, KS] = dk_all[here, :].astype(BF)
        out[:, VS] = dv_all[here, :].astype(BF)
        wide, values = source[:, KL].astype(F32), source[:, VL]
        out[:, QL] = dq[...]
        out[:, KL] = ((mm(values, high, NT) + mm(values, low, NT)) * unit_slope(wide)).astype(BF)
        out[:, VL] = mm3(unit_plus(wide), total).astype(BF)


def output_kernel(own, pair, dq, dk, dv):
    core, _, _ = places()
    for source, first in ((own, core * DH), (pair, (1 - core) * DH)):
        for index, out in enumerate((dq, dk, dv)):
            out[0, :, at(first)] = source[:, index * DH : (index + 1) * DH]
            out[0, :, at(SOFT + first)] = source[:, (3 + index) * DH : (4 + index) * DH]


def weight_join_kernel(both, got, _, out):
    _, _, dp = places()
    way = links(True)
    width = both.shape[1] // 2
    for source, index, step in ((both, 0, 0), (both, 1, way["step"]), (got, 0, way["other"]), (got, 1, 3)):
        out[:, at((dp ^ step) * width, width)] = source[:, index * width : (index + 1) * width].astype(F32)


def body(n_dp, n_z, queries, key_rows, value_rows, out_grad, out_weight, norm_gain):
    rows, model = out_grad.shape[1:]
    axes = ("z", "core")
    pair_perm = [(0, 1), (1, 0)]
    core = lax.axis_index("core")
    direct = n_z == HEADS and n_dp == 4
    width = model // n_dp
    half = DH // 2

    scale = 1.0 / math.sqrt(n_dp * n_z * 2 * rows)

    def over_core(value):
        return lax.ppermute(value, "core", pair_perm)

    def over_z(value, which, back=False):
        pairs = []
        for z in range(n_z):
            for c in range(2):
                if direct:
                    there = z ^ (1 + 2 * c, 3 - 2 * c, 2)[which]
                else:
                    there = (z + (1 if (which == 1) != back else -1)) % n_z
                pairs.append((2 * z + c, 2 * there + c))
        return lax.ppermute(value, axes, pairs)

    def over_dp(value, which):
        pairs = [
            (2 * d + c, 2 * (d ^ (1 + c, 2 - c)[which]) + c) for d in range(n_dp) for c in range(2)
        ]
        return lax.ppermute(value, ("dp", "core"), pairs)

    vmem = pl.BlockSpec(memory_space=pltpu.VMEM)

    def hbm(value):
        return pltpu.with_memory_space_constraint(value, pltpu.HBM)

    q_pair, k_pair, v_pair = over_core(queries), over_core(key_rows), over_core(value_rows)
    og_recv = over_core(out_grad[0])
    mine, og, w_part, gain = call(
        pack_kernel, "pack",
        [
            like((rows, 6 * DH), BF), like((rows, model), BF),
            like((out_weight.shape[0], width), BF), like((1, DH), F32),
        ],
        [hbm(x) for x in (queries, key_rows, value_rows, out_grad, out_weight, norm_gain)],
        scratch=[pltpu.SemaphoreType.DMA((9,))],
        spaces=[pl.BlockSpec(memory_space=pltpu.HBM)] * 6,
    )
    wide = 4 * DH if direct else 2 * DH
    state, pair, to_a, to_b, *rest = call(
        functools.partial(state_kernel, direct), "state",
        [like((DH, DH), F32), like((rows, 6 * DH), BF), like((rows, wide), BF), like((rows, wide), BF)]
        + [like((rows, 2 * DH), BF)] * direct,
        [mine, q_pair, k_pair, v_pair] + [w_part] * direct,
        flops=4 * 2 * rows * DH * DH,
    )
    if direct:
        a, b, c = over_z(to_a, 0), over_z(to_b, 1), [over_z(rest[0], 2)]
        w_keep, w_send = call(
            relay_kernel, "relay", [like((2, half, width), BF)] * 2, [w_part, a, b] + c,
            scratch=[pltpu.VMEM((HEADS, half, width), BF)],
        )
        w_own = call(
            w_rows_kernel, "w_rows", [like((2 * DH, width), BF)], [w_keep, over_core(w_send)]
        )[0]
        w_got = over_dp(w_own, 0)
    else:
        a, b, c = over_z(to_a, 0), over_z(to_b, 1), []
        state = lax.psum(state, "z")
        weights = lax.all_gather(out_weight, axes, axis=0, tiled=True).reshape(2, 2, DH, model)
        weights = [jnp.where(core == 0, weights[:, 0], weights[:, 1]).reshape(2 * DH, model)]

    span = 2 * rows + 2 * HALF
    keep_width = 2 * width if direct else model
    wg_flops = 2 * 2 * rows * DH * model
    qs, ks, vs, ogs, probs, attn, keep_soft, *soft_send = call(
        functools.partial(soft_forward_kernel, direct), "soft_forward",
        [
            like((2 * rows, DH), BF), like((span, DH), BF), like((span, DH), BF),
            like((2 * rows, model), BF), like((2, rows, rows + 2 * HALF), F32), like((2 * rows, DH), F32),
            like((DH, keep_width), F32),
        ] + [like((DH, 2 * width), BF)] * direct,
        [mine, pair, og, og_recv, a, b],
        flops=wg_flops,
    )
    u, total, keep_lin, *sent = call(
        functools.partial(lin_forward_kernel, direct), "lin_forward",
        [like((2 * rows, DH), F32), like((DH, DH), F32), like((DH, keep_width), F32)]
        + [like((2 * DH, 2 * width), BF)] * direct,
        [state, mine, pair, ogs, gain] + ([a, b] + c + soft_send if direct else []),
        flops=wg_flops,
    )
    if direct:
        got = over_dp(sent[0], 0)
        keep, sent = call(
            fold_kernel, "fold", [like((2 * DH, width), F32), like((2 * DH, width), BF)],
            [keep_soft, keep_lin, got],
        )
        w_half = call(
            join_kernel, "w_half", [like((2 * DH, 2 * width), BF)], [w_own, w_got, sent]
        )[0]
        weights = [w_half, over_dp(w_half, 1)]
        got = over_dp(sent, 1)
        row_own, row_send = call(
            rows_kernel, "rows", [like((2 * half, width), F32)] * 2, [keep, got],
            scratch=[pltpu.VMEM((2 * DH, width), F32)],
        )
        row_recv = over_core(row_send)
        piece_send, piece_keep = call(
            chunk_kernel, "chunk", [like((DH, width), BF), like((DH, width), F32)],
            [row_own, row_recv], scratch=[pltpu.VMEM((HEADS, half, width), F32)],
        )
        piece_got = over_z(piece_send, 0)
        weights.append(piece_keep)
    dq_lin, dq_lin_pair, dstate, dq_soft, dk_soft, dv_soft = call(
        functools.partial(backward_kernel, direct), "backward",
        [
            like((rows, DH), BF), like((rows, DH), BF), like((DH, DH), F32),
            like((2 * rows, DH), F32), like((span, DH), F32), like((span, DH), F32),
        ],
        weights + [ogs, u, total, mine, pair, gain, qs, ks, vs, probs, attn],
        scratch=[pltpu.VMEM((2 * rows, 2 * DH), F32), pltpu.VMEM((2 * rows, DH), F32)]
        + [pltpu.VMEM((2 * DH, model), BF)] * direct,
        flops=5 * wg_flops,
    )
    wide = 3 * DH if direct else 2 * DH
    if direct:
        chunk, to_c = call(
            second_kernel, "second", [like((half, width), F32), like((rows, 2 * DH), BF)],
            [piece_keep, piece_got, dstate],
        )
        c = [over_z(to_c, 2)]
        summed = call(
            functools.partial(weight_sum_kernel, scale), "weight_sum", [like((half, width), BF)],
            [chunk] + c,
        )[0]
        got = over_dp(summed, 0)
        both = call(join_kernel, "both", [like((half, 2 * width), BF)], [summed, got])[0]
        gathered = over_dp(both, 1)
    to_a, to_b = call(
        functools.partial(halo_kernel, direct), "halo", [like((rows, wide), BF)] * 2,
        [dk_soft, dv_soft] + ([dstate, summed] if direct else []),
    )
    a, b = over_z(to_a, 0, True), over_z(to_b, 1, True)
    if not direct:
        dstate = lax.psum(dstate, "z")
        groups = jnp.stack([keep_soft, keep_lin])
        slots = jnp.stack([jnp.where(core == head, groups, 0.0) for head in range(2)], axis=1)
        local = lax.psum_scatter(
            slots.reshape(HEADS * DH, model), axes, scatter_dimension=0, tiled=True
        )
        weight_grad = lax.psum(local, "dp") * scale
    own_out, to_pair = call(
        functools.partial(final_kernel, direct), "final",
        [like((rows, 6 * DH), BF), like((rows, 6 * DH), BF)],
        [dstate, mine, pair, dq_soft, dk_soft, dv_soft, dq_lin, dq_lin_pair, a, b]
        + (c + [gathered] if direct else []),
        scratch=[pltpu.VMEM((2 * rows, DH), F32)] * 2,
        flops=wg_flops // 4,
    )
    from_pair = over_core(to_pair)
    shape = like((1, rows, HEADS * DH), BF)
    dq, dk, dv = call(output_kernel, "outputs", [shape] * 3, [own_out, from_pair])
    if direct:
        weight_grad = call(
            weight_join_kernel, "weight_join", [like((half, model), F32)], [both, gathered, hbm(dq)],
            spaces=[vmem, vmem, pl.BlockSpec(memory_space=pltpu.HBM)],
        )[0]
    return dq, dk, dv, weight_grad


def solution(mesh):
    n_dp, n_seq = mesh.shape["dp"], mesh.shape["seq"]
    blocks = Mesh(mesh.devices.reshape(n_dp, n_seq // 2, 2), ("dp", "z", "core"))
    tokens, heads = P("dp", ("z", "core"), None), P(("z", "core"), None)
    return jax.shard_map(
        functools.partial(body, n_dp, n_seq // 2),
        mesh=blocks,
        in_specs=(tokens, tokens, tokens, tokens, heads, P()),
        out_specs=(tokens, tokens, tokens, heads),
        check_vma=False,
    )
```

```python
import functools
import math

import jax
import jax.numpy as jnp
from jax import lax
from jax.experimental import pallas as pl
from jax.experimental.pallas import tpu as pltpu
from jax.sharding import Mesh
from jax.sharding import PartitionSpec as P

DH = 128
SOFT_HEADS = 2
LIN_HEADS = 2
HEADS = SOFT_HEADS + LIN_HEADS
WINDOW = 256
HALF = 128
norm_eps = 1e-06
FACTOR = DH ** (-0.5)
BF = jnp.bfloat16
F32 = jnp.float32
NN = (((1,), (0,)), ((), ()))
NT = (((1,), (1,)), ((), ()))
TN = (((0,), (0,)), ((), ()))


def unit_plus(values):
    return jnp.where(values > 0, values + 1.0, jnp.exp(jnp.minimum(values, 0.0)))


def unit_slope(values):
    return jnp.where(values > 0, 1.0, jnp.exp(jnp.minimum(values, 0.0)))


def mm(a, b, dims=NN):
    return lax.dot_general(a, b, dims, preferred_element_type=F32)


def halves(x):
    high = x.astype(BF)
    return high, (x - high.astype(F32)).astype(BF)


def mm3(a, b, dims=NN):
    a_high, a_low = halves(a)
    b_high, b_low = halves(b)
    return mm(a_high, b_high, dims) + (mm(a_high, b_low, dims) + mm(a_low, b_high, dims))


def mm2(a, b, dims=NN):
    a_high, a_low = halves(a)
    return mm(a_high, b, dims) + mm(a_low, b, dims)


def at(start, size=DH):
    return pl.ds(pl.multiple_of(start, size), size)


def places():
    return lax.axis_index("core"), lax.axis_index("z"), lax.axis_index("dp")


def call(kernel, name, outs, args, scratch=(), flops=0, spaces=None):
    vmem = pl.BlockSpec(memory_space=pltpu.VMEM)
    size = sum(math.prod(x.shape) * x.dtype.itemsize for x in list(args) + list(outs))
    return pl.pallas_call(
        kernel,
        name=name,
        out_shape=list(outs),
        in_specs=spaces or [vmem] * len(args),
        out_specs=[vmem] * len(outs),
        scratch_shapes=list(scratch),
        compiler_params=pltpu.CompilerParams(vmem_limit_bytes=24 * 2**20),
        cost_estimate=pl.CostEstimate(flops=flops, bytes_accessed=size, transcendentals=0),
    )(*args)


def like(shape, dtype):
    return jax.ShapeDtypeStruct(shape, dtype)


QS, KS, VS, QL, KL, VL = (slice(i * DH, (i + 1) * DH) for i in range(6))
SOFT = SOFT_HEADS * DH


def links(direct):
    core, z, dp = places()
    step = 1 + core
    turn = lax.rem(z + core, 2) if direct else 1
    return dict(
        first=1 + 2 * core, second=3 - 2 * core, step=step, other=3 - step,
        block_a=1 - turn, block_b=turn,
        halo_a=(1 - turn if direct else 1), halo_b=(turn if direct else 0),
    )


def pack_kernel(q, k, v, og, w, gain, mine_out, og_out, w_out, gain_out, sems):
    core, _, dp = places()
    mine = core * DH
    copies = []

    def fetch(source, target):
        copy = pltpu.make_async_copy(source, target, sems.at[len(copies)])
        copy.start()
        copies.append(copy)

    for index, array in enumerate((q, k, v)):
        for group in range(2):
            cols = slice((3 * group + index) * DH, (3 * group + index + 1) * DH)
            fetch(array.at[0, :, at(SOFT * group + mine)], mine_out.at[:, cols])
    width = w_out.shape[1]
    fetch(w.at[:, at(dp * width, width)], w_out)
    fetch(og.at[0], og_out)
    fetch(gain.at[at(mine)], gain_out.at[0])
    for copy in copies:
        copy.wait()


def state_kernel(direct, mine, q_pair, k_pair, v_pair, *refs):
    if direct:
        w, state, pair, to_a, to_b, to_c = refs
    else:
        state, pair, to_a, to_b = refs
    core, _, _ = places()
    own = core * DH
    for index, source in enumerate((q_pair, k_pair, v_pair)):
        for group in range(2):
            first = (3 * group + index) * DH
            pair[:, first : first + DH] = source[0, :, at(SOFT * group + own)]
    total = mm2(unit_plus(mine[:, KL].astype(F32)), mine[:, VL], TN) + mm2(
        unit_plus(pair[:, KL].astype(F32)), pair[:, VL], TN
    )
    state[...] = total
    way = links(direct)
    for out, block in ((to_a, way["block_a"]), (to_b, way["block_b"])):
        here = block == core
        out[:, :DH] = jnp.where(here, mine[:, KS], pair[:, KS])
        out[:, DH : 2 * DH] = jnp.where(here, mine[:, VS], pair[:, VS])
    if direct:
        rows = w.shape[0]
        for out, first in ((to_a, 2 * DH), (to_b, 2 * DH), (to_c, 0)):
            out[:, first : first + DH] = total.astype(BF)
            out[:rows, first + DH :] = w[:, :DH]
            out[rows:, first + DH :] = w[:, DH:]


def relay_kernel(w, a, b, c, keep, send, heads):
    core, z, _ = places()
    way = links(True)
    rows = w.shape[0]
    heads[z] = w[...]
    for source, first, step in ((a, 3 * DH, way["first"]), (b, 3 * DH, way["second"]), (c, DH, 2)):
        heads[z ^ step, :, :DH] = source[:rows, first:]
        heads[z ^ step, :, DH:] = source[rows:, first:]
    for group in range(2):
        keep[group] = heads[2 * group + core]
        send[group] = heads[2 * group + 1 - core]


def w_rows_kernel(keep, got, out):
    core, _, _ = places()
    half = keep.shape[1]
    for group in range(2):
        out[at(group * DH + core * half, half), :] = keep[group]
        out[at(group * DH + (1 - core) * half, half), :] = got[group]


def join_kernel(first, second, *refs):
    out = refs[-1]
    width = first.shape[1]
    out[:, :width] = first[...]
    out[:, width:] = second[...]


def weight_parts(direct, attn, ogs, send, keep):
    high, low = halves(attn)
    if not direct:
        keep[...] = mm(high, ogs[...], TN) + mm(low, ogs[...], TN)
        return
    _, _, dp = places()
    way = links(True)
    width = send.shape[1] // 2
    for index, step in enumerate((0, way["other"])):
        cols = slice(index * width, (index + 1) * width)
        near, far = at((dp ^ step) * width, width), at((dp ^ step ^ way["step"]) * width, width)
        keep[:, cols] = mm(high, ogs[:, near], TN) + mm(low, ogs[:, near], TN)
        send[:, cols] = (mm(high, ogs[:, far], TN) + mm(low, ogs[:, far], TN)).astype(BF)


def soft_forward_kernel(
    direct, mine, pair, og, og_recv, a, b, qs, ks, vs, ogs, probs, attn, keep, *send
):
    core, _, _ = places()
    way = links(direct)
    rows = og.shape[0]
    own_at, pair_at = core * rows, (1 - core) * rows
    for source, first in ((mine, own_at), (pair, pair_at)):
        qs[at(first, rows), :] = source[:, QS]
        ks[at(HALF + first, rows), :] = source[:, KS]
        vs[at(HALF + first, rows), :] = source[:, VS]
    for source, side in ((a, way["halo_a"]), (b, way["halo_b"])):
        first = side * (HALF + 2 * rows)
        ks[at(first), :] = source[:, :DH]
        vs[at(first), :] = source[:, DH : 2 * DH]
    ogs[at(own_at, rows), :] = og[...]
    ogs[at(pair_at, rows), :] = og_recv[...]
    span = rows + 2 * HALF
    row_pos = lax.broadcasted_iota(jnp.int32, (rows, span), 0)
    col_pos = lax.broadcasted_iota(jnp.int32, (rows, span), 1)
    inside = (col_pos >= row_pos) & (col_pos < row_pos + WINDOW)
    for block in range(2):
        here, window = slice(block * rows, (block + 1) * rows), slice(block * rows, block * rows + span)
        scores = mm(qs[here, :], ks[window, :], NT) * FACTOR
        scores = jnp.where(inside, scores, -1e30)
        peak = jnp.max(scores, axis=1, keepdims=True)
        terms = jnp.where(inside, jnp.exp(scores - peak), 0.0)
        share = terms / jnp.sum(terms, axis=1, keepdims=True)
        probs[block] = share
        attn[here, :] = mm(share.astype(BF), vs[window, :])
    weight_parts(direct, attn[...], ogs, send[0] if send else None, keep)


def lin_forward_kernel(direct, state, mine, pair, ogs, gain, *refs):
    core, _, _ = places()
    rows = mine.shape[0]
    total = state[...]
    if direct:
        a, b, c, soft_send, _, u_out, total_out, keep, out = refs
        total = total + a[:, 2 * DH : 3 * DH].astype(F32) + b[:, 2 * DH : 3 * DH].astype(F32)
        total = total + c[:, :DH].astype(F32)
    else:
        u_out, total_out, keep = refs
    total_out[...] = total
    u_out[at(core * rows, rows), :] = mm3(unit_plus(mine[:, QL].astype(F32)), total)
    u_out[at((1 - core) * rows, rows), :] = mm3(unit_plus(pair[:, QL].astype(F32)), total)
    u = u_out[...]
    r = lax.rsqrt(jnp.mean(u * u, axis=1, keepdims=True) + norm_eps)
    attn = gain[...] * u * r
    weight_parts(direct, attn, ogs, out.at[DH:, :] if direct else None, keep)
    if direct:
        out[:DH, :] = soft_send[...]


def fold_kernel(keep_soft, keep_lin, got, keep, send):
    width = keep.shape[1]
    for rows, source in ((slice(0, DH), keep_soft), (slice(DH, 2 * DH), keep_lin)):
        keep[rows, :] = source[:, :width] + got[rows, :width].astype(F32)
        send[rows, :] = (source[:, width:] + got[rows, width:].astype(F32)).astype(BF)


def rows_kernel(keep, got, own, send, total):
    core, _, _ = places()
    half = DH // 2
    total[...] = keep[...] + got[...].astype(F32)
    for group in range(2):
        out = slice(group * half, (group + 1) * half)
        own[out, :] = total[at(group * DH + core * half, half), :]
        send[out, :] = total[at(group * DH + (1 - core) * half, half), :]


def lin_backward(u, total, dattn, mine, pair, gain, dq_own, dq_pair, dstate, grads):
    core, _, _ = places()
    rows = mine.shape[0]
    u_all = u[...]
    r = lax.rsqrt(jnp.mean(u_all * u_all, axis=1, keepdims=True) + norm_eps)
    lin_grad = gain[...] * dattn[:, DH:]
    grads[...] = r * lin_grad - u_all * (r * r * r) * jnp.mean(lin_grad * u_all, axis=1, keepdims=True)
    total_state = total[...]
    result = jnp.zeros(dstate.shape, F32)
    for first, source, out in ((core * rows, mine, dq_own), ((1 - core) * rows, pair, dq_pair)):
        wide = source[:, QL].astype(F32)
        part = grads[at(first, rows), :]
        result = result + mm3(unit_plus(wide), part, TN)
        out[...] = (mm3(part, total_state, NT) * unit_slope(wide)).astype(BF)
    dstate[...] = result


def soft_backward(qs, ks, vs, probs, attn, dattn, dq_all, dk_all, dv_all):
    rows = qs.shape[0] // 2
    span = rows + 2 * HALF
    dk_all[...] = jnp.zeros_like(dk_all)
    dv_all[...] = jnp.zeros_like(dv_all)
    for block in range(2):
        here, window = slice(block * rows, (block + 1) * rows), slice(block * rows, block * rows + span)
        grad = dattn[here, :DH].astype(BF)
        share = probs[block]
        delta = jnp.sum(grad.astype(F32) * attn[here, :], axis=1, keepdims=True)
        dscore = (share * (mm(grad, vs[window, :], NT) - delta)).astype(BF)
        dq_all[here, :] = mm(dscore, ks[window, :]) * FACTOR
        dk_all[window, :] += mm(dscore, qs[here, :], TN) * FACTOR
        dv_all[window, :] += mm(share.astype(BF), grad, TN)


def backward_kernel(direct, *refs):
    if direct:
        sent, got = refs[:2]
        refs = refs[3:]
    else:
        weights = refs[0]
        refs = refs[1:]
    (ogs, u, total, mine, pair, gain, qs, ks, vs, probs, attn,
     dq_lin, dq_lin_pair, dstate, dq_soft, dk_soft, dv_soft, dattn, grads, *scratch) = refs
    if direct:
        _, _, dp = places()
        way = links(True)
        weights = scratch[0]
        width = weights.shape[1] // 4
        for source, index, step in (
            (sent, 0, 0), (sent, 1, way["step"]), (got, 0, way["other"]), (got, 1, 3),
        ):
            weights[:, at((dp ^ step) * width, width)] = source[:, index * width : (index + 1) * width]
    dattn[...] = mm(ogs[...], weights[...], NT)
    lin_backward(u, total, dattn, mine, pair, gain, dq_lin, dq_lin_pair, dstate, grads)
    soft_backward(qs, ks, vs, probs, attn, dattn, dq_soft, dk_soft, dv_soft)


def halo_part(out, first, dk_soft, dv_soft, side):
    start = side * (dk_soft.shape[0] - HALF)
    out[:, first : first + DH] = dk_soft[at(start), :].astype(BF)
    out[:, first + DH : first + 2 * DH] = dv_soft[at(start), :].astype(BF)


def halo_kernel(dk_soft, dv_soft, to_a, to_b):
    way = links(False)
    halo_part(to_a, 0, dk_soft, dv_soft, way["halo_a"])
    halo_part(to_b, 0, dk_soft, dv_soft, way["halo_b"])


def chunk_kernel(own, got, send, keep, heads):
    core, z, _ = places()
    way = links(True)
    half = own.shape[0] // 2
    for group in range(2):
        rows = slice(group * half, (group + 1) * half)
        heads[2 * group + core] = own[rows, :]
        heads[2 * group + 1 - core] = got[rows, :]
    for index, step in enumerate((1, 3)):
        send[index * half : (index + 1) * half, :] = heads[z ^ step].astype(BF)
    for index, step in enumerate((0, 2)):
        keep[index * half : (index + 1) * half, :] = heads[z ^ step]


def second_kernel(keep, got, dstate, dk_soft, dv_soft, chunk, to_a, to_b, to_c):
    way = links(True)
    half = chunk.shape[0]
    chunk[...] = keep[:half, :] + got[:half, :].astype(F32)
    for side in range(2):
        cols, rows = slice(side * DH, (side + 1) * DH), slice(side * half, (side + 1) * half)
        piece = keep[half:, cols] + got[half:, cols].astype(F32)
        to_c[rows, DH:] = piece.astype(BF)
    halo_part(to_a, 0, dk_soft, dv_soft, way["halo_a"])
    halo_part(to_b, 0, dk_soft, dv_soft, way["halo_b"])
    low = dstate[...].astype(BF)
    to_a[:, 2 * DH :] = low
    to_b[:, 2 * DH :] = low
    to_c[:, :DH] = low


def weight_sum_kernel(scale, chunk, got, summed):
    half = chunk.shape[0]
    for side in range(2):
        cols, rows = slice(side * DH, (side + 1) * DH), slice(side * half, (side + 1) * half)
        summed[:, cols] = (scale * (chunk[:, cols] + got[rows, DH:].astype(F32))).astype(summed.dtype)


def final_kernel(
    direct, dstate, mine, pair, dq_soft, dk_soft, dv_soft, dq_lin, dq_lin_pair, a, b, *refs
):
    core, _, _ = places()
    way = links(direct)
    rows = mine.shape[0]
    total = dstate[...]
    own_out, pair_out, dk_all, dv_all = refs[-4:]
    if direct:
        total = total + a[:, 2 * DH :].astype(F32) + b[:, 2 * DH :].astype(F32)
        total = total + refs[0][:, :DH].astype(F32)
    for source, out, cols in ((dk_soft, dk_all, slice(0, DH)), (dv_soft, dv_all, slice(DH, 2 * DH))):
        out[...] = source[HALF : HALF + 2 * rows, :]
        out[at(way["block_a"] * rows, rows), :] += a[:, cols].astype(F32)
        out[at(way["block_b"] * rows, rows), :] += b[:, cols].astype(F32)
    high, low = halves(total)
    for source, dq, out, place in ((mine, dq_lin, own_out, core), (pair, dq_lin_pair, pair_out, 1 - core)):
        here = at(place * rows, rows)
        out[:, QS] = dq_soft[here, :].astype(BF)
        out[:, KS] = dk_all[here, :].astype(BF)
        out[:, VS] = dv_all[here, :].astype(BF)
        wide, values = source[:, KL].astype(F32), source[:, VL]
        out[:, QL] = dq[...]
        out[:, KL] = ((mm(values, high, NT) + mm(values, low, NT)) * unit_slope(wide)).astype(BF)
        out[:, VL] = mm3(unit_plus(wide), total).astype(BF)


def output_kernel(own, pair, dq, dk, dv):
    core, _, _ = places()
    for source, first in ((own, core * DH), (pair, (1 - core) * DH)):
        for index, out in enumerate((dq, dk, dv)):
            out[0, :, at(first)] = source[:, index * DH : (index + 1) * DH]
            out[0, :, at(SOFT + first)] = source[:, (3 + index) * DH : (4 + index) * DH]


def weight_join_kernel(both, got, _, out):
    _, _, dp = places()
    way = links(True)
    width = both.shape[1] // 2
    for source, index, step in ((both, 0, 0), (both, 1, way["step"]), (got, 0, way["other"]), (got, 1, 3)):
        out[:, at((dp ^ step) * width, width)] = source[:, index * width : (index + 1) * width].astype(F32)


def body(n_dp, n_z, queries, key_rows, value_rows, out_grad, out_weight, norm_gain):
    rows, model = out_grad.shape[1:]
    axes = ("z", "core")
    pair_perm = [(0, 1), (1, 0)]
    core = lax.axis_index("core")
    direct = n_z == HEADS and n_dp == 4
    width = model // n_dp
    half = DH // 2

    scale = 1.0 / math.sqrt(n_dp * n_z * 2 * rows)

    def over_core(value):
        return lax.ppermute(value, "core", pair_perm)

    def over_z(value, which, back=False):
        pairs = []
        for z in range(n_z):
            for c in range(2):
                if direct:
                    there = z ^ (1 + 2 * c, 3 - 2 * c, 2, 1)[which]
                else:
                    there = (z + (1 if (which == 1) != back else -1)) % n_z
                pairs.append((2 * z + c, 2 * there + c))
        return lax.ppermute(value, axes, pairs)

    def over_dp(value, which):
        pairs = [
            (2 * d + c, 2 * (d ^ (1 + c, 2 - c)[which]) + c) for d in range(n_dp) for c in range(2)
        ]
        return lax.ppermute(value, ("dp", "core"), pairs)

    vmem = pl.BlockSpec(memory_space=pltpu.VMEM)

    def hbm(value):
        return pltpu.with_memory_space_constraint(value, pltpu.HBM)

    q_pair, k_pair, v_pair = over_core(queries), over_core(key_rows), over_core(value_rows)
    og_recv = over_core(out_grad[0])
    mine, og, w_part, gain = call(
        pack_kernel, "pack",
        [
            like((rows, 6 * DH), BF), like((rows, model), BF),
            like((out_weight.shape[0], width), BF), like((1, DH), F32),
        ],
        [hbm(x) for x in (queries, key_rows, value_rows, out_grad, out_weight, norm_gain)],
        scratch=[pltpu.SemaphoreType.DMA((9,))],
        spaces=[pl.BlockSpec(memory_space=pltpu.HBM)] * 6,
    )
    wide = 4 * DH if direct else 2 * DH
    state, pair, to_a, to_b, *rest = call(
        functools.partial(state_kernel, direct), "state",
        [like((DH, DH), F32), like((rows, 6 * DH), BF), like((rows, wide), BF), like((rows, wide), BF)]
        + [like((rows, 2 * DH), BF)] * direct,
        [mine, q_pair, k_pair, v_pair] + [w_part] * direct,
        flops=4 * 2 * rows * DH * DH,
    )
    if direct:
        a, b, c = over_z(to_a, 0), over_z(to_b, 1), [over_z(rest[0], 2)]
        w_keep, w_send = call(
            relay_kernel, "relay", [like((2, half, width), BF)] * 2, [w_part, a, b] + c,
            scratch=[pltpu.VMEM((HEADS, half, width), BF)],
        )
        w_own = call(
            w_rows_kernel, "w_rows", [like((2 * DH, width), BF)], [w_keep, over_core(w_send)]
        )[0]
        w_got = over_dp(w_own, 0)
    else:
        a, b, c = over_z(to_a, 0), over_z(to_b, 1), []
        state = lax.psum(state, "z")
        weights = lax.all_gather(out_weight, axes, axis=0, tiled=True).reshape(2, 2, DH, model)
        weights = [jnp.where(core == 0, weights[:, 0], weights[:, 1]).reshape(2 * DH, model)]

    span = 2 * rows + 2 * HALF
    keep_width = 2 * width if direct else model
    wg_flops = 2 * 2 * rows * DH * model
    qs, ks, vs, ogs, probs, attn, keep_soft, *soft_send = call(
        functools.partial(soft_forward_kernel, direct), "soft_forward",
        [
            like((2 * rows, DH), BF), like((span, DH), BF), like((span, DH), BF),
            like((2 * rows, model), BF), like((2, rows, rows + 2 * HALF), F32), like((2 * rows, DH), F32),
            like((DH, keep_width), F32),
        ] + [like((DH, 2 * width), BF)] * direct,
        [mine, pair, og, og_recv, a, b],
        flops=wg_flops,
    )
    u, total, keep_lin, *sent = call(
        functools.partial(lin_forward_kernel, direct), "lin_forward",
        [like((2 * rows, DH), F32), like((DH, DH), F32), like((DH, keep_width), F32)]
        + [like((2 * DH, 2 * width), BF)] * direct,
        [state, mine, pair, ogs, gain] + ([a, b] + c + soft_send + [w_own] if direct else []),
        flops=wg_flops,
    )
    if direct:
        got = over_dp(sent[0], 0)
        keep, sent = call(
            fold_kernel, "fold", [like((2 * DH, width), F32), like((2 * DH, width), BF)],
            [keep_soft, keep_lin, got],
        )
        w_half = call(
            join_kernel, "w_half", [like((2 * DH, 2 * width), BF)], [w_own, w_got, sent]
        )[0]
        weights = [w_half, over_dp(w_half, 1)]
        got = over_dp(sent, 1)
        row_own, row_send = call(
            rows_kernel, "rows", [like((2 * half, width), F32)] * 2, [keep, got],
            scratch=[pltpu.VMEM((2 * DH, width), F32)],
        )
        row_recv = over_core(row_send)
        piece_send, piece_keep = call(
            chunk_kernel, "chunk", [like((DH, width), BF), like((DH, width), F32)],
            [row_own, row_recv], scratch=[pltpu.VMEM((HEADS, half, width), F32)],
        )
        piece_got = over_z(piece_send, 3)
        weights.append(piece_keep)
    dq_lin, dq_lin_pair, dstate, dq_soft, dk_soft, dv_soft = call(
        functools.partial(backward_kernel, direct), "backward",
        [
            like((rows, DH), BF), like((rows, DH), BF), like((DH, DH), F32),
            like((2 * rows, DH), F32), like((span, DH), F32), like((span, DH), F32),
        ],
        weights + [ogs, u, total, mine, pair, gain, qs, ks, vs, probs, attn],
        scratch=[pltpu.VMEM((2 * rows, 2 * DH), F32), pltpu.VMEM((2 * rows, DH), F32)]
        + [pltpu.VMEM((2 * DH, model), BF)] * direct,
        flops=5 * wg_flops,
    )
    wide = 3 * DH if direct else 2 * DH
    if direct:
        chunk, to_a, to_b, to_c = call(
            second_kernel, "second",
            [
                like((half, width), F32), like((rows, 3 * DH), BF), like((rows, 3 * DH), BF),
                like((rows, 2 * DH), BF),
            ],
            [piece_keep, piece_got, dstate, dk_soft, dv_soft],
        )
        a, b, c = over_z(to_a, 0), over_z(to_b, 1), [over_z(to_c, 2)]
        summed = call(
            functools.partial(weight_sum_kernel, scale), "weight_sum", [like((half, width), BF)],
            [chunk] + c,
        )[0]
        got = over_dp(summed, 0)
        both = call(join_kernel, "both", [like((half, 2 * width), BF)], [summed, got])[0]
        gathered = over_dp(both, 1)
    else:
        to_a, to_b = call(halo_kernel, "halo", [like((rows, 2 * DH), BF)] * 2, [dk_soft, dv_soft])
        a, b = over_z(to_a, 0, True), over_z(to_b, 1, True)
    if not direct:
        dstate = lax.psum(dstate, "z")
        groups = jnp.stack([keep_soft, keep_lin])
        slots = jnp.stack([jnp.where(core == head, groups, 0.0) for head in range(2)], axis=1)
        local = lax.psum_scatter(
            slots.reshape(HEADS * DH, model), axes, scatter_dimension=0, tiled=True
        )
        weight_grad = lax.psum(local, "dp") * scale
    own_out, to_pair = call(
        functools.partial(final_kernel, direct), "final",
        [like((rows, 6 * DH), BF), like((rows, 6 * DH), BF)],
        [dstate, mine, pair, dq_soft, dk_soft, dv_soft, dq_lin, dq_lin_pair, a, b]
        + (c + [both] if direct else []),
        scratch=[pltpu.VMEM((2 * rows, DH), F32)] * 2,
        flops=wg_flops // 4,
    )
    from_pair = over_core(to_pair)
    shape = like((1, rows, HEADS * DH), BF)
    dq, dk, dv = call(output_kernel, "outputs", [shape] * 3, [own_out, from_pair])
    if direct:
        weight_grad = call(
            weight_join_kernel, "weight_join", [like((half, model), F32)], [both, gathered, hbm(dq)],
            spaces=[vmem, vmem, pl.BlockSpec(memory_space=pltpu.HBM)],
        )[0]
    return dq, dk, dv, weight_grad


def solution(mesh):
    n_dp, n_seq = mesh.shape["dp"], mesh.shape["seq"]
    blocks = Mesh(mesh.devices.reshape(n_dp, n_seq // 2, 2), ("dp", "z", "core"))
    tokens, heads = P("dp", ("z", "core"), None), P(("z", "core"), None)
    return jax.shard_map(
        functools.partial(body, n_dp, n_seq // 2),
        mesh=blocks,
        in_specs=(tokens, tokens, tokens, tokens, heads, P()),
        out_specs=(tokens, tokens, tokens, heads),
        check_vma=False,
    )
```

```python
import functools
import math

import jax
import jax.numpy as jnp
from jax import lax
from jax.experimental import pallas as pl
from jax.experimental.pallas import tpu as pltpu
from jax.sharding import Mesh
from jax.sharding import PartitionSpec as P

DH = 128
SOFT_HEADS = 2
LIN_HEADS = 2
HEADS = SOFT_HEADS + LIN_HEADS
WINDOW = 256
HALF = 128
norm_eps = 1e-06
FACTOR = DH ** (-0.5)
BF = jnp.bfloat16
F32 = jnp.float32
NN = (((1,), (0,)), ((), ()))
NT = (((1,), (1,)), ((), ()))
TN = (((0,), (0,)), ((), ()))


def unit_plus(values):
    return jnp.where(values > 0, values + 1.0, jnp.exp(jnp.minimum(values, 0.0)))


def unit_slope(values):
    return jnp.where(values > 0, 1.0, jnp.exp(jnp.minimum(values, 0.0)))


def mm(a, b, dims=NN):
    return lax.dot_general(a, b, dims, preferred_element_type=F32)


def halves(x):
    high = x.astype(BF)
    return high, (x - high.astype(F32)).astype(BF)


def mm3(a, b, dims=NN):
    a_high, a_low = halves(a)
    b_high, b_low = halves(b)
    return mm(a_high, b_high, dims) + (mm(a_high, b_low, dims) + mm(a_low, b_high, dims))


def mm2(a, b, dims=NN):
    a_high, a_low = halves(a)
    return mm(a_high, b, dims) + mm(a_low, b, dims)


def at(start, size=DH):
    return pl.ds(pl.multiple_of(start, size), size)


def places():
    return lax.axis_index("core"), lax.axis_index("z"), lax.axis_index("dp")


def call(kernel, name, outs, args, scratch=(), flops=0, spaces=None):
    vmem = pl.BlockSpec(memory_space=pltpu.VMEM)
    size = sum(math.prod(x.shape) * x.dtype.itemsize for x in list(args) + list(outs))
    return pl.pallas_call(
        kernel,
        name=name,
        out_shape=list(outs),
        in_specs=spaces or [vmem] * len(args),
        out_specs=[vmem] * len(outs),
        scratch_shapes=list(scratch),
        compiler_params=pltpu.CompilerParams(vmem_limit_bytes=24 * 2**20),
        cost_estimate=pl.CostEstimate(flops=flops, bytes_accessed=size, transcendentals=0),
    )(*args)


def like(shape, dtype):
    return jax.ShapeDtypeStruct(shape, dtype)


QS, KS, VS, QL, KL, VL = (slice(i * DH, (i + 1) * DH) for i in range(6))
SOFT = SOFT_HEADS * DH


def links(direct):
    core, z, dp = places()
    step = 1 + core
    turn = lax.rem(z + core, 2) if direct else 1
    return dict(
        first=1 + 2 * core, second=3 - 2 * core, step=step, other=3 - step,
        block_a=1 - turn, block_b=turn,
        halo_a=(1 - turn if direct else 1), halo_b=(turn if direct else 0),
    )


def pack_kernel(q, k, v, og, w, gain, mine_out, og_out, w_out, gain_out, sems):
    core, _, dp = places()
    mine = core * DH
    copies = []

    def fetch(source, target):
        copy = pltpu.make_async_copy(source, target, sems.at[len(copies)])
        copy.start()
        copies.append(copy)

    for index, array in enumerate((q, k, v)):
        for group in range(2):
            cols = slice((3 * group + index) * DH, (3 * group + index + 1) * DH)
            fetch(array.at[0, :, at(SOFT * group + mine)], mine_out.at[:, cols])
    width = w_out.shape[1]
    fetch(w.at[:, at(dp * width, width)], w_out)
    fetch(og.at[0], og_out)
    fetch(gain.at[at(mine)], gain_out.at[0])
    for copy in copies:
        copy.wait()


def state_kernel(direct, mine, q_pair, k_pair, v_pair, *refs):
    if direct:
        w, state, pair, to_a, to_b, to_c = refs
    else:
        state, pair, to_a, to_b = refs
    core, _, _ = places()
    own = core * DH
    for index, source in enumerate((q_pair, k_pair, v_pair)):
        for group in range(2):
            first = (3 * group + index) * DH
            pair[:, first : first + DH] = source[0, :, at(SOFT * group + own)]
    total = mm2(unit_plus(mine[:, KL].astype(F32)), mine[:, VL], TN) + mm2(
        unit_plus(pair[:, KL].astype(F32)), pair[:, VL], TN
    )
    state[...] = total
    way = links(direct)
    for out, block in ((to_a, way["block_a"]), (to_b, way["block_b"])):
        here = block == core
        out[:, :DH] = jnp.where(here, mine[:, KS], pair[:, KS])
        out[:, DH : 2 * DH] = jnp.where(here, mine[:, VS], pair[:, VS])
    if direct:
        rows = w.shape[0]
        for out, first in ((to_a, 2 * DH), (to_b, 2 * DH), (to_c, 0)):
            out[:, first : first + DH] = total.astype(BF)
            out[:rows, first + DH :] = w[:, :DH]
            out[rows:, first + DH :] = w[:, DH:]


def relay_kernel(w, a, b, c, keep, send, heads):
    core, z, _ = places()
    way = links(True)
    rows = w.shape[0]
    heads[z] = w[...]
    for source, first, step in ((a, 3 * DH, way["first"]), (b, 3 * DH, way["second"]), (c, DH, 2)):
        heads[z ^ step, :, :DH] = source[:rows, first:]
        heads[z ^ step, :, DH:] = source[rows:, first:]
    for group in range(2):
        keep[group] = heads[2 * group + core]
        send[group] = heads[2 * group + 1 - core]


def w_rows_kernel(keep, got, out):
    core, _, _ = places()
    half = keep.shape[1]
    for group in range(2):
        out[at(group * DH + core * half, half), :] = keep[group]
        out[at(group * DH + (1 - core) * half, half), :] = got[group]


def join_kernel(first, second, *refs):
    out = refs[-1]
    width = first.shape[1]
    out[:, :width] = first[...]
    out[:, width:] = second[...]


def weight_parts(direct, attn, ogs, send, keep):
    high, low = halves(attn)
    if not direct:
        keep[...] = mm(high, ogs[...], TN) + mm(low, ogs[...], TN)
        return
    _, _, dp = places()
    way = links(True)
    width = send.shape[1] // 2
    for index, step in enumerate((0, way["other"])):
        cols = slice(index * width, (index + 1) * width)
        near, far = at((dp ^ step) * width, width), at((dp ^ step ^ way["step"]) * width, width)
        keep[:, cols] = mm(high, ogs[:, near], TN) + mm(low, ogs[:, near], TN)
        send[:, cols] = (mm(high, ogs[:, far], TN) + mm(low, ogs[:, far], TN)).astype(BF)


def soft_forward_kernel(
    direct, mine, pair, og, og_recv, a, b, qs, ks, vs, ogs, probs, attn, keep, *send
):
    core, _, _ = places()
    way = links(direct)
    rows = og.shape[0]
    own_at, pair_at = core * rows, (1 - core) * rows
    for source, first in ((mine, own_at), (pair, pair_at)):
        qs[at(first, rows), :] = source[:, QS]
        ks[at(HALF + first, rows), :] = source[:, KS]
        vs[at(HALF + first, rows), :] = source[:, VS]
    for source, side in ((a, way["halo_a"]), (b, way["halo_b"])):
        first = side * (HALF + 2 * rows)
        ks[at(first), :] = source[:, :DH]
        vs[at(first), :] = source[:, DH : 2 * DH]
    ogs[at(own_at, rows), :] = og[...]
    ogs[at(pair_at, rows), :] = og_recv[...]
    span = rows + 2 * HALF
    row_pos = lax.broadcasted_iota(jnp.int32, (rows, span), 0)
    col_pos = lax.broadcasted_iota(jnp.int32, (rows, span), 1)
    inside = (col_pos >= row_pos) & (col_pos < row_pos + WINDOW)
    for block in range(2):
        here, window = slice(block * rows, (block + 1) * rows), slice(block * rows, block * rows + span)
        scores = mm(qs[here, :], ks[window, :], NT) * FACTOR
        scores = jnp.where(inside, scores, -1e30)
        peak = jnp.max(scores, axis=1, keepdims=True)
        terms = jnp.exp(scores - peak)
        share = terms * (1.0 / jnp.sum(terms, axis=1, keepdims=True))
        probs[block] = share
        attn[here, :] = mm(share.astype(BF), vs[window, :])
    weight_parts(direct, attn[...], ogs, send[0] if send else None, keep)


def lin_forward_kernel(direct, state, mine, pair, ogs, gain, *refs):
    core, _, _ = places()
    rows = mine.shape[0]
    total = state[...]
    if direct:
        a, b, c, soft_send, u_out, total_out, keep, out = refs
        total = total + a[:, 2 * DH : 3 * DH].astype(F32) + b[:, 2 * DH : 3 * DH].astype(F32)
        total = total + c[:, :DH].astype(F32)
    else:
        u_out, total_out, keep = refs
    total_out[...] = total
    u_out[at(core * rows, rows), :] = mm3(unit_plus(mine[:, QL].astype(F32)), total)
    u_out[at((1 - core) * rows, rows), :] = mm3(unit_plus(pair[:, QL].astype(F32)), total)
    u = u_out[...]
    r = lax.rsqrt(jnp.mean(u * u, axis=1, keepdims=True) + norm_eps)
    attn = gain[...] * u * r
    weight_parts(direct, attn, ogs, out.at[DH:, :] if direct else None, keep)
    if direct:
        out[:DH, :] = soft_send[...]


def fold_kernel(keep_soft, keep_lin, got, keep, send):
    width = keep.shape[1]
    for rows, source in ((slice(0, DH), keep_soft), (slice(DH, 2 * DH), keep_lin)):
        keep[rows, :] = source[:, :width] + got[rows, :width].astype(F32)
        send[rows, :] = (source[:, width:] + got[rows, width:].astype(F32)).astype(BF)


def rows_kernel(keep, got, own, send, total):
    core, _, _ = places()
    half = DH // 2
    total[...] = keep[...] + got[...].astype(F32)
    for group in range(2):
        out = slice(group * half, (group + 1) * half)
        own[out, :] = total[at(group * DH + core * half, half), :]
        send[out, :] = total[at(group * DH + (1 - core) * half, half), :]


def lin_backward(u, total, dattn, mine, pair, gain, dq_own, dq_pair, dstate, grads):
    core, _, _ = places()
    rows = mine.shape[0]
    u_all = u[...]
    r = lax.rsqrt(jnp.mean(u_all * u_all, axis=1, keepdims=True) + norm_eps)
    lin_grad = gain[...] * dattn[:, DH:]
    grads[...] = r * lin_grad - u_all * (r * r * r) * jnp.mean(lin_grad * u_all, axis=1, keepdims=True)
    total_state = total[...]
    result = jnp.zeros(dstate.shape, F32)
    for first, source, out in ((core * rows, mine, dq_own), ((1 - core) * rows, pair, dq_pair)):
        wide = source[:, QL].astype(F32)
        part = grads[at(first, rows), :]
        result = result + mm3(unit_plus(wide), part, TN)
        out[...] = (mm3(part, total_state, NT) * unit_slope(wide)).astype(BF)
    dstate[...] = result


def soft_backward(qs, ks, vs, probs, attn, dattn, dq_all, dk_all, dv_all):
    rows = qs.shape[0] // 2
    span = rows + 2 * HALF
    dk_all[...] = jnp.zeros_like(dk_all)
    dv_all[...] = jnp.zeros_like(dv_all)
    for block in range(2):
        here, window = slice(block * rows, (block + 1) * rows), slice(block * rows, block * rows + span)
        grad = dattn[here, :DH].astype(BF)
        share = probs[block]
        delta = jnp.sum(grad.astype(F32) * attn[here, :], axis=1, keepdims=True)
        dscore = (share * (mm(grad, vs[window, :], NT) - delta)).astype(BF)
        dq_all[here, :] = mm(dscore, ks[window, :]) * FACTOR
        dk_all[window, :] += mm(dscore, qs[here, :], TN) * FACTOR
        dv_all[window, :] += mm(share.astype(BF), grad, TN)


def backward_kernel(direct, *refs):
    if direct:
        sent, got = refs[:2]
        refs = refs[3:]
    else:
        weights = refs[0]
        refs = refs[1:]
    (ogs, u, total, mine, pair, gain, qs, ks, vs, probs, attn,
     dq_lin, dq_lin_pair, dstate, dq_soft, dk_soft, dv_soft, dattn, grads, *scratch) = refs
    if direct:
        _, _, dp = places()
        way = links(True)
        weights = scratch[0]
        width = weights.shape[1] // 4
        for source, index, step in (
            (sent, 0, 0), (sent, 1, way["step"]), (got, 0, way["other"]), (got, 1, 3),
        ):
            weights[:, at((dp ^ step) * width, width)] = source[:, index * width : (index + 1) * width]
    dattn[...] = mm(ogs[...], weights[...], NT)
    lin_backward(u, total, dattn, mine, pair, gain, dq_lin, dq_lin_pair, dstate, grads)
    soft_backward(qs, ks, vs, probs, attn, dattn, dq_soft, dk_soft, dv_soft)


def halo_part(out, first, dk_soft, dv_soft, side):
    start = side * (dk_soft.shape[0] - HALF)
    out[:, first : first + DH] = dk_soft[at(start), :].astype(BF)
    out[:, first + DH : first + 2 * DH] = dv_soft[at(start), :].astype(BF)


def halo_kernel(dk_soft, dv_soft, to_a, to_b):
    way = links(False)
    halo_part(to_a, 0, dk_soft, dv_soft, way["halo_a"])
    halo_part(to_b, 0, dk_soft, dv_soft, way["halo_b"])


def chunk_kernel(own, got, send, keep, heads):
    core, z, _ = places()
    way = links(True)
    half = own.shape[0] // 2
    for group in range(2):
        rows = slice(group * half, (group + 1) * half)
        heads[2 * group + core] = own[rows, :]
        heads[2 * group + 1 - core] = got[rows, :]
    for index, step in enumerate((way["first"], way["second"])):
        send[index * half : (index + 1) * half, :] = heads[z ^ step].astype(BF)
    for index, step in enumerate((0, 2)):
        keep[index * half : (index + 1) * half, :] = heads[z ^ step]


def second_kernel(keep, got, dstate, dk_soft, dv_soft, chunk, to_a, to_b, to_c):
    way = links(True)
    half = chunk.shape[0]
    chunk[...] = keep[:half, :] + got[:half, :].astype(F32)
    for side in range(2):
        cols, rows = slice(side * DH, (side + 1) * DH), slice(side * half, (side + 1) * half)
        piece = keep[half:, cols] + got[half:, cols].astype(F32)
        to_c[rows, DH:] = piece.astype(BF)
    halo_part(to_a, 0, dk_soft, dv_soft, way["halo_a"])
    halo_part(to_b, 0, dk_soft, dv_soft, way["halo_b"])
    low = dstate[...].astype(BF)
    to_a[:, 2 * DH :] = low
    to_b[:, 2 * DH :] = low
    to_c[:, :DH] = low


def weight_sum_kernel(scale, chunk, got, summed):
    half = chunk.shape[0]
    for side in range(2):
        cols, rows = slice(side * DH, (side + 1) * DH), slice(side * half, (side + 1) * half)
        summed[:, cols] = (scale * (chunk[:, cols] + got[rows, DH:].astype(F32))).astype(summed.dtype)


def final_kernel(
    direct, dstate, mine, pair, dq_soft, dk_soft, dv_soft, dq_lin, dq_lin_pair, a, b, *refs
):
    core, _, _ = places()
    way = links(direct)
    rows = mine.shape[0]
    total = dstate[...]
    own_out, pair_out, dk_all, dv_all = refs[-4:]
    if direct:
        total = total + a[:, 2 * DH :].astype(F32) + b[:, 2 * DH :].astype(F32)
        total = total + refs[0][:, :DH].astype(F32)
    for source, out, cols in ((dk_soft, dk_all, slice(0, DH)), (dv_soft, dv_all, slice(DH, 2 * DH))):
        out[...] = source[HALF : HALF + 2 * rows, :]
        out[at(way["block_a"] * rows, rows), :] += a[:, cols].astype(F32)
        out[at(way["block_b"] * rows, rows), :] += b[:, cols].astype(F32)
    high, low = halves(total)
    for source, dq, out, place in ((mine, dq_lin, own_out, core), (pair, dq_lin_pair, pair_out, 1 - core)):
        here = at(place * rows, rows)
        out[:, QS] = dq_soft[here, :].astype(BF)
        out[:, KS] = dk_all[here, :].astype(BF)
        out[:, VS] = dv_all[here, :].astype(BF)
        wide, values = source[:, KL].astype(F32), source[:, VL]
        out[:, QL] = dq[...]
        out[:, KL] = ((mm(values, high, NT) + mm(values, low, NT)) * unit_slope(wide)).astype(BF)
        out[:, VL] = mm3(unit_plus(wide), total).astype(BF)


def output_kernel(own, pair, dq, dk, dv):
    core, _, _ = places()
    for source, first in ((own, core * DH), (pair, (1 - core) * DH)):
        for index, out in enumerate((dq, dk, dv)):
            out[0, :, at(first)] = source[:, index * DH : (index + 1) * DH]
            out[0, :, at(SOFT + first)] = source[:, (3 + index) * DH : (4 + index) * DH]


def weight_join_kernel(own, near, next_near, far, out):
    _, _, dp = places()
    way = links(True)
    width = own.shape[1]
    for source, step in ((own, 0), (near, way["step"]), (next_near, way["other"]), (far, 3)):
        out[:, at((dp ^ step) * width, width)] = source[...].astype(F32)


def body(n_dp, n_z, queries, key_rows, value_rows, out_grad, out_weight, norm_gain):
    rows, model = out_grad.shape[1:]
    axes = ("z", "core")
    pair_perm = [(0, 1), (1, 0)]
    core = lax.axis_index("core")
    direct = n_z == HEADS and n_dp == 4
    width = model // n_dp
    half = DH // 2

    scale = 1.0 / math.sqrt(n_dp * n_z * 2 * rows)

    def over_core(value):
        return lax.ppermute(value, "core", pair_perm)

    def over_z(value, which, back=False):
        pairs = []
        for z in range(n_z):
            for c in range(2):
                if direct:
                    there = z ^ (1 + 2 * c, 3 - 2 * c, 2)[which]
                else:
                    there = (z + (1 if (which == 1) != back else -1)) % n_z
                pairs.append((2 * z + c, 2 * there + c))
        return lax.ppermute(value, axes, pairs)

    def over_dp(value, which):
        pairs = [
            (2 * d + c, 2 * (d ^ (1 + c, 2 - c, 3)[which]) + c) for d in range(n_dp) for c in range(2)
        ]
        return lax.ppermute(value, ("dp", "core"), pairs)

    vmem = pl.BlockSpec(memory_space=pltpu.VMEM)

    def hbm(value):
        return pltpu.with_memory_space_constraint(value, pltpu.HBM)

    q_pair, k_pair, v_pair = over_core(queries), over_core(key_rows), over_core(value_rows)
    og_recv = over_core(out_grad[0])
    mine, og, w_part, gain = call(
        pack_kernel, "pack",
        [
            like((rows, 6 * DH), BF), like((rows, model), BF),
            like((out_weight.shape[0], width), BF), like((1, DH), F32),
        ],
        [hbm(x) for x in (queries, key_rows, value_rows, out_grad, out_weight, norm_gain)],
        scratch=[pltpu.SemaphoreType.DMA((9,))],
        spaces=[pl.BlockSpec(memory_space=pltpu.HBM)] * 6,
    )
    wide = 4 * DH if direct else 2 * DH
    state, pair, to_a, to_b, *rest = call(
        functools.partial(state_kernel, direct), "state",
        [like((DH, DH), F32), like((rows, 6 * DH), BF), like((rows, wide), BF), like((rows, wide), BF)]
        + [like((rows, 2 * DH), BF)] * direct,
        [mine, q_pair, k_pair, v_pair] + [w_part] * direct,
        flops=4 * 2 * rows * DH * DH,
    )
    if direct:
        a, b, c = over_z(to_a, 0), over_z(to_b, 1), [over_z(rest[0], 2)]
        w_keep, w_send = call(
            relay_kernel, "relay", [like((2, half, width), BF)] * 2, [w_part, a, b] + c,
            scratch=[pltpu.VMEM((HEADS, half, width), BF)],
        )
        w_own = call(
            w_rows_kernel, "w_rows", [like((2 * DH, width), BF)], [w_keep, over_core(w_send)]
        )[0]
        w_got = over_dp(w_own, 0)
    else:
        a, b, c = over_z(to_a, 0), over_z(to_b, 1), []
        state = lax.psum(state, "z")
        weights = lax.all_gather(out_weight, axes, axis=0, tiled=True).reshape(2, 2, DH, model)
        weights = [jnp.where(core == 0, weights[:, 0], weights[:, 1]).reshape(2 * DH, model)]

    span = 2 * rows + 2 * HALF
    keep_width = 2 * width if direct else model
    wg_flops = 2 * 2 * rows * DH * model
    qs, ks, vs, ogs, probs, attn, keep_soft, *soft_send = call(
        functools.partial(soft_forward_kernel, direct), "soft_forward",
        [
            like((2 * rows, DH), BF), like((span, DH), BF), like((span, DH), BF),
            like((2 * rows, model), BF), like((2, rows, rows + 2 * HALF), F32), like((2 * rows, DH), F32),
            like((DH, keep_width), F32),
        ] + [like((DH, 2 * width), BF)] * direct,
        [mine, pair, og, og_recv, a, b],
        flops=wg_flops,
    )
    u, total, keep_lin, *sent = call(
        functools.partial(lin_forward_kernel, direct), "lin_forward",
        [like((2 * rows, DH), F32), like((DH, DH), F32), like((DH, keep_width), F32)]
        + [like((2 * DH, 2 * width), BF)] * direct,
        [state, mine, pair, ogs, gain] + ([a, b] + c + soft_send if direct else []),
        flops=wg_flops,
    )
    if direct:
        got = over_dp(sent[0], 0)
        keep, sent = call(
            fold_kernel, "fold", [like((2 * DH, width), F32), like((2 * DH, width), BF)],
            [keep_soft, keep_lin, got],
        )
        w_half = call(
            join_kernel, "w_half", [like((2 * DH, 2 * width), BF)], [w_own, w_got, sent]
        )[0]
        weights = [w_half, over_dp(w_half, 1)]
        got = over_dp(sent, 1)
        row_own, row_send = call(
            rows_kernel, "rows", [like((2 * half, width), F32)] * 2, [keep, got],
            scratch=[pltpu.VMEM((2 * DH, width), F32)],
        )
        row_recv = over_core(row_send)
        piece_send, piece_keep = call(
            chunk_kernel, "chunk", [like((DH, width), BF), like((DH, width), F32)],
            [row_own, row_recv], scratch=[pltpu.VMEM((HEADS, half, width), F32)],
        )
        piece_got = over_z(piece_send, 0)
        weights.append(piece_keep)
    dq_lin, dq_lin_pair, dstate, dq_soft, dk_soft, dv_soft = call(
        functools.partial(backward_kernel, direct), "backward",
        [
            like((rows, DH), BF), like((rows, DH), BF), like((DH, DH), F32),
            like((2 * rows, DH), F32), like((span, DH), F32), like((span, DH), F32),
        ],
        weights + [ogs, u, total, mine, pair, gain, qs, ks, vs, probs, attn],
        scratch=[pltpu.VMEM((2 * rows, 2 * DH), F32), pltpu.VMEM((2 * rows, DH), F32)]
        + [pltpu.VMEM((2 * DH, model), BF)] * direct,
        flops=5 * wg_flops,
    )
    wide = 3 * DH if direct else 2 * DH
    if direct:
        chunk, to_a, to_b, to_c = call(
            second_kernel, "second",
            [
                like((half, width), F32), like((rows, 3 * DH), BF), like((rows, 3 * DH), BF),
                like((rows, 2 * DH), BF),
            ],
            [piece_keep, piece_got, dstate, dk_soft, dv_soft],
        )
        a, b, c = over_z(to_a, 0), over_z(to_b, 1), [over_z(to_c, 2)]
        summed = call(
            functools.partial(weight_sum_kernel, scale), "weight_sum", [like((half, width), BF)],
            [chunk] + c,
        )[0]
        gathered = [over_dp(summed, which) for which in range(3)]
        weight_grad = call(
            weight_join_kernel, "weight_join", [like((half, model), F32)], [summed] + gathered
        )[0]
    else:
        to_a, to_b = call(halo_kernel, "halo", [like((rows, 2 * DH), BF)] * 2, [dk_soft, dv_soft])
        a, b = over_z(to_a, 0, True), over_z(to_b, 1, True)
    if not direct:
        dstate = lax.psum(dstate, "z")
        groups = jnp.stack([keep_soft, keep_lin])
        slots = jnp.stack([jnp.where(core == head, groups, 0.0) for head in range(2)], axis=1)
        local = lax.psum_scatter(
            slots.reshape(HEADS * DH, model), axes, scatter_dimension=0, tiled=True
        )
        weight_grad = lax.psum(local, "dp") * scale
    own_out, to_pair = call(
        functools.partial(final_kernel, direct), "final",
        [like((rows, 6 * DH), BF), like((rows, 6 * DH), BF)],
        [dstate, mine, pair, dq_soft, dk_soft, dv_soft, dq_lin, dq_lin_pair, a, b]
        + (c + gathered if direct else []),
        scratch=[pltpu.VMEM((2 * rows, DH), F32)] * 2,
        flops=wg_flops // 4,
    )
    from_pair = over_core(to_pair)
    shape = like((1, rows, HEADS * DH), BF)
    dq, dk, dv = call(output_kernel, "outputs", [shape] * 3, [own_out, from_pair])
    return dq, dk, dv, weight_grad


def solution(mesh):
    n_dp, n_seq = mesh.shape["dp"], mesh.shape["seq"]
    blocks = Mesh(mesh.devices.reshape(n_dp, n_seq // 2, 2), ("dp", "z", "core"))
    tokens, heads = P("dp", ("z", "core"), None), P(("z", "core"), None)
    return jax.shard_map(
        functools.partial(body, n_dp, n_seq // 2),
        mesh=blocks,
        in_specs=(tokens, tokens, tokens, tokens, heads, P()),
        out_specs=(tokens, tokens, tokens, heads),
        check_vma=False,
    )
```

```python
import functools
import math

import jax
import jax.numpy as jnp
from jax import lax
from jax.experimental import pallas as pl
from jax.experimental.pallas import tpu as pltpu
from jax.sharding import Mesh
from jax.sharding import PartitionSpec as P

DH = 128
SOFT_HEADS = 2
LIN_HEADS = 2
HEADS = SOFT_HEADS + LIN_HEADS
WINDOW = 256
HALF = 128
norm_eps = 1e-06
FACTOR = DH ** (-0.5)
BF = jnp.bfloat16
F32 = jnp.float32
NN = (((1,), (0,)), ((), ()))
NT = (((1,), (1,)), ((), ()))
TN = (((0,), (0,)), ((), ()))


def unit_plus(values):
    return jnp.where(values > 0, values + 1.0, jnp.exp(jnp.minimum(values, 0.0)))


def unit_slope(values):
    return jnp.where(values > 0, 1.0, jnp.exp(jnp.minimum(values, 0.0)))


def mm(a, b, dims=NN):
    return lax.dot_general(a, b, dims, preferred_element_type=F32)


def halves(x):
    high = x.astype(BF)
    return high, (x - high.astype(F32)).astype(BF)


def mm3(a, b, dims=NN):
    a_high, a_low = halves(a)
    b_high, b_low = halves(b)
    return mm(a_high, b_high, dims) + (mm(a_high, b_low, dims) + mm(a_low, b_high, dims))


def mm2(a, b, dims=NN):
    a_high, a_low = halves(a)
    return mm(a_high, b, dims) + mm(a_low, b, dims)


def at(start, size=DH):
    return pl.ds(pl.multiple_of(start, size), size)


def places():
    return lax.axis_index("core"), lax.axis_index("z"), lax.axis_index("dp")


def call(kernel, name, outs, args, scratch=(), flops=0, spaces=None):
    vmem = pl.BlockSpec(memory_space=pltpu.VMEM)
    size = sum(math.prod(x.shape) * x.dtype.itemsize for x in list(args) + list(outs))
    return pl.pallas_call(
        kernel,
        name=name,
        out_shape=list(outs),
        in_specs=spaces or [vmem] * len(args),
        out_specs=[vmem] * len(outs),
        scratch_shapes=list(scratch),
        compiler_params=pltpu.CompilerParams(vmem_limit_bytes=24 * 2**20),
        cost_estimate=pl.CostEstimate(flops=flops, bytes_accessed=size, transcendentals=0),
    )(*args)


def like(shape, dtype):
    return jax.ShapeDtypeStruct(shape, dtype)


QS, KS, VS, QL, KL, VL = (slice(i * DH, (i + 1) * DH) for i in range(6))
SOFT = SOFT_HEADS * DH


def links(direct):
    core, z, dp = places()
    step = 1 + core
    turn = lax.rem(z + core, 2) if direct else 1
    return dict(
        first=1 + 2 * core, second=3 - 2 * core, step=step, other=3 - step,
        block_a=1 - turn, block_b=turn,
        halo_a=(1 - turn if direct else 1), halo_b=(turn if direct else 0),
    )


def pack_kernel(q, k, v, og, w, gain, mine_out, og_out, w_out, gain_out, sems):
    core, _, dp = places()
    mine = core * DH
    copies = []

    def fetch(source, target):
        copy = pltpu.make_async_copy(source, target, sems.at[len(copies)])
        copy.start()
        copies.append(copy)

    for index, array in enumerate((q, k, v)):
        for group in range(2):
            cols = slice((3 * group + index) * DH, (3 * group + index + 1) * DH)
            fetch(array.at[0, :, at(SOFT * group + mine)], mine_out.at[:, cols])
    width = w_out.shape[1]
    fetch(w.at[:, at(dp * width, width)], w_out)
    fetch(og.at[0], og_out)
    fetch(gain.at[at(mine)], gain_out.at[0])
    for copy in copies:
        copy.wait()


def state_kernel(direct, mine, q_pair, k_pair, v_pair, *refs):
    if direct:
        w, state, pair, to_a, to_b, to_c = refs
    else:
        state, pair, to_a, to_b = refs
    core, _, _ = places()
    own = core * DH
    for index, source in enumerate((q_pair, k_pair, v_pair)):
        for group in range(2):
            first = (3 * group + index) * DH
            pair[:, first : first + DH] = source[0, :, at(SOFT * group + own)]
    total = mm2(unit_plus(mine[:, KL].astype(F32)), mine[:, VL], TN) + mm2(
        unit_plus(pair[:, KL].astype(F32)), pair[:, VL], TN
    )
    state[...] = total
    way = links(direct)
    for out, block in ((to_a, way["block_a"]), (to_b, way["block_b"])):
        here = block == core
        out[:, :DH] = jnp.where(here, mine[:, KS], pair[:, KS])
        out[:, DH : 2 * DH] = jnp.where(here, mine[:, VS], pair[:, VS])
    if direct:
        rows = w.shape[0]
        for out, first in ((to_a, 2 * DH), (to_b, 2 * DH), (to_c, 0)):
            out[:, first : first + DH] = total.astype(BF)
            out[:rows, first + DH :] = w[:, :DH]
            out[rows:, first + DH :] = w[:, DH:]


def relay_kernel(w, a, b, c, keep, send, heads):
    core, z, _ = places()
    way = links(True)
    rows = w.shape[0]
    heads[z] = w[...]
    for source, first, step in ((a, 3 * DH, way["first"]), (b, 3 * DH, way["second"]), (c, DH, 2)):
        heads[z ^ step, :, :DH] = source[:rows, first:]
        heads[z ^ step, :, DH:] = source[rows:, first:]
    for group in range(2):
        keep[group] = heads[2 * group + core]
        send[group] = heads[2 * group + 1 - core]


def w_rows_kernel(keep, got, out):
    core, _, _ = places()
    half = keep.shape[1]
    for group in range(2):
        out[at(group * DH + core * half, half), :] = keep[group]
        out[at(group * DH + (1 - core) * half, half), :] = got[group]


def join_kernel(first, second, *refs):
    out = refs[-1]
    width = first.shape[1]
    out[:, :width] = first[...]
    out[:, width:] = second[...]


def weight_parts(direct, attn, ogs, send, keep):
    high, low = halves(attn)
    if not direct:
        keep[...] = mm(high, ogs[...], TN) + mm(low, ogs[...], TN)
        return
    _, _, dp = places()
    way = links(True)
    width = send.shape[1] // 2
    for index, step in enumerate((0, way["other"])):
        cols = slice(index * width, (index + 1) * width)
        near, far = at((dp ^ step) * width, width), at((dp ^ step ^ way["step"]) * width, width)
        keep[:, cols] = mm(high, ogs[:, near], TN) + mm(low, ogs[:, near], TN)
        send[:, cols] = (mm(high, ogs[:, far], TN) + mm(low, ogs[:, far], TN)).astype(BF)


def soft_forward_kernel(
    direct, mine, pair, og, og_recv, a, b, qs, ks, vs, ogs, probs, attn, keep, *send
):
    core, _, _ = places()
    way = links(direct)
    rows = og.shape[0]
    own_at, pair_at = core * rows, (1 - core) * rows
    for source, first in ((mine, own_at), (pair, pair_at)):
        qs[at(first, rows), :] = source[:, QS]
        ks[at(HALF + first, rows), :] = source[:, KS]
        vs[at(HALF + first, rows), :] = source[:, VS]
    for source, side in ((a, way["halo_a"]), (b, way["halo_b"])):
        first = side * (HALF + 2 * rows)
        ks[at(first), :] = source[:, :DH]
        vs[at(first), :] = source[:, DH : 2 * DH]
    ogs[at(own_at, rows), :] = og[...]
    ogs[at(pair_at, rows), :] = og_recv[...]
    span = rows + 2 * HALF
    row_pos = lax.broadcasted_iota(jnp.int32, (rows, span), 0)
    col_pos = lax.broadcasted_iota(jnp.int32, (rows, span), 1)
    inside = (col_pos >= row_pos) & (col_pos < row_pos + WINDOW)
    for block in range(2):
        here, window = slice(block * rows, (block + 1) * rows), slice(block * rows, block * rows + span)
        scores = mm(qs[here, :], ks[window, :], NT) * FACTOR
        scores = jnp.where(inside, scores, -1e30)
        peak = jnp.max(scores, axis=1, keepdims=True)
        terms = jnp.exp(scores - peak)
        share = terms * (1.0 / jnp.sum(terms, axis=1, keepdims=True))
        probs[block] = share
        attn[here, :] = mm(share.astype(BF), vs[window, :])
    weight_parts(direct, attn[...], ogs, send[0] if send else None, keep)


def lin_forward_kernel(direct, state, mine, pair, ogs, gain, *refs):
    core, _, _ = places()
    rows = mine.shape[0]
    total = state[...]
    if direct:
        a, b, c, soft_send, u_out, total_out, keep, out = refs
        total = total + a[:, 2 * DH : 3 * DH].astype(F32) + b[:, 2 * DH : 3 * DH].astype(F32)
        total = total + c[:, :DH].astype(F32)
    else:
        u_out, total_out, keep = refs
    total_out[...] = total
    u_out[at(core * rows, rows), :] = mm3(unit_plus(mine[:, QL].astype(F32)), total)
    u_out[at((1 - core) * rows, rows), :] = mm3(unit_plus(pair[:, QL].astype(F32)), total)
    u = u_out[...]
    r = lax.rsqrt(jnp.mean(u * u, axis=1, keepdims=True) + norm_eps)
    attn = gain[...] * u * r
    weight_parts(direct, attn, ogs, out.at[DH:, :] if direct else None, keep)
    if direct:
        out[:DH, :] = soft_send[...]


def fold_kernel(keep_soft, keep_lin, got, keep, send):
    width = keep.shape[1]
    for rows, source in ((slice(0, DH), keep_soft), (slice(DH, 2 * DH), keep_lin)):
        keep[rows, :] = source[:, :width] + got[rows, :width].astype(F32)
        send[rows, :] = (source[:, width:] + got[rows, width:].astype(F32)).astype(BF)


def rows_kernel(keep, got, own, send, total):
    core, _, _ = places()
    half = DH // 2
    total[...] = keep[...] + got[...].astype(F32)
    for group in range(2):
        out = slice(group * half, (group + 1) * half)
        own[out, :] = total[at(group * DH + core * half, half), :]
        send[out, :] = total[at(group * DH + (1 - core) * half, half), :]


def lin_backward(u, total, dattn, mine, pair, gain, dq_own, dq_pair, dstate, grads):
    core, _, _ = places()
    rows = mine.shape[0]
    u_all = u[...]
    r = lax.rsqrt(jnp.mean(u_all * u_all, axis=1, keepdims=True) + norm_eps)
    lin_grad = gain[...] * dattn[:, DH:]
    grads[...] = r * lin_grad - u_all * (r * r * r) * jnp.mean(lin_grad * u_all, axis=1, keepdims=True)
    total_state = total[...]
    result = jnp.zeros(dstate.shape, F32)
    for first, source, out in ((core * rows, mine, dq_own), ((1 - core) * rows, pair, dq_pair)):
        wide = source[:, QL].astype(F32)
        part = grads[at(first, rows), :]
        result = result + mm3(unit_plus(wide), part, TN)
        out[...] = (mm3(part, total_state, NT) * unit_slope(wide)).astype(BF)
    dstate[...] = result


def soft_backward(qs, ks, vs, probs, attn, dattn, dq_all, dk_all, dv_all):
    rows = qs.shape[0] // 2
    span = rows + 2 * HALF
    dk_all[...] = jnp.zeros_like(dk_all)
    dv_all[...] = jnp.zeros_like(dv_all)
    for block in range(2):
        here, window = slice(block * rows, (block + 1) * rows), slice(block * rows, block * rows + span)
        grad = dattn[here, :DH].astype(BF)
        share = probs[block]
        delta = jnp.sum(grad.astype(F32) * attn[here, :], axis=1, keepdims=True)
        dscore = (share * (mm(grad, vs[window, :], NT) - delta)).astype(BF)
        dq_all[here, :] = mm(dscore, ks[window, :]) * FACTOR
        dk_all[window, :] += mm(dscore, qs[here, :], TN) * FACTOR
        dv_all[window, :] += mm(share.astype(BF), grad, TN)


def backward_kernel(direct, *refs):
    if direct:
        sent, got = refs[:2]
        refs = refs[3:]
    else:
        weights = refs[0]
        refs = refs[1:]
    (ogs, u, total, mine, pair, gain, qs, ks, vs, probs, attn,
     dq_lin, dq_lin_pair, dstate, dq_soft, dk_soft, dv_soft, dattn, grads, *scratch) = refs
    if direct:
        _, _, dp = places()
        way = links(True)
        weights = scratch[0]
        width = weights.shape[1] // 4
        for source, index, step in (
            (sent, 0, 0), (sent, 1, way["step"]), (got, 0, way["other"]), (got, 1, 3),
        ):
            weights[:, at((dp ^ step) * width, width)] = source[:, index * width : (index + 1) * width]
    dattn[...] = mm(ogs[...], weights[...], NT)
    lin_backward(u, total, dattn, mine, pair, gain, dq_lin, dq_lin_pair, dstate, grads)
    soft_backward(qs, ks, vs, probs, attn, dattn, dq_soft, dk_soft, dv_soft)


def halo_part(out, first, dk_soft, dv_soft, side):
    start = side * (dk_soft.shape[0] - HALF)
    out[:, first : first + DH] = dk_soft[at(start), :].astype(BF)
    out[:, first + DH : first + 2 * DH] = dv_soft[at(start), :].astype(BF)


def halo_kernel(dk_soft, dv_soft, to_a, to_b):
    way = links(False)
    halo_part(to_a, 0, dk_soft, dv_soft, way["halo_a"])
    halo_part(to_b, 0, dk_soft, dv_soft, way["halo_b"])


def chunk_kernel(own, got, send, keep, heads):
    core, z, _ = places()
    way = links(True)
    half = own.shape[0] // 2
    for group in range(2):
        rows = slice(group * half, (group + 1) * half)
        heads[2 * group + core] = own[rows, :]
        heads[2 * group + 1 - core] = got[rows, :]
    for index, step in enumerate((way["first"], way["second"])):
        send[index * half : (index + 1) * half, :] = heads[z ^ step].astype(BF)
    for index, step in enumerate((0, 2)):
        keep[index * half : (index + 1) * half, :] = heads[z ^ step]


def second_kernel(keep, got, dstate, dk_soft, dv_soft, chunk, to_a, to_b, to_c):
    way = links(True)
    half = chunk.shape[0]
    chunk[...] = keep[:half, :] + got[:half, :].astype(F32)
    for side in range(2):
        cols, rows = slice(side * DH, (side + 1) * DH), slice(side * half, (side + 1) * half)
        piece = keep[half:, cols] + got[half:, cols].astype(F32)
        to_c[rows, DH:] = piece.astype(BF)
    halo_part(to_a, 0, dk_soft, dv_soft, way["halo_a"])
    halo_part(to_b, 0, dk_soft, dv_soft, way["halo_b"])
    low = dstate[...].astype(BF)
    to_a[:, 2 * DH :] = low
    to_b[:, 2 * DH :] = low
    to_c[:, :DH] = low


def weight_sum_kernel(scale, chunk, got, summed):
    half = chunk.shape[0]
    for side in range(2):
        cols, rows = slice(side * DH, (side + 1) * DH), slice(side * half, (side + 1) * half)
        summed[:, cols] = (scale * (chunk[:, cols] + got[rows, DH:].astype(F32))).astype(summed.dtype)


def final_kernel(
    direct, dstate, mine, pair, dq_soft, dk_soft, dv_soft, dq_lin, dq_lin_pair, a, b, *refs
):
    core, _, _ = places()
    way = links(direct)
    rows = mine.shape[0]
    total = dstate[...]
    own_out, pair_out, dk_all, dv_all = refs[-4:]
    if direct:
        total = total + a[:, 2 * DH :].astype(F32) + b[:, 2 * DH :].astype(F32)
        total = total + refs[0][:, :DH].astype(F32)
    for source, out, cols in ((dk_soft, dk_all, slice(0, DH)), (dv_soft, dv_all, slice(DH, 2 * DH))):
        out[...] = source[HALF : HALF + 2 * rows, :]
        out[at(way["block_a"] * rows, rows), :] += a[:, cols].astype(F32)
        out[at(way["block_b"] * rows, rows), :] += b[:, cols].astype(F32)
    high, low = halves(total)
    for source, dq, out, place in ((mine, dq_lin, own_out, core), (pair, dq_lin_pair, pair_out, 1 - core)):
        here = at(place * rows, rows)
        out[:, QS] = dq_soft[here, :].astype(BF)
        out[:, KS] = dk_all[here, :].astype(BF)
        out[:, VS] = dv_all[here, :].astype(BF)
        wide, values = source[:, KL].astype(F32), source[:, VL]
        out[:, QL] = dq[...]
        out[:, KL] = ((mm(values, high, NT) + mm(values, low, NT)) * unit_slope(wide)).astype(BF)
        out[:, VL] = mm3(unit_plus(wide), total).astype(BF)


def output_kernel(own, pair, dq, dk, dv):
    core, _, _ = places()
    for source, first in ((own, core * DH), (pair, (1 - core) * DH)):
        for index, out in enumerate((dq, dk, dv)):
            out[0, :, at(first)] = source[:, index * DH : (index + 1) * DH]
            out[0, :, at(SOFT + first)] = source[:, (3 + index) * DH : (4 + index) * DH]


def weight_join_kernel(own, far, near, next_near, out):
    _, _, dp = places()
    way = links(True)
    width = own.shape[1]
    for source, step in ((own, 0), (near, way["step"]), (next_near, way["other"]), (far, 3)):
        out[:, at((dp ^ step) * width, width)] = source[...].astype(F32)


def body(n_dp, n_z, queries, key_rows, value_rows, out_grad, out_weight, norm_gain):
    rows, model = out_grad.shape[1:]
    axes = ("z", "core")
    pair_perm = [(0, 1), (1, 0)]
    core = lax.axis_index("core")
    direct = n_z == HEADS and n_dp == 4
    width = model // n_dp
    half = DH // 2

    scale = 1.0 / math.sqrt(n_dp * n_z * 2 * rows)

    def over_core(value):
        return lax.ppermute(value, "core", pair_perm)

    def over_z(value, which, back=False):
        pairs = []
        for z in range(n_z):
            for c in range(2):
                if direct:
                    there = z ^ (1 + 2 * c, 3 - 2 * c, 2)[which]
                else:
                    there = (z + (1 if (which == 1) != back else -1)) % n_z
                pairs.append((2 * z + c, 2 * there + c))
        return lax.ppermute(value, axes, pairs)

    def over_dp(value, which):
        pairs = [
            (2 * d + c, 2 * (d ^ (1 + c, 2 - c, 3)[which]) + c) for d in range(n_dp) for c in range(2)
        ]
        return lax.ppermute(value, ("dp", "core"), pairs)

    vmem = pl.BlockSpec(memory_space=pltpu.VMEM)

    def hbm(value):
        return pltpu.with_memory_space_constraint(value, pltpu.HBM)

    q_pair, k_pair, v_pair = over_core(queries), over_core(key_rows), over_core(value_rows)
    og_recv = over_core(out_grad[0])
    mine, og, w_part, gain = call(
        pack_kernel, "pack",
        [
            like((rows, 6 * DH), BF), like((rows, model), BF),
            like((out_weight.shape[0], width), BF), like((1, DH), F32),
        ],
        [hbm(x) for x in (queries, key_rows, value_rows, out_grad, out_weight, norm_gain)],
        scratch=[pltpu.SemaphoreType.DMA((9,))],
        spaces=[pl.BlockSpec(memory_space=pltpu.HBM)] * 6,
    )
    wide = 4 * DH if direct else 2 * DH
    state, pair, to_a, to_b, *rest = call(
        functools.partial(state_kernel, direct), "state",
        [like((DH, DH), F32), like((rows, 6 * DH), BF), like((rows, wide), BF), like((rows, wide), BF)]
        + [like((rows, 2 * DH), BF)] * direct,
        [mine, q_pair, k_pair, v_pair] + [w_part] * direct,
        flops=4 * 2 * rows * DH * DH,
    )
    if direct:
        a, b, c = over_z(to_a, 0), over_z(to_b, 1), [over_z(rest[0], 2)]
        w_keep, w_send = call(
            relay_kernel, "relay", [like((2, half, width), BF)] * 2, [w_part, a, b] + c,
            scratch=[pltpu.VMEM((HEADS, half, width), BF)],
        )
        w_own = call(
            w_rows_kernel, "w_rows", [like((2 * DH, width), BF)], [w_keep, over_core(w_send)]
        )[0]
        w_got = over_dp(w_own, 0)
    else:
        a, b, c = over_z(to_a, 0), over_z(to_b, 1), []
        state = lax.psum(state, "z")
        weights = lax.all_gather(out_weight, axes, axis=0, tiled=True).reshape(2, 2, DH, model)
        weights = [jnp.where(core == 0, weights[:, 0], weights[:, 1]).reshape(2 * DH, model)]

    span = 2 * rows + 2 * HALF
    keep_width = 2 * width if direct else model
    wg_flops = 2 * 2 * rows * DH * model
    qs, ks, vs, ogs, probs, attn, keep_soft, *soft_send = call(
        functools.partial(soft_forward_kernel, direct), "soft_forward",
        [
            like((2 * rows, DH), BF), like((span, DH), BF), like((span, DH), BF),
            like((2 * rows, model), BF), like((2, rows, rows + 2 * HALF), F32), like((2 * rows, DH), F32),
            like((DH, keep_width), F32),
        ] + [like((DH, 2 * width), BF)] * direct,
        [mine, pair, og, og_recv, a, b],
        flops=wg_flops,
    )
    u, total, keep_lin, *sent = call(
        functools.partial(lin_forward_kernel, direct), "lin_forward",
        [like((2 * rows, DH), F32), like((DH, DH), F32), like((DH, keep_width), F32)]
        + [like((2 * DH, 2 * width), BF)] * direct,
        [state, mine, pair, ogs, gain] + ([a, b] + c + soft_send if direct else []),
        flops=wg_flops,
    )
    if direct:
        got = over_dp(sent[0], 0)
        keep, sent = call(
            fold_kernel, "fold", [like((2 * DH, width), F32), like((2 * DH, width), BF)],
            [keep_soft, keep_lin, got],
        )
        w_half = call(
            join_kernel, "w_half", [like((2 * DH, 2 * width), BF)], [w_own, w_got, sent]
        )[0]
        weights = [w_half, over_dp(w_half, 1)]
        got = over_dp(sent, 1)
        row_own, row_send = call(
            rows_kernel, "rows", [like((2 * half, width), F32)] * 2, [keep, got],
            scratch=[pltpu.VMEM((2 * DH, width), F32)],
        )
        row_recv = over_core(row_send)
        piece_send, piece_keep = call(
            chunk_kernel, "chunk", [like((DH, width), BF), like((DH, width), F32)],
            [row_own, row_recv], scratch=[pltpu.VMEM((HEADS, half, width), F32)],
        )
        piece_got = over_z(piece_send, 0)
        weights.append(piece_keep)
    dq_lin, dq_lin_pair, dstate, dq_soft, dk_soft, dv_soft = call(
        functools.partial(backward_kernel, direct), "backward",
        [
            like((rows, DH), BF), like((rows, DH), BF), like((DH, DH), F32),
            like((2 * rows, DH), F32), like((span, DH), F32), like((span, DH), F32),
        ],
        weights + [ogs, u, total, mine, pair, gain, qs, ks, vs, probs, attn],
        scratch=[pltpu.VMEM((2 * rows, 2 * DH), F32), pltpu.VMEM((2 * rows, DH), F32)]
        + [pltpu.VMEM((2 * DH, model), BF)] * direct,
        flops=5 * wg_flops,
    )
    wide = 3 * DH if direct else 2 * DH
    if direct:
        chunk, to_a, to_b, to_c = call(
            second_kernel, "second",
            [
                like((half, width), F32), like((rows, 3 * DH), BF), like((rows, 3 * DH), BF),
                like((rows, 2 * DH), BF),
            ],
            [piece_keep, piece_got, dstate, dk_soft, dv_soft],
        )
        a, b, c = over_z(to_a, 0), over_z(to_b, 1), [over_z(to_c, 2)]
        summed = call(
            functools.partial(weight_sum_kernel, scale), "weight_sum", [like((half, width), BF)],
            [chunk] + c,
        )[0]
        gathered = [over_dp(summed, which) for which in (2, 0, 1)]
        weight_grad = call(
            weight_join_kernel, "weight_join", [like((half, model), F32)], [summed] + gathered
        )[0]
    else:
        to_a, to_b = call(halo_kernel, "halo", [like((rows, 2 * DH), BF)] * 2, [dk_soft, dv_soft])
        a, b = over_z(to_a, 0, True), over_z(to_b, 1, True)
    if not direct:
        dstate = lax.psum(dstate, "z")
        groups = jnp.stack([keep_soft, keep_lin])
        slots = jnp.stack([jnp.where(core == head, groups, 0.0) for head in range(2)], axis=1)
        local = lax.psum_scatter(
            slots.reshape(HEADS * DH, model), axes, scatter_dimension=0, tiled=True
        )
        weight_grad = lax.psum(local, "dp") * scale
    own_out, to_pair = call(
        functools.partial(final_kernel, direct), "final",
        [like((rows, 6 * DH), BF), like((rows, 6 * DH), BF)],
        [dstate, mine, pair, dq_soft, dk_soft, dv_soft, dq_lin, dq_lin_pair, a, b]
        + (c + gathered if direct else []),
        scratch=[pltpu.VMEM((2 * rows, DH), F32)] * 2,
        flops=wg_flops // 4,
    )
    from_pair = over_core(to_pair)
    shape = like((1, rows, HEADS * DH), BF)
    dq, dk, dv = call(output_kernel, "outputs", [shape] * 3, [own_out, from_pair])
    return dq, dk, dv, weight_grad


def solution(mesh):
    n_dp, n_seq = mesh.shape["dp"], mesh.shape["seq"]
    blocks = Mesh(mesh.devices.reshape(n_dp, n_seq // 2, 2), ("dp", "z", "core"))
    tokens, heads = P("dp", ("z", "core"), None), P(("z", "core"), None)
    return jax.shard_map(
        functools.partial(body, n_dp, n_seq // 2),
        mesh=blocks,
        in_specs=(tokens, tokens, tokens, tokens, heads, P()),
        out_specs=(tokens, tokens, tokens, heads),
        check_vma=False,
    )
```

```python
import functools
import math

import jax
import jax.numpy as jnp
from jax import lax
from jax.experimental import pallas as pl
from jax.experimental.pallas import tpu as pltpu
from jax.sharding import Mesh
from jax.sharding import PartitionSpec as P

DH = 128
SOFT_HEADS = 2
LIN_HEADS = 2
HEADS = SOFT_HEADS + LIN_HEADS
WINDOW = 256
HALF = 128
norm_eps = 1e-06
FACTOR = DH ** (-0.5)
BF = jnp.bfloat16
F32 = jnp.float32
NN = (((1,), (0,)), ((), ()))
NT = (((1,), (1,)), ((), ()))
TN = (((0,), (0,)), ((), ()))


def unit_plus(values):
    return jnp.where(values > 0, values + 1.0, jnp.exp(jnp.minimum(values, 0.0)))


def unit_slope(values):
    return jnp.where(values > 0, 1.0, jnp.exp(jnp.minimum(values, 0.0)))


def mm(a, b, dims=NN):
    return lax.dot_general(a, b, dims, preferred_element_type=F32)


def halves(x):
    high = x.astype(BF)
    return high, (x - high.astype(F32)).astype(BF)


def mm3(a, b, dims=NN):
    a_high, a_low = halves(a)
    b_high, b_low = halves(b)
    return mm(a_high, b_high, dims) + (mm(a_high, b_low, dims) + mm(a_low, b_high, dims))


def mm2(a, b, dims=NN):
    a_high, a_low = halves(a)
    return mm(a_high, b, dims) + mm(a_low, b, dims)


def at(start, size=DH):
    return pl.ds(pl.multiple_of(start, size), size)


def places():
    return lax.axis_index("core"), lax.axis_index("z"), lax.axis_index("dp")


def call(kernel, name, outs, args, scratch=(), flops=0, spaces=None):
    vmem = pl.BlockSpec(memory_space=pltpu.VMEM)
    size = sum(math.prod(x.shape) * x.dtype.itemsize for x in list(args) + list(outs))
    return pl.pallas_call(
        kernel,
        name=name,
        out_shape=list(outs),
        in_specs=spaces or [vmem] * len(args),
        out_specs=[vmem] * len(outs),
        scratch_shapes=list(scratch),
        compiler_params=pltpu.CompilerParams(vmem_limit_bytes=24 * 2**20),
        cost_estimate=pl.CostEstimate(flops=flops, bytes_accessed=size, transcendentals=0),
    )(*args)


def like(shape, dtype):
    return jax.ShapeDtypeStruct(shape, dtype)


QS, KS, VS, QL, KL, VL = (slice(i * DH, (i + 1) * DH) for i in range(6))
SOFT = SOFT_HEADS * DH


def links(direct):
    core, z, dp = places()
    step = 1 + core
    turn = lax.rem(z + core, 2) if direct else 1
    return dict(
        first=1 + 2 * core, second=3 - 2 * core, step=step, other=3 - step,
        block_a=1 - turn, block_b=turn,
        halo_a=(1 - turn if direct else 1), halo_b=(turn if direct else 0),
    )


def pack_kernel(q, k, v, og, w, gain, mine_out, og_out, w_out, gain_out, sems):
    core, _, dp = places()
    mine = core * DH
    copies = []

    def fetch(source, target):
        copy = pltpu.make_async_copy(source, target, sems.at[len(copies)])
        copy.start()
        copies.append(copy)

    for index, array in enumerate((q, k, v)):
        for group in range(2):
            cols = slice((3 * group + index) * DH, (3 * group + index + 1) * DH)
            fetch(array.at[0, :, at(SOFT * group + mine)], mine_out.at[:, cols])
    width = w_out.shape[1]
    fetch(w.at[:, at(dp * width, width)], w_out)
    fetch(og.at[0], og_out)
    fetch(gain.at[at(mine)], gain_out.at[0])
    for copy in copies:
        copy.wait()


def state_kernel(direct, mine, q_pair, k_pair, v_pair, *refs):
    if direct:
        w, state, pair, to_a, to_b, to_c = refs
    else:
        state, pair, to_a, to_b = refs
    core, _, _ = places()
    own = core * DH
    for index, source in enumerate((q_pair, k_pair, v_pair)):
        for group in range(2):
            first = (3 * group + index) * DH
            pair[:, first : first + DH] = source[0, :, at(SOFT * group + own)]
    total = mm2(unit_plus(mine[:, KL].astype(F32)), mine[:, VL], TN) + mm2(
        unit_plus(pair[:, KL].astype(F32)), pair[:, VL], TN
    )
    state[...] = total
    way = links(direct)
    for out, block in ((to_a, way["block_a"]), (to_b, way["block_b"])):
        here = block == core
        out[:, :DH] = jnp.where(here, mine[:, KS], pair[:, KS])
        out[:, DH : 2 * DH] = jnp.where(here, mine[:, VS], pair[:, VS])
    if direct:
        rows = w.shape[0]
        for out, first in ((to_a, 2 * DH), (to_b, 2 * DH), (to_c, 0)):
            out[:, first : first + DH] = total.astype(BF)
            out[:rows, first + DH :] = w[:, :DH]
            out[rows:, first + DH :] = w[:, DH:]


def relay_kernel(w, a, b, c, keep, send, heads):
    core, z, _ = places()
    way = links(True)
    rows = w.shape[0]
    heads[z] = w[...]
    for source, first, step in ((a, 3 * DH, way["first"]), (b, 3 * DH, way["second"]), (c, DH, 2)):
        heads[z ^ step, :, :DH] = source[:rows, first:]
        heads[z ^ step, :, DH:] = source[rows:, first:]
    for group in range(2):
        keep[group] = heads[2 * group + core]
        send[group] = heads[2 * group + 1 - core]


def w_rows_kernel(keep, got, out):
    core, _, _ = places()
    half = keep.shape[1]
    for group in range(2):
        out[at(group * DH + core * half, half), :] = keep[group]
        out[at(group * DH + (1 - core) * half, half), :] = got[group]


def join_kernel(first, second, *refs):
    out = refs[-1]
    width = first.shape[1]
    out[:, :width] = first[...]
    out[:, width:] = second[...]


def weight_parts(direct, attn, ogs, send, keep):
    high, low = halves(attn)
    if not direct:
        keep[...] = mm(high, ogs[...], TN) + mm(low, ogs[...], TN)
        return
    _, _, dp = places()
    way = links(True)
    width = send.shape[1] // 2
    for index, step in enumerate((0, way["other"])):
        cols = slice(index * width, (index + 1) * width)
        near, far = at((dp ^ step) * width, width), at((dp ^ step ^ way["step"]) * width, width)
        keep[:, cols] = mm(high, ogs[:, near], TN) + mm(low, ogs[:, near], TN)
        send[:, cols] = (mm(high, ogs[:, far], TN) + mm(low, ogs[:, far], TN)).astype(BF)


def prep_kernel(
    mine, pair, og, og_recv, qs, ks, vs, ogs, scores, phi_high, phi_low, slope
):
    core, _, _ = places()
    rows = og.shape[0]
    for source, wide, place in ((mine, og, core), (pair, og_recv, 1 - core)):
        here = at(place * rows, rows)
        qs[here, :] = source[:, QS]
        ks[here, :] = source[:, KS]
        vs[here, :] = source[:, VS]
        ogs[here, :] = wide[...]
        lin = source[:, QL].astype(F32)
        phi_high[here, :], phi_low[here, :] = halves(unit_plus(lin))
        slope[here, :] = unit_slope(lin)
    for block in range(2):
        scores[block] = mm(qs[block * rows : (block + 1) * rows, :], ks[...], NT) * FACTOR


def soft_forward_kernel(direct, qs, k_chip, v_chip, ogs, chip_scores, a, b, *refs):
    ks, vs, probs, attn, keep, *send = refs
    way = links(direct)
    rows = qs.shape[0] // 2
    span = rows + 2 * HALF
    ks[HALF : HALF + 2 * rows, :] = k_chip[...]
    vs[HALF : HALF + 2 * rows, :] = v_chip[...]
    for source, side in ((a, way["halo_a"]), (b, way["halo_b"])):
        first = side * (HALF + 2 * rows)
        ks[at(first), :] = source[:, :DH]
        vs[at(first), :] = source[:, DH : 2 * DH]
    row_pos = lax.broadcasted_iota(jnp.int32, (rows, span), 0)
    col_pos = lax.broadcasted_iota(jnp.int32, (rows, span), 1)
    inside = (col_pos >= row_pos) & (col_pos < row_pos + WINDOW)
    for block in range(2):
        here, window = slice(block * rows, (block + 1) * rows), slice(block * rows, block * rows + span)
        halo = slice(0, HALF) if block == 0 else slice(HALF + 2 * rows, 2 * HALF + 2 * rows)
        edge = mm(qs[here, :], ks[halo, :], NT) * FACTOR
        parts = [edge, chip_scores[block]] if block == 0 else [chip_scores[block], edge]
        scores = jnp.where(inside, jnp.concatenate(parts, axis=1), -1e30)
        peak = jnp.max(scores, axis=1, keepdims=True)
        terms = jnp.exp(scores - peak)
        share = terms * (1.0 / jnp.sum(terms, axis=1, keepdims=True))
        probs[block] = share
        attn[here, :] = mm(share.astype(BF), vs[window, :])
    weight_parts(direct, attn[...], ogs, send[0] if send else None, keep)


def lin_forward_kernel(direct, state, phi_high, phi_low, ogs, gain, *refs):
    total = state[...]
    if direct:
        a, b, c, soft_send, u_out, total_out, keep, out = refs
        total = total + a[:, 2 * DH : 3 * DH].astype(F32) + b[:, 2 * DH : 3 * DH].astype(F32)
        total = total + c[:, :DH].astype(F32)
    else:
        u_out, total_out, keep = refs
    total_out[...] = total
    high, low = halves(total)
    u = mm(phi_high[...], high) + (mm(phi_high[...], low) + mm(phi_low[...], high))
    u_out[...] = u
    r = lax.rsqrt(jnp.mean(u * u, axis=1, keepdims=True) + norm_eps)
    attn = gain[...] * u * r
    weight_parts(direct, attn, ogs, out.at[DH:, :] if direct else None, keep)
    if direct:
        out[:DH, :] = soft_send[...]


def fold_kernel(keep_soft, keep_lin, got, keep, send):
    width = keep.shape[1]
    for rows, source in ((slice(0, DH), keep_soft), (slice(DH, 2 * DH), keep_lin)):
        keep[rows, :] = source[:, :width] + got[rows, :width].astype(F32)
        send[rows, :] = (source[:, width:] + got[rows, width:].astype(F32)).astype(BF)


def rows_kernel(keep, got, own, send, total):
    core, _, _ = places()
    half = DH // 2
    total[...] = keep[...] + got[...].astype(F32)
    for group in range(2):
        out = slice(group * half, (group + 1) * half)
        own[out, :] = total[at(group * DH + core * half, half), :]
        send[out, :] = total[at(group * DH + (1 - core) * half, half), :]


def lin_backward(u, total, dattn, phi_high, phi_low, slope, gain, dq, dstate):
    u_all = u[...]
    r = lax.rsqrt(jnp.mean(u_all * u_all, axis=1, keepdims=True) + norm_eps)
    lin_grad = gain[...] * dattn[:, DH:]
    grads = r * lin_grad - u_all * (r * r * r) * jnp.mean(lin_grad * u_all, axis=1, keepdims=True)
    high, low = halves(grads)
    dstate[...] = mm(phi_high[...], high, TN) + (mm(phi_high[...], low, TN) + mm(phi_low[...], high, TN))
    dq[...] = (mm3(grads, total[...], NT) * slope[...]).astype(BF)


def soft_backward(qs, ks, vs, probs, attn, dattn, dq_all, dk_all, dv_all):
    rows = qs.shape[0] // 2
    span = rows + 2 * HALF
    dk_all[...] = jnp.zeros_like(dk_all)
    dv_all[...] = jnp.zeros_like(dv_all)
    for block in range(2):
        here, window = slice(block * rows, (block + 1) * rows), slice(block * rows, block * rows + span)
        grad = dattn[here, :DH].astype(BF)
        share = probs[block]
        delta = jnp.sum(grad.astype(F32) * attn[here, :], axis=1, keepdims=True)
        dscore = (share * (mm(grad, vs[window, :], NT) - delta)).astype(BF)
        dq_all[here, :] = mm(dscore, ks[window, :]) * FACTOR
        dk_all[window, :] += mm(dscore, qs[here, :], TN) * FACTOR
        dv_all[window, :] += mm(share.astype(BF), grad, TN)


def backward_kernel(direct, *refs):
    if direct:
        sent, got = refs[:2]
        refs = refs[3:]
    else:
        weights = refs[0]
        refs = refs[1:]
    (ogs, u, total, phi_high, phi_low, slope, gain, qs, ks, vs, probs, attn,
     dq_lin, dstate, dq_soft, dk_soft, dv_soft, dattn, *scratch) = refs
    if direct:
        _, _, dp = places()
        way = links(True)
        weights = scratch[0]
        width = weights.shape[1] // 4
        for source, index, step in (
            (sent, 0, 0), (sent, 1, way["step"]), (got, 0, way["other"]), (got, 1, 3),
        ):
            weights[:, at((dp ^ step) * width, width)] = source[:, index * width : (index + 1) * width]
    dattn[...] = mm(ogs[...], weights[...], NT)
    lin_backward(u, total, dattn, phi_high, phi_low, slope, gain, dq_lin, dstate)
    soft_backward(qs, ks, vs, probs, attn, dattn, dq_soft, dk_soft, dv_soft)


def halo_part(out, first, dk_soft, dv_soft, side):
    start = side * (dk_soft.shape[0] - HALF)
    out[:, first : first + DH] = dk_soft[at(start), :].astype(BF)
    out[:, first + DH : first + 2 * DH] = dv_soft[at(start), :].astype(BF)


def halo_kernel(dk_soft, dv_soft, to_a, to_b):
    way = links(False)
    halo_part(to_a, 0, dk_soft, dv_soft, way["halo_a"])
    halo_part(to_b, 0, dk_soft, dv_soft, way["halo_b"])


def chunk_kernel(own, got, send, keep, heads):
    core, z, _ = places()
    way = links(True)
    half = own.shape[0] // 2
    for group in range(2):
        rows = slice(group * half, (group + 1) * half)
        heads[2 * group + core] = own[rows, :]
        heads[2 * group + 1 - core] = got[rows, :]
    for index, step in enumerate((way["first"], way["second"])):
        send[index * half : (index + 1) * half, :] = heads[z ^ step].astype(BF)
    for index, step in enumerate((0, 2)):
        keep[index * half : (index + 1) * half, :] = heads[z ^ step]


def second_kernel(keep, got, dstate, dk_soft, dv_soft, chunk, to_a, to_b, to_c):
    way = links(True)
    half = chunk.shape[0]
    chunk[...] = keep[:half, :] + got[:half, :].astype(F32)
    for side in range(2):
        cols, rows = slice(side * DH, (side + 1) * DH), slice(side * half, (side + 1) * half)
        piece = keep[half:, cols] + got[half:, cols].astype(F32)
        to_c[rows, DH:] = piece.astype(BF)
    halo_part(to_a, 0, dk_soft, dv_soft, way["halo_a"])
    halo_part(to_b, 0, dk_soft, dv_soft, way["halo_b"])
    low = dstate[...].astype(BF)
    to_a[:, 2 * DH :] = low
    to_b[:, 2 * DH :] = low
    to_c[:, :DH] = low


def weight_sum_kernel(scale, chunk, got, summed):
    half = chunk.shape[0]
    for side in range(2):
        cols, rows = slice(side * DH, (side + 1) * DH), slice(side * half, (side + 1) * half)
        summed[:, cols] = (scale * (chunk[:, cols] + got[rows, DH:].astype(F32))).astype(summed.dtype)


def final_kernel(
    direct, dstate, mine, pair, dq_soft, dk_soft, dv_soft, dq_lin, a, b, *refs
):
    core, _, _ = places()
    way = links(direct)
    rows = mine.shape[0]
    total = dstate[...]
    own_out, pair_out, dk_all, dv_all = refs[-4:]
    if direct:
        total = total + a[:, 2 * DH :].astype(F32) + b[:, 2 * DH :].astype(F32)
        total = total + refs[0][:, :DH].astype(F32)
    for source, out, cols in ((dk_soft, dk_all, slice(0, DH)), (dv_soft, dv_all, slice(DH, 2 * DH))):
        out[...] = source[HALF : HALF + 2 * rows, :]
        out[at(way["block_a"] * rows, rows), :] += a[:, cols].astype(F32)
        out[at(way["block_b"] * rows, rows), :] += b[:, cols].astype(F32)
    high, low = halves(total)
    for source, out, place in ((mine, own_out, core), (pair, pair_out, 1 - core)):
        here = at(place * rows, rows)
        out[:, QS] = dq_soft[here, :].astype(BF)
        out[:, KS] = dk_all[here, :].astype(BF)
        out[:, VS] = dv_all[here, :].astype(BF)
        wide, values = source[:, KL].astype(F32), source[:, VL]
        out[:, QL] = dq_lin[here, :]
        out[:, KL] = ((mm(values, high, NT) + mm(values, low, NT)) * unit_slope(wide)).astype(BF)
        out[:, VL] = mm3(unit_plus(wide), total).astype(BF)


def output_kernel(own, pair, dq, dk, dv):
    core, _, _ = places()
    for source, first in ((own, core * DH), (pair, (1 - core) * DH)):
        for index, out in enumerate((dq, dk, dv)):
            out[0, :, at(first)] = source[:, index * DH : (index + 1) * DH]
            out[0, :, at(SOFT + first)] = source[:, (3 + index) * DH : (4 + index) * DH]


def weight_join_kernel(both, got, _, out):
    _, _, dp = places()
    way = links(True)
    width = both.shape[1] // 2
    for source, index, step in ((both, 0, 0), (both, 1, way["step"]), (got, 0, way["other"]), (got, 1, 3)):
        out[:, at((dp ^ step) * width, width)] = source[:, index * width : (index + 1) * width].astype(F32)


def body(n_dp, n_z, queries, key_rows, value_rows, out_grad, out_weight, norm_gain):
    rows, model = out_grad.shape[1:]
    axes = ("z", "core")
    pair_perm = [(0, 1), (1, 0)]
    core = lax.axis_index("core")
    direct = n_z == HEADS and n_dp == 4
    width = model // n_dp
    half = DH // 2

    scale = 1.0 / math.sqrt(n_dp * n_z * 2 * rows)

    def over_core(value):
        return lax.ppermute(value, "core", pair_perm)

    def over_z(value, which, back=False):
        pairs = []
        for z in range(n_z):
            for c in range(2):
                if direct:
                    there = z ^ (1 + 2 * c, 3 - 2 * c, 2)[which]
                else:
                    there = (z + (1 if (which == 1) != back else -1)) % n_z
                pairs.append((2 * z + c, 2 * there + c))
        return lax.ppermute(value, axes, pairs)

    def over_dp(value, which):
        pairs = [
            (2 * d + c, 2 * (d ^ (1 + c, 2 - c)[which]) + c) for d in range(n_dp) for c in range(2)
        ]
        return lax.ppermute(value, ("dp", "core"), pairs)

    vmem = pl.BlockSpec(memory_space=pltpu.VMEM)

    def hbm(value):
        return pltpu.with_memory_space_constraint(value, pltpu.HBM)

    q_pair, k_pair, v_pair = over_core(queries), over_core(key_rows), over_core(value_rows)
    og_recv = over_core(out_grad[0])
    mine, og, w_part, gain = call(
        pack_kernel, "pack",
        [
            like((rows, 6 * DH), BF), like((rows, model), BF),
            like((out_weight.shape[0], width), BF), like((1, DH), F32),
        ],
        [hbm(x) for x in (queries, key_rows, value_rows, out_grad, out_weight, norm_gain)],
        scratch=[pltpu.SemaphoreType.DMA((9,))],
        spaces=[pl.BlockSpec(memory_space=pltpu.HBM)] * 6,
    )
    wide = 4 * DH if direct else 2 * DH
    state, pair, to_a, to_b, *rest = call(
        functools.partial(state_kernel, direct), "state",
        [like((DH, DH), F32), like((rows, 6 * DH), BF), like((rows, wide), BF), like((rows, wide), BF)]
        + [like((rows, 2 * DH), BF)] * direct,
        [mine, q_pair, k_pair, v_pair] + [w_part] * direct,
        flops=4 * 2 * rows * DH * DH,
    )
    if direct:
        a, b, c = over_z(to_a, 0), over_z(to_b, 1), [over_z(rest[0], 2)]
        w_keep, w_send = call(
            relay_kernel, "relay", [like((2, half, width), BF)] * 2, [w_part, a, b] + c,
            scratch=[pltpu.VMEM((HEADS, half, width), BF)],
        )
        w_own = call(
            w_rows_kernel, "w_rows", [like((2 * DH, width), BF)], [w_keep, over_core(w_send)]
        )[0]
        w_got = over_dp(w_own, 0)
    else:
        a, b, c = over_z(to_a, 0), over_z(to_b, 1), []
        state = lax.psum(state, "z")
        weights = lax.all_gather(out_weight, axes, axis=0, tiled=True).reshape(2, 2, DH, model)
        weights = [jnp.where(core == 0, weights[:, 0], weights[:, 1]).reshape(2 * DH, model)]

    span = 2 * rows + 2 * HALF
    keep_width = 2 * width if direct else model
    wg_flops = 2 * 2 * rows * DH * model
    tokens = like((2 * rows, DH), BF)
    qs, k_chip, v_chip, ogs, chip_scores, phi_high, phi_low, slope = call(
        prep_kernel, "prep",
        [
            tokens, tokens, tokens, like((2 * rows, model), BF), like((2, rows, 2 * rows), F32),
            tokens, tokens, like((2 * rows, DH), F32),
        ],
        [mine, pair, og, og_recv],
        flops=wg_flops // 4,
    )
    ks, vs, probs, attn, keep_soft, *soft_send = call(
        functools.partial(soft_forward_kernel, direct), "soft_forward",
        [
            like((span, DH), BF), like((span, DH), BF), like((2, rows, rows + 2 * HALF), F32),
            like((2 * rows, DH), F32), like((DH, keep_width), F32),
        ] + [like((DH, 2 * width), BF)] * direct,
        [qs, k_chip, v_chip, ogs, chip_scores, a, b],
        flops=wg_flops,
    )
    u, total, keep_lin, *sent = call(
        functools.partial(lin_forward_kernel, direct), "lin_forward",
        [like((2 * rows, DH), F32), like((DH, DH), F32), like((DH, keep_width), F32)]
        + [like((2 * DH, 2 * width), BF)] * direct,
        [state, phi_high, phi_low, ogs, gain] + ([a, b] + c + soft_send if direct else []),
        flops=wg_flops,
    )
    if direct:
        got = over_dp(sent[0], 0)
        keep, sent = call(
            fold_kernel, "fold", [like((2 * DH, width), F32), like((2 * DH, width), BF)],
            [keep_soft, keep_lin, got],
        )
        w_half = call(
            join_kernel, "w_half", [like((2 * DH, 2 * width), BF)], [w_own, w_got, sent]
        )[0]
        weights = [w_half, over_dp(w_half, 1)]
        got = over_dp(sent, 1)
        row_own, row_send = call(
            rows_kernel, "rows", [like((2 * half, width), F32)] * 2, [keep, got],
            scratch=[pltpu.VMEM((2 * DH, width), F32)],
        )
        row_recv = over_core(row_send)
        piece_send, piece_keep = call(
            chunk_kernel, "chunk", [like((DH, width), BF), like((DH, width), F32)],
            [row_own, row_recv], scratch=[pltpu.VMEM((HEADS, half, width), F32)],
        )
        piece_got = over_z(piece_send, 0)
        weights.append(piece_keep)
    dq_lin, dstate, dq_soft, dk_soft, dv_soft = call(
        functools.partial(backward_kernel, direct), "backward",
        [
            tokens, like((DH, DH), F32),
            like((2 * rows, DH), F32), like((span, DH), F32), like((span, DH), F32),
        ],
        weights + [ogs, u, total, phi_high, phi_low, slope, gain, qs, ks, vs, probs, attn],
        scratch=[pltpu.VMEM((2 * rows, 2 * DH), F32)]
        + [pltpu.VMEM((2 * DH, model), BF)] * direct,
        flops=5 * wg_flops,
    )
    wide = 3 * DH if direct else 2 * DH
    if direct:
        chunk, to_a, to_b, to_c = call(
            second_kernel, "second",
            [
                like((half, width), F32), like((rows, 3 * DH), BF), like((rows, 3 * DH), BF),
                like((rows, 2 * DH), BF),
            ],
            [piece_keep, piece_got, dstate, dk_soft, dv_soft],
        )
        a, b, c = over_z(to_a, 0), over_z(to_b, 1), [over_z(to_c, 2)]
        summed = call(
            functools.partial(weight_sum_kernel, scale), "weight_sum", [like((half, width), BF)],
            [chunk] + c,
        )[0]
        got = over_dp(summed, 0)
        both = call(join_kernel, "both", [like((half, 2 * width), BF)], [summed, got])[0]
        gathered = over_dp(both, 1)
    else:
        to_a, to_b = call(halo_kernel, "halo", [like((rows, 2 * DH), BF)] * 2, [dk_soft, dv_soft])
        a, b = over_z(to_a, 0, True), over_z(to_b, 1, True)
    if not direct:
        dstate = lax.psum(dstate, "z")
        groups = jnp.stack([keep_soft, keep_lin])
        slots = jnp.stack([jnp.where(core == head, groups, 0.0) for head in range(2)], axis=1)
        local = lax.psum_scatter(
            slots.reshape(HEADS * DH, model), axes, scatter_dimension=0, tiled=True
        )
        weight_grad = lax.psum(local, "dp") * scale
    own_out, to_pair = call(
        functools.partial(final_kernel, direct), "final",
        [like((rows, 6 * DH), BF), like((rows, 6 * DH), BF)],
        [dstate, mine, pair, dq_soft, dk_soft, dv_soft, dq_lin, a, b]
        + (c + [both] if direct else []),
        scratch=[pltpu.VMEM((2 * rows, DH), F32)] * 2,
        flops=wg_flops // 4,
    )
    from_pair = over_core(to_pair)
    shape = like((1, rows, HEADS * DH), BF)
    dq, dk, dv = call(output_kernel, "outputs", [shape] * 3, [own_out, from_pair])
    if direct:
        weight_grad = call(
            weight_join_kernel, "weight_join", [like((half, model), F32)], [both, gathered, hbm(dq)],
            spaces=[vmem, vmem, pl.BlockSpec(memory_space=pltpu.HBM)],
        )[0]
    return dq, dk, dv, weight_grad


def solution(mesh):
    n_dp, n_seq = mesh.shape["dp"], mesh.shape["seq"]
    blocks = Mesh(mesh.devices.reshape(n_dp, n_seq // 2, 2), ("dp", "z", "core"))
    tokens, heads = P("dp", ("z", "core"), None), P(("z", "core"), None)
    return jax.shard_map(
        functools.partial(body, n_dp, n_seq // 2),
        mesh=blocks,
        in_specs=(tokens, tokens, tokens, tokens, heads, P()),
        out_specs=(tokens, tokens, tokens, heads),
        check_vma=False,
    )
```

```python
import functools
import math

import jax
import jax.numpy as jnp
from jax import lax
from jax.experimental import pallas as pl
from jax.experimental.pallas import tpu as pltpu
from jax.sharding import Mesh
from jax.sharding import PartitionSpec as P

DH = 128
SOFT_HEADS = 2
LIN_HEADS = 2
HEADS = SOFT_HEADS + LIN_HEADS
WINDOW = 256
HALF = 128
norm_eps = 1e-06
FACTOR = DH ** (-0.5)
BF = jnp.bfloat16
F32 = jnp.float32
NN = (((1,), (0,)), ((), ()))
NT = (((1,), (1,)), ((), ()))
TN = (((0,), (0,)), ((), ()))


def unit_plus(values):
    return jnp.where(values > 0, values + 1.0, jnp.exp(jnp.minimum(values, 0.0)))


def unit_slope(values):
    return jnp.where(values > 0, 1.0, jnp.exp(jnp.minimum(values, 0.0)))


def mm(a, b, dims=NN):
    return lax.dot_general(a, b, dims, preferred_element_type=F32)


def halves(x):
    high = x.astype(BF)
    return high, (x - high.astype(F32)).astype(BF)


def mm3(a, b, dims=NN):
    a_high, a_low = halves(a)
    b_high, b_low = halves(b)
    return mm(a_high, b_high, dims) + (mm(a_high, b_low, dims) + mm(a_low, b_high, dims))


def mm2(a, b, dims=NN):
    a_high, a_low = halves(a)
    return mm(a_high, b, dims) + mm(a_low, b, dims)


def at(start, size=DH):
    return pl.ds(pl.multiple_of(start, size), size)


def places():
    return lax.axis_index("core"), lax.axis_index("z"), lax.axis_index("dp")


def call(kernel, name, outs, args, scratch=(), flops=0, spaces=None):
    vmem = pl.BlockSpec(memory_space=pltpu.VMEM)
    size = sum(math.prod(x.shape) * x.dtype.itemsize for x in list(args) + list(outs))
    return pl.pallas_call(
        kernel,
        name=name,
        out_shape=list(outs),
        in_specs=spaces or [vmem] * len(args),
        out_specs=[vmem] * len(outs),
        scratch_shapes=list(scratch),
        compiler_params=pltpu.CompilerParams(vmem_limit_bytes=24 * 2**20),
        cost_estimate=pl.CostEstimate(flops=flops, bytes_accessed=size, transcendentals=0),
    )(*args)


def like(shape, dtype):
    return jax.ShapeDtypeStruct(shape, dtype)


QS, KS, VS, QL, KL, VL = (slice(i * DH, (i + 1) * DH) for i in range(6))
SOFT = SOFT_HEADS * DH


def links(direct):
    core, z, dp = places()
    step = 1 + core
    turn = lax.rem(z + core, 2) if direct else 1
    return dict(
        first=1 + 2 * core, second=3 - 2 * core, step=step, other=3 - step,
        block_a=1 - turn, block_b=turn,
        halo_a=(1 - turn if direct else 1), halo_b=(turn if direct else 0),
    )


def pack_kernel(q, k, v, og, w, gain, mine_out, og_out, w_out, gain_out, sems):
    core, _, dp = places()
    mine = core * DH
    copies = []

    def fetch(source, target):
        copy = pltpu.make_async_copy(source, target, sems.at[len(copies)])
        copy.start()
        copies.append(copy)

    for index, array in enumerate((q, k, v)):
        for group in range(2):
            cols = slice((3 * group + index) * DH, (3 * group + index + 1) * DH)
            fetch(array.at[0, :, at(SOFT * group + mine)], mine_out.at[:, cols])
    width = w_out.shape[1]
    fetch(w.at[:, at(dp * width, width)], w_out)
    fetch(og.at[0], og_out)
    fetch(gain.at[at(mine)], gain_out.at[0])
    for copy in copies:
        copy.wait()


def state_kernel(direct, mine, q_pair, k_pair, v_pair, *refs):
    if direct:
        w, state, pair, to_a, to_b, to_c = refs
    else:
        state, pair, to_a, to_b = refs
    core, _, _ = places()
    own = core * DH
    for index, source in enumerate((q_pair, k_pair, v_pair)):
        for group in range(2):
            first = (3 * group + index) * DH
            pair[:, first : first + DH] = source[0, :, at(SOFT * group + own)]
    total = mm2(unit_plus(mine[:, KL].astype(F32)), mine[:, VL], TN) + mm2(
        unit_plus(pair[:, KL].astype(F32)), pair[:, VL], TN
    )
    state[...] = total
    way = links(direct)
    for out, block in ((to_a, way["block_a"]), (to_b, way["block_b"])):
        here = block == core
        out[:, :DH] = jnp.where(here, mine[:, KS], pair[:, KS])
        out[:, DH : 2 * DH] = jnp.where(here, mine[:, VS], pair[:, VS])
    if direct:
        rows = w.shape[0]
        for out, first in ((to_a, 2 * DH), (to_b, 2 * DH), (to_c, 0)):
            out[:, first : first + DH] = total.astype(BF)
            out[:rows, first + DH :] = w[:, :DH]
            out[rows:, first + DH :] = w[:, DH:]


def relay_kernel(w, a, b, c, keep, send, heads):
    core, z, _ = places()
    way = links(True)
    rows = w.shape[0]
    heads[z] = w[...]
    for source, first, step in ((a, 3 * DH, way["first"]), (b, 3 * DH, way["second"]), (c, DH, 2)):
        heads[z ^ step, :, :DH] = source[:rows, first:]
        heads[z ^ step, :, DH:] = source[rows:, first:]
    for group in range(2):
        keep[group] = heads[2 * group + core]
        send[group] = heads[2 * group + 1 - core]


def w_rows_kernel(keep, got, out):
    core, _, _ = places()
    half = keep.shape[1]
    for group in range(2):
        out[at(group * DH + core * half, half), :] = keep[group]
        out[at(group * DH + (1 - core) * half, half), :] = got[group]


def join_kernel(first, second, *refs):
    out = refs[-1]
    width = first.shape[1]
    out[:, :width] = first[...]
    out[:, width:] = second[...]


def weight_parts(direct, attn, ogs, send, keep):
    both = jnp.concatenate(halves(attn), axis=1)

    def product(cols):
        wide = mm(both, cols, TN)
        return wide[:DH] + wide[DH:]

    if not direct:
        keep[...] = product(ogs[...])
        return
    _, _, dp = places()
    way = links(True)
    width = send.shape[1] // 2
    for index, step in enumerate((0, way["other"])):
        cols = slice(index * width, (index + 1) * width)
        near, far = at((dp ^ step) * width, width), at((dp ^ step ^ way["step"]) * width, width)
        keep[:, cols] = product(ogs[:, near])
        send[:, cols] = product(ogs[:, far]).astype(BF)


def mm_pair(a_high, a_low, b, dims, axis):
    b_high, b_low = halves(b)
    wide = mm(a_high, jnp.concatenate([b_high, b_low], axis=axis), dims)
    return wide[:, :DH] + (wide[:, DH:] + mm(a_low, b_high, dims))


def prep_kernel(
    mine, pair, og, og_recv, qs, ks, vs, ogs, scores, phi_high, phi_low, slope
):
    core, _, _ = places()
    rows = og.shape[0]
    for source, wide, place in ((mine, og, core), (pair, og_recv, 1 - core)):
        here = at(place * rows, rows)
        qs[here, :] = source[:, QS]
        ks[here, :] = source[:, KS]
        vs[here, :] = source[:, VS]
        ogs[here, :] = wide[...]
        lin = source[:, QL].astype(F32)
        phi_high[here, :], phi_low[here, :] = halves(unit_plus(lin))
        slope[here, :] = unit_slope(lin)
    for block in range(2):
        scores[block] = mm(qs[block * rows : (block + 1) * rows, :], ks[...], NT) * FACTOR


def soft_forward_kernel(direct, qs, k_chip, v_chip, ogs, chip_scores, a, b, *refs):
    ks, vs, probs, attn, keep, *send = refs
    way = links(direct)
    rows = qs.shape[0] // 2
    span = rows + 2 * HALF
    ks[HALF : HALF + 2 * rows, :] = k_chip[...]
    vs[HALF : HALF + 2 * rows, :] = v_chip[...]
    for source, side in ((a, way["halo_a"]), (b, way["halo_b"])):
        first = side * (HALF + 2 * rows)
        ks[at(first), :] = source[:, :DH]
        vs[at(first), :] = source[:, DH : 2 * DH]
    row_pos = lax.broadcasted_iota(jnp.int32, (rows, span), 0)
    col_pos = lax.broadcasted_iota(jnp.int32, (rows, span), 1)
    inside = (col_pos >= row_pos) & (col_pos < row_pos + WINDOW)
    for block in range(2):
        here, window = slice(block * rows, (block + 1) * rows), slice(block * rows, block * rows + span)
        halo = slice(0, HALF) if block == 0 else slice(HALF + 2 * rows, 2 * HALF + 2 * rows)
        edge = mm(qs[here, :], ks[halo, :], NT) * FACTOR
        parts = [edge, chip_scores[block]] if block == 0 else [chip_scores[block], edge]
        scores = jnp.where(inside, jnp.concatenate(parts, axis=1), -1e30)
        peak = jnp.max(scores, axis=1, keepdims=True)
        terms = jnp.exp(scores - peak)
        share = terms * (1.0 / jnp.sum(terms, axis=1, keepdims=True))
        probs[block] = share
        attn[here, :] = mm(share.astype(BF), vs[window, :])
    weight_parts(direct, attn[...], ogs, send[0] if send else None, keep)


def lin_forward_kernel(direct, state, phi_high, phi_low, ogs, gain, *refs):
    total = state[...]
    if direct:
        a, b, c, soft_send, u_out, total_out, keep, out = refs
        total = total + a[:, 2 * DH : 3 * DH].astype(F32) + b[:, 2 * DH : 3 * DH].astype(F32)
        total = total + c[:, :DH].astype(F32)
    else:
        u_out, total_out, keep = refs
    total_out[...] = total
    u = mm_pair(phi_high[...], phi_low[...], total, NN, 1)
    u_out[...] = u
    r = lax.rsqrt(jnp.mean(u * u, axis=1, keepdims=True) + norm_eps)
    attn = gain[...] * u * r
    weight_parts(direct, attn, ogs, out.at[DH:, :] if direct else None, keep)
    if direct:
        out[:DH, :] = soft_send[...]


def fold_kernel(keep_soft, keep_lin, got, keep, send):
    width = keep.shape[1]
    for rows, source in ((slice(0, DH), keep_soft), (slice(DH, 2 * DH), keep_lin)):
        keep[rows, :] = source[:, :width] + got[rows, :width].astype(F32)
        send[rows, :] = (source[:, width:] + got[rows, width:].astype(F32)).astype(BF)


def rows_kernel(keep, got, own, send, total):
    core, _, _ = places()
    half = DH // 2
    total[...] = keep[...] + got[...].astype(F32)
    for group in range(2):
        out = slice(group * half, (group + 1) * half)
        own[out, :] = total[at(group * DH + core * half, half), :]
        send[out, :] = total[at(group * DH + (1 - core) * half, half), :]


def lin_backward(u, total, dattn, phi_high, phi_low, slope, gain, dq, dstate):
    u_all = u[...]
    r = lax.rsqrt(jnp.mean(u_all * u_all, axis=1, keepdims=True) + norm_eps)
    lin_grad = gain[...] * dattn[:, DH:]
    grads = r * lin_grad - u_all * (r * r * r) * jnp.mean(lin_grad * u_all, axis=1, keepdims=True)
    dstate[...] = mm_pair(phi_high[...], phi_low[...], grads, TN, 1)
    dq[...] = (mm_pair(*halves(grads), total[...], NT, 0) * slope[...]).astype(BF)


def soft_backward(qs, ks, vs, probs, attn, dattn, dq_all, dk_all, dv_all):
    rows = qs.shape[0] // 2
    span = rows + 2 * HALF
    dk_all[...] = jnp.zeros_like(dk_all)
    dv_all[...] = jnp.zeros_like(dv_all)
    for block in range(2):
        here, window = slice(block * rows, (block + 1) * rows), slice(block * rows, block * rows + span)
        grad = dattn[here, :DH].astype(BF)
        share = probs[block]
        delta = jnp.sum(grad.astype(F32) * attn[here, :], axis=1, keepdims=True)
        dscore = (share * (mm(grad, vs[window, :], NT) - delta)).astype(BF)
        dq_all[here, :] = mm(dscore, ks[window, :]) * FACTOR
        dk_all[window, :] += mm(dscore, qs[here, :], TN) * FACTOR
        dv_all[window, :] += mm(share.astype(BF), grad, TN)


def backward_kernel(direct, *refs):
    if direct:
        sent, got = refs[:2]
        refs = refs[3:]
    else:
        weights = refs[0]
        refs = refs[1:]
    (ogs, u, total, phi_high, phi_low, slope, gain, qs, ks, vs, probs, attn,
     dq_lin, dstate, dq_soft, dk_soft, dv_soft, dattn, *scratch) = refs
    if direct:
        _, _, dp = places()
        way = links(True)
        weights = scratch[0]
        width = weights.shape[1] // 4
        for source, index, step in (
            (sent, 0, 0), (sent, 1, way["step"]), (got, 0, way["other"]), (got, 1, 3),
        ):
            weights[:, at((dp ^ step) * width, width)] = source[:, index * width : (index + 1) * width]
    dattn[...] = mm(ogs[...], weights[...], NT)
    lin_backward(u, total, dattn, phi_high, phi_low, slope, gain, dq_lin, dstate)
    soft_backward(qs, ks, vs, probs, attn, dattn, dq_soft, dk_soft, dv_soft)


def halo_part(out, first, dk_soft, dv_soft, side):
    start = side * (dk_soft.shape[0] - HALF)
    out[:, first : first + DH] = dk_soft[at(start), :].astype(BF)
    out[:, first + DH : first + 2 * DH] = dv_soft[at(start), :].astype(BF)


def halo_kernel(dk_soft, dv_soft, to_a, to_b):
    way = links(False)
    halo_part(to_a, 0, dk_soft, dv_soft, way["halo_a"])
    halo_part(to_b, 0, dk_soft, dv_soft, way["halo_b"])


def chunk_kernel(own, got, send, keep, heads):
    core, z, _ = places()
    way = links(True)
    half = own.shape[0] // 2
    for group in range(2):
        rows = slice(group * half, (group + 1) * half)
        heads[2 * group + core] = own[rows, :]
        heads[2 * group + 1 - core] = got[rows, :]
    for index, step in enumerate((way["first"], way["second"])):
        send[index * half : (index + 1) * half, :] = heads[z ^ step].astype(BF)
    for index, step in enumerate((0, 2)):
        keep[index * half : (index + 1) * half, :] = heads[z ^ step]


def second_kernel(keep, got, dstate, dk_soft, dv_soft, chunk, to_a, to_b, to_c):
    way = links(True)
    half = chunk.shape[0]
    chunk[...] = keep[:half, :] + got[:half, :].astype(F32)
    for side in range(2):
        cols, rows = slice(side * DH, (side + 1) * DH), slice(side * half, (side + 1) * half)
        piece = keep[half:, cols] + got[half:, cols].astype(F32)
        to_c[rows, DH:] = piece.astype(BF)
    halo_part(to_a, 0, dk_soft, dv_soft, way["halo_a"])
    halo_part(to_b, 0, dk_soft, dv_soft, way["halo_b"])
    low = dstate[...].astype(BF)
    to_a[:, 2 * DH :] = low
    to_b[:, 2 * DH :] = low
    to_c[:, :DH] = low


def weight_sum_kernel(scale, chunk, got, summed):
    half = chunk.shape[0]
    for side in range(2):
        cols, rows = slice(side * DH, (side + 1) * DH), slice(side * half, (side + 1) * half)
        summed[:, cols] = (scale * (chunk[:, cols] + got[rows, DH:].astype(F32))).astype(summed.dtype)


def final_kernel(
    direct, dstate, mine, pair, dq_soft, dk_soft, dv_soft, dq_lin, a, b, *refs
):
    core, _, _ = places()
    way = links(direct)
    rows = mine.shape[0]
    total = dstate[...]
    own_out, pair_out, dk_all, dv_all = refs[-4:]
    if direct:
        total = total + a[:, 2 * DH :].astype(F32) + b[:, 2 * DH :].astype(F32)
        total = total + refs[0][:, :DH].astype(F32)
    for source, out, cols in ((dk_soft, dk_all, slice(0, DH)), (dv_soft, dv_all, slice(DH, 2 * DH))):
        out[...] = source[HALF : HALF + 2 * rows, :]
        out[at(way["block_a"] * rows, rows), :] += a[:, cols].astype(F32)
        out[at(way["block_b"] * rows, rows), :] += b[:, cols].astype(F32)
    high, low = halves(total)
    for source, out, place in ((mine, own_out, core), (pair, pair_out, 1 - core)):
        here = at(place * rows, rows)
        out[:, QS] = dq_soft[here, :].astype(BF)
        out[:, KS] = dk_all[here, :].astype(BF)
        out[:, VS] = dv_all[here, :].astype(BF)
        wide, values = source[:, KL].astype(F32), source[:, VL]
        out[:, QL] = dq_lin[here, :]
        out[:, KL] = ((mm(values, high, NT) + mm(values, low, NT)) * unit_slope(wide)).astype(BF)
        out[:, VL] = mm3(unit_plus(wide), total).astype(BF)


def output_kernel(own, pair, dq, dk, dv):
    core, _, _ = places()
    for source, first in ((own, core * DH), (pair, (1 - core) * DH)):
        for index, out in enumerate((dq, dk, dv)):
            out[0, :, at(first)] = source[:, index * DH : (index + 1) * DH]
            out[0, :, at(SOFT + first)] = source[:, (3 + index) * DH : (4 + index) * DH]


def weight_join_kernel(both, got, _, out):
    _, _, dp = places()
    way = links(True)
    width = both.shape[1] // 2
    for source, index, step in ((both, 0, 0), (both, 1, way["step"]), (got, 0, way["other"]), (got, 1, 3)):
        out[:, at((dp ^ step) * width, width)] = source[:, index * width : (index + 1) * width].astype(F32)


def body(n_dp, n_z, queries, key_rows, value_rows, out_grad, out_weight, norm_gain):
    rows, model = out_grad.shape[1:]
    axes = ("z", "core")
    pair_perm = [(0, 1), (1, 0)]
    core = lax.axis_index("core")
    direct = n_z == HEADS and n_dp == 4
    width = model // n_dp
    half = DH // 2

    scale = 1.0 / math.sqrt(n_dp * n_z * 2 * rows)

    def over_core(value):
        return lax.ppermute(value, "core", pair_perm)

    def over_z(value, which, back=False):
        pairs = []
        for z in range(n_z):
            for c in range(2):
                if direct:
                    there = z ^ (1 + 2 * c, 3 - 2 * c, 2)[which]
                else:
                    there = (z + (1 if (which == 1) != back else -1)) % n_z
                pairs.append((2 * z + c, 2 * there + c))
        return lax.ppermute(value, axes, pairs)

    def over_dp(value, which):
        pairs = [
            (2 * d + c, 2 * (d ^ (1 + c, 2 - c)[which]) + c) for d in range(n_dp) for c in range(2)
        ]
        return lax.ppermute(value, ("dp", "core"), pairs)

    vmem = pl.BlockSpec(memory_space=pltpu.VMEM)

    def hbm(value):
        return pltpu.with_memory_space_constraint(value, pltpu.HBM)

    q_pair, k_pair, v_pair = over_core(queries), over_core(key_rows), over_core(value_rows)
    og_recv = over_core(out_grad[0])
    mine, og, w_part, gain = call(
        pack_kernel, "pack",
        [
            like((rows, 6 * DH), BF), like((rows, model), BF),
            like((out_weight.shape[0], width), BF), like((1, DH), F32),
        ],
        [hbm(x) for x in (queries, key_rows, value_rows, out_grad, out_weight, norm_gain)],
        scratch=[pltpu.SemaphoreType.DMA((9,))],
        spaces=[pl.BlockSpec(memory_space=pltpu.HBM)] * 6,
    )
    wide = 4 * DH if direct else 2 * DH
    state, pair, to_a, to_b, *rest = call(
        functools.partial(state_kernel, direct), "state",
        [like((DH, DH), F32), like((rows, 6 * DH), BF), like((rows, wide), BF), like((rows, wide), BF)]
        + [like((rows, 2 * DH), BF)] * direct,
        [mine, q_pair, k_pair, v_pair] + [w_part] * direct,
        flops=4 * 2 * rows * DH * DH,
    )
    if direct:
        a, b, c = over_z(to_a, 0), over_z(to_b, 1), [over_z(rest[0], 2)]
        w_keep, w_send = call(
            relay_kernel, "relay", [like((2, half, width), BF)] * 2, [w_part, a, b] + c,
            scratch=[pltpu.VMEM((HEADS, half, width), BF)],
        )
        w_own = call(
            w_rows_kernel, "w_rows", [like((2 * DH, width), BF)], [w_keep, over_core(w_send)]
        )[0]
        w_got = over_dp(w_own, 0)
    else:
        a, b, c = over_z(to_a, 0), over_z(to_b, 1), []
        state = lax.psum(state, "z")
        weights = lax.all_gather(out_weight, axes, axis=0, tiled=True).reshape(2, 2, DH, model)
        weights = [jnp.where(core == 0, weights[:, 0], weights[:, 1]).reshape(2 * DH, model)]

    span = 2 * rows + 2 * HALF
    keep_width = 2 * width if direct else model
    wg_flops = 2 * 2 * rows * DH * model
    tokens = like((2 * rows, DH), BF)
    qs, k_chip, v_chip, ogs, chip_scores, phi_high, phi_low, slope = call(
        prep_kernel, "prep",
        [
            tokens, tokens, tokens, like((2 * rows, model), BF), like((2, rows, 2 * rows), F32),
            tokens, tokens, like((2 * rows, DH), F32),
        ],
        [mine, pair, og, og_recv],
        flops=wg_flops // 4,
    )
    ks, vs, probs, attn, keep_soft, *soft_send = call(
        functools.partial(soft_forward_kernel, direct), "soft_forward",
        [
            like((span, DH), BF), like((span, DH), BF), like((2, rows, rows + 2 * HALF), F32),
            like((2 * rows, DH), F32), like((DH, keep_width), F32),
        ] + [like((DH, 2 * width), BF)] * direct,
        [qs, k_chip, v_chip, ogs, chip_scores, a, b],
        flops=wg_flops,
    )
    u, total, keep_lin, *sent = call(
        functools.partial(lin_forward_kernel, direct), "lin_forward",
        [like((2 * rows, DH), F32), like((DH, DH), F32), like((DH, keep_width), F32)]
        + [like((2 * DH, 2 * width), BF)] * direct,
        [state, phi_high, phi_low, ogs, gain] + ([a, b] + c + soft_send if direct else []),
        flops=wg_flops,
    )
    if direct:
        got = over_dp(sent[0], 0)
        keep, sent = call(
            fold_kernel, "fold", [like((2 * DH, width), F32), like((2 * DH, width), BF)],
            [keep_soft, keep_lin, got],
        )
        w_half = call(
            join_kernel, "w_half", [like((2 * DH, 2 * width), BF)], [w_own, w_got, sent]
        )[0]
        weights = [w_half, over_dp(w_half, 1)]
        got = over_dp(sent, 1)
        row_own, row_send = call(
            rows_kernel, "rows", [like((2 * half, width), F32)] * 2, [keep, got],
            scratch=[pltpu.VMEM((2 * DH, width), F32)],
        )
        row_recv = over_core(row_send)
        piece_send, piece_keep = call(
            chunk_kernel, "chunk", [like((DH, width), BF), like((DH, width), F32)],
            [row_own, row_recv], scratch=[pltpu.VMEM((HEADS, half, width), F32)],
        )
        piece_got = over_z(piece_send, 0)
        weights.append(piece_keep)
    dq_lin, dstate, dq_soft, dk_soft, dv_soft = call(
        functools.partial(backward_kernel, direct), "backward",
        [
            tokens, like((DH, DH), F32),
            like((2 * rows, DH), F32), like((span, DH), F32), like((span, DH), F32),
        ],
        weights + [ogs, u, total, phi_high, phi_low, slope, gain, qs, ks, vs, probs, attn],
        scratch=[pltpu.VMEM((2 * rows, 2 * DH), F32)]
        + [pltpu.VMEM((2 * DH, model), BF)] * direct,
        flops=5 * wg_flops,
    )
    wide = 3 * DH if direct else 2 * DH
    if direct:
        chunk, to_a, to_b, to_c = call(
            second_kernel, "second",
            [
                like((half, width), F32), like((rows, 3 * DH), BF), like((rows, 3 * DH), BF),
                like((rows, 2 * DH), BF),
            ],
            [piece_keep, piece_got, dstate, dk_soft, dv_soft],
        )
        a, b, c = over_z(to_a, 0), over_z(to_b, 1), [over_z(to_c, 2)]
        summed = call(
            functools.partial(weight_sum_kernel, scale), "weight_sum", [like((half, width), BF)],
            [chunk] + c,
        )[0]
        got = over_dp(summed, 0)
        both = call(join_kernel, "both", [like((half, 2 * width), BF)], [summed, got])[0]
        gathered = over_dp(both, 1)
    else:
        to_a, to_b = call(halo_kernel, "halo", [like((rows, 2 * DH), BF)] * 2, [dk_soft, dv_soft])
        a, b = over_z(to_a, 0, True), over_z(to_b, 1, True)
    if not direct:
        dstate = lax.psum(dstate, "z")
        groups = jnp.stack([keep_soft, keep_lin])
        slots = jnp.stack([jnp.where(core == head, groups, 0.0) for head in range(2)], axis=1)
        local = lax.psum_scatter(
            slots.reshape(HEADS * DH, model), axes, scatter_dimension=0, tiled=True
        )
        weight_grad = lax.psum(local, "dp") * scale
    own_out, to_pair = call(
        functools.partial(final_kernel, direct), "final",
        [like((rows, 6 * DH), BF), like((rows, 6 * DH), BF)],
        [dstate, mine, pair, dq_soft, dk_soft, dv_soft, dq_lin, a, b]
        + (c + [both] if direct else []),
        scratch=[pltpu.VMEM((2 * rows, DH), F32)] * 2,
        flops=wg_flops // 4,
    )
    from_pair = over_core(to_pair)
    shape = like((1, rows, HEADS * DH), BF)
    dq, dk, dv = call(output_kernel, "outputs", [shape] * 3, [own_out, from_pair])
    if direct:
        weight_grad = call(
            weight_join_kernel, "weight_join", [like((half, model), F32)], [both, gathered, hbm(dq)],
            spaces=[vmem, vmem, pl.BlockSpec(memory_space=pltpu.HBM)],
        )[0]
    return dq, dk, dv, weight_grad


def solution(mesh):
    n_dp, n_seq = mesh.shape["dp"], mesh.shape["seq"]
    blocks = Mesh(mesh.devices.reshape(n_dp, n_seq // 2, 2), ("dp", "z", "core"))
    tokens, heads = P("dp", ("z", "core"), None), P(("z", "core"), None)
    return jax.shard_map(
        functools.partial(body, n_dp, n_seq // 2),
        mesh=blocks,
        in_specs=(tokens, tokens, tokens, tokens, heads, P()),
        out_specs=(tokens, tokens, tokens, heads),
        check_vma=False,
    )
```

```python
import functools
import math

import jax
import jax.numpy as jnp
from jax import lax
from jax.experimental import pallas as pl
from jax.experimental.pallas import tpu as pltpu
from jax.sharding import Mesh
from jax.sharding import PartitionSpec as P

DH = 128
SOFT_HEADS = 2
LIN_HEADS = 2
HEADS = SOFT_HEADS + LIN_HEADS
WINDOW = 256
HALF = 128
norm_eps = 1e-06
FACTOR = DH ** (-0.5)
BF = jnp.bfloat16
F32 = jnp.float32
NN = (((1,), (0,)), ((), ()))
NT = (((1,), (1,)), ((), ()))
TN = (((0,), (0,)), ((), ()))


def unit_plus(values):
    return jnp.where(values > 0, values + 1.0, jnp.exp(jnp.minimum(values, 0.0)))


def unit_slope(values):
    return jnp.where(values > 0, 1.0, jnp.exp(jnp.minimum(values, 0.0)))


def mm(a, b, dims=NN):
    return lax.dot_general(a, b, dims, preferred_element_type=F32)


def halves(x):
    high = x.astype(BF)
    return high, (x - high.astype(F32)).astype(BF)


def mm3(a, b, dims=NN):
    a_high, a_low = halves(a)
    b_high, b_low = halves(b)
    return mm(a_high, b_high, dims) + (mm(a_high, b_low, dims) + mm(a_low, b_high, dims))


def mm2(a, b, dims=NN):
    a_high, a_low = halves(a)
    return mm(a_high, b, dims) + mm(a_low, b, dims)


def at(start, size=DH):
    return pl.ds(pl.multiple_of(start, size), size)


def places():
    return lax.axis_index("core"), lax.axis_index("z"), lax.axis_index("dp")


def call(kernel, name, outs, args, scratch=(), flops=0, spaces=None):
    vmem = pl.BlockSpec(memory_space=pltpu.VMEM)
    size = sum(math.prod(x.shape) * x.dtype.itemsize for x in list(args) + list(outs))
    return pl.pallas_call(
        kernel,
        name=name,
        out_shape=list(outs),
        in_specs=spaces or [vmem] * len(args),
        out_specs=[vmem] * len(outs),
        scratch_shapes=list(scratch),
        compiler_params=pltpu.CompilerParams(vmem_limit_bytes=24 * 2**20),
        cost_estimate=pl.CostEstimate(flops=flops, bytes_accessed=size, transcendentals=0),
    )(*args)


def like(shape, dtype):
    return jax.ShapeDtypeStruct(shape, dtype)


QS, KS, VS, QL, KL, VL = (slice(i * DH, (i + 1) * DH) for i in range(6))
SOFT = SOFT_HEADS * DH


def links(direct):
    core, z, dp = places()
    step = 1 + core
    turn = lax.rem(z + core, 2) if direct else 1
    return dict(
        first=1 + 2 * core, second=3 - 2 * core, step=step, other=3 - step,
        block_a=1 - turn, block_b=turn,
        halo_a=(1 - turn if direct else 1), halo_b=(turn if direct else 0),
    )


def pack_kernel(q, k, v, og, w, gain, mine_out, og_out, w_out, gain_out, sems):
    core, _, dp = places()
    mine = core * DH
    copies = []

    def fetch(source, target):
        copy = pltpu.make_async_copy(source, target, sems.at[len(copies)])
        copy.start()
        copies.append(copy)

    for index, array in enumerate((q, k, v)):
        for group in range(2):
            cols = slice((3 * group + index) * DH, (3 * group + index + 1) * DH)
            fetch(array.at[0, :, at(SOFT * group + mine)], mine_out.at[:, cols])
    width = w_out.shape[1]
    fetch(w.at[:, at(dp * width, width)], w_out)
    fetch(og.at[0], og_out)
    fetch(gain.at[at(mine)], gain_out.at[0])
    for copy in copies:
        copy.wait()


def state_kernel(direct, mine, q_pair, k_pair, v_pair, *refs):
    if direct:
        w, state, pair, to_a, to_b, to_c = refs
    else:
        state, pair, to_a, to_b = refs
    core, _, _ = places()
    own = core * DH
    for index, source in enumerate((q_pair, k_pair, v_pair)):
        for group in range(2):
            first = (3 * group + index) * DH
            pair[:, first : first + DH] = source[0, :, at(SOFT * group + own)]
    total = mm2(unit_plus(mine[:, KL].astype(F32)), mine[:, VL], TN) + mm2(
        unit_plus(pair[:, KL].astype(F32)), pair[:, VL], TN
    )
    state[...] = total
    way = links(direct)
    for out, block in ((to_a, way["block_a"]), (to_b, way["block_b"])):
        here = block == core
        out[:, :DH] = jnp.where(here, mine[:, KS], pair[:, KS])
        out[:, DH : 2 * DH] = jnp.where(here, mine[:, VS], pair[:, VS])
    if direct:
        rows = w.shape[0]
        for out, first in ((to_a, 2 * DH), (to_b, 2 * DH), (to_c, 0)):
            out[:, first : first + DH] = total.astype(BF)
            out[:rows, first + DH :] = w[:, :DH]
            out[rows:, first + DH :] = w[:, DH:]


def relay_kernel(w, a, b, c, keep, send, heads):
    core, z, _ = places()
    way = links(True)
    rows = w.shape[0]
    heads[z] = w[...]
    for source, first, step in ((a, 3 * DH, way["first"]), (b, 3 * DH, way["second"]), (c, DH, 2)):
        heads[z ^ step, :, :DH] = source[:rows, first:]
        heads[z ^ step, :, DH:] = source[rows:, first:]
    for group in range(2):
        keep[group] = heads[2 * group + core]
        send[group] = heads[2 * group + 1 - core]


def w_rows_kernel(keep, got, out):
    core, _, _ = places()
    half = keep.shape[1]
    for group in range(2):
        out[at(group * DH + core * half, half), :] = keep[group]
        out[at(group * DH + (1 - core) * half, half), :] = got[group]


def join_kernel(first, second, *refs):
    out = refs[-1]
    width = first.shape[1]
    out[:, :width] = first[...]
    out[:, width:] = second[...]


def weight_parts(direct, attn, ogs, send, keep):
    high, low = halves(attn)
    if not direct:
        keep[...] = mm(high, ogs[...], TN) + mm(low, ogs[...], TN)
        return
    _, _, dp = places()
    way = links(True)
    width = send.shape[1] // 2
    for index, step in enumerate((0, way["other"])):
        cols = slice(index * width, (index + 1) * width)
        near, far = at((dp ^ step) * width, width), at((dp ^ step ^ way["step"]) * width, width)
        keep[:, cols] = mm(high, ogs[:, near], TN) + mm(low, ogs[:, near], TN)
        send[:, cols] = (mm(high, ogs[:, far], TN) + mm(low, ogs[:, far], TN)).astype(BF)


def prep_kernel(
    mine, pair, og, og_recv, qs, ks, vs, ogs, scores, phi_high, phi_low, slope
):
    core, _, _ = places()
    rows = og.shape[0]
    for source, wide, place in ((mine, og, core), (pair, og_recv, 1 - core)):
        here = at(place * rows, rows)
        qs[here, :] = source[:, QS]
        ks[here, :] = source[:, KS]
        vs[here, :] = source[:, VS]
        ogs[here, :] = wide[...]
        lin = source[:, QL].astype(F32)
        phi_high[here, :], phi_low[here, :] = halves(unit_plus(lin))
        slope[here, :] = unit_slope(lin)
    for block in range(2):
        scores[block] = mm(qs[block * rows : (block + 1) * rows, :], ks[...], NT) * FACTOR


def soft_forward_kernel(direct, qs, k_chip, v_chip, ogs, chip_scores, a, b, *refs):
    ks, vs, probs, attn, keep, *send = refs
    way = links(direct)
    rows = qs.shape[0] // 2
    span = rows + 2 * HALF
    ks[HALF : HALF + 2 * rows, :] = k_chip[...]
    vs[HALF : HALF + 2 * rows, :] = v_chip[...]
    for source, side in ((a, way["halo_a"]), (b, way["halo_b"])):
        first = side * (HALF + 2 * rows)
        ks[at(first), :] = source[:, :DH]
        vs[at(first), :] = source[:, DH : 2 * DH]
    row_pos = lax.broadcasted_iota(jnp.int32, (rows, span), 0)
    col_pos = lax.broadcasted_iota(jnp.int32, (rows, span), 1)
    inside = (col_pos >= row_pos) & (col_pos < row_pos + WINDOW)
    for block in range(2):
        here, window = slice(block * rows, (block + 1) * rows), slice(block * rows, block * rows + span)
        halo = slice(0, HALF) if block == 0 else slice(HALF + 2 * rows, 2 * HALF + 2 * rows)
        edge = mm(qs[here, :], ks[halo, :], NT) * FACTOR
        parts = [edge, chip_scores[block]] if block == 0 else [chip_scores[block], edge]
        scores = jnp.where(inside, jnp.concatenate(parts, axis=1), -1e30)
        peak = jnp.max(scores, axis=1, keepdims=True)
        terms = jnp.exp(scores - peak)
        share = terms * (1.0 / jnp.sum(terms, axis=1, keepdims=True))
        probs[block] = share
        attn[here, :] = mm(share.astype(BF), vs[window, :])
    weight_parts(direct, attn[...], ogs, send[0] if send else None, keep)


def lin_forward_kernel(direct, state, phi_high, phi_low, ogs, gain, *refs):
    total = state[...]
    if direct:
        a, b, c, soft_send, u_out, total_out, keep, out = refs
        total = total + a[:, 2 * DH : 3 * DH].astype(F32) + b[:, 2 * DH : 3 * DH].astype(F32)
        total = total + c[:, :DH].astype(F32)
    else:
        u_out, total_out, keep = refs
    total_out[...] = total
    high, low = halves(total)
    u = mm(phi_high[...], high) + (mm(phi_high[...], low) + mm(phi_low[...], high))
    u_out[...] = u
    r = lax.rsqrt(jnp.mean(u * u, axis=1, keepdims=True) + norm_eps)
    attn = gain[...] * u * r
    weight_parts(direct, attn, ogs, out.at[DH:, :] if direct else None, keep)
    if direct:
        out[:DH, :] = soft_send[...]


def fold_kernel(keep_soft, keep_lin, got, keep, send):
    width = keep.shape[1]
    for rows, source in ((slice(0, DH), keep_soft), (slice(DH, 2 * DH), keep_lin)):
        keep[rows, :] = source[:, :width] + got[rows, :width].astype(F32)
        send[rows, :] = (source[:, width:] + got[rows, width:].astype(F32)).astype(BF)


def rows_kernel(keep, got, own, send, total):
    core, _, _ = places()
    half = DH // 2
    total[...] = keep[...] + got[...].astype(F32)
    for group in range(2):
        out = slice(group * half, (group + 1) * half)
        own[out, :] = total[at(group * DH + core * half, half), :]
        send[out, :] = total[at(group * DH + (1 - core) * half, half), :]


def lin_backward(u, total, dattn, phi_high, phi_low, slope, gain, dq, dstate):
    u_all = u[...]
    r = lax.rsqrt(jnp.mean(u_all * u_all, axis=1, keepdims=True) + norm_eps)
    lin_grad = gain[...] * dattn[:, DH:]
    grads = r * lin_grad - u_all * (r * r * r) * jnp.mean(lin_grad * u_all, axis=1, keepdims=True)
    high, low = halves(grads)
    dstate[...] = mm(phi_high[...], high, TN) + (mm(phi_high[...], low, TN) + mm(phi_low[...], high, TN))
    dq[...] = (mm3(grads, total[...], NT) * slope[...]).astype(BF)


def soft_backward(qs, ks, vs, probs, attn, dattn, dq_all, dk_all, dv_all):
    rows = qs.shape[0] // 2
    span = rows + 2 * HALF
    dk_all[...] = jnp.zeros_like(dk_all)
    dv_all[...] = jnp.zeros_like(dv_all)
    for block in range(2):
        here, window = slice(block * rows, (block + 1) * rows), slice(block * rows, block * rows + span)
        grad = dattn[here, :DH].astype(BF)
        share = probs[block]
        delta = jnp.sum(grad.astype(F32) * attn[here, :], axis=1, keepdims=True)
        dscore = (share * (mm(grad, vs[window, :], NT) - delta)).astype(BF)
        dq_all[here, :] = mm(dscore, ks[window, :]) * FACTOR
        dk_all[window, :] += mm(dscore, qs[here, :], TN) * FACTOR
        dv_all[window, :] += mm(share.astype(BF), grad, TN)


def backward_kernel(direct, *refs):
    if direct:
        sent, got = refs[:2]
        refs = refs[3:]
    else:
        weights = refs[0]
        refs = refs[1:]
    (ogs, u, total, phi_high, phi_low, slope, gain, qs, ks, vs, probs, attn,
     dq_lin, dstate, dq_soft, dk_soft, dv_soft, dattn, *scratch) = refs
    if direct:
        _, _, dp = places()
        way = links(True)
        weights = scratch[0]
        width = weights.shape[1] // 4
        for source, index, step in (
            (sent, 0, 0), (sent, 1, way["step"]), (got, 0, way["other"]), (got, 1, 3),
        ):
            weights[:, at((dp ^ step) * width, width)] = source[:, index * width : (index + 1) * width]
    dattn[...] = mm(ogs[...], weights[...], NT)
    lin_backward(u, total, dattn, phi_high, phi_low, slope, gain, dq_lin, dstate)
    soft_backward(qs, ks, vs, probs, attn, dattn, dq_soft, dk_soft, dv_soft)


def halo_part(out, first, dk_soft, dv_soft, side):
    start = side * (dk_soft.shape[0] - HALF)
    out[:, first : first + DH] = dk_soft[at(start), :].astype(BF)
    out[:, first + DH : first + 2 * DH] = dv_soft[at(start), :].astype(BF)


def halo_kernel(dk_soft, dv_soft, to_a, to_b):
    way = links(False)
    halo_part(to_a, 0, dk_soft, dv_soft, way["halo_a"])
    halo_part(to_b, 0, dk_soft, dv_soft, way["halo_b"])


def chunk_kernel(own, got, send, keep, heads):
    core, z, _ = places()
    way = links(True)
    half = own.shape[0] // 2
    for group in range(2):
        rows = slice(group * half, (group + 1) * half)
        heads[2 * group + core] = own[rows, :]
        heads[2 * group + 1 - core] = got[rows, :]
    for index, step in enumerate((way["first"], way["second"])):
        send[index * half : (index + 1) * half, :] = heads[z ^ step].astype(BF)
    for index, step in enumerate((0, 2)):
        keep[index * half : (index + 1) * half, :] = heads[z ^ step]


def second_kernel(keep, got, chunk, send):
    half = chunk.shape[0]
    chunk[...] = keep[:half, :] + got[:half, :].astype(F32)
    send[...] = (keep[half:, :] + got[half:, :].astype(F32)).astype(BF)


def halo_direct_kernel(dstate, dk_soft, dv_soft, to_a, to_b, to_c):
    way = links(True)
    halo_part(to_a, 0, dk_soft, dv_soft, way["halo_a"])
    halo_part(to_b, 0, dk_soft, dv_soft, way["halo_b"])
    low = dstate[...].astype(BF)
    to_a[:, 2 * DH :] = low
    to_b[:, 2 * DH :] = low
    to_c[...] = low


def weight_sum_kernel(scale, chunk, got, summed):
    summed[...] = (scale * (chunk[...] + got[...].astype(F32))).astype(summed.dtype)


def final_kernel(
    direct, dstate, mine, pair, dq_soft, dk_soft, dv_soft, dq_lin, a, b, *refs
):
    core, _, _ = places()
    way = links(direct)
    rows = mine.shape[0]
    total = dstate[...]
    own_out, pair_out, dk_all, dv_all = refs[-4:]
    if direct:
        total = total + a[:, 2 * DH :].astype(F32) + b[:, 2 * DH :].astype(F32)
        total = total + refs[0][...].astype(F32)
    for source, out, cols in ((dk_soft, dk_all, slice(0, DH)), (dv_soft, dv_all, slice(DH, 2 * DH))):
        out[...] = source[HALF : HALF + 2 * rows, :]
        out[at(way["block_a"] * rows, rows), :] += a[:, cols].astype(F32)
        out[at(way["block_b"] * rows, rows), :] += b[:, cols].astype(F32)
    high, low = halves(total)
    for source, out, place in ((mine, own_out, core), (pair, pair_out, 1 - core)):
        here = at(place * rows, rows)
        out[:, QS] = dq_soft[here, :].astype(BF)
        out[:, KS] = dk_all[here, :].astype(BF)
        out[:, VS] = dv_all[here, :].astype(BF)
        wide, values = source[:, KL].astype(F32), source[:, VL]
        out[:, QL] = dq_lin[here, :]
        out[:, KL] = ((mm(values, high, NT) + mm(values, low, NT)) * unit_slope(wide)).astype(BF)
        out[:, VL] = mm3(unit_plus(wide), total).astype(BF)


def output_kernel(own, pair, dq, dk, dv):
    core, _, _ = places()
    for source, first in ((own, core * DH), (pair, (1 - core) * DH)):
        for index, out in enumerate((dq, dk, dv)):
            out[0, :, at(first)] = source[:, index * DH : (index + 1) * DH]
            out[0, :, at(SOFT + first)] = source[:, (3 + index) * DH : (4 + index) * DH]


def weight_join_kernel(both, got, _, out):
    _, _, dp = places()
    way = links(True)
    width = both.shape[1] // 2
    for source, index, step in ((both, 0, 0), (both, 1, way["step"]), (got, 0, way["other"]), (got, 1, 3)):
        out[:, at((dp ^ step) * width, width)] = source[:, index * width : (index + 1) * width].astype(F32)


def body(n_dp, n_z, queries, key_rows, value_rows, out_grad, out_weight, norm_gain):
    rows, model = out_grad.shape[1:]
    axes = ("z", "core")
    pair_perm = [(0, 1), (1, 0)]
    core = lax.axis_index("core")
    direct = n_z == HEADS and n_dp == 4
    width = model // n_dp
    half = DH // 2

    scale = 1.0 / math.sqrt(n_dp * n_z * 2 * rows)

    def over_core(value):
        return lax.ppermute(value, "core", pair_perm)

    def over_z(value, which, back=False):
        pairs = []
        for z in range(n_z):
            for c in range(2):
                if direct:
                    there = z ^ (1 + 2 * c, 3 - 2 * c, 2)[which]
                else:
                    there = (z + (1 if (which == 1) != back else -1)) % n_z
                pairs.append((2 * z + c, 2 * there + c))
        return lax.ppermute(value, axes, pairs)

    def over_dp(value, which):
        pairs = [
            (2 * d + c, 2 * (d ^ (1 + c, 2 - c)[which]) + c) for d in range(n_dp) for c in range(2)
        ]
        return lax.ppermute(value, ("dp", "core"), pairs)

    vmem = pl.BlockSpec(memory_space=pltpu.VMEM)

    def hbm(value):
        return pltpu.with_memory_space_constraint(value, pltpu.HBM)

    q_pair, k_pair, v_pair = over_core(queries), over_core(key_rows), over_core(value_rows)
    og_recv = over_core(out_grad[0])
    mine, og, w_part, gain = call(
        pack_kernel, "pack",
        [
            like((rows, 6 * DH), BF), like((rows, model), BF),
            like((out_weight.shape[0], width), BF), like((1, DH), F32),
        ],
        [hbm(x) for x in (queries, key_rows, value_rows, out_grad, out_weight, norm_gain)],
        scratch=[pltpu.SemaphoreType.DMA((9,))],
        spaces=[pl.BlockSpec(memory_space=pltpu.HBM)] * 6,
    )
    wide = 4 * DH if direct else 2 * DH
    state, pair, to_a, to_b, *rest = call(
        functools.partial(state_kernel, direct), "state",
        [like((DH, DH), F32), like((rows, 6 * DH), BF), like((rows, wide), BF), like((rows, wide), BF)]
        + [like((rows, 2 * DH), BF)] * direct,
        [mine, q_pair, k_pair, v_pair] + [w_part] * direct,
        flops=4 * 2 * rows * DH * DH,
    )
    if direct:
        a, b, c = over_z(to_a, 0), over_z(to_b, 1), [over_z(rest[0], 2)]
        w_keep, w_send = call(
            relay_kernel, "relay", [like((2, half, width), BF)] * 2, [w_part, a, b] + c,
            scratch=[pltpu.VMEM((HEADS, half, width), BF)],
        )
        w_own = call(
            w_rows_kernel, "w_rows", [like((2 * DH, width), BF)], [w_keep, over_core(w_send)]
        )[0]
        w_got = over_dp(w_own, 0)
    else:
        a, b, c = over_z(to_a, 0), over_z(to_b, 1), []
        state = lax.psum(state, "z")
        weights = lax.all_gather(out_weight, axes, axis=0, tiled=True).reshape(2, 2, DH, model)
        weights = [jnp.where(core == 0, weights[:, 0], weights[:, 1]).reshape(2 * DH, model)]

    span = 2 * rows + 2 * HALF
    keep_width = 2 * width if direct else model
    wg_flops = 2 * 2 * rows * DH * model
    tokens = like((2 * rows, DH), BF)
    qs, k_chip, v_chip, ogs, chip_scores, phi_high, phi_low, slope = call(
        prep_kernel, "prep",
        [
            tokens, tokens, tokens, like((2 * rows, model), BF), like((2, rows, 2 * rows), F32),
            tokens, tokens, like((2 * rows, DH), F32),
        ],
        [mine, pair, og, og_recv],
        flops=wg_flops // 4,
    )
    ks, vs, probs, attn, keep_soft, *soft_send = call(
        functools.partial(soft_forward_kernel, direct), "soft_forward",
        [
            like((span, DH), BF), like((span, DH), BF), like((2, rows, rows + 2 * HALF), F32),
            like((2 * rows, DH), F32), like((DH, keep_width), F32),
        ] + [like((DH, 2 * width), BF)] * direct,
        [qs, k_chip, v_chip, ogs, chip_scores, a, b],
        flops=wg_flops,
    )
    u, total, keep_lin, *sent = call(
        functools.partial(lin_forward_kernel, direct), "lin_forward",
        [like((2 * rows, DH), F32), like((DH, DH), F32), like((DH, keep_width), F32)]
        + [like((2 * DH, 2 * width), BF)] * direct,
        [state, phi_high, phi_low, ogs, gain] + ([a, b] + c + soft_send if direct else []),
        flops=wg_flops,
    )
    if direct:
        got = over_dp(sent[0], 0)
        keep, sent = call(
            fold_kernel, "fold", [like((2 * DH, width), F32), like((2 * DH, width), BF)],
            [keep_soft, keep_lin, got],
        )
        w_half = call(
            join_kernel, "w_half", [like((2 * DH, 2 * width), BF)], [w_own, w_got, sent]
        )[0]
        weights = [w_half, over_dp(w_half, 1)]
        got = over_dp(sent, 1)
        row_own, row_send = call(
            rows_kernel, "rows", [like((2 * half, width), F32)] * 2, [keep, got],
            scratch=[pltpu.VMEM((2 * DH, width), F32)],
        )
        row_recv = over_core(row_send)
        piece_send, piece_keep = call(
            chunk_kernel, "chunk", [like((DH, width), BF), like((DH, width), F32)],
            [row_own, row_recv], scratch=[pltpu.VMEM((HEADS, half, width), F32)],
        )
        piece_got = over_z(piece_send, 0)
        weights.append(piece_keep)
    dq_lin, dstate, dq_soft, dk_soft, dv_soft = call(
        functools.partial(backward_kernel, direct), "backward",
        [
            tokens, like((DH, DH), F32),
            like((2 * rows, DH), F32), like((span, DH), F32), like((span, DH), F32),
        ],
        weights + [ogs, u, total, phi_high, phi_low, slope, gain, qs, ks, vs, probs, attn],
        scratch=[pltpu.VMEM((2 * rows, 2 * DH), F32)]
        + [pltpu.VMEM((2 * DH, model), BF)] * direct,
        flops=5 * wg_flops,
    )
    wide = 3 * DH if direct else 2 * DH
    if direct:
        chunk, piece = call(
            second_kernel, "second", [like((half, width), F32), like((half, width), BF)],
            [piece_keep, piece_got],
        )
        summed = call(
            functools.partial(weight_sum_kernel, scale), "weight_sum", [like((half, width), BF)],
            [chunk, over_z(piece, 2)],
        )[0]
        to_a, to_b, to_c = call(
            halo_direct_kernel, "halo", [like((rows, 3 * DH), BF)] * 2 + [like((DH, DH), BF)],
            [dstate, dk_soft, dv_soft],
        )
        a, b, c = over_z(to_a, 0), over_z(to_b, 1), [over_z(to_c, 2)]
        got = over_dp(summed, 0)
        both = call(join_kernel, "both", [like((half, 2 * width), BF)], [summed, got])[0]
        gathered = over_dp(both, 1)
    else:
        to_a, to_b = call(halo_kernel, "halo", [like((rows, 2 * DH), BF)] * 2, [dk_soft, dv_soft])
        a, b = over_z(to_a, 0, True), over_z(to_b, 1, True)
    if not direct:
        dstate = lax.psum(dstate, "z")
        groups = jnp.stack([keep_soft, keep_lin])
        slots = jnp.stack([jnp.where(core == head, groups, 0.0) for head in range(2)], axis=1)
        local = lax.psum_scatter(
            slots.reshape(HEADS * DH, model), axes, scatter_dimension=0, tiled=True
        )
        weight_grad = lax.psum(local, "dp") * scale
    own_out, to_pair = call(
        functools.partial(final_kernel, direct), "final",
        [like((rows, 6 * DH), BF), like((rows, 6 * DH), BF)],
        [dstate, mine, pair, dq_soft, dk_soft, dv_soft, dq_lin, a, b]
        + (c + [gathered] if direct else []),
        scratch=[pltpu.VMEM((2 * rows, DH), F32)] * 2,
        flops=wg_flops // 4,
    )
    from_pair = over_core(to_pair)
    shape = like((1, rows, HEADS * DH), BF)
    dq, dk, dv = call(output_kernel, "outputs", [shape] * 3, [own_out, from_pair])
    if direct:
        weight_grad = call(
            weight_join_kernel, "weight_join", [like((half, model), F32)], [both, gathered, hbm(dq)],
            spaces=[vmem, vmem, pl.BlockSpec(memory_space=pltpu.HBM)],
        )[0]
    return dq, dk, dv, weight_grad


def solution(mesh):
    n_dp, n_seq = mesh.shape["dp"], mesh.shape["seq"]
    blocks = Mesh(mesh.devices.reshape(n_dp, n_seq // 2, 2), ("dp", "z", "core"))
    tokens, heads = P("dp", ("z", "core"), None), P(("z", "core"), None)
    return jax.shard_map(
        functools.partial(body, n_dp, n_seq // 2),
        mesh=blocks,
        in_specs=(tokens, tokens, tokens, tokens, heads, P()),
        out_specs=(tokens, tokens, tokens, heads),
        check_vma=False,
    )
```

```python
import functools
import math

import jax
import jax.numpy as jnp
from jax import lax
from jax.experimental import pallas as pl
from jax.experimental.pallas import tpu as pltpu
from jax.sharding import Mesh
from jax.sharding import PartitionSpec as P

DH = 128
SOFT_HEADS = 2
LIN_HEADS = 2
HEADS = SOFT_HEADS + LIN_HEADS
WINDOW = 256
HALF = 128
norm_eps = 1e-06
FACTOR = DH ** (-0.5)
BF = jnp.bfloat16
F32 = jnp.float32
NN = (((1,), (0,)), ((), ()))
NT = (((1,), (1,)), ((), ()))
TN = (((0,), (0,)), ((), ()))


def unit_plus(values):
    return jnp.where(values > 0, values + 1.0, jnp.exp(jnp.minimum(values, 0.0)))


def unit_slope(values):
    return jnp.where(values > 0, 1.0, jnp.exp(jnp.minimum(values, 0.0)))


def mm(a, b, dims=NN):
    return lax.dot_general(a, b, dims, preferred_element_type=F32)


def halves(x):
    high = x.astype(BF)
    return high, (x - high.astype(F32)).astype(BF)


def mm3(a, b, dims=NN):
    a_high, a_low = halves(a)
    b_high, b_low = halves(b)
    return mm(a_high, b_high, dims) + (mm(a_high, b_low, dims) + mm(a_low, b_high, dims))


def mm2(a, b, dims=NN):
    a_high, a_low = halves(a)
    return mm(a_high, b, dims) + mm(a_low, b, dims)


def at(start, size=DH):
    return pl.ds(pl.multiple_of(start, size), size)


def places():
    return lax.axis_index("core"), lax.axis_index("z"), lax.axis_index("dp")


def call(kernel, name, outs, args, scratch=(), flops=0, spaces=None):
    vmem = pl.BlockSpec(memory_space=pltpu.VMEM)
    size = sum(math.prod(x.shape) * x.dtype.itemsize for x in list(args) + list(outs))
    return pl.pallas_call(
        kernel,
        name=name,
        out_shape=list(outs),
        in_specs=spaces or [vmem] * len(args),
        out_specs=[vmem] * len(outs),
        scratch_shapes=list(scratch),
        compiler_params=pltpu.CompilerParams(vmem_limit_bytes=24 * 2**20),
        cost_estimate=pl.CostEstimate(flops=flops, bytes_accessed=size, transcendentals=0),
    )(*args)


def like(shape, dtype):
    return jax.ShapeDtypeStruct(shape, dtype)


QS, KS, VS, QL, KL, VL = (slice(i * DH, (i + 1) * DH) for i in range(6))
SOFT = SOFT_HEADS * DH


def links(direct):
    core, z, dp = places()
    step = 1 + core
    turn = lax.rem(z + core, 2) if direct else 1
    return dict(
        first=1 + 2 * core, second=3 - 2 * core, step=step, other=3 - step,
        block_a=1 - turn, block_b=turn,
        halo_a=(1 - turn if direct else 1), halo_b=(turn if direct else 0),
    )


def pack_kernel(q, k, v, og, w, gain, mine_out, og_out, w_out, gain_out, sems):
    core, _, dp = places()
    mine = core * DH
    copies = []

    def fetch(source, target):
        copy = pltpu.make_async_copy(source, target, sems.at[len(copies)])
        copy.start()
        copies.append(copy)

    for index, array in enumerate((q, k, v)):
        for group in range(2):
            cols = slice((3 * group + index) * DH, (3 * group + index + 1) * DH)
            fetch(array.at[0, :, at(SOFT * group + mine)], mine_out.at[:, cols])
    width = w_out.shape[1]
    fetch(w.at[:, at(dp * width, width)], w_out)
    fetch(og.at[0], og_out)
    fetch(gain.at[at(mine)], gain_out.at[0])
    for copy in copies:
        copy.wait()


def state_kernel(direct, mine, q_pair, k_pair, v_pair, *refs):
    if direct:
        w, state, pair, to_a, to_b, to_c = refs
    else:
        state, pair, to_a, to_b = refs
    core, _, _ = places()
    own = core * DH
    for index, source in enumerate((q_pair, k_pair, v_pair)):
        for group in range(2):
            first = (3 * group + index) * DH
            pair[:, first : first + DH] = source[0, :, at(SOFT * group + own)]
    total = mm2(unit_plus(mine[:, KL].astype(F32)), mine[:, VL], TN) + mm2(
        unit_plus(pair[:, KL].astype(F32)), pair[:, VL], TN
    )
    state[...] = total
    way = links(direct)
    for out, block in ((to_a, way["block_a"]), (to_b, way["block_b"])):
        here = block == core
        out[:, :DH] = jnp.where(here, mine[:, KS], pair[:, KS])
        out[:, DH : 2 * DH] = jnp.where(here, mine[:, VS], pair[:, VS])
    if direct:
        rows = w.shape[0]
        for out, first in ((to_a, 2 * DH), (to_b, 2 * DH), (to_c, 0)):
            out[:, first : first + DH] = total.astype(BF)
            out[:rows, first + DH :] = w[:, :DH]
            out[rows:, first + DH :] = w[:, DH:]


def relay_kernel(w, a, b, c, keep, send, heads):
    core, z, _ = places()
    way = links(True)
    rows = w.shape[0]
    heads[z] = w[...]
    for source, first, step in ((a, 3 * DH, way["first"]), (b, 3 * DH, way["second"]), (c, DH, 2)):
        heads[z ^ step, :, :DH] = source[:rows, first:]
        heads[z ^ step, :, DH:] = source[rows:, first:]
    for group in range(2):
        keep[group] = heads[2 * group + core]
        send[group] = heads[2 * group + 1 - core]


def w_rows_kernel(keep, got, out):
    core, _, _ = places()
    half = keep.shape[1]
    for group in range(2):
        out[at(group * DH + core * half, half), :] = keep[group]
        out[at(group * DH + (1 - core) * half, half), :] = got[group]


def join_kernel(first, second, *refs):
    out = refs[-1]
    width = first.shape[1]
    out[:, :width] = first[...]
    out[:, width:] = second[...]


def weight_parts(direct, attn, ogs, send, keep):
    high, low = halves(attn)
    if not direct:
        keep[...] = mm(high, ogs[...], TN) + mm(low, ogs[...], TN)
        return
    _, _, dp = places()
    way = links(True)
    width = send.shape[1] // 2
    for index, step in enumerate((0, way["other"])):
        cols = slice(index * width, (index + 1) * width)
        near, far = at((dp ^ step) * width, width), at((dp ^ step ^ way["step"]) * width, width)
        keep[:, cols] = mm(high, ogs[:, near], TN) + mm(low, ogs[:, near], TN)
        send[:, cols] = (mm(high, ogs[:, far], TN) + mm(low, ogs[:, far], TN)).astype(BF)


def prep_kernel(
    mine, pair, og, og_recv, qs, ks, vs, ogs, scores, phi_high, phi_low, slope
):
    core, _, _ = places()
    rows = og.shape[0]
    for source, wide, place in ((mine, og, core), (pair, og_recv, 1 - core)):
        here = at(place * rows, rows)
        qs[here, :] = source[:, QS]
        ks[here, :] = source[:, KS]
        vs[here, :] = source[:, VS]
        ogs[here, :] = wide[...]
        lin = source[:, QL].astype(F32)
        phi_high[here, :], phi_low[here, :] = halves(unit_plus(lin))
        slope[here, :] = unit_slope(lin)
    for block in range(2):
        scores[block] = mm(qs[block * rows : (block + 1) * rows, :], ks[...], NT) * FACTOR


def soft_forward_kernel(direct, qs, k_chip, v_chip, ogs, chip_scores, a, b, *refs):
    ks, vs, probs, attn, keep, *send = refs
    way = links(direct)
    rows = qs.shape[0] // 2
    span = rows + 2 * HALF
    ks[HALF : HALF + 2 * rows, :] = k_chip[...]
    vs[HALF : HALF + 2 * rows, :] = v_chip[...]
    for source, side in ((a, way["halo_a"]), (b, way["halo_b"])):
        first = side * (HALF + 2 * rows)
        ks[at(first), :] = source[:, :DH]
        vs[at(first), :] = source[:, DH : 2 * DH]
    row_pos = lax.broadcasted_iota(jnp.int32, (rows, span), 0)
    col_pos = lax.broadcasted_iota(jnp.int32, (rows, span), 1)
    inside = (col_pos >= row_pos) & (col_pos < row_pos + WINDOW)
    for block in range(2):
        here, window = slice(block * rows, (block + 1) * rows), slice(block * rows, block * rows + span)
        halo = slice(0, HALF) if block == 0 else slice(HALF + 2 * rows, 2 * HALF + 2 * rows)
        edge = mm(qs[here, :], ks[halo, :], NT) * FACTOR
        parts = [edge, chip_scores[block]] if block == 0 else [chip_scores[block], edge]
        scores = jnp.where(inside, jnp.concatenate(parts, axis=1), -1e30)
        peak = jnp.max(scores, axis=1, keepdims=True)
        terms = jnp.exp(scores - peak)
        share = terms * (1.0 / jnp.sum(terms, axis=1, keepdims=True))
        probs[block] = share
        attn[here, :] = mm(share.astype(BF), vs[window, :])
    weight_parts(direct, attn[...], ogs, send[0] if send else None, keep)


def lin_forward_kernel(direct, state, phi_high, phi_low, ogs, gain, *refs):
    total = state[...]
    if direct:
        a, b, c, soft_send, u_out, total_out, keep, out = refs
        total = total + a[:, 2 * DH : 3 * DH].astype(F32) + b[:, 2 * DH : 3 * DH].astype(F32)
        total = total + c[:, :DH].astype(F32)
    else:
        u_out, total_out, keep = refs
    total_out[...] = total
    high, low = halves(total)
    u = mm(phi_high[...], high) + (mm(phi_high[...], low) + mm(phi_low[...], high))
    u_out[...] = u
    r = lax.rsqrt(jnp.mean(u * u, axis=1, keepdims=True) + norm_eps)
    attn = gain[...] * u * r
    weight_parts(direct, attn, ogs, out.at[DH:, :] if direct else None, keep)
    if direct:
        out[:DH, :] = soft_send[...]


def fold_kernel(keep_soft, keep_lin, got, keep, send):
    width = keep.shape[1]
    for rows, source in ((slice(0, DH), keep_soft), (slice(DH, 2 * DH), keep_lin)):
        keep[rows, :] = source[:, :width] + got[rows, :width].astype(F32)
        send[rows, :] = (source[:, width:] + got[rows, width:].astype(F32)).astype(BF)


def rows_kernel(keep, got, own, send, total):
    core, _, _ = places()
    half = DH // 2
    total[...] = keep[...] + got[...].astype(F32)
    for group in range(2):
        out = slice(group * half, (group + 1) * half)
        own[out, :] = total[at(group * DH + core * half, half), :]
        send[out, :] = total[at(group * DH + (1 - core) * half, half), :]


def lin_backward(u, total, dattn, phi_high, phi_low, slope, gain, dq, dstate):
    u_all = u[...]
    r = lax.rsqrt(jnp.mean(u_all * u_all, axis=1, keepdims=True) + norm_eps)
    lin_grad = gain[...] * dattn[:, DH:]
    grads = r * lin_grad - u_all * (r * r * r) * jnp.mean(lin_grad * u_all, axis=1, keepdims=True)
    high, low = halves(grads)
    dstate[...] = mm(phi_high[...], high, TN) + (mm(phi_high[...], low, TN) + mm(phi_low[...], high, TN))
    dq[...] = (mm3(grads, total[...], NT) * slope[...]).astype(BF)


def soft_backward(qs, ks, vs, probs, attn, dattn, dq_all, dk_all, dv_all):
    rows = qs.shape[0] // 2
    span = rows + 2 * HALF
    dk_all[...] = jnp.zeros_like(dk_all)
    dv_all[...] = jnp.zeros_like(dv_all)
    for block in range(2):
        here, window = slice(block * rows, (block + 1) * rows), slice(block * rows, block * rows + span)
        grad = dattn[here, :DH].astype(BF)
        share = probs[block]
        delta = jnp.sum(grad.astype(F32) * attn[here, :], axis=1, keepdims=True)
        dscore = (share * (mm(grad, vs[window, :], NT) - delta)).astype(BF)
        dq_all[here, :] = mm(dscore, ks[window, :]) * FACTOR
        dk_all[window, :] += mm(dscore, qs[here, :], TN) * FACTOR
        dv_all[window, :] += mm(share.astype(BF), grad, TN)


def backward_kernel(direct, *refs):
    if direct:
        sent, got = refs[:2]
        refs = refs[3:]
    else:
        weights = refs[0]
        refs = refs[1:]
    (ogs, u, total, phi_high, phi_low, slope, gain, qs, ks, vs, probs, attn,
     dq_lin, dstate, dq_soft, dk_soft, dv_soft, dattn, *scratch) = refs
    if direct:
        _, _, dp = places()
        way = links(True)
        weights = scratch[0]
        width = weights.shape[1] // 4
        for source, index, step in (
            (sent, 0, 0), (sent, 1, way["step"]), (got, 0, way["other"]), (got, 1, 3),
        ):
            weights[:, at((dp ^ step) * width, width)] = source[:, index * width : (index + 1) * width]
    dattn[...] = mm(ogs[...], weights[...], NT)
    lin_backward(u, total, dattn, phi_high, phi_low, slope, gain, dq_lin, dstate)
    soft_backward(qs, ks, vs, probs, attn, dattn, dq_soft, dk_soft, dv_soft)


def halo_part(out, first, dk_soft, dv_soft, side):
    start = side * (dk_soft.shape[0] - HALF)
    out[:, first : first + DH] = dk_soft[at(start), :].astype(BF)
    out[:, first + DH : first + 2 * DH] = dv_soft[at(start), :].astype(BF)


def halo_kernel(dk_soft, dv_soft, to_a, to_b):
    way = links(False)
    halo_part(to_a, 0, dk_soft, dv_soft, way["halo_a"])
    halo_part(to_b, 0, dk_soft, dv_soft, way["halo_b"])


def chunk_kernel(own, got, send, keep, heads):
    core, z, _ = places()
    way = links(True)
    half = own.shape[0] // 2
    for group in range(2):
        rows = slice(group * half, (group + 1) * half)
        heads[2 * group + core] = own[rows, :]
        heads[2 * group + 1 - core] = got[rows, :]
    for index, step in enumerate((way["first"], way["second"])):
        send[index * half : (index + 1) * half, :] = heads[z ^ step].astype(BF)
    for index, step in enumerate((0, 2)):
        keep[index * half : (index + 1) * half, :] = heads[z ^ step]


def second_kernel(keep, got, chunk, send):
    half = chunk.shape[0]
    chunk[...] = keep[:half, :] + got[:half, :].astype(F32)
    send[...] = (keep[half:, :] + got[half:, :].astype(F32)).astype(BF)


def halo_direct_kernel(dstate, dk_soft, dv_soft, to_a, to_b, to_c):
    way = links(True)
    halo_part(to_a, 0, dk_soft, dv_soft, way["halo_a"])
    halo_part(to_b, 0, dk_soft, dv_soft, way["halo_b"])
    low = dstate[...].astype(BF)
    to_a[:, 2 * DH :] = low
    to_b[:, 2 * DH :] = low
    to_c[...] = low


def weight_sum_kernel(scale, chunk, got, summed):
    summed[...] = (scale * (chunk[...] + got[...].astype(F32))).astype(summed.dtype)


def final_kernel(
    direct, dstate, mine, pair, dq_soft, dk_soft, dv_soft, dq_lin, a, b, *refs
):
    core, _, _ = places()
    way = links(direct)
    rows = mine.shape[0]
    total = dstate[...]
    own_out, pair_out, dk_all, dv_all = refs[-4:]
    if direct:
        total = total + a[:, 2 * DH :].astype(F32) + b[:, 2 * DH :].astype(F32)
        total = total + refs[0][...].astype(F32)
    for source, out, cols in ((dk_soft, dk_all, slice(0, DH)), (dv_soft, dv_all, slice(DH, 2 * DH))):
        out[...] = source[HALF : HALF + 2 * rows, :]
        out[at(way["block_a"] * rows, rows), :] += a[:, cols].astype(F32)
        out[at(way["block_b"] * rows, rows), :] += b[:, cols].astype(F32)
    high, low = halves(total)
    for source, out, place in ((mine, own_out, core), (pair, pair_out, 1 - core)):
        here = at(place * rows, rows)
        out[:, QS] = dq_soft[here, :].astype(BF)
        out[:, KS] = dk_all[here, :].astype(BF)
        out[:, VS] = dv_all[here, :].astype(BF)
        wide, values = source[:, KL].astype(F32), source[:, VL]
        out[:, QL] = dq_lin[here, :]
        out[:, KL] = ((mm(values, high, NT) + mm(values, low, NT)) * unit_slope(wide)).astype(BF)
        out[:, VL] = mm3(unit_plus(wide), total).astype(BF)


def output_kernel(own, pair, dq, dk, dv):
    core, _, _ = places()
    for source, first in ((own, core * DH), (pair, (1 - core) * DH)):
        for index, out in enumerate((dq, dk, dv)):
            out[0, :, at(first)] = source[:, index * DH : (index + 1) * DH]
            out[0, :, at(SOFT + first)] = source[:, (3 + index) * DH : (4 + index) * DH]


def weight_join_kernel(both, got, _, out):
    _, _, dp = places()
    way = links(True)
    width = both.shape[1] // 2
    for source, index, step in ((both, 0, 0), (both, 1, way["step"]), (got, 0, way["other"]), (got, 1, 3)):
        out[:, at((dp ^ step) * width, width)] = source[:, index * width : (index + 1) * width].astype(F32)


def body(n_dp, n_z, queries, key_rows, value_rows, out_grad, out_weight, norm_gain):
    rows, model = out_grad.shape[1:]
    axes = ("z", "core")
    pair_perm = [(0, 1), (1, 0)]
    core = lax.axis_index("core")
    direct = n_z == HEADS and n_dp == 4
    width = model // n_dp
    half = DH // 2

    scale = 1.0 / math.sqrt(n_dp * n_z * 2 * rows)

    def over_core(value):
        return lax.ppermute(value, "core", pair_perm)

    def over_z(value, which, back=False):
        pairs = []
        for z in range(n_z):
            for c in range(2):
                if direct:
                    there = z ^ (1 + 2 * c, 3 - 2 * c, 2)[which]
                else:
                    there = (z + (1 if (which == 1) != back else -1)) % n_z
                pairs.append((2 * z + c, 2 * there + c))
        return lax.ppermute(value, axes, pairs)

    def over_dp(value, which):
        pairs = [
            (2 * d + c, 2 * (d ^ (1 + c, 2 - c)[which]) + c) for d in range(n_dp) for c in range(2)
        ]
        return lax.ppermute(value, ("dp", "core"), pairs)

    vmem = pl.BlockSpec(memory_space=pltpu.VMEM)

    def hbm(value):
        return pltpu.with_memory_space_constraint(value, pltpu.HBM)

    q_pair, k_pair, v_pair = over_core(queries), over_core(key_rows), over_core(value_rows)
    og_recv = over_core(out_grad[0])
    mine, og, w_part, gain = call(
        pack_kernel, "pack",
        [
            like((rows, 6 * DH), BF), like((rows, model), BF),
            like((out_weight.shape[0], width), BF), like((1, DH), F32),
        ],
        [hbm(x) for x in (queries, key_rows, value_rows, out_grad, out_weight, norm_gain)],
        scratch=[pltpu.SemaphoreType.DMA((9,))],
        spaces=[pl.BlockSpec(memory_space=pltpu.HBM)] * 6,
    )
    wide = 4 * DH if direct else 2 * DH
    state, pair, to_a, to_b, *rest = call(
        functools.partial(state_kernel, direct), "state",
        [like((DH, DH), F32), like((rows, 6 * DH), BF), like((rows, wide), BF), like((rows, wide), BF)]
        + [like((rows, 2 * DH), BF)] * direct,
        [mine, q_pair, k_pair, v_pair] + [w_part] * direct,
        flops=4 * 2 * rows * DH * DH,
    )
    if direct:
        a, b, c = over_z(to_a, 0), over_z(to_b, 1), [over_z(rest[0], 2)]
        w_keep, w_send = call(
            relay_kernel, "relay", [like((2, half, width), BF)] * 2, [w_part, a, b] + c,
            scratch=[pltpu.VMEM((HEADS, half, width), BF)],
        )
        w_own = call(
            w_rows_kernel, "w_rows", [like((2 * DH, width), BF)], [w_keep, over_core(w_send)]
        )[0]
        w_got = over_dp(w_own, 0)
    else:
        a, b, c = over_z(to_a, 0), over_z(to_b, 1), []
        state = lax.psum(state, "z")
        weights = lax.all_gather(out_weight, axes, axis=0, tiled=True).reshape(2, 2, DH, model)
        weights = [jnp.where(core == 0, weights[:, 0], weights[:, 1]).reshape(2 * DH, model)]

    span = 2 * rows + 2 * HALF
    keep_width = 2 * width if direct else model
    wg_flops = 2 * 2 * rows * DH * model
    tokens = like((2 * rows, DH), BF)
    qs, k_chip, v_chip, ogs, chip_scores, phi_high, phi_low, slope = call(
        prep_kernel, "prep",
        [
            tokens, tokens, tokens, like((2 * rows, model), BF), like((2, rows, 2 * rows), F32),
            tokens, tokens, like((2 * rows, DH), F32),
        ],
        [mine, pair, og, og_recv],
        flops=wg_flops // 4,
    )
    ks, vs, probs, attn, keep_soft, *soft_send = call(
        functools.partial(soft_forward_kernel, direct), "soft_forward",
        [
            like((span, DH), BF), like((span, DH), BF), like((2, rows, rows + 2 * HALF), F32),
            like((2 * rows, DH), F32), like((DH, keep_width), F32),
        ] + [like((DH, 2 * width), BF)] * direct,
        [qs, k_chip, v_chip, ogs, chip_scores, a, b],
        flops=wg_flops,
    )
    u, total, keep_lin, *sent = call(
        functools.partial(lin_forward_kernel, direct), "lin_forward",
        [like((2 * rows, DH), F32), like((DH, DH), F32), like((DH, keep_width), F32)]
        + [like((2 * DH, 2 * width), BF)] * direct,
        [state, phi_high, phi_low, ogs, gain] + ([a, b] + c + soft_send if direct else []),
        flops=wg_flops,
    )
    if direct:
        got = over_dp(sent[0], 0)
        keep, sent = call(
            fold_kernel, "fold", [like((2 * DH, width), F32), like((2 * DH, width), BF)],
            [keep_soft, keep_lin, got],
        )
        w_half = call(
            join_kernel, "w_half", [like((2 * DH, 2 * width), BF)], [w_own, w_got, sent]
        )[0]
        weights = [w_half, over_dp(w_half, 1)]
        got = over_dp(sent, 1)
        row_own, row_send = call(
            rows_kernel, "rows", [like((2 * half, width), F32)] * 2, [keep, got],
            scratch=[pltpu.VMEM((2 * DH, width), F32)],
        )
        row_recv = over_core(row_send)
        piece_send, piece_keep = call(
            chunk_kernel, "chunk", [like((DH, width), BF), like((DH, width), F32)],
            [row_own, row_recv], scratch=[pltpu.VMEM((HEADS, half, width), F32)],
        )
        piece_got = over_z(piece_send, 0)
        weights.append(piece_keep)
    dq_lin, dstate, dq_soft, dk_soft, dv_soft = call(
        functools.partial(backward_kernel, direct), "backward",
        [
            tokens, like((DH, DH), F32),
            like((2 * rows, DH), F32), like((span, DH), F32), like((span, DH), F32),
        ],
        weights + [ogs, u, total, phi_high, phi_low, slope, gain, qs, ks, vs, probs, attn],
        scratch=[pltpu.VMEM((2 * rows, 2 * DH), F32)]
        + [pltpu.VMEM((2 * DH, model), BF)] * direct,
        flops=5 * wg_flops,
    )
    wide = 3 * DH if direct else 2 * DH
    if direct:
        chunk, piece = call(
            second_kernel, "second", [like((half, width), F32), like((half, width), BF)],
            [piece_keep, piece_got],
        )
        summed = call(
            functools.partial(weight_sum_kernel, scale), "weight_sum", [like((half, width), BF)],
            [chunk, over_z(piece, 2)],
        )[0]
        to_a, to_b, to_c = call(
            halo_direct_kernel, "halo", [like((rows, 3 * DH), BF)] * 2 + [like((DH, DH), BF)],
            [dstate, dk_soft, dv_soft],
        )
        a, b, c = over_z(to_a, 0), over_z(to_b, 1), [over_z(to_c, 2)]
        got = over_dp(summed, 0)
        both = call(join_kernel, "both", [like((half, 2 * width), BF)], [summed, got])[0]
        gathered = over_dp(both, 1)
    else:
        to_a, to_b = call(halo_kernel, "halo", [like((rows, 2 * DH), BF)] * 2, [dk_soft, dv_soft])
        a, b = over_z(to_a, 0, True), over_z(to_b, 1, True)
    if not direct:
        dstate = lax.psum(dstate, "z")
        groups = jnp.stack([keep_soft, keep_lin])
        slots = jnp.stack([jnp.where(core == head, groups, 0.0) for head in range(2)], axis=1)
        local = lax.psum_scatter(
            slots.reshape(HEADS * DH, model), axes, scatter_dimension=0, tiled=True
        )
        weight_grad = lax.psum(local, "dp") * scale
    own_out, to_pair = call(
        functools.partial(final_kernel, direct), "final",
        [like((rows, 6 * DH), BF), like((rows, 6 * DH), BF)],
        [dstate, mine, pair, dq_soft, dk_soft, dv_soft, dq_lin, a, b]
        + (c + [both] if direct else []),
        scratch=[pltpu.VMEM((2 * rows, DH), F32)] * 2,
        flops=wg_flops // 4,
    )
    from_pair = over_core(to_pair)
    shape = like((1, rows, HEADS * DH), BF)
    dq, dk, dv = call(output_kernel, "outputs", [shape] * 3, [own_out, from_pair])
    if direct:
        weight_grad = call(
            weight_join_kernel, "weight_join", [like((half, model), F32)], [both, gathered, hbm(dq)],
            spaces=[vmem, vmem, pl.BlockSpec(memory_space=pltpu.HBM)],
        )[0]
    return dq, dk, dv, weight_grad


def solution(mesh):
    n_dp, n_seq = mesh.shape["dp"], mesh.shape["seq"]
    blocks = Mesh(mesh.devices.reshape(n_dp, n_seq // 2, 2), ("dp", "z", "core"))
    tokens, heads = P("dp", ("z", "core"), None), P(("z", "core"), None)
    return jax.shard_map(
        functools.partial(body, n_dp, n_seq // 2),
        mesh=blocks,
        in_specs=(tokens, tokens, tokens, tokens, heads, P()),
        out_specs=(tokens, tokens, tokens, heads),
        check_vma=False,
    )
```
